32 devices in a mesh: seq: 4 (over y, x), fsdp: 8 (over z, core).
Axes of the slice: x: 2, y: 2, z: 4, core: 2. Of those that a mesh axis runs over, the one named last changes fastest.
Arguments:
- clip_tokens: float32 [16, 1024, 1024], P('fsdp', 'seq'), may hold values from -6 to 6
- patch_coords: int32 [3, 16, 1024], P(None, 'fsdp', 'seq'), may hold values from 0 to 15, as said below
- out_cotangent: float32 [16, 1024, 1024], P('fsdp', 'seq'), may hold values from -6 to 6
- vector_params: float32 [2, 13312], P(None, 'fsdp'), may hold values from -0.6 to 1.4, as said below
- qkv_weight: float32 [2, 1024, 3072], P(None, 'fsdp'), may hold values from -0.1875 to 0.1875
- proj_weight: float32 [2, 1024, 1024], P(None, 'fsdp'), may hold values from -0.75 to 0.75
- up_weight: float32 [2, 1024, 4096], P(None, 'fsdp'), may hold values from -0.1875 to 0.1875
- down_weight: float32 [2, 4096, 1024], P(None, 'fsdp'), may hold values from -0.09375 to 0.09375
- first_vector: float32 [2, 13312], P(None, 'fsdp'), may hold values from -1 to 1
- first_qkv: float32 [2, 1024, 3072], P(None, 'fsdp'), may hold values from -1 to 1
- first_proj: float32 [2, 1024, 1024], P(None, 'fsdp'), may hold values from -1 to 1
- first_up: float32 [2, 1024, 4096], P(None, 'fsdp'), may hold values from -1 to 1
- first_down: float32 [2, 4096, 1024], P(None, 'fsdp'), may hold values from -1 to 1
- second_vector: float32 [2, 13312], P(None, 'fsdp'), may hold values from 0.005 to 0.1
- second_qkv: float32 [2, 1024, 3072], P(None, 'fsdp'), may hold values from 0.005 to 0.1
- second_proj: float32 [2, 1024, 1024], P(None, 'fsdp'), may hold values from 0.005 to 0.1
- second_up: float32 [2, 1024, 4096], P(None, 'fsdp'), may hold values from 0.005 to 0.1
- second_down: float32 [2, 4096, 1024], P(None, 'fsdp'), may hold values from 0.005 to 0.1
Outputs:
- block_output: float32 [16, 1024, 1024], P('fsdp', 'seq')
- input_grad: float32 [16, 1024, 1024], P('fsdp', 'seq')
- grad_vector: float32 [2, 13312], P(None, 'fsdp')
- grad_qkv: float32 [2, 1024, 3072], P(None, 'fsdp')
- grad_proj: float32 [2, 1024, 1024], P(None, 'fsdp')
- grad_up: float32 [2, 1024, 4096], P(None, 'fsdp')
- grad_down: float32 [2, 4096, 1024], P(None, 'fsdp')
- grad_norm: float32 [1], replicated
- new_first_vector: float32 [2, 13312], P(None, 'fsdp')
- new_first_qkv: float32 [2, 1024, 3072], P(None, 'fsdp')
- new_first_proj: float32 [2, 1024, 1024], P(None, 'fsdp')
- new_first_up: float32 [2, 1024, 4096], P(None, 'fsdp')
- new_first_down: float32 [2, 4096, 1024], P(None, 'fsdp')
- new_second_vector: float32 [2, 13312], P(None, 'fsdp')
- new_second_qkv: float32 [2, 1024, 3072], P(None, 'fsdp')
- new_second_proj: float32 [2, 1024, 1024], P(None, 'fsdp')
- new_second_up: float32 [2, 1024, 4096], P(None, 'fsdp')
- new_second_down: float32 [2, 4096, 1024], P(None, 'fsdp')
- new_vector: float32 [2, 13312], P(None, 'fsdp')
- new_qkv: float32 [2, 1024, 3072], P(None, 'fsdp')
- new_proj: float32 [2, 1024, 1024], P(None, 'fsdp')
- new_up: float32 [2, 1024, 4096], P(None, 'fsdp')
- new_down: float32 [2, 4096, 1024], P(None, 'fsdp')
- copy_vector: bfloat16 [2, 13312], P(None, 'fsdp')
- copy_qkv: bfloat16 [2, 1024, 3072], P(None, 'fsdp')
- copy_proj: bfloat16 [2, 1024, 1024], P(None, 'fsdp')
- copy_up: bfloat16 [2, 1024, 4096], P(None, 'fsdp')
- copy_down: bfloat16 [2, 4096, 1024], P(None, 'fsdp')
The draws below stay inside these ranges and needn't reach their ends.
Inputs may be any that keep to these rules, and one draw needn't show every extreme that they name: patch_coords[0] is a token's frame among 8, patch_coords[1] and [2] its row and column among 16; the 1024 patches of a clip are distinct and in raster order. `vector_params`: gains lie within 0.6 to 1.4, biases within -0.6 to 0.6.
All inputs are finite; a program needn't handle non-finite values.
Results may differ from the reference program's by a relative error of at most 0.01.
The reference program's roundings to bfloat16 on the way count: a program that leaves them out, or rounds other values in their place, can miss the bound.
Values may be sent and summed in bfloat16 or wider, within the bound.
A program may use at most 576 MiB of HBM per device.

```python
import math
import jax
import jax.numpy as jnp
from jax import lax

D = 1024
HEADS = 16
HEAD_DIM = 64
FF = 4096
LAYERS = 2
SEQ_LEN = 1024
SIDE = 16
CLIPS = 16
FRAMES = 8
VEC = 13312


def draw_patch_coords(key, part):
    grid_cells = FRAMES * SIDE * SIDE
    clip_keys = jax.random.split(key, CLIPS)

    def one_clip(clip_key):
        chosen = jnp.sort(jax.random.permutation(clip_key, grid_cells)[:SEQ_LEN])
        frame_index = chosen // (SIDE * SIDE)
        row_index = chosen // SIDE % SIDE
        column_index = chosen % SIDE
        return jnp.stack([frame_index, row_index, column_index])
    per_clip = jax.vmap(one_clip)(clip_keys)
    return jnp.transpose(per_clip, (1, 0, 2)).astype(jnp.int32)


def draw_vector_params(key, part):
    gain_key = jax.random.fold_in(key, 11)
    bias_key = jax.random.fold_in(key, 23)
    width_total = 9 * D + FF
    positions = jnp.arange(width_total)
    is_gain = jnp.logical_or(positions < D, jnp.logical_and(positions >= 2 * D, positions < 3 * D))
    gains = 1.0 + jax.random.uniform(gain_key, (LAYERS, width_total), jnp.float32, -0.4, 0.4)
    biases = jax.random.uniform(bias_key, (LAYERS, width_total), jnp.float32, -0.6, 0.6)
    return jnp.where(is_gain[None, :], gains, biases).astype(jnp.float32)


def steps_of(rng, extent, shards, smallest, high):
    gain, own = 1.0, jax.random.fold_in(rng, 6)
    for dim, parts in shards:
        heights = jnp.exp(jax.random.uniform(jax.random.fold_in(own, dim), (parts,), jnp.float32, smallest / len(shards), high / len(shards)))
        gain = gain * jnp.repeat(heights, extent[dim] // parts).reshape([-1 if axis == dim else 1 for axis in range(len(extent))])
    return gain


def normal_values(key, extent, scale, reach, cuts=(), held_as=jnp.bfloat16):
    level = steps_of(key, extent, cuts, -0.22, 0.18) if cuts else 1.0
    drawn = jax.random.normal(key, extent, jnp.float32) * scale * level
    return jnp.minimum(jnp.maximum(drawn, -reach), reach).astype(held_as)


def setup_inputs(seed: int = 0) -> dict:
    splits = jax.random.split(jax.random.key(seed), 19)
    return {
        "clip_tokens": normal_values(splits[0], (CLIPS, SEQ_LEN, D), 1.0, 6.0, ((0, 8), (1, 4)), jnp.float32),
        "patch_coords": draw_patch_coords(jax.random.fold_in(splits[18], 71), 0),
        "out_cotangent": normal_values(splits[2], (CLIPS, SEQ_LEN, D), 1.0, 6.0, ((0, 8), (1, 4)), jnp.float32),
        "vector_params": draw_vector_params(jax.random.fold_in(splits[18], 71), 0),
        "qkv_weight": normal_values(splits[4], (LAYERS, D, 3 * D), D ** -0.5, 0.1875, ((1, 8),), jnp.float32),
        "proj_weight": normal_values(splits[5], (LAYERS, D, D), (D // 16) ** -0.5, 0.75, ((1, 8),), jnp.float32),
        "up_weight": normal_values(splits[6], (LAYERS, D, FF), D ** -0.5, 0.1875, ((1, 8),), jnp.float32),
        "down_weight": normal_values(splits[7], (LAYERS, FF, D), FF ** -0.5, 0.09375, ((1, 8),), jnp.float32),
        "first_vector": normal_values(splits[8], (LAYERS, VEC), 0.2, 1.0, ((1, 8),), jnp.float32),
        "first_qkv": normal_values(splits[9], (LAYERS, D, 3 * D), 0.2, 1.0, ((1, 8),), jnp.float32),
        "first_proj": normal_values(splits[10], (LAYERS, D, D), 0.2, 1.0, ((1, 8),), jnp.float32),
        "first_up": normal_values(splits[11], (LAYERS, D, FF), 0.2, 1.0, ((1, 8),), jnp.float32),
        "first_down": normal_values(splits[12], (LAYERS, FF, D), 0.2, 1.0, ((1, 8),), jnp.float32),
        "second_vector": jnp.clip(jnp.exp(math.log(0.1) - 2.9957323 * jax.random.uniform(splits[13], (LAYERS, VEC), jnp.float32) ** steps_of(splits[13], (LAYERS, VEC), ((1, 8),), -0.2, 0.2)), 0.005, 0.1),
        "second_qkv": jnp.clip(jnp.exp(math.log(0.1) - 2.9957323 * jax.random.uniform(splits[14], (LAYERS, D, 3 * D), jnp.float32) ** steps_of(splits[14], (LAYERS, D, 3 * D), ((1, 8),), -0.2, 0.2)), 0.005, 0.1),
        "second_proj": jnp.clip(jnp.exp(math.log(0.1) - 2.9957323 * jax.random.uniform(splits[15], (LAYERS, D, D), jnp.float32) ** steps_of(splits[15], (LAYERS, D, D), ((1, 8),), -0.2, 0.2)), 0.005, 0.1),
        "second_up": jnp.clip(jnp.exp(math.log(0.1) - 2.9957323 * jax.random.uniform(splits[16], (LAYERS, D, FF), jnp.float32) ** steps_of(splits[16], (LAYERS, D, FF), ((1, 8),), -0.2, 0.2)), 0.005, 0.1),
        "second_down": jnp.clip(jnp.exp(math.log(0.1) - 2.9957323 * jax.random.uniform(splits[17], (LAYERS, FF, D), jnp.float32) ** steps_of(splits[17], (LAYERS, FF, D), ((1, 8),), -0.2, 0.2)), 0.005, 0.1),
    }


BETA_ONE = 0.5
BETA_TWO = 0.75
LEARN_RATE = 0.1
DECAY_RATE = 0.1
CLIP_RATIO = 0.2
ADAM_EPS = 1e-08
ROPE_BASE = 10000.0

@jax.custom_vjp
def low(v):
    return lax.optimization_barrier(v.astype(jnp.bfloat16)).astype(jnp.float32)

@jax.custom_vjp
def low_back(v):
    return v

def low_keep(v):
    return (low(v), None)

def low_pass(kept, grad):
    return (grad,)

def back_keep(v):
    return (v, None)

def back_low(kept, grad):
    return (low(grad),)
low.defvjp(low_keep, low_pass)
low_back.defvjp(back_keep, back_low)

def matmul_high(left_side, right_side):
    return jnp.dot(left_side, right_side, precision=lax.Precision.HIGHEST, preferred_element_type=jnp.float32)

def pieces(vector):
    return (vector[0:D], vector[D:2 * D], vector[2 * D:3 * D], vector[3 * D:4 * D], vector[4 * D:5 * D], vector[5 * D:6 * D], vector[6 * D:9 * D], vector[9 * D:])

def layer_norm(hidden, ln_gain, ln_shift):
    center = hidden - lax.optimization_barrier(jnp.mean(hidden, axis=-1, keepdims=True))
    spread = lax.optimization_barrier(jnp.mean(center * center, axis=-1, keepdims=True))
    return center * lax.rsqrt(spread + 1e-06) * ln_gain + ln_shift

def gelu_exact(upward):
    return 0.5 * upward * (1.0 + jax.scipy.special.erf(upward * (1.0 / math.sqrt(2.0))))

def rotary_tables(coords_clip, pair_count):
    pair_index = jnp.arange(pair_count, dtype=jnp.int32)
    side_pairs = pair_count // 3
    time_pairs = pair_count - 2 * side_pairs
    in_time = pair_index < time_pairs
    in_height = jnp.logical_and(pair_index >= time_pairs, pair_index < time_pairs + side_pairs)
    offset = jnp.where(in_time, 0, jnp.where(in_height, time_pairs, time_pairs + side_pairs))
    seg_span = jnp.where(in_time, time_pairs, side_pairs)
    local_rank = (pair_index - offset).astype(jnp.float32)
    frequency = jnp.exp(-math.log(ROPE_BASE) * local_rank / seg_span.astype(jnp.float32))
    positions = coords_clip.astype(jnp.float32)
    chosen = jnp.where(in_time[None, :], positions[0][:, None], jnp.where(in_height[None, :], positions[1][:, None], positions[2][:, None]))
    angles = chosen * frequency[None, :]
    return (jnp.cos(angles), jnp.sin(angles))

def rotate(values_in, cosine, sine_table):
    half_width = values_in.shape[-1] // 2
    first_half = values_in[..., :half_width]
    second_half = values_in[..., half_width:]
    cos_wide = cosine[:, None, :]
    sin_wide = sine_table[:, None, :]
    return jnp.concatenate([first_half * cos_wide - second_half * sin_wide, first_half * sin_wide + second_half * cos_wide], axis=-1)

def attention(queries, key_rows, value_rows):
    raw_scores = jnp.einsum('qhd,khd->hqk', queries, key_rows, precision=lax.Precision.HIGHEST)
    scores = low_back(raw_scores) * HEAD_DIM ** (-0.5)
    row_max = lax.optimization_barrier(jnp.max(scores, axis=-1, keepdims=True))
    exponent = jnp.exp(scores - row_max)
    prob_rows = exponent / lax.optimization_barrier(jnp.sum(exponent, axis=-1, keepdims=True))
    mixed_rows = jnp.einsum('hqk,khd->qhd', low(prob_rows), value_rows, precision=lax.Precision.HIGHEST)
    return low_back(low(mixed_rows))

def layer_forward(hidden, cosine, sine_table, params):
    vector, qkv_w, proj_w, up_w, down_w = params
    gain_one, shift_one, gain_two, shift_two, proj_bias, down_bias, qkv_bias, up_bias = pieces(vector)
    row_count = hidden.shape[0]
    normed = low(layer_norm(hidden, gain_one, shift_one))
    qkv_all = low_back(matmul_high(normed, qkv_w)) + qkv_bias
    split_qkv = qkv_all.reshape(row_count, 3, HEADS, HEAD_DIM)
    queries = low_back(low(rotate(split_qkv[:, 0], cosine, sine_table)))
    key_rows = low_back(low(rotate(split_qkv[:, 1], cosine, sine_table)))
    value_rows = low_back(low(split_qkv[:, 2]))
    mixed_rows = attention(queries, key_rows, value_rows).reshape(row_count, D)
    after_attn = hidden + low_back(matmul_high(mixed_rows, proj_w)) + proj_bias
    normed_two = low(layer_norm(after_attn, gain_two, shift_two))
    upward = low_back(matmul_high(normed_two, up_w)) + up_bias
    active = low(gelu_exact(upward))
    return after_attn + low_back(matmul_high(active, down_w)) + down_bias

def block_forward(hidden, coords_clip, params):
    cosine, sine_table = rotary_tables(coords_clip, HEAD_DIM // 2)
    for layer_idx in range(LAYERS):
        hidden = layer_forward(hidden, cosine, sine_table, tuple((param_item[layer_idx] for param_item in params)))
    return hidden

def adam_update(master, grad_item, first_old, second_old, factor):
    clipped = grad_item * factor
    first_new = BETA_ONE * first_old + (1.0 - BETA_ONE) * clipped
    second_new = BETA_TWO * second_old + (1.0 - BETA_TWO) * clipped * clipped
    updated = master - LEARN_RATE * (first_new / (jnp.sqrt(second_new) + ADAM_EPS) + DECAY_RATE * master)
    return (first_new, second_new, updated)

def reference(clip_tokens, patch_coords, out_cotangent, vector_params, qkv_weight, proj_weight, up_weight, down_weight, first_vector, first_qkv, first_proj, first_up, first_down, second_vector, second_qkv, second_proj, second_up, second_down):
    masters = (vector_params, qkv_weight, proj_weight, up_weight, down_weight)
    firsts = (first_vector, first_qkv, first_proj, first_up, first_down)
    seconds = (second_vector, second_qkv, second_proj, second_up, second_down)
    zero_grads = tuple((jnp.zeros_like(master) for master in masters))

    def one_clip(totals, clip_in):
        tokens_in, coords_clip, cot_in = clip_in

        def forward_clip(tokens_arg, params_arg):
            return block_forward(tokens_arg, coords_clip, tuple((low(master) for master in params_arg)))
        result, pullback = jax.vjp(forward_clip, tokens_in, masters)
        token_grad, param_grads = pullback(cot_in)
        totals = tuple((left_part + right_part for left_part, right_part in zip(totals, param_grads)))
        return (totals, (result, token_grad))
    summed, (block_output, input_grad) = lax.scan(one_clip, zero_grads, (clip_tokens, jnp.transpose(patch_coords, (1, 0, 2)), out_cotangent))
    grad_all = tuple((total_item / CLIPS for total_item in summed))
    squares = sum((jnp.sum(grad_item * grad_item) for grad_item in grad_all))
    norm_value = jnp.sqrt(squares)
    param_count = sum((master.size for master in masters))
    factor = jnp.minimum(1.0, CLIP_RATIO * math.sqrt(float(param_count)) / (norm_value + 1e-06))
    updates = [adam_update(master, grad_item, first_old, second_old, factor) for master, grad_item, first_old, second_old in zip(masters, grad_all, firsts, seconds)]
    return (block_output, input_grad, grad_all[0], grad_all[1], grad_all[2], grad_all[3], grad_all[4], norm_value.reshape(1), updates[0][0], updates[1][0], updates[2][0], updates[3][0], updates[4][0], updates[0][1], updates[1][1], updates[2][1], updates[3][1], updates[4][1], updates[0][2], updates[1][2], updates[2][2], updates[3][2], updates[4][2], updates[0][2].astype(jnp.bfloat16), updates[1][2].astype(jnp.bfloat16), updates[2][2].astype(jnp.bfloat16), updates[3][2].astype(jnp.bfloat16), updates[4][2].astype(jnp.bfloat16))
```

```python
from functools import partial
import math

import jax
import jax.numpy as jnp
from jax import lax
from jax.experimental import pallas as pl
from jax.experimental.pallas import tpu as pltpu
from jax.sharding import PartitionSpec as P

D = 1024
HEADS = 16
HEAD_DIM = 64


BETA_ONE = 0.5
BETA_TWO = 0.75
LEARN_RATE = 0.1
DECAY_RATE = 0.1
CLIP_RATIO = 0.2
ADAM_EPS = 1e-08
ROPE_BASE = 10000.0


def pieces(vector):
    return (
        vector[0:D],
        vector[D : 2 * D],
        vector[2 * D : 3 * D],
        vector[3 * D : 4 * D],
        vector[4 * D : 5 * D],
        vector[5 * D : 6 * D],
        vector[6 * D : 9 * D],
        vector[9 * D :],
    )


def layer_norm(hidden, ln_gain, ln_shift):
    center = hidden - jnp.mean(hidden, axis=-1, keepdims=True)
    spread = jnp.mean(center * center, axis=-1, keepdims=True)
    return center * lax.rsqrt(spread + 1e-06) * ln_gain + ln_shift


def gelu_exact(upward):
    return 0.5 * upward * (1.0 + jax.scipy.special.erf(upward * (1.0 / math.sqrt(2.0))))


def rotary_tables(coords_clip, pair_count):
    pair_index = jnp.arange(pair_count, dtype=jnp.int32)
    side_pairs = pair_count // 3
    time_pairs = pair_count - 2 * side_pairs
    in_time = pair_index < time_pairs
    in_height = jnp.logical_and(pair_index >= time_pairs, pair_index < time_pairs + side_pairs)
    offset = jnp.where(in_time, 0, jnp.where(in_height, time_pairs, time_pairs + side_pairs))
    seg_span = jnp.where(in_time, time_pairs, side_pairs)
    local_rank = (pair_index - offset).astype(jnp.float32)
    frequency = jnp.exp(-math.log(ROPE_BASE) * local_rank / seg_span.astype(jnp.float32))
    positions = coords_clip.astype(jnp.float32)
    chosen = jnp.where(
        in_time[None, :],
        positions[0][:, None],
        jnp.where(in_height[None, :], positions[1][:, None], positions[2][:, None]),
    )
    angles = chosen * frequency[None, :]
    return (jnp.cos(angles), jnp.sin(angles))


def rotate(values_in, cosine, sine_table):
    half_width = values_in.shape[-1] // 2
    first_half = values_in[..., :half_width]
    second_half = values_in[..., half_width:]
    cos_wide = cosine[:, None, :]
    sin_wide = sine_table[:, None, :]
    return jnp.concatenate(
        [
            first_half * cos_wide - second_half * sin_wide,
            first_half * sin_wide + second_half * cos_wide,
        ],
        axis=-1,
    )


def attend_forward(queries, key_rows, value_rows):
    full_len = queries.shape[0]
    block_rows = min(512, full_len)
    score_scale = HEAD_DIM ** (-0.5)
    query_blocks = queries.reshape(
        full_len // block_rows, block_rows, queries.shape[1], queries.shape[2]
    )

    def one_block(query_block):
        scores = (
            jnp.einsum("qhd,khd->hqk", query_block, key_rows, preferred_element_type=jnp.float32)
            * score_scale
        )
        row_max = jnp.max(scores, axis=-1, keepdims=True)
        exponent = jnp.exp(scores - row_max)
        row_total = jnp.sum(exponent, axis=-1, keepdims=True)
        prob_low = (exponent / row_total).astype(jnp.bfloat16)
        mixed_rows = jnp.einsum(
            "hqk,khd->qhd", prob_low, value_rows, preferred_element_type=jnp.float32
        )
        return (mixed_rows, row_max[..., 0] + jnp.log(row_total[..., 0]))

    mixed_rows, log_sums = lax.map(one_block, query_blocks)
    return (mixed_rows.reshape(queries.shape), log_sums)


def attend_backward(queries, key_rows, value_rows, log_sums, head_grad):
    full_len = queries.shape[0]
    block_rows = min(512, full_len)
    score_scale = HEAD_DIM ** (-0.5)
    block_shape = (full_len // block_rows, block_rows, queries.shape[1], queries.shape[2])

    def one_block(carry, block_in):
        key_grad, value_grad = carry
        query_block, grad_block, lse_block = block_in
        scores = (
            jnp.einsum("qhd,khd->hqk", query_block, key_rows, preferred_element_type=jnp.float32)
            * score_scale
        )
        prob_rows = jnp.exp(scores - lse_block[..., None])
        prob_low = prob_rows.astype(jnp.bfloat16)
        value_grad = value_grad + jnp.einsum(
            "hqk,qhd->khd", prob_low, grad_block, preferred_element_type=jnp.float32
        )
        prob_grad = jnp.einsum(
            "qhd,khd->hqk", grad_block, value_rows, preferred_element_type=jnp.float32
        )
        score_grad = prob_rows * (
            prob_grad - jnp.sum(prob_rows * prob_grad, axis=-1, keepdims=True)
        )
        score_low = (score_grad * score_scale).astype(jnp.bfloat16)
        query_grad = jnp.einsum(
            "hqk,khd->qhd", score_low, key_rows, preferred_element_type=jnp.float32
        )
        key_grad = key_grad + jnp.einsum(
            "hqk,qhd->khd", score_low, query_block, preferred_element_type=jnp.float32
        )
        return ((key_grad, value_grad), query_grad)

    zero_heads = jnp.zeros(queries.shape, jnp.float32)
    (key_grad, value_grad), query_grad = lax.scan(
        one_block,
        (zero_heads, zero_heads),
        (queries.reshape(block_shape), head_grad.reshape(block_shape), log_sums),
    )
    return (query_grad.reshape(queries.shape), key_grad, value_grad)


def layer_forward(hidden, cosine, sine_table, weights, seq_parts):
    vector_low, qkv_w, proj_w, up_w, down_w = weights
    gain_one, shift_one, gain_two, shift_two, proj_bias, down_bias, qkv_bias, up_bias = pieces(
        vector_low.astype(jnp.float32)
    )
    row_count = hidden.shape[0]
    local_heads = HEADS // seq_parts
    normed = layer_norm(hidden, gain_one, shift_one).astype(jnp.bfloat16)
    qkv_all = jnp.dot(normed, qkv_w, preferred_element_type=jnp.float32) + qkv_bias
    split_qkv = qkv_all.reshape(row_count, 3, HEADS, HEAD_DIM)
    stacked = jnp.stack(
        [
            rotate(split_qkv[:, 0], cosine, sine_table),
            rotate(split_qkv[:, 1], cosine, sine_table),
            split_qkv[:, 2],
        ],
        axis=1,
    ).astype(jnp.bfloat16)
    packed = stacked.reshape(row_count, 3, seq_parts, local_heads * HEAD_DIM)
    by_heads = lax.all_to_all(packed, "seq", split_axis=2, concat_axis=0, tiled=True)
    full_len = by_heads.shape[0]
    by_heads = by_heads.reshape(full_len, 3, local_heads, HEAD_DIM)
    mixed_rows, log_sums = attend_forward(by_heads[:, 0], by_heads[:, 1], by_heads[:, 2])
    mixed_low = mixed_rows.astype(jnp.bfloat16).reshape(full_len, 1, local_heads * HEAD_DIM)
    by_tokens = lax.all_to_all(mixed_low, "seq", split_axis=0, concat_axis=1, tiled=True).reshape(
        row_count, D
    )
    after_attn = hidden + jnp.dot(by_tokens, proj_w, preferred_element_type=jnp.float32) + proj_bias
    normed_two = layer_norm(after_attn, gain_two, shift_two).astype(jnp.bfloat16)
    upward = jnp.dot(normed_two, up_w, preferred_element_type=jnp.float32) + up_bias
    active = gelu_exact(upward).astype(jnp.bfloat16)
    result = after_attn + jnp.dot(active, down_w, preferred_element_type=jnp.float32) + down_bias
    saved_state = (
        hidden,
        normed,
        by_heads,
        log_sums,
        by_tokens,
        after_attn,
        normed_two,
        upward,
        active,
    )
    return (result, saved_state)


def layer_backward(grad_out, saved_state, weights, cosine, sine_table, seq_parts):
    vector_low, qkv_w, proj_w, up_w, down_w = weights
    gain_one, shift_one, gain_two, shift_two, proj_bias, down_bias, qkv_bias, up_bias = pieces(
        vector_low.astype(jnp.float32)
    )
    hidden, normed, by_heads, log_sums, by_tokens, after_attn, normed_two, upward, active = (
        saved_state
    )
    row_count = hidden.shape[0]
    local_heads = HEADS // seq_parts
    down_bias_grad = jnp.sum(grad_out, axis=0)
    grad_low = grad_out.astype(jnp.bfloat16)
    down_grad = jnp.dot(active.T, grad_low, preferred_element_type=jnp.float32)
    active_grad = jnp.dot(grad_low, down_w.T, preferred_element_type=jnp.float32)
    gelu_value, gelu_pull = jax.vjp(gelu_exact, upward)
    upward_grad = gelu_pull(active_grad)[0]
    up_bias_grad = jnp.sum(upward_grad, axis=0)
    upward_low = upward_grad.astype(jnp.bfloat16)
    up_grad = jnp.dot(normed_two.T, upward_low, preferred_element_type=jnp.float32)
    normed_two_grad = jnp.dot(upward_low, up_w.T, preferred_element_type=jnp.float32)
    norm_value_two, norm_pull_two = jax.vjp(layer_norm, after_attn, gain_two, shift_two)
    attn_in_grad, gain_two_grad, shift_two_grad = norm_pull_two(normed_two_grad)
    after_grad = grad_out + attn_in_grad
    proj_bias_grad = jnp.sum(after_grad, axis=0)
    after_low = after_grad.astype(jnp.bfloat16)
    proj_grad = jnp.dot(by_tokens.T, after_low, preferred_element_type=jnp.float32)
    mixed_grad = jnp.dot(after_low, proj_w.T, preferred_element_type=jnp.float32).astype(
        jnp.bfloat16
    )
    head_grad = lax.all_to_all(
        mixed_grad.reshape(row_count, seq_parts, local_heads * HEAD_DIM),
        "seq",
        split_axis=1,
        concat_axis=0,
        tiled=True,
    )
    full_len = head_grad.shape[0]
    head_grad = head_grad.reshape(full_len, local_heads, HEAD_DIM)
    query_grad, key_grad, value_grad = attend_backward(
        by_heads[:, 0], by_heads[:, 1], by_heads[:, 2], log_sums, head_grad
    )
    stacked_grad = (
        jnp.stack([query_grad, key_grad, value_grad], axis=1)
        .astype(jnp.bfloat16)
        .reshape(full_len, 3, 1, local_heads * HEAD_DIM)
    )
    token_grad = (
        lax.all_to_all(stacked_grad, "seq", split_axis=0, concat_axis=2, tiled=True)
        .reshape(row_count, 3, HEADS, HEAD_DIM)
        .astype(jnp.float32)
    )
    pair_grad_in = token_grad[:, :2].reshape(row_count, 2 * HEADS, HEAD_DIM)
    rotated_value, rotate_pull = jax.vjp(
        partial(rotate, cosine=cosine, sine_table=sine_table), pair_grad_in
    )
    pair_grad = rotate_pull(pair_grad_in)[0].reshape(row_count, 2, HEADS, HEAD_DIM)
    qkv_grad = jnp.concatenate([pair_grad, token_grad[:, 2:]], axis=1).reshape(row_count, 3 * D)
    qkv_bias_grad = jnp.sum(qkv_grad, axis=0)
    qkv_low = qkv_grad.astype(jnp.bfloat16)
    qkv_w_grad = jnp.dot(normed.T, qkv_low, preferred_element_type=jnp.float32)
    normed_grad = jnp.dot(qkv_low, qkv_w.T, preferred_element_type=jnp.float32)
    norm_value_one, norm_pull_one = jax.vjp(layer_norm, hidden, gain_one, shift_one)
    in_grad, gain_one_grad, shift_one_grad = norm_pull_one(normed_grad)
    input_grad = after_grad + in_grad
    vector_grad = jnp.concatenate(
        [
            gain_one_grad,
            shift_one_grad,
            gain_two_grad,
            shift_two_grad,
            proj_bias_grad,
            down_bias_grad,
            qkv_bias_grad,
            up_bias_grad,
        ]
    )
    return (input_grad, (vector_grad, qkv_w_grad, proj_grad, up_grad, down_grad))


def adam_update(master, grad_item, first_old, second_old, factor):
    clipped = grad_item * factor
    first_new = BETA_ONE * first_old + (1.0 - BETA_ONE) * clipped
    second_new = BETA_TWO * second_old + (1.0 - BETA_TWO) * clipped * clipped
    updated = master - LEARN_RATE * (
        first_new / (jnp.sqrt(second_new) + ADAM_EPS) + DECAY_RATE * master
    )
    return (first_new, second_new, updated)


def general_device(
    clip_tokens,
    patch_coords,
    out_cotangent,
    vector_params,
    qkv_weight,
    proj_weight,
    up_weight,
    down_weight,
    first_vector,
    first_qkv,
    first_proj,
    first_up,
    first_down,
    second_vector,
    second_qkv,
    second_proj,
    second_up,
    second_down,
):
    masters = (vector_params, qkv_weight, proj_weight, up_weight, down_weight)
    firsts = (first_vector, first_qkv, first_proj, first_up, first_down)
    seconds = (second_vector, second_qkv, second_proj, second_up, second_down)
    lowered = tuple((master.astype(jnp.bfloat16) for master in masters))
    layer_count = vector_params.shape[0]
    batch_local = clip_tokens.shape[0]
    seq_parts = lax.axis_size("seq")
    fsdp_parts = lax.axis_size("fsdp")
    grad_accum = tuple(
        (
            jnp.zeros((layer_count, master.shape[1] * fsdp_parts) + master.shape[2:], jnp.float32)
            for master in masters
        )
    )
    output_rows = []
    input_rows = []
    for batch_idx in range(batch_local):
        cosine, sine_table = rotary_tables(patch_coords[:, batch_idx], HEAD_DIM // 2)
        hidden = clip_tokens[batch_idx]
        saved_layers = []
        for layer_idx in range(layer_count):
            weights = (
                lax.all_gather(lowered[0][layer_idx], "fsdp", axis=0, tiled=True),
                lax.all_gather(lowered[1][layer_idx], "fsdp", axis=0, tiled=True),
                lax.all_gather(lowered[2][layer_idx], "fsdp", axis=0, tiled=True),
                lax.all_gather(lowered[3][layer_idx], "fsdp", axis=0, tiled=True),
                lax.all_gather(lowered[4][layer_idx], "fsdp", axis=0, tiled=True),
            )
            hidden, saved_state = layer_forward(hidden, cosine, sine_table, weights, seq_parts)
            saved_layers.append(saved_state)
        output_rows.append(hidden)
        grad_rows = out_cotangent[batch_idx]
        for layer_idx in reversed(range(layer_count)):
            weights = (
                lax.all_gather(lowered[0][layer_idx], "fsdp", axis=0, tiled=True),
                lax.all_gather(lowered[1][layer_idx], "fsdp", axis=0, tiled=True),
                lax.all_gather(lowered[2][layer_idx], "fsdp", axis=0, tiled=True),
                lax.all_gather(lowered[3][layer_idx], "fsdp", axis=0, tiled=True),
                lax.all_gather(lowered[4][layer_idx], "fsdp", axis=0, tiled=True),
            )
            grad_rows, layer_grads = layer_backward(
                grad_rows, saved_layers[layer_idx], weights, cosine, sine_table, seq_parts
            )
            grad_accum = tuple(
                (
                    accum_item.at[layer_idx].add(grad_item)
                    for accum_item, grad_item in zip(grad_accum, layer_grads)
                )
            )
        input_rows.append(grad_rows)
    shard_sums = (
        lax.psum_scatter(grad_accum[0], "fsdp", scatter_dimension=1, tiled=True),
        lax.psum_scatter(grad_accum[1], "fsdp", scatter_dimension=1, tiled=True),
        lax.psum_scatter(grad_accum[2], "fsdp", scatter_dimension=1, tiled=True),
        lax.psum_scatter(grad_accum[3], "fsdp", scatter_dimension=1, tiled=True),
        lax.psum_scatter(grad_accum[4], "fsdp", scatter_dimension=1, tiled=True),
    )
    seq_sums = lax.psum(
        (shard_sums[0], shard_sums[1], shard_sums[2], shard_sums[3], shard_sums[4]), "seq"
    )
    clip_count = batch_local * fsdp_parts
    grad_shards = tuple((sum_item / clip_count for sum_item in seq_sums))
    local_squares = sum((jnp.sum(grad_item * grad_item) for grad_item in grad_shards))
    squares_total = lax.psum(local_squares, "fsdp")
    norm_value = jnp.sqrt(squares_total)
    param_count = sum((master.size for master in masters)) * fsdp_parts
    factor = jnp.minimum(1.0, CLIP_RATIO * math.sqrt(float(param_count)) / (norm_value + 1e-06))
    updates = [
        adam_update(master, grad_item, first_old, second_old, factor)
        for master, grad_item, first_old, second_old in zip(masters, grad_shards, firsts, seconds)
    ]
    return (
        jnp.stack(output_rows),
        jnp.stack(input_rows),
        grad_shards[0],
        grad_shards[1],
        grad_shards[2],
        grad_shards[3],
        grad_shards[4],
        norm_value.reshape(1),
        updates[0][0],
        updates[1][0],
        updates[2][0],
        updates[3][0],
        updates[4][0],
        updates[0][1],
        updates[1][1],
        updates[2][1],
        updates[3][1],
        updates[4][1],
        updates[0][2],
        updates[1][2],
        updates[2][2],
        updates[3][2],
        updates[4][2],
        updates[0][2].astype(jnp.bfloat16),
        updates[1][2].astype(jnp.bfloat16),
        updates[2][2].astype(jnp.bfloat16),
        updates[3][2].astype(jnp.bfloat16),
        updates[4][2].astype(jnp.bfloat16),
    )


ROWS_Q = 256
PAIR = 2 * HEAD_DIM
BF = jnp.bfloat16
F32 = jnp.float32
VMEM_LIMIT = 56 * 1024 * 1024


def fits_fast(mesh):
    return dict(mesh.shape) == {"seq": 4, "fsdp": 8}


def swap_core(item):
    parts = lax.axis_size("fsdp")
    return lax.ppermute(item, "fsdp", [(idx, idx ^ 1) for idx in range(parts)])


def send_up(item):
    parts = lax.axis_size("fsdp")
    return lax.ppermute(item, "fsdp", [(idx, (idx + 2) % parts) for idx in range(parts)])


def swap_seq(item, mask):
    parts = lax.axis_size("seq")
    return lax.ppermute(item, "seq", [(idx, idx ^ mask) for idx in range(parts)])


def pick(item, index, axis=0):
    return lax.dynamic_index_in_dim(item, index, axis, keepdims=False)


def swap_halves(item):
    lane = lax.broadcasted_iota(jnp.int32, item.shape, 1)
    half = HEAD_DIM // 2
    width = item.shape[1]
    ahead = pltpu.roll(item, width - half, 1)
    behind = pltpu.roll(item, half, 1)
    return jnp.where(lane % HEAD_DIM < half, ahead, behind)


NT = (((1,), (1,)), ((), ()))


def head_mask(item, head):
    lane = lax.broadcasted_iota(jnp.int32, item.shape, 1)
    return jnp.where(lane // HEAD_DIM == head, item, jnp.zeros_like(item))


def attn_fwd_kernel(qkv_ref, cos_ref, sin_ref, mixed_ref, low_ref, lse_ref, qs_ref):
    cosine, sine = cos_ref[...], sin_ref[...]
    queries = qkv_ref[:, 0:PAIR]
    key_rows = qkv_ref[:, PAIR : 2 * PAIR]
    values = qkv_ref[:, 2 * PAIR : 3 * PAIR]
    queries = (queries * cosine + swap_halves(queries) * sine).astype(BF)
    key_rows = (key_rows * cosine + swap_halves(key_rows) * sine).astype(BF)
    low_ref[:, 0:PAIR] = queries
    low_ref[:, PAIR : 2 * PAIR] = key_rows
    low_ref[:, 2 * PAIR : 3 * PAIR] = values.astype(BF)
    qs_ref[...] = queries * jnp.asarray(HEAD_DIM**-0.5, BF)
    values_t = values.T.astype(BF)
    keys_by_head = [head_mask(key_rows, head) for head in range(2)]
    length = qs_ref.shape[0]

    @pl.loop(0, length // ROWS_Q)
    def _(step):
        rows = pl.ds(pl.multiple_of(step * ROWS_Q, ROWS_Q), ROWS_Q)
        block = qs_ref[rows, :]
        outs = []
        for head in range(2):
            scores = lax.dot_general(keys_by_head[head], block, NT, preferred_element_type=F32)
            top = jnp.max(scores, axis=0, keepdims=True)
            exponent = jnp.exp(scores - top)
            total = jnp.sum(exponent, axis=0, keepdims=True)
            lse_ref[0, head : head + 1, rows] = top + jnp.log(total)
            probs = (exponent * (1.0 / total)).astype(BF)
            outs.append(
                jnp.dot(
                    values_t[head * HEAD_DIM : (head + 1) * HEAD_DIM],
                    probs,
                    preferred_element_type=F32,
                )
            )
        mixed_ref[rows, :] = jnp.concatenate(outs, axis=0).T.astype(BF)


def attend(qkv_all, cos_wide, sin_wide):
    length, width = qkv_all.shape
    pairs = width // (3 * PAIR)
    table = pl.BlockSpec((length, PAIR), lambda pair: (0, 0))
    triple = pl.BlockSpec((length, 3 * PAIR), lambda pair: (0, pair))
    return pl.pallas_call(
        attn_fwd_kernel,
        grid=(pairs,),
        in_specs=[triple, table, table],
        out_specs=[
            pl.BlockSpec((length, PAIR), lambda pair: (0, pair)),
            triple,
            pl.BlockSpec((1, 8, length), lambda pair: (pair, 0, 0)),
        ],
        out_shape=[
            jax.ShapeDtypeStruct((length, pairs * PAIR), BF),
            jax.ShapeDtypeStruct((length, width), BF),
            jax.ShapeDtypeStruct((pairs, 8, length), F32),
        ],
        scratch_shapes=[pltpu.VMEM((length, PAIR), BF)],
        compiler_params=pltpu.CompilerParams(vmem_limit_bytes=VMEM_LIMIT),
        cost_estimate=pl.CostEstimate(
            flops=16 * pairs * length * length * PAIR,
            bytes_accessed=length * width * 8,
            transcendentals=2 * pairs * length * length,
        ),
        name="attend",
    )(qkv_all, cos_wide, sin_wide)


def attn_bwd_kernel(
    low_ref, dout_ref, lse_ref, cos_ref, sin_ref, grad_ref, bias_ref, dq_ref, dk_ref, dv_ref
):
    length = low_ref.shape[0]
    key_rows = low_ref[:, PAIR : 2 * PAIR]
    values = low_ref[:, 2 * PAIR : 3 * PAIR]
    keys_t = key_rows.astype(F32).T.astype(BF)
    keys_by_head = [head_mask(key_rows, head) for head in range(2)]
    values_by_head = [head_mask(values, head) for head in range(2)]
    scale = HEAD_DIM**-0.5
    dk_ref[...] = jnp.zeros_like(dk_ref)
    dv_ref[...] = jnp.zeros_like(dv_ref)

    @pl.loop(0, length // ROWS_Q)
    def _(step):
        rows = pl.ds(pl.multiple_of(step * ROWS_Q, ROWS_Q), ROWS_Q)
        block = low_ref[rows, 0:PAIR]
        scaled = block * jnp.asarray(scale, BF)
        dout = dout_ref[rows, :]
        outs = []
        for head in range(2):
            scores = lax.dot_general(keys_by_head[head], scaled, NT, preferred_element_type=F32)
            probs = jnp.exp(scores - lse_ref[0, head : head + 1, rows])
            prob_grad = lax.dot_general(values_by_head[head], dout, NT, preferred_element_type=F32)
            delta = jnp.sum(probs * prob_grad, axis=0, keepdims=True)
            score_low = (probs * (prob_grad - delta) * scale).astype(BF)
            dv_ref[head] += jnp.dot(probs.astype(BF), dout, preferred_element_type=F32)
            dk_ref[head] += jnp.dot(score_low, block, preferred_element_type=F32)
            outs.append(
                jnp.dot(
                    keys_t[head * HEAD_DIM : (head + 1) * HEAD_DIM],
                    score_low,
                    preferred_element_type=F32,
                )
            )
        dq_ref[rows, :] = jnp.concatenate(outs, axis=0).T

    lane = lax.broadcasted_iota(jnp.int32, (length, PAIR), 1)
    first = lane // HEAD_DIM == 0
    cosine, sine = cos_ref[...], sin_ref[...]

    def rounded(item):
        return item.astype(BF).astype(F32)

    def back(item):
        return item * cosine - swap_halves(item) * sine

    parts = [
        back(rounded(dq_ref[...])),
        back(rounded(jnp.where(first, dk_ref[0], dk_ref[1]))),
        rounded(jnp.where(first, dv_ref[0], dv_ref[1])),
    ]
    for idx, part in enumerate(parts):
        cols = slice(idx * PAIR, (idx + 1) * PAIR)
        grad_ref[:, cols] = part.astype(BF)
        bias_ref[:, cols] = jnp.broadcast_to(jnp.sum(part, axis=0, keepdims=True), (8, PAIR))


def attend_grad(low_all, mixed_grad, lse, cos_wide, sin_wide):
    length, width = low_all.shape
    pairs = width // (3 * PAIR)
    table = pl.BlockSpec((length, PAIR), lambda pair: (0, 0))
    triple = pl.BlockSpec((length, 3 * PAIR), lambda pair: (0, pair))
    return pl.pallas_call(
        attn_bwd_kernel,
        grid=(pairs,),
        in_specs=[
            triple,
            pl.BlockSpec((length, PAIR), lambda pair: (0, pair)),
            pl.BlockSpec((1, 8, length), lambda pair: (pair, 0, 0)),
            table,
            table,
        ],
        out_specs=[triple, pl.BlockSpec((8, 3 * PAIR), lambda pair: (0, pair))],
        out_shape=[
            jax.ShapeDtypeStruct((length, width), BF),
            jax.ShapeDtypeStruct((8, width), F32),
        ],
        scratch_shapes=[
            pltpu.VMEM((length, PAIR), F32),
            pltpu.VMEM((2, length, PAIR), F32),
            pltpu.VMEM((2, length, PAIR), F32),
        ],
        compiler_params=pltpu.CompilerParams(vmem_limit_bytes=VMEM_LIMIT),
        cost_estimate=pl.CostEstimate(
            flops=40 * pairs * length * length * PAIR,
            bytes_accessed=length * width * 6,
            transcendentals=2 * pairs * length * length,
        ),
        name="attend_grad",
    )(low_all, mixed_grad, lse, cos_wide, sin_wide)


def place_kernel(plans, n_pieces, *refs):
    n_out = len(plans)
    owns = refs[:n_out]
    pieces = refs[n_out : n_out + n_pieces]
    outs = refs[n_out + n_pieces : 2 * n_out + n_pieces]
    sem = refs[-1]
    chip = lax.axis_index("fsdp") // 2
    ring = lax.axis_size("fsdp") // 2
    seq = lax.axis_index("seq")
    copies = []
    for (quarter, first, blocks), own, out in zip(plans, owns, outs):
        slab = 4 * quarter
        copies.append((own, out.at[pl.ds(pl.multiple_of(chip * slab, slab), slab), :]))
        for idx, piece in enumerate(pieces):
            hop, mask = idx // 4 + 1, idx % 4
            place = lax.rem(chip - hop + ring, ring) * slab + (seq ^ mask) * quarter
            rows = pl.ds(pl.multiple_of(place, quarter), quarter)
            for block in range(blocks):
                copies.append(
                    (
                        piece.at[pl.ds(first + block * quarter, quarter), :],
                        out.at[rows, pl.ds(block * 512, 512)],
                    )
                )
    made = [pltpu.make_async_copy(src, dst, sem.at[idx]) for idx, (src, dst) in enumerate(copies)]
    for item in made:
        item.start()
    for item in made:
        item.wait()


def gather_group(slabs):
    seq = lax.axis_index("seq")
    packed = []
    plans = []
    first = 0
    for slab in slabs:
        quarter = slab.shape[0] // 4
        mine = lax.dynamic_slice_in_dim(slab, seq * quarter, quarter, 0)
        blocks = slab.shape[1] // 512
        packed += [mine[:, block * 512 : (block + 1) * 512] for block in range(blocks)]
        plans.append((quarter, first, blocks))
        first += quarter * blocks
    current = jnp.concatenate(packed, axis=0)
    ring = lax.axis_size("fsdp") // 2
    half = first // 2
    pieces = []
    for hop in range(1, ring):
        current = send_up(current)
        over_x = swap_seq(current, 1)
        over_y = swap_seq(current, 2)
        if hop % 3 == 0:
            far = swap_seq(over_x, 2)
        elif hop % 3 == 1:
            far = swap_seq(over_y, 1)
        else:
            far = jnp.concatenate(
                [swap_seq(over_x[:half], 2), swap_seq(over_y[half:], 1)], axis=0
            )
        pieces += [current, over_x, over_y, far]
    n_copies = sum(1 + len(pieces) * plan[2] for plan in plans)
    anywhere = pl.BlockSpec(memory_space=pl.ANY)
    return pl.pallas_call(
        partial(place_kernel, plans, len(pieces)),
        in_specs=[anywhere] * (len(slabs) + len(pieces)),
        out_specs=[pl.BlockSpec(memory_space=pltpu.VMEM)] * len(slabs),
        out_shape=[jax.ShapeDtypeStruct((ring * slab.shape[0], slab.shape[1]), BF) for slab in slabs],
        scratch_shapes=[pltpu.SemaphoreType.DMA((n_copies,))],
        compiler_params=pltpu.CompilerParams(vmem_limit_bytes=VMEM_LIMIT),
        cost_estimate=pl.CostEstimate(
            flops=0,
            bytes_accessed=sum(ring * slab.size * 4 for slab in slabs),
            transcendentals=0,
        ),
        name="place",
    )(*slabs, *pieces)


def ring_sum(item):
    ring = item.shape[0]
    chip = lax.axis_index("fsdp") // 2

    def own(back):
        return pick(item, lax.rem(chip - back + ring, ring))

    moving = own(1)
    for hop in range(2, ring + 1):
        moving = (send_up(moving).astype(F32) + own(hop).astype(F32)).astype(BF)
    return moving


def plane_sum(item, axis, x_first):
    seq = lax.axis_index("seq")
    at_x, at_y = lax.rem(seq, 2), seq // 2

    def one(data, dim, place, mask):
        other = swap_seq(pick(data, 1 - place, dim), mask)
        return (pick(data, place, dim).astype(F32) + other.astype(F32)).astype(BF)

    if x_first:
        return one(one(item, axis + 1, at_x, 1), axis, at_y, 2)
    return one(one(item, axis, at_y, 2), axis, at_x, 1)


def norm_parts(hidden):
    center = hidden - jnp.mean(hidden, axis=-1, keepdims=True)
    spread = jnp.mean(center * center, axis=-1, keepdims=True)
    inverse = lax.rsqrt(spread + 1e-06)
    return center * inverse, inverse


def norm_forward(hidden, gain, shift):
    scaled, _ = norm_parts(hidden)
    return (scaled * gain + shift).astype(BF)


def norm_backward(hidden, gain, grad):
    scaled, inverse = norm_parts(hidden)
    entry = grad * gain
    mean_one = jnp.mean(entry, axis=-1, keepdims=True)
    mean_two = jnp.mean(entry * scaled, axis=-1, keepdims=True)
    result = inverse * (entry - mean_one - scaled * mean_two)
    return result, jnp.sum(grad * scaled, axis=0), jnp.sum(grad, axis=0)


def gelu_and_slope(upward):
    erf_part = 0.5 * (1.0 + lax.erf(upward * (1.0 / math.sqrt(2.0))))
    density = jnp.exp(-0.5 * upward * upward) * (1.0 / math.sqrt(2.0 * math.pi))
    return upward * erf_part, erf_part + upward * density


def dot(left, right):
    return jnp.dot(left, right, preferred_element_type=F32)


def dot_nt(left, right):
    return lax.dot_general(left, right, NT, preferred_element_type=F32)


def dot_tn(left, right):
    return lax.dot_general(left, right, (((0,), (0,)), ((), ())), preferred_element_type=F32)


def own_bias(bias, core, fsdp_parts, kinds):
    width = bias.shape[0] // (kinds * fsdp_parts)
    view = bias.reshape(kinds, fsdp_parts // 2, 2, width)
    mine = pick(view, core, 2)
    return mine.transpose(1, 0, 2).reshape(-1)


def spread_bias(grad, core, fsdp_parts, kinds):
    width = grad.shape[0] // (kinds * (fsdp_parts // 2))
    view = grad.reshape(fsdp_parts // 2, kinds, width).transpose(1, 0, 2)
    zero = jnp.zeros_like(view)
    first = jnp.where(core == 0, view, zero)
    second = jnp.where(core == 0, zero, view)
    return jnp.stack([first, second], axis=2).reshape(-1)


def fast_device(
    clip_tokens,
    patch_coords,
    out_cotangent,
    vector_params,
    qkv_weight,
    proj_weight,
    up_weight,
    down_weight,
    first_vector,
    first_qkv,
    first_proj,
    first_up,
    first_down,
    second_vector,
    second_qkv,
    second_proj,
    second_up,
    second_down,
):
    masters = (vector_params, qkv_weight, proj_weight, up_weight, down_weight)
    firsts = (first_vector, first_qkv, first_proj, first_up, first_down)
    seconds = (second_vector, second_qkv, second_proj, second_up, second_down)
    layer_count = vector_params.shape[0]
    batch_local, chunk_len = clip_tokens.shape[:2]
    seq_parts = lax.axis_size("seq")
    parts = lax.axis_size("fsdp")
    ring = parts // 2
    seq = lax.axis_index("seq")
    shard = lax.axis_index("fsdp")
    core = lax.rem(shard, 2)
    even = lax.rem(seq, 2) == 0

    def to_clips(item, extra=None):
        halves = []
        for turn in range(2):
            piece = jnp.where(even, item[turn], item[1 - turn])
            pairs = []
            for src_seq in range(seq_parts):
                for src in range(parts):
                    dst_seq = 2 * (src % 2) + (src_seq + turn) % 2
                    dst = src - src % 2 + src_seq // 2
                    pairs.append((src_seq * parts + src, dst_seq * parts + dst))
            halves.append(lax.ppermute(piece, ("seq", "fsdp"), pairs))
        mine = jnp.where(
            even, jnp.stack([halves[0], halves[1]]), jnp.stack([halves[1], halves[0]])
        )
        other = swap_core(mine)
        both = jnp.where(core == 0, jnp.stack([mine, other]), jnp.stack([other, mine]))
        return both.reshape((4,) + item.shape[1:])

    def from_clips(item):
        mine = pick(item.reshape((2, 2, chunk_len) + item.shape[1:]), core)
        pieces = [None, None]
        for turn in range(2):
            piece = jnp.where(even, mine[turn], mine[1 - turn])
            pairs = []
            for src_seq in range(seq_parts):
                for src in range(parts):
                    dst_seq = 2 * (src % 2) + (src_seq + turn) % 2
                    dst = src - src % 2 + src_seq // 2
                    pairs.append((dst_seq * parts + dst, src_seq * parts + src))
            pieces[turn] = lax.ppermute(piece, ("seq", "fsdp"), pairs)
        return jnp.where(
            even, jnp.stack([pieces[0], pieces[1]]), jnp.stack([pieces[1], pieces[0]])
        )

    coord_rows = jnp.zeros((batch_local, 8, D), F32)
    coord_rows = lax.dynamic_update_slice(
        coord_rows, jnp.swapaxes(patch_coords, 0, 1).astype(F32), (0, 0, 0)
    )
    arrived = to_clips(jnp.concatenate([clip_tokens, coord_rows], axis=1))
    hidden = arrived[:, :chunk_len].reshape(4 * chunk_len, D)
    coords = arrived[:, chunk_len : chunk_len + 3, :chunk_len]
    coords = jnp.swapaxes(coords, 0, 1).reshape(3, 4 * chunk_len)
    cosine, sine = rotary_tables(coords, HEAD_DIM // 2)
    cos_wide = jnp.concatenate([cosine] * 4, axis=1)
    sin_wide = jnp.concatenate([-sine, sine, -sine, sine], axis=1)

    vector_all = lax.all_gather(vector_params.astype(BF), "fsdp", axis=1, tiled=True).astype(F32)

    def by_core(low, kinds):
        rows = low.shape[0]
        width = low.shape[1] // (kinds * parts)
        view = low.reshape(rows, kinds, ring, 2, width)
        mine = pick(view, core, 3).transpose(0, 2, 1, 3).reshape(rows, -1)
        away = pick(view, 1 - core, 3).transpose(0, 2, 1, 3).reshape(rows, -1)
        other = swap_core(away)
        return jnp.where(
            core == 0, jnp.stack([mine, other]), jnp.stack([other, mine])
        ).reshape(2 * rows, -1)

    layers = []
    for idx in range(layer_count):
        qkv_slab = by_core(qkv_weight[idx].astype(BF), 3)
        up_slab = by_core(up_weight[idx].astype(BF), 1)
        qkv_w, proj_w = gather_group([qkv_slab, proj_weight[idx].astype(BF)])
        up_w, down_w = gather_group([up_slab, down_weight[idx].astype(BF)])
        proj_other = swap_core(proj_w)
        layers.append((qkv_w, proj_w, proj_other, up_w, down_w))

    saved = []
    for idx in range(layer_count):
        qkv_w, proj_w, proj_other, up_w, down_w = layers[idx]
        gain_one, shift_one, gain_two, shift_two, proj_bias, down_bias, qkv_bias, up_bias = pieces(
            vector_all[idx]
        )
        qkv_bias = own_bias(qkv_bias, core, parts, 3)
        up_bias = own_bias(up_bias, core, parts, 1)
        normed = norm_forward(hidden, gain_one, shift_one)
        qkv_all = dot(normed, qkv_w) + qkv_bias
        mixed, low_all, lse = attend(qkv_all, cos_wide, sin_wide)
        mixed_other = swap_core(mixed)
        after_attn = hidden + (dot(mixed, proj_w) + dot(mixed_other, proj_other)) + proj_bias
        normed_two = norm_forward(after_attn, gain_two, shift_two)
        upward = dot(normed_two, up_w) + up_bias
        active, slope = gelu_and_slope(upward)
        active, slope = active.astype(BF), slope.astype(BF)
        part = dot(active, down_w)
        other = swap_core(part.astype(BF))
        result = after_attn + (part + other.astype(F32)) + down_bias
        saved.append((hidden, normed, low_all, lse, mixed, after_attn, normed_two, active, slope))
        hidden = result
    block_output = from_clips(hidden)

    grad = to_clips(out_cotangent).reshape(4 * chunk_len, D)
    sums = [None] * layer_count
    vector_sums = [None] * layer_count
    for idx in reversed(range(layer_count)):
        qkv_w, proj_w, proj_other, up_w, down_w = layers[idx]
        entry, normed, low_all, lse, mixed, after_attn, normed_two, active, slope = saved[idx]
        gain_one, shift_one, gain_two, shift_two, proj_bias, down_bias, qkv_bias, up_bias = pieces(
            vector_all[idx]
        )
        down_bias_grad = jnp.sum(grad, axis=0)
        grad_low = grad.astype(BF)
        upward_grad = dot_nt(grad_low, down_w) * slope.astype(F32)
        up_bias_grad = jnp.sum(upward_grad, axis=0)
        upward_low = upward_grad.astype(BF)
        part = dot_nt(upward_low, up_w)
        other = swap_core(part.astype(BF))
        down_grad = dot_tn(active, grad_low).astype(BF)
        up_grad = dot_tn(normed_two, upward_low).astype(BF)
        attn_in, gain_two_grad, shift_two_grad = norm_backward(
            after_attn, gain_two, part + other.astype(F32)
        )
        after_grad = grad + attn_in
        proj_bias_grad = jnp.sum(after_grad, axis=0)
        after_low = after_grad.astype(BF)
        mixed_grad = dot_nt(after_low, proj_w).astype(BF)
        proj_grad = dot_tn(mixed, after_low).astype(BF)
        qkv_low, bias_rows = attend_grad(low_all, mixed_grad, lse, cos_wide, sin_wide)
        part = dot_nt(qkv_low, qkv_w)
        other = swap_core(part.astype(BF))
        qkv_grad = dot_tn(normed, qkv_low).astype(BF)
        attn_in, gain_one_grad, shift_one_grad = norm_backward(
            entry, gain_one, part + other.astype(F32)
        )
        grad = after_grad + attn_in

        shared = jnp.concatenate(
            [
                gain_one_grad,
                shift_one_grad,
                gain_two_grad,
                shift_two_grad,
                proj_bias_grad,
                down_bias_grad,
            ]
        )
        vector_sums[idx] = jnp.concatenate(
            [
                jnp.where(core == 0, shared, jnp.zeros_like(shared)),
                spread_bias(bias_rows[0], core, parts, 3),
                spread_bias(up_bias_grad, core, parts, 1),
            ]
        )

        def owner_view(item, halves):
            rows = item.shape[0] // (ring * halves * 4)
            return item.reshape(ring, halves, 2, 2, rows, item.shape[1])

        def to_core(item):
            other = swap_core(pick(item, 1 - core))
            mine = pick(item, core)
            return jnp.where(core == 0, jnp.stack([mine, other]), jnp.stack([other, mine]))

        down_sum = ring_sum(plane_sum(owner_view(down_grad, 1), 2, False))[0]
        up_sum = to_core(ring_sum(plane_sum(owner_view(up_grad, 2), 2, True)))
        proj_sum = plane_sum(ring_sum(owner_view(proj_grad, 1)), 1, False)[0]
        qkv_sum = to_core(plane_sum(ring_sum(owner_view(qkv_grad, 2)), 1, True))
        rows = up_sum.shape[1]
        up_sum = up_sum.reshape(2, rows, ring, -1).transpose(1, 2, 0, 3).reshape(rows, -1)
        rows = qkv_sum.shape[1]
        qkv_sum = qkv_sum.reshape(2, rows, ring, 3, -1).transpose(1, 3, 2, 0, 4).reshape(rows, -1)
        sums[idx] = (qkv_sum, proj_sum, up_sum, down_sum)
    input_grad = from_clips(grad)

    clip_count = batch_local * parts
    quarter_sums = tuple(
        jnp.stack([sums[idx][kind] for idx in range(layer_count)]) for kind in range(4)
    )
    local_squares = sum(
        jnp.sum(jnp.square(item.astype(F32) * (1.0 / clip_count))) for item in quarter_sums
    )
    vector_total = lax.psum(jnp.stack(vector_sums), ("seq", "fsdp")) / clip_count
    squares = lax.psum(local_squares, ("seq", "fsdp")) + jnp.sum(vector_total * vector_total)
    norm_value = jnp.sqrt(squares)
    param_count = sum(master.size for master in masters) * parts
    factor = jnp.minimum(1.0, CLIP_RATIO * math.sqrt(float(param_count)) / (norm_value + 1e-06))

    share = vector_params.shape[1]
    grad_shards = [lax.dynamic_slice_in_dim(vector_total, shard * share, share, 1)]
    for item in quarter_sums:
        whole = lax.all_gather(item, "seq", axis=1, tiled=True)
        grad_shards.append(whole.astype(F32) / clip_count)
    updates = [
        adam_update(master, grad_item, first_old, second_old, factor)
        for master, grad_item, first_old, second_old in zip(masters, grad_shards, firsts, seconds)
    ]
    return (
        block_output,
        input_grad,
        *grad_shards,
        norm_value.reshape(1),
        *[item[0] for item in updates],
        *[item[1] for item in updates],
        *[item[2] for item in updates],
        *[item[2].astype(BF) for item in updates],
    )


def solution(mesh):
    in_specs = (
        P("fsdp", "seq", None),
        P(None, "fsdp", "seq"),
        P("fsdp", "seq", None),
        P(None, "fsdp"),
        P(None, "fsdp", None),
        P(None, "fsdp", None),
        P(None, "fsdp", None),
        P(None, "fsdp", None),
        P(None, "fsdp"),
        P(None, "fsdp", None),
        P(None, "fsdp", None),
        P(None, "fsdp", None),
        P(None, "fsdp", None),
        P(None, "fsdp"),
        P(None, "fsdp", None),
        P(None, "fsdp", None),
        P(None, "fsdp", None),
        P(None, "fsdp", None),
    )
    out_specs = (
        P("fsdp", "seq", None),
        P("fsdp", "seq", None),
        P(None, "fsdp"),
        P(None, "fsdp", None),
        P(None, "fsdp", None),
        P(None, "fsdp", None),
        P(None, "fsdp", None),
        P(),
        P(None, "fsdp"),
        P(None, "fsdp", None),
        P(None, "fsdp", None),
        P(None, "fsdp", None),
        P(None, "fsdp", None),
        P(None, "fsdp"),
        P(None, "fsdp", None),
        P(None, "fsdp", None),
        P(None, "fsdp", None),
        P(None, "fsdp", None),
        P(None, "fsdp"),
        P(None, "fsdp", None),
        P(None, "fsdp", None),
        P(None, "fsdp", None),
        P(None, "fsdp", None),
        P(None, "fsdp"),
        P(None, "fsdp", None),
        P(None, "fsdp", None),
        P(None, "fsdp", None),
        P(None, "fsdp", None),
    )
    body = fast_device if fits_fast(mesh) else general_device
    return jax.shard_map(
        body, mesh=mesh, in_specs=in_specs, out_specs=out_specs, check_vma=False
    )
```

```python
from functools import partial
import math

import jax
import jax.numpy as jnp
from jax import lax
from jax.experimental import pallas as pl
from jax.experimental.pallas import tpu as pltpu
from jax.sharding import PartitionSpec as P

D = 1024
HEADS = 16
HEAD_DIM = 64


BETA_ONE = 0.5
BETA_TWO = 0.75
LEARN_RATE = 0.1
DECAY_RATE = 0.1
CLIP_RATIO = 0.2
ADAM_EPS = 1e-08
ROPE_BASE = 10000.0


def pieces(vector):
    return (
        vector[0:D],
        vector[D : 2 * D],
        vector[2 * D : 3 * D],
        vector[3 * D : 4 * D],
        vector[4 * D : 5 * D],
        vector[5 * D : 6 * D],
        vector[6 * D : 9 * D],
        vector[9 * D :],
    )


def layer_norm(hidden, ln_gain, ln_shift):
    center = hidden - jnp.mean(hidden, axis=-1, keepdims=True)
    spread = jnp.mean(center * center, axis=-1, keepdims=True)
    return center * lax.rsqrt(spread + 1e-06) * ln_gain + ln_shift


def gelu_exact(upward):
    return 0.5 * upward * (1.0 + jax.scipy.special.erf(upward * (1.0 / math.sqrt(2.0))))


def rotary_tables(coords_clip, pair_count):
    pair_index = jnp.arange(pair_count, dtype=jnp.int32)
    side_pairs = pair_count // 3
    time_pairs = pair_count - 2 * side_pairs
    in_time = pair_index < time_pairs
    in_height = jnp.logical_and(pair_index >= time_pairs, pair_index < time_pairs + side_pairs)
    offset = jnp.where(in_time, 0, jnp.where(in_height, time_pairs, time_pairs + side_pairs))
    seg_span = jnp.where(in_time, time_pairs, side_pairs)
    local_rank = (pair_index - offset).astype(jnp.float32)
    frequency = jnp.exp(-math.log(ROPE_BASE) * local_rank / seg_span.astype(jnp.float32))
    positions = coords_clip.astype(jnp.float32)
    chosen = jnp.where(
        in_time[None, :],
        positions[0][:, None],
        jnp.where(in_height[None, :], positions[1][:, None], positions[2][:, None]),
    )
    angles = chosen * frequency[None, :]
    return (jnp.cos(angles), jnp.sin(angles))


def rotate(values_in, cosine, sine_table):
    half_width = values_in.shape[-1] // 2
    first_half = values_in[..., :half_width]
    second_half = values_in[..., half_width:]
    cos_wide = cosine[:, None, :]
    sin_wide = sine_table[:, None, :]
    return jnp.concatenate(
        [
            first_half * cos_wide - second_half * sin_wide,
            first_half * sin_wide + second_half * cos_wide,
        ],
        axis=-1,
    )


def attend_forward(queries, key_rows, value_rows):
    full_len = queries.shape[0]
    block_rows = min(512, full_len)
    score_scale = HEAD_DIM ** (-0.5)
    query_blocks = queries.reshape(
        full_len // block_rows, block_rows, queries.shape[1], queries.shape[2]
    )

    def one_block(query_block):
        scores = (
            jnp.einsum("qhd,khd->hqk", query_block, key_rows, preferred_element_type=jnp.float32)
            * score_scale
        )
        row_max = jnp.max(scores, axis=-1, keepdims=True)
        exponent = jnp.exp(scores - row_max)
        row_total = jnp.sum(exponent, axis=-1, keepdims=True)
        prob_low = (exponent / row_total).astype(jnp.bfloat16)
        mixed_rows = jnp.einsum(
            "hqk,khd->qhd", prob_low, value_rows, preferred_element_type=jnp.float32
        )
        return (mixed_rows, row_max[..., 0] + jnp.log(row_total[..., 0]))

    mixed_rows, log_sums = lax.map(one_block, query_blocks)
    return (mixed_rows.reshape(queries.shape), log_sums)


def attend_backward(queries, key_rows, value_rows, log_sums, head_grad):
    full_len = queries.shape[0]
    block_rows = min(512, full_len)
    score_scale = HEAD_DIM ** (-0.5)
    block_shape = (full_len // block_rows, block_rows, queries.shape[1], queries.shape[2])

    def one_block(carry, block_in):
        key_grad, value_grad = carry
        query_block, grad_block, lse_block = block_in
        scores = (
            jnp.einsum("qhd,khd->hqk", query_block, key_rows, preferred_element_type=jnp.float32)
            * score_scale
        )
        prob_rows = jnp.exp(scores - lse_block[..., None])
        prob_low = prob_rows.astype(jnp.bfloat16)
        value_grad = value_grad + jnp.einsum(
            "hqk,qhd->khd", prob_low, grad_block, preferred_element_type=jnp.float32
        )
        prob_grad = jnp.einsum(
            "qhd,khd->hqk", grad_block, value_rows, preferred_element_type=jnp.float32
        )
        score_grad = prob_rows * (
            prob_grad - jnp.sum(prob_rows * prob_grad, axis=-1, keepdims=True)
        )
        score_low = (score_grad * score_scale).astype(jnp.bfloat16)
        query_grad = jnp.einsum(
            "hqk,khd->qhd", score_low, key_rows, preferred_element_type=jnp.float32
        )
        key_grad = key_grad + jnp.einsum(
            "hqk,qhd->khd", score_low, query_block, preferred_element_type=jnp.float32
        )
        return ((key_grad, value_grad), query_grad)

    zero_heads = jnp.zeros(queries.shape, jnp.float32)
    (key_grad, value_grad), query_grad = lax.scan(
        one_block,
        (zero_heads, zero_heads),
        (queries.reshape(block_shape), head_grad.reshape(block_shape), log_sums),
    )
    return (query_grad.reshape(queries.shape), key_grad, value_grad)


def layer_forward(hidden, cosine, sine_table, weights, seq_parts):
    vector_low, qkv_w, proj_w, up_w, down_w = weights
    gain_one, shift_one, gain_two, shift_two, proj_bias, down_bias, qkv_bias, up_bias = pieces(
        vector_low.astype(jnp.float32)
    )
    row_count = hidden.shape[0]
    local_heads = HEADS // seq_parts
    normed = layer_norm(hidden, gain_one, shift_one).astype(jnp.bfloat16)
    qkv_all = jnp.dot(normed, qkv_w, preferred_element_type=jnp.float32) + qkv_bias
    split_qkv = qkv_all.reshape(row_count, 3, HEADS, HEAD_DIM)
    stacked = jnp.stack(
        [
            rotate(split_qkv[:, 0], cosine, sine_table),
            rotate(split_qkv[:, 1], cosine, sine_table),
            split_qkv[:, 2],
        ],
        axis=1,
    ).astype(jnp.bfloat16)
    packed = stacked.reshape(row_count, 3, seq_parts, local_heads * HEAD_DIM)
    by_heads = lax.all_to_all(packed, "seq", split_axis=2, concat_axis=0, tiled=True)
    full_len = by_heads.shape[0]
    by_heads = by_heads.reshape(full_len, 3, local_heads, HEAD_DIM)
    mixed_rows, log_sums = attend_forward(by_heads[:, 0], by_heads[:, 1], by_heads[:, 2])
    mixed_low = mixed_rows.astype(jnp.bfloat16).reshape(full_len, 1, local_heads * HEAD_DIM)
    by_tokens = lax.all_to_all(mixed_low, "seq", split_axis=0, concat_axis=1, tiled=True).reshape(
        row_count, D
    )
    after_attn = hidden + jnp.dot(by_tokens, proj_w, preferred_element_type=jnp.float32) + proj_bias
    normed_two = layer_norm(after_attn, gain_two, shift_two).astype(jnp.bfloat16)
    upward = jnp.dot(normed_two, up_w, preferred_element_type=jnp.float32) + up_bias
    active = gelu_exact(upward).astype(jnp.bfloat16)
    result = after_attn + jnp.dot(active, down_w, preferred_element_type=jnp.float32) + down_bias
    saved_state = (
        hidden,
        normed,
        by_heads,
        log_sums,
        by_tokens,
        after_attn,
        normed_two,
        upward,
        active,
    )
    return (result, saved_state)


def layer_backward(grad_out, saved_state, weights, cosine, sine_table, seq_parts):
    vector_low, qkv_w, proj_w, up_w, down_w = weights
    gain_one, shift_one, gain_two, shift_two, proj_bias, down_bias, qkv_bias, up_bias = pieces(
        vector_low.astype(jnp.float32)
    )
    hidden, normed, by_heads, log_sums, by_tokens, after_attn, normed_two, upward, active = (
        saved_state
    )
    row_count = hidden.shape[0]
    local_heads = HEADS // seq_parts
    down_bias_grad = jnp.sum(grad_out, axis=0)
    grad_low = grad_out.astype(jnp.bfloat16)
    down_grad = jnp.dot(active.T, grad_low, preferred_element_type=jnp.float32)
    active_grad = jnp.dot(grad_low, down_w.T, preferred_element_type=jnp.float32)
    gelu_value, gelu_pull = jax.vjp(gelu_exact, upward)
    upward_grad = gelu_pull(active_grad)[0]
    up_bias_grad = jnp.sum(upward_grad, axis=0)
    upward_low = upward_grad.astype(jnp.bfloat16)
    up_grad = jnp.dot(normed_two.T, upward_low, preferred_element_type=jnp.float32)
    normed_two_grad = jnp.dot(upward_low, up_w.T, preferred_element_type=jnp.float32)
    norm_value_two, norm_pull_two = jax.vjp(layer_norm, after_attn, gain_two, shift_two)
    attn_in_grad, gain_two_grad, shift_two_grad = norm_pull_two(normed_two_grad)
    after_grad = grad_out + attn_in_grad
    proj_bias_grad = jnp.sum(after_grad, axis=0)
    after_low = after_grad.astype(jnp.bfloat16)
    proj_grad = jnp.dot(by_tokens.T, after_low, preferred_element_type=jnp.float32)
    mixed_grad = jnp.dot(after_low, proj_w.T, preferred_element_type=jnp.float32).astype(
        jnp.bfloat16
    )
    head_grad = lax.all_to_all(
        mixed_grad.reshape(row_count, seq_parts, local_heads * HEAD_DIM),
        "seq",
        split_axis=1,
        concat_axis=0,
        tiled=True,
    )
    full_len = head_grad.shape[0]
    head_grad = head_grad.reshape(full_len, local_heads, HEAD_DIM)
    query_grad, key_grad, value_grad = attend_backward(
        by_heads[:, 0], by_heads[:, 1], by_heads[:, 2], log_sums, head_grad
    )
    stacked_grad = (
        jnp.stack([query_grad, key_grad, value_grad], axis=1)
        .astype(jnp.bfloat16)
        .reshape(full_len, 3, 1, local_heads * HEAD_DIM)
    )
    token_grad = (
        lax.all_to_all(stacked_grad, "seq", split_axis=0, concat_axis=2, tiled=True)
        .reshape(row_count, 3, HEADS, HEAD_DIM)
        .astype(jnp.float32)
    )
    pair_grad_in = token_grad[:, :2].reshape(row_count, 2 * HEADS, HEAD_DIM)
    rotated_value, rotate_pull = jax.vjp(
        partial(rotate, cosine=cosine, sine_table=sine_table), pair_grad_in
    )
    pair_grad = rotate_pull(pair_grad_in)[0].reshape(row_count, 2, HEADS, HEAD_DIM)
    qkv_grad = jnp.concatenate([pair_grad, token_grad[:, 2:]], axis=1).reshape(row_count, 3 * D)
    qkv_bias_grad = jnp.sum(qkv_grad, axis=0)
    qkv_low = qkv_grad.astype(jnp.bfloat16)
    qkv_w_grad = jnp.dot(normed.T, qkv_low, preferred_element_type=jnp.float32)
    normed_grad = jnp.dot(qkv_low, qkv_w.T, preferred_element_type=jnp.float32)
    norm_value_one, norm_pull_one = jax.vjp(layer_norm, hidden, gain_one, shift_one)
    in_grad, gain_one_grad, shift_one_grad = norm_pull_one(normed_grad)
    input_grad = after_grad + in_grad
    vector_grad = jnp.concatenate(
        [
            gain_one_grad,
            shift_one_grad,
            gain_two_grad,
            shift_two_grad,
            proj_bias_grad,
            down_bias_grad,
            qkv_bias_grad,
            up_bias_grad,
        ]
    )
    return (input_grad, (vector_grad, qkv_w_grad, proj_grad, up_grad, down_grad))


def adam_update(master, grad_item, first_old, second_old, factor):
    clipped = grad_item * factor
    first_new = BETA_ONE * first_old + (1.0 - BETA_ONE) * clipped
    second_new = BETA_TWO * second_old + (1.0 - BETA_TWO) * clipped * clipped
    updated = master - LEARN_RATE * (
        first_new / (jnp.sqrt(second_new) + ADAM_EPS) + DECAY_RATE * master
    )
    return (first_new, second_new, updated)


def general_device(
    clip_tokens,
    patch_coords,
    out_cotangent,
    vector_params,
    qkv_weight,
    proj_weight,
    up_weight,
    down_weight,
    first_vector,
    first_qkv,
    first_proj,
    first_up,
    first_down,
    second_vector,
    second_qkv,
    second_proj,
    second_up,
    second_down,
):
    masters = (vector_params, qkv_weight, proj_weight, up_weight, down_weight)
    firsts = (first_vector, first_qkv, first_proj, first_up, first_down)
    seconds = (second_vector, second_qkv, second_proj, second_up, second_down)
    lowered = tuple((master.astype(jnp.bfloat16) for master in masters))
    layer_count = vector_params.shape[0]
    batch_local = clip_tokens.shape[0]
    seq_parts = lax.axis_size("seq")
    fsdp_parts = lax.axis_size("fsdp")
    grad_accum = tuple(
        (
            jnp.zeros((layer_count, master.shape[1] * fsdp_parts) + master.shape[2:], jnp.float32)
            for master in masters
        )
    )
    output_rows = []
    input_rows = []
    for batch_idx in range(batch_local):
        cosine, sine_table = rotary_tables(patch_coords[:, batch_idx], HEAD_DIM // 2)
        hidden = clip_tokens[batch_idx]
        saved_layers = []
        for layer_idx in range(layer_count):
            weights = (
                lax.all_gather(lowered[0][layer_idx], "fsdp", axis=0, tiled=True),
                lax.all_gather(lowered[1][layer_idx], "fsdp", axis=0, tiled=True),
                lax.all_gather(lowered[2][layer_idx], "fsdp", axis=0, tiled=True),
                lax.all_gather(lowered[3][layer_idx], "fsdp", axis=0, tiled=True),
                lax.all_gather(lowered[4][layer_idx], "fsdp", axis=0, tiled=True),
            )
            hidden, saved_state = layer_forward(hidden, cosine, sine_table, weights, seq_parts)
            saved_layers.append(saved_state)
        output_rows.append(hidden)
        grad_rows = out_cotangent[batch_idx]
        for layer_idx in reversed(range(layer_count)):
            weights = (
                lax.all_gather(lowered[0][layer_idx], "fsdp", axis=0, tiled=True),
                lax.all_gather(lowered[1][layer_idx], "fsdp", axis=0, tiled=True),
                lax.all_gather(lowered[2][layer_idx], "fsdp", axis=0, tiled=True),
                lax.all_gather(lowered[3][layer_idx], "fsdp", axis=0, tiled=True),
                lax.all_gather(lowered[4][layer_idx], "fsdp", axis=0, tiled=True),
            )
            grad_rows, layer_grads = layer_backward(
                grad_rows, saved_layers[layer_idx], weights, cosine, sine_table, seq_parts
            )
            grad_accum = tuple(
                (
                    accum_item.at[layer_idx].add(grad_item)
                    for accum_item, grad_item in zip(grad_accum, layer_grads)
                )
            )
        input_rows.append(grad_rows)
    shard_sums = (
        lax.psum_scatter(grad_accum[0], "fsdp", scatter_dimension=1, tiled=True),
        lax.psum_scatter(grad_accum[1], "fsdp", scatter_dimension=1, tiled=True),
        lax.psum_scatter(grad_accum[2], "fsdp", scatter_dimension=1, tiled=True),
        lax.psum_scatter(grad_accum[3], "fsdp", scatter_dimension=1, tiled=True),
        lax.psum_scatter(grad_accum[4], "fsdp", scatter_dimension=1, tiled=True),
    )
    seq_sums = lax.psum(
        (shard_sums[0], shard_sums[1], shard_sums[2], shard_sums[3], shard_sums[4]), "seq"
    )
    clip_count = batch_local * fsdp_parts
    grad_shards = tuple((sum_item / clip_count for sum_item in seq_sums))
    local_squares = sum((jnp.sum(grad_item * grad_item) for grad_item in grad_shards))
    squares_total = lax.psum(local_squares, "fsdp")
    norm_value = jnp.sqrt(squares_total)
    param_count = sum((master.size for master in masters)) * fsdp_parts
    factor = jnp.minimum(1.0, CLIP_RATIO * math.sqrt(float(param_count)) / (norm_value + 1e-06))
    updates = [
        adam_update(master, grad_item, first_old, second_old, factor)
        for master, grad_item, first_old, second_old in zip(masters, grad_shards, firsts, seconds)
    ]
    return (
        jnp.stack(output_rows),
        jnp.stack(input_rows),
        grad_shards[0],
        grad_shards[1],
        grad_shards[2],
        grad_shards[3],
        grad_shards[4],
        norm_value.reshape(1),
        updates[0][0],
        updates[1][0],
        updates[2][0],
        updates[3][0],
        updates[4][0],
        updates[0][1],
        updates[1][1],
        updates[2][1],
        updates[3][1],
        updates[4][1],
        updates[0][2],
        updates[1][2],
        updates[2][2],
        updates[3][2],
        updates[4][2],
        updates[0][2].astype(jnp.bfloat16),
        updates[1][2].astype(jnp.bfloat16),
        updates[2][2].astype(jnp.bfloat16),
        updates[3][2].astype(jnp.bfloat16),
        updates[4][2].astype(jnp.bfloat16),
    )


ROWS_Q = 256
PAIR = 2 * HEAD_DIM
BF = jnp.bfloat16
F32 = jnp.float32
VMEM_LIMIT = 56 * 1024 * 1024


def fits_fast(mesh):
    return dict(mesh.shape) == {"seq": 4, "fsdp": 8}


def swap_core(item):
    parts = lax.axis_size("fsdp")
    return lax.ppermute(item, "fsdp", [(idx, idx ^ 1) for idx in range(parts)])


def send_up(item):
    parts = lax.axis_size("fsdp")
    return lax.ppermute(item, "fsdp", [(idx, (idx + 2) % parts) for idx in range(parts)])


def swap_seq(item, mask):
    parts = lax.axis_size("seq")
    return lax.ppermute(item, "seq", [(idx, idx ^ mask) for idx in range(parts)])


def pick(item, index, axis=0):
    return lax.dynamic_index_in_dim(item, index, axis, keepdims=False)


def swap_halves(item):
    lane = lax.broadcasted_iota(jnp.int32, item.shape, 1)
    half = HEAD_DIM // 2
    width = item.shape[1]
    ahead = pltpu.roll(item, width - half, 1)
    behind = pltpu.roll(item, half, 1)
    return jnp.where(lane % HEAD_DIM < half, ahead, behind)


NT = (((1,), (1,)), ((), ()))


def head_mask(item, head):
    lane = lax.broadcasted_iota(jnp.int32, item.shape, 1)
    return jnp.where(lane // HEAD_DIM == head, item, jnp.zeros_like(item))


def attn_fwd_kernel(qkv_ref, cos_ref, sin_ref, mixed_ref, low_ref, lse_ref, qs_ref):
    cosine, sine = cos_ref[...], sin_ref[...]
    queries = qkv_ref[:, 0:PAIR]
    key_rows = qkv_ref[:, PAIR : 2 * PAIR]
    values = qkv_ref[:, 2 * PAIR : 3 * PAIR]
    queries = (queries * cosine + swap_halves(queries) * sine).astype(BF)
    key_rows = (key_rows * cosine + swap_halves(key_rows) * sine).astype(BF)
    low_ref[:, 0:PAIR] = queries
    low_ref[:, PAIR : 2 * PAIR] = key_rows
    low_ref[:, 2 * PAIR : 3 * PAIR] = values.astype(BF)
    qs_ref[...] = queries * jnp.asarray(HEAD_DIM**-0.5, BF)
    values_t = values.T.astype(BF)
    keys_by_head = [head_mask(key_rows, head) for head in range(2)]
    length = qs_ref.shape[0]

    @pl.loop(0, length // ROWS_Q)
    def _(step):
        rows = pl.ds(pl.multiple_of(step * ROWS_Q, ROWS_Q), ROWS_Q)
        block = qs_ref[rows, :]
        outs = []
        for head in range(2):
            scores = lax.dot_general(keys_by_head[head], block, NT, preferred_element_type=F32)
            top = jnp.max(scores, axis=0, keepdims=True)
            exponent = jnp.exp(scores - top)
            total = jnp.sum(exponent, axis=0, keepdims=True)
            lse_ref[0, head : head + 1, rows] = top + jnp.log(total)
            probs = (exponent * (1.0 / total)).astype(BF)
            outs.append(
                jnp.dot(
                    values_t[head * HEAD_DIM : (head + 1) * HEAD_DIM],
                    probs,
                    preferred_element_type=F32,
                )
            )
        mixed_ref[rows, :] = jnp.concatenate(outs, axis=0).T.astype(BF)


def attend(qkv_all, cos_wide, sin_wide):
    length, width = qkv_all.shape
    pairs = width // (3 * PAIR)
    table = pl.BlockSpec((length, PAIR), lambda pair: (0, 0))
    triple = pl.BlockSpec((length, 3 * PAIR), lambda pair: (0, pair))
    return pl.pallas_call(
        attn_fwd_kernel,
        grid=(pairs,),
        in_specs=[triple, table, table],
        out_specs=[
            pl.BlockSpec((length, PAIR), lambda pair: (0, pair)),
            triple,
            pl.BlockSpec((1, 8, length), lambda pair: (pair, 0, 0)),
        ],
        out_shape=[
            jax.ShapeDtypeStruct((length, pairs * PAIR), BF),
            jax.ShapeDtypeStruct((length, width), BF),
            jax.ShapeDtypeStruct((pairs, 8, length), F32),
        ],
        scratch_shapes=[pltpu.VMEM((length, PAIR), BF)],
        compiler_params=pltpu.CompilerParams(vmem_limit_bytes=VMEM_LIMIT),
        cost_estimate=pl.CostEstimate(
            flops=16 * pairs * length * length * PAIR,
            bytes_accessed=length * width * 8,
            transcendentals=2 * pairs * length * length,
        ),
        name="attend",
    )(qkv_all, cos_wide, sin_wide)


def attn_bwd_kernel(
    low_ref, dout_ref, lse_ref, cos_ref, sin_ref, grad_ref, bias_ref, dq_ref, dk_ref, dv_ref
):
    length = low_ref.shape[0]
    key_rows = low_ref[:, PAIR : 2 * PAIR]
    values = low_ref[:, 2 * PAIR : 3 * PAIR]
    keys_t = key_rows.astype(F32).T.astype(BF)
    keys_by_head = [head_mask(key_rows, head) for head in range(2)]
    values_by_head = [head_mask(values, head) for head in range(2)]
    scale = HEAD_DIM**-0.5
    dk_ref[...] = jnp.zeros_like(dk_ref)
    dv_ref[...] = jnp.zeros_like(dv_ref)

    @pl.loop(0, length // ROWS_Q)
    def _(step):
        rows = pl.ds(pl.multiple_of(step * ROWS_Q, ROWS_Q), ROWS_Q)
        block = low_ref[rows, 0:PAIR]
        scaled = block * jnp.asarray(scale, BF)
        dout = dout_ref[rows, :]
        outs = []
        for head in range(2):
            scores = lax.dot_general(keys_by_head[head], scaled, NT, preferred_element_type=F32)
            probs = jnp.exp(scores - lse_ref[0, head : head + 1, rows])
            prob_grad = lax.dot_general(values_by_head[head], dout, NT, preferred_element_type=F32)
            delta = jnp.sum(probs * prob_grad, axis=0, keepdims=True)
            score_low = (probs * (prob_grad - delta) * scale).astype(BF)
            dv_ref[head] += jnp.dot(probs.astype(BF), dout, preferred_element_type=F32)
            dk_ref[head] += jnp.dot(score_low, block, preferred_element_type=F32)
            outs.append(
                jnp.dot(
                    keys_t[head * HEAD_DIM : (head + 1) * HEAD_DIM],
                    score_low,
                    preferred_element_type=F32,
                )
            )
        dq_ref[rows, :] = jnp.concatenate(outs, axis=0).T

    lane = lax.broadcasted_iota(jnp.int32, (length, PAIR), 1)
    first = lane // HEAD_DIM == 0
    cosine, sine = cos_ref[...], sin_ref[...]

    def rounded(item):
        return item.astype(BF).astype(F32)

    def back(item):
        return item * cosine - swap_halves(item) * sine

    parts = [
        back(rounded(dq_ref[...])),
        back(rounded(jnp.where(first, dk_ref[0], dk_ref[1]))),
        rounded(jnp.where(first, dv_ref[0], dv_ref[1])),
    ]
    for idx, part in enumerate(parts):
        cols = slice(idx * PAIR, (idx + 1) * PAIR)
        grad_ref[:, cols] = part.astype(BF)
        bias_ref[:, cols] = jnp.broadcast_to(jnp.sum(part, axis=0, keepdims=True), (8, PAIR))


def attend_grad(low_all, mixed_grad, lse, cos_wide, sin_wide):
    length, width = low_all.shape
    pairs = width // (3 * PAIR)
    table = pl.BlockSpec((length, PAIR), lambda pair: (0, 0))
    triple = pl.BlockSpec((length, 3 * PAIR), lambda pair: (0, pair))
    return pl.pallas_call(
        attn_bwd_kernel,
        grid=(pairs,),
        in_specs=[
            triple,
            pl.BlockSpec((length, PAIR), lambda pair: (0, pair)),
            pl.BlockSpec((1, 8, length), lambda pair: (pair, 0, 0)),
            table,
            table,
        ],
        out_specs=[triple, pl.BlockSpec((8, 3 * PAIR), lambda pair: (0, pair))],
        out_shape=[
            jax.ShapeDtypeStruct((length, width), BF),
            jax.ShapeDtypeStruct((8, width), F32),
        ],
        scratch_shapes=[
            pltpu.VMEM((length, PAIR), F32),
            pltpu.VMEM((2, length, PAIR), F32),
            pltpu.VMEM((2, length, PAIR), F32),
        ],
        compiler_params=pltpu.CompilerParams(vmem_limit_bytes=VMEM_LIMIT),
        cost_estimate=pl.CostEstimate(
            flops=40 * pairs * length * length * PAIR,
            bytes_accessed=length * width * 6,
            transcendentals=2 * pairs * length * length,
        ),
        name="attend_grad",
    )(low_all, mixed_grad, lse, cos_wide, sin_wide)


def gather_kernel(
    qkv_mine, qkv_away, up_mine, up_away, down_in, proj_in,
    qkv_out, up_out, down_out, proj_out,
    qkv_slab, up_slab, down_slab, proj_slab,
    z_send, z_recv, p_send, p_recv, d_send, d_recv, c_send, c_recv, l_in, l_out,
):
    shard, seq = lax.axis_index("fsdp"), lax.axis_index("seq")
    parts = lax.axis_size("fsdp")
    ring = parts // 2
    chip, core = shard // 2, lax.rem(shard, 2)
    other = {"fsdp": shard + 1 - 2 * core}
    up_chip = {"fsdp": lax.rem(shard + 2, parts)}
    down_chip = {"fsdp": lax.rem(shard + parts - 2, parts)}
    at_x, at_y = lax.rem(seq, 2), seq // 2
    over_x = {"seq": 2 * at_y + 1 - at_x}
    over_y = {"seq": 2 * (1 - at_y) + at_x}
    near_x, near_y = 2 * at_y + 1 - at_x, 2 * (1 - at_y) + at_x
    layers = qkv_mine.shape[0]

    barrier = pltpu.get_barrier_semaphore()
    for target in (other, up_chip, down_chip, over_x, over_y):
        pl.semaphore_signal(barrier, inc=1, device_id=target, device_id_type=pl.DeviceIdType.MESH)
    pl.semaphore_wait(barrier, 5)

    def remote(src, dst, send, recv, target):
        return pltpu.make_async_remote_copy(
            src_ref=src,
            dst_ref=dst,
            send_sem=send,
            recv_sem=recv,
            device_id=target,
            device_id_type=pl.DeviceIdType.MESH,
        )

    outs = {"qkv": qkv_out, "up": up_out, "down": down_out, "proj": proj_out}
    slabs = {"qkv": qkv_slab, "up": up_slab, "down": down_slab, "proj": proj_slab}
    items = [(name, layer) for layer in range(layers) for name in ("qkv", "proj", "up", "down")]

    def place(name, layer, chip_at, part):
        slab = slabs[name].shape[1]
        if part is None:
            start, size = chip_at * slab, slab
        else:
            size = slab // 4
            start = chip_at * slab + part * size
        rows = pl.ds(pl.multiple_of(start, size), size)
        if name == "proj":
            return outs[name].at[layer, 0, rows, :]
        return outs[name].at[layer, rows, :]

    local_in, swaps = [], []
    for idx, (name, layer) in enumerate(items):
        slab = slabs[name]
        if name in ("qkv", "up"):
            mine, away = (qkv_mine, qkv_away) if name == "qkv" else (up_mine, up_away)
            half = mine.shape[1]
            rows = pl.ds(pl.multiple_of(core * half, half), half)
            swap = remote(
                away.at[layer], slab.at[layer, rows, :], c_send.at[idx], c_recv.at[idx], other
            )
            local = pltpu.make_async_copy(mine.at[layer], slab.at[layer, rows, :], l_in.at[idx])
        else:
            swap = None
            source = down_in if name == "down" else proj_in
            local = pltpu.make_async_copy(source.at[layer], slab.at[layer], l_in.at[idx])
        swaps.append(swap)
        local_in.append(local)
        if swap is not None:
            swap.start()
        local.start()

    hops = ring - 1
    order = []
    for first in range(0, len(items), 2):
        for hop in range(hops):
            order += [(first, hop), (first + 1, hop)]

    stores = []
    z_copies = {}

    def begin(idx):
        name, layer = items[idx]
        local_in[idx].wait()
        if swaps[idx] is not None:
            swaps[idx].wait_recv()
        store = pltpu.make_async_copy(
            slabs[name].at[layer], place(name, layer, chip, None), l_out.at[idx]
        )
        store.start()
        stores.append(store)

    def z_copy(idx, hop):
        name, layer = items[idx]
        part = None if name == "proj" else seq
        source = place(name, layer, lax.rem(chip - hop + ring, ring), part)
        if hop == 0:
            if part is None:
                from_ref = slabs[name].at[layer]
            else:
                size = slabs[name].shape[1] // 4
                from_ref = slabs[name].at[layer, pl.ds(pl.multiple_of(seq * size, size), size), :]
        else:
            from_ref = source
        slot = idx * hops + hop
        copy = remote(from_ref, source, z_send.at[slot], z_recv.at[slot], up_chip)
        copy.start()
        z_copies[idx, hop] = copy

    plane, far = {}, {}

    def plane_copies(idx, hop):
        name, layer = items[idx]
        ref = place(name, layer, lax.rem(chip - hop - 1 + ring, ring), seq)
        slot = 2 * (idx * hops + hop)
        plane[idx, hop] = [
            remote(ref, ref, p_send.at[slot], p_recv.at[slot], over_x),
            remote(ref, ref, p_send.at[slot + 1], p_recv.at[slot + 1], over_y),
        ]
        for copy in plane[idx, hop]:
            copy.start()

    def far_copies(idx, hop):
        name, layer = items[idx]
        slot = 2 * (idx * hops + hop)
        size = slabs[name].shape[1] // 4
        half = size // 2
        base = lax.rem(chip - hop - 1 + ring, ring) * 4 * size
        for copy in plane[idx, hop]:
            copy.wait_recv()
        made = []
        for turn, (origin, target) in enumerate(((near_y, over_x), (near_x, over_y))):
            rows = pl.ds(pl.multiple_of(base + origin * size + turn * half, half), half)
            ref = outs[name].at[layer, rows, :]
            made.append(
                remote(ref, ref, d_send.at[slot + turn], d_recv.at[slot + turn], target)
            )
        far[idx, hop] = made
        for copy in made:
            copy.start()

    pending = []
    proj_swaps = []
    begin(0)
    z_copy(0, 0)
    begin(1)
    z_copy(1, 0)
    for idx, hop in order:
        z_copies[idx, hop].wait_recv()
        if hop + 1 < hops:
            z_copy(idx, hop + 1)
        elif idx + 2 < len(items):
            begin(idx + 2)
            z_copy(idx + 2, 0)
        name, layer = items[idx]
        if name == "proj":
            if hop + 1 == hops:
                stores[idx].wait()
                slot = len(items) + layer
                swap = remote(
                    proj_out.at[layer, 0],
                    proj_out.at[layer, 1],
                    c_send.at[slot],
                    c_recv.at[slot],
                    other,
                )
                swap.start()
                proj_swaps.append(swap)
        else:
            plane_copies(idx, hop)
            pending.append((idx, hop))
            if len(pending) > 1:
                far_copies(*pending.pop(0))
    while pending:
        far_copies(*pending.pop(0))

    for key, made in far.items():
        for copy in made:
            copy.wait()
    for made in plane.values():
        for copy in made:
            copy.wait_send()
    for copy in z_copies.values():
        copy.wait_send()
    for copy in swaps:
        if copy is not None:
            copy.wait_send()
    for copy in proj_swaps:
        copy.wait()
    for idx, store in enumerate(stores):
        if items[idx][0] != "proj":
            store.wait()


def gather_weights(qkv_mine, qkv_away, up_mine, up_away, down_low, proj_low):
    layers = qkv_mine.shape[0]
    ring = lax.axis_size("fsdp") // 2
    count = 4 * layers
    hops = ring - 1
    anywhere = pl.BlockSpec(memory_space=pl.ANY)
    dma = pltpu.SemaphoreType.DMA
    qkv_rows, up_rows = 2 * qkv_mine.shape[1], 2 * up_mine.shape[1]
    down_rows, proj_rows = down_low.shape[1], proj_low.shape[1]
    width = down_low.shape[2]
    shapes = [
        (layers, ring * qkv_rows, qkv_mine.shape[2]),
        (layers, ring * up_rows, up_mine.shape[2]),
        (layers, ring * down_rows, width),
        (layers, 2, ring * proj_rows, width),
    ]
    return pl.pallas_call(
        gather_kernel,
        in_specs=[anywhere] * 6,
        out_specs=[anywhere] * 4,
        out_shape=[jax.ShapeDtypeStruct(shape, BF) for shape in shapes],
        scratch_shapes=[
            pltpu.VMEM((layers, qkv_rows, qkv_mine.shape[2]), BF),
            pltpu.VMEM((layers, up_rows, up_mine.shape[2]), BF),
            pltpu.VMEM((layers, down_rows, width), BF),
            pltpu.VMEM((layers, proj_rows, width), BF),
            dma((count * hops,)),
            dma((count * hops,)),
            dma((2 * count * hops,)),
            dma((2 * count * hops,)),
            dma((2 * count * hops,)),
            dma((2 * count * hops,)),
            dma((count + layers,)),
            dma((count + layers,)),
            dma((count,)),
            dma((count,)),
        ],
        compiler_params=pltpu.CompilerParams(
            collective_id=0, has_side_effects=True, vmem_limit_bytes=VMEM_LIMIT
        ),
        cost_estimate=pl.CostEstimate(
            flops=0, bytes_accessed=600_000_000, transcendentals=0
        ),
        name="gather_weights",
    )(qkv_mine, qkv_away, up_mine, up_away, down_low, proj_low)


def ring_sum(item):
    ring = item.shape[0]
    chip = lax.axis_index("fsdp") // 2

    def own(back):
        return pick(item, lax.rem(chip - back + ring, ring))

    moving = own(1)
    for hop in range(2, ring + 1):
        moving = (send_up(moving).astype(F32) + own(hop).astype(F32)).astype(BF)
    return moving


def plane_sum(item, axis, x_first):
    seq = lax.axis_index("seq")
    at_x, at_y = lax.rem(seq, 2), seq // 2

    def one(data, dim, place, mask):
        other = swap_seq(pick(data, 1 - place, dim), mask)
        return (pick(data, place, dim).astype(F32) + other.astype(F32)).astype(BF)

    if x_first:
        return one(one(item, axis + 1, at_x, 1), axis, at_y, 2)
    return one(one(item, axis, at_y, 2), axis, at_x, 1)


def norm_parts(hidden):
    center = hidden - jnp.mean(hidden, axis=-1, keepdims=True)
    spread = jnp.mean(center * center, axis=-1, keepdims=True)
    inverse = lax.rsqrt(spread + 1e-06)
    return center * inverse, inverse


def norm_forward(hidden, gain, shift):
    scaled, _ = norm_parts(hidden)
    return (scaled * gain + shift).astype(BF)


def norm_backward(hidden, gain, grad):
    scaled, inverse = norm_parts(hidden)
    entry = grad * gain
    mean_one = jnp.mean(entry, axis=-1, keepdims=True)
    mean_two = jnp.mean(entry * scaled, axis=-1, keepdims=True)
    result = inverse * (entry - mean_one - scaled * mean_two)
    return result, jnp.sum(grad * scaled, axis=0), jnp.sum(grad, axis=0)


def gelu_and_slope(upward):
    erf_part = 0.5 * (1.0 + lax.erf(upward * (1.0 / math.sqrt(2.0))))
    density = jnp.exp(-0.5 * upward * upward) * (1.0 / math.sqrt(2.0 * math.pi))
    return upward * erf_part, erf_part + upward * density


def dot(left, right):
    return jnp.dot(left, right, preferred_element_type=F32)


def dot_nt(left, right):
    return lax.dot_general(left, right, NT, preferred_element_type=F32)


def dot_tn(left, right):
    return lax.dot_general(left, right, (((0,), (0,)), ((), ())), preferred_element_type=F32)


def own_bias(bias, core, fsdp_parts, kinds):
    width = bias.shape[0] // (kinds * fsdp_parts)
    view = bias.reshape(kinds, fsdp_parts // 2, 2, width)
    mine = pick(view, core, 2)
    return mine.transpose(1, 0, 2).reshape(-1)


def spread_bias(grad, core, fsdp_parts, kinds):
    width = grad.shape[0] // (kinds * (fsdp_parts // 2))
    view = grad.reshape(fsdp_parts // 2, kinds, width).transpose(1, 0, 2)
    zero = jnp.zeros_like(view)
    first = jnp.where(core == 0, view, zero)
    second = jnp.where(core == 0, zero, view)
    return jnp.stack([first, second], axis=2).reshape(-1)


def fast_device(
    clip_tokens,
    patch_coords,
    out_cotangent,
    vector_params,
    qkv_weight,
    proj_weight,
    up_weight,
    down_weight,
    first_vector,
    first_qkv,
    first_proj,
    first_up,
    first_down,
    second_vector,
    second_qkv,
    second_proj,
    second_up,
    second_down,
):
    masters = (vector_params, qkv_weight, proj_weight, up_weight, down_weight)
    firsts = (first_vector, first_qkv, first_proj, first_up, first_down)
    seconds = (second_vector, second_qkv, second_proj, second_up, second_down)
    layer_count = vector_params.shape[0]
    batch_local, chunk_len = clip_tokens.shape[:2]
    seq_parts = lax.axis_size("seq")
    parts = lax.axis_size("fsdp")
    ring = parts // 2
    seq = lax.axis_index("seq")
    shard = lax.axis_index("fsdp")
    core = lax.rem(shard, 2)
    even = lax.rem(seq, 2) == 0

    def to_clips(item, extra=None):
        halves = []
        for turn in range(2):
            piece = jnp.where(even, item[turn], item[1 - turn])
            pairs = []
            for src_seq in range(seq_parts):
                for src in range(parts):
                    dst_seq = 2 * (src % 2) + (src_seq + turn) % 2
                    dst = src - src % 2 + src_seq // 2
                    pairs.append((src_seq * parts + src, dst_seq * parts + dst))
            halves.append(lax.ppermute(piece, ("seq", "fsdp"), pairs))
        mine = jnp.where(
            even, jnp.stack([halves[0], halves[1]]), jnp.stack([halves[1], halves[0]])
        )
        other = swap_core(mine)
        both = jnp.where(core == 0, jnp.stack([mine, other]), jnp.stack([other, mine]))
        return both.reshape((4,) + item.shape[1:])

    def from_clips(item):
        mine = pick(item.reshape((2, 2, chunk_len) + item.shape[1:]), core)
        pieces = [None, None]
        for turn in range(2):
            piece = jnp.where(even, mine[turn], mine[1 - turn])
            pairs = []
            for src_seq in range(seq_parts):
                for src in range(parts):
                    dst_seq = 2 * (src % 2) + (src_seq + turn) % 2
                    dst = src - src % 2 + src_seq // 2
                    pairs.append((dst_seq * parts + dst, src_seq * parts + src))
            pieces[turn] = lax.ppermute(piece, ("seq", "fsdp"), pairs)
        return jnp.where(
            even, jnp.stack([pieces[0], pieces[1]]), jnp.stack([pieces[1], pieces[0]])
        )

    coord_rows = jnp.zeros((batch_local, 8, D), F32)
    coord_rows = lax.dynamic_update_slice(
        coord_rows, jnp.swapaxes(patch_coords, 0, 1).astype(F32), (0, 0, 0)
    )
    arrived = to_clips(jnp.concatenate([clip_tokens, coord_rows], axis=1))
    hidden = arrived[:, :chunk_len].reshape(4 * chunk_len, D)
    coords = arrived[:, chunk_len : chunk_len + 3, :chunk_len]
    coords = jnp.swapaxes(coords, 0, 1).reshape(3, 4 * chunk_len)
    cosine, sine = rotary_tables(coords, HEAD_DIM // 2)
    cos_wide = jnp.concatenate([cosine] * 4, axis=1)
    sin_wide = jnp.concatenate([-sine, sine, -sine, sine], axis=1)

    vector_all = lax.all_gather(vector_params.astype(BF), "fsdp", axis=1, tiled=True).astype(F32)

    def by_core(low, kinds):
        width = low.shape[2] // (kinds * parts)
        view = low.reshape(layer_count, low.shape[1], kinds, ring, 2, width)

        def half(which):
            cut = pick(view, which, 4).transpose(0, 1, 3, 2, 4)
            return cut.reshape(layer_count, low.shape[1], -1)

        return half(core), half(1 - core)

    gathered = gather_weights(
        *by_core(qkv_weight.astype(BF), 3),
        *by_core(up_weight.astype(BF), 1),
        down_weight.astype(BF),
        proj_weight.astype(BF),
    )
    layers = [
        (gathered[0][idx], gathered[3][idx, 0], gathered[3][idx, 1], gathered[1][idx], gathered[2][idx])
        for idx in range(layer_count)
    ]

    saved = []
    for idx in range(layer_count):
        qkv_w, proj_w, proj_other, up_w, down_w = layers[idx]
        gain_one, shift_one, gain_two, shift_two, proj_bias, down_bias, qkv_bias, up_bias = pieces(
            vector_all[idx]
        )
        qkv_bias = own_bias(qkv_bias, core, parts, 3)
        up_bias = own_bias(up_bias, core, parts, 1)
        normed = norm_forward(hidden, gain_one, shift_one)
        qkv_all = dot(normed, qkv_w) + qkv_bias
        mixed, low_all, lse = attend(qkv_all, cos_wide, sin_wide)
        mixed_other = swap_core(mixed)
        after_attn = hidden + (dot(mixed, proj_w) + dot(mixed_other, proj_other)) + proj_bias
        normed_two = norm_forward(after_attn, gain_two, shift_two)
        upward = dot(normed_two, up_w) + up_bias
        active, slope = gelu_and_slope(upward)
        active, slope = active.astype(BF), slope.astype(BF)
        part = dot(active, down_w)
        other = swap_core(part.astype(BF))
        result = after_attn + (part + other.astype(F32)) + down_bias
        saved.append((hidden, normed, low_all, lse, mixed, after_attn, normed_two, active, slope))
        hidden = result
    block_output = from_clips(hidden)

    grad = to_clips(out_cotangent).reshape(4 * chunk_len, D)
    sums = [None] * layer_count
    vector_sums = [None] * layer_count
    for idx in reversed(range(layer_count)):
        qkv_w, proj_w, proj_other, up_w, down_w = layers[idx]
        entry, normed, low_all, lse, mixed, after_attn, normed_two, active, slope = saved[idx]
        gain_one, shift_one, gain_two, shift_two, proj_bias, down_bias, qkv_bias, up_bias = pieces(
            vector_all[idx]
        )
        down_bias_grad = jnp.sum(grad, axis=0)
        grad_low = grad.astype(BF)
        upward_grad = dot_nt(grad_low, down_w) * slope.astype(F32)
        up_bias_grad = jnp.sum(upward_grad, axis=0)
        upward_low = upward_grad.astype(BF)
        part = dot_nt(upward_low, up_w)
        other = swap_core(part.astype(BF))
        down_grad = dot_tn(active, grad_low).astype(BF)
        up_grad = dot_tn(normed_two, upward_low).astype(BF)
        attn_in, gain_two_grad, shift_two_grad = norm_backward(
            after_attn, gain_two, part + other.astype(F32)
        )
        after_grad = grad + attn_in
        proj_bias_grad = jnp.sum(after_grad, axis=0)
        after_low = after_grad.astype(BF)
        mixed_grad = dot_nt(after_low, proj_w).astype(BF)
        proj_grad = dot_tn(mixed, after_low).astype(BF)
        qkv_low, bias_rows = attend_grad(low_all, mixed_grad, lse, cos_wide, sin_wide)
        part = dot_nt(qkv_low, qkv_w)
        other = swap_core(part.astype(BF))
        qkv_grad = dot_tn(normed, qkv_low).astype(BF)
        attn_in, gain_one_grad, shift_one_grad = norm_backward(
            entry, gain_one, part + other.astype(F32)
        )
        grad = after_grad + attn_in

        shared = jnp.concatenate(
            [
                gain_one_grad,
                shift_one_grad,
                gain_two_grad,
                shift_two_grad,
                proj_bias_grad,
                down_bias_grad,
            ]
        )
        vector_sums[idx] = jnp.concatenate(
            [
                jnp.where(core == 0, shared, jnp.zeros_like(shared)),
                spread_bias(bias_rows[0], core, parts, 3),
                spread_bias(up_bias_grad, core, parts, 1),
            ]
        )

        def owner_view(item, halves):
            rows = item.shape[0] // (ring * halves * 4)
            return item.reshape(ring, halves, 2, 2, rows, item.shape[1])

        def to_core(item):
            other = swap_core(pick(item, 1 - core))
            mine = pick(item, core)
            return jnp.where(core == 0, jnp.stack([mine, other]), jnp.stack([other, mine]))

        down_sum = ring_sum(plane_sum(owner_view(down_grad, 1), 2, False))[0]
        up_sum = to_core(ring_sum(plane_sum(owner_view(up_grad, 2), 2, True)))
        proj_sum = plane_sum(ring_sum(owner_view(proj_grad, 1)), 1, False)[0]
        qkv_sum = to_core(plane_sum(ring_sum(owner_view(qkv_grad, 2)), 1, True))
        rows = up_sum.shape[1]
        up_sum = up_sum.reshape(2, rows, ring, -1).transpose(1, 2, 0, 3).reshape(rows, -1)
        rows = qkv_sum.shape[1]
        qkv_sum = qkv_sum.reshape(2, rows, ring, 3, -1).transpose(1, 3, 2, 0, 4).reshape(rows, -1)
        sums[idx] = (qkv_sum, proj_sum, up_sum, down_sum)
    input_grad = from_clips(grad)

    clip_count = batch_local * parts
    quarter_sums = tuple(
        jnp.stack([sums[idx][kind] for idx in range(layer_count)]) for kind in range(4)
    )
    local_squares = sum(
        jnp.sum(jnp.square(item.astype(F32) * (1.0 / clip_count))) for item in quarter_sums
    )
    vector_total = lax.psum(jnp.stack(vector_sums), ("seq", "fsdp")) / clip_count
    squares = lax.psum(local_squares, ("seq", "fsdp")) + jnp.sum(vector_total * vector_total)
    norm_value = jnp.sqrt(squares)
    param_count = sum(master.size for master in masters) * parts
    factor = jnp.minimum(1.0, CLIP_RATIO * math.sqrt(float(param_count)) / (norm_value + 1e-06))

    share = vector_params.shape[1]
    grad_shards = [lax.dynamic_slice_in_dim(vector_total, shard * share, share, 1)]
    for item in quarter_sums:
        whole = lax.all_gather(item, "seq", axis=1, tiled=True)
        grad_shards.append(whole.astype(F32) / clip_count)
    updates = [
        adam_update(master, grad_item, first_old, second_old, factor)
        for master, grad_item, first_old, second_old in zip(masters, grad_shards, firsts, seconds)
    ]
    return (
        block_output,
        input_grad,
        *grad_shards,
        norm_value.reshape(1),
        *[item[0] for item in updates],
        *[item[1] for item in updates],
        *[item[2] for item in updates],
        *[item[2].astype(BF) for item in updates],
    )


def solution(mesh):
    in_specs = (
        P("fsdp", "seq", None),
        P(None, "fsdp", "seq"),
        P("fsdp", "seq", None),
        P(None, "fsdp"),
        P(None, "fsdp", None),
        P(None, "fsdp", None),
        P(None, "fsdp", None),
        P(None, "fsdp", None),
        P(None, "fsdp"),
        P(None, "fsdp", None),
        P(None, "fsdp", None),
        P(None, "fsdp", None),
        P(None, "fsdp", None),
        P(None, "fsdp"),
        P(None, "fsdp", None),
        P(None, "fsdp", None),
        P(None, "fsdp", None),
        P(None, "fsdp", None),
    )
    out_specs = (
        P("fsdp", "seq", None),
        P("fsdp", "seq", None),
        P(None, "fsdp"),
        P(None, "fsdp", None),
        P(None, "fsdp", None),
        P(None, "fsdp", None),
        P(None, "fsdp", None),
        P(),
        P(None, "fsdp"),
        P(None, "fsdp", None),
        P(None, "fsdp", None),
        P(None, "fsdp", None),
        P(None, "fsdp", None),
        P(None, "fsdp"),
        P(None, "fsdp", None),
        P(None, "fsdp", None),
        P(None, "fsdp", None),
        P(None, "fsdp", None),
        P(None, "fsdp"),
        P(None, "fsdp", None),
        P(None, "fsdp", None),
        P(None, "fsdp", None),
        P(None, "fsdp", None),
        P(None, "fsdp"),
        P(None, "fsdp", None),
        P(None, "fsdp", None),
        P(None, "fsdp", None),
        P(None, "fsdp", None),
    )
    body = fast_device if fits_fast(mesh) else general_device
    return jax.shard_map(
        body, mesh=mesh, in_specs=in_specs, out_specs=out_specs, check_vma=False
    )
```

```python
from functools import partial
import math

import jax
import jax.numpy as jnp
from jax import lax
from jax.experimental import pallas as pl
from jax.experimental.pallas import tpu as pltpu
from jax.sharding import PartitionSpec as P

D = 1024
HEADS = 16
HEAD_DIM = 64


BETA_ONE = 0.5
BETA_TWO = 0.75
LEARN_RATE = 0.1
DECAY_RATE = 0.1
CLIP_RATIO = 0.2
ADAM_EPS = 1e-08
ROPE_BASE = 10000.0


def pieces(vector):
    return (
        vector[0:D],
        vector[D : 2 * D],
        vector[2 * D : 3 * D],
        vector[3 * D : 4 * D],
        vector[4 * D : 5 * D],
        vector[5 * D : 6 * D],
        vector[6 * D : 9 * D],
        vector[9 * D :],
    )


def layer_norm(hidden, ln_gain, ln_shift):
    center = hidden - jnp.mean(hidden, axis=-1, keepdims=True)
    spread = jnp.mean(center * center, axis=-1, keepdims=True)
    return center * lax.rsqrt(spread + 1e-06) * ln_gain + ln_shift


def gelu_exact(upward):
    return 0.5 * upward * (1.0 + jax.scipy.special.erf(upward * (1.0 / math.sqrt(2.0))))


def rotary_tables(coords_clip, pair_count):
    pair_index = jnp.arange(pair_count, dtype=jnp.int32)
    side_pairs = pair_count // 3
    time_pairs = pair_count - 2 * side_pairs
    in_time = pair_index < time_pairs
    in_height = jnp.logical_and(pair_index >= time_pairs, pair_index < time_pairs + side_pairs)
    offset = jnp.where(in_time, 0, jnp.where(in_height, time_pairs, time_pairs + side_pairs))
    seg_span = jnp.where(in_time, time_pairs, side_pairs)
    local_rank = (pair_index - offset).astype(jnp.float32)
    frequency = jnp.exp(-math.log(ROPE_BASE) * local_rank / seg_span.astype(jnp.float32))
    positions = coords_clip.astype(jnp.float32)
    chosen = jnp.where(
        in_time[None, :],
        positions[0][:, None],
        jnp.where(in_height[None, :], positions[1][:, None], positions[2][:, None]),
    )
    angles = chosen * frequency[None, :]
    return (jnp.cos(angles), jnp.sin(angles))


def rotate(values_in, cosine, sine_table):
    half_width = values_in.shape[-1] // 2
    first_half = values_in[..., :half_width]
    second_half = values_in[..., half_width:]
    cos_wide = cosine[:, None, :]
    sin_wide = sine_table[:, None, :]
    return jnp.concatenate(
        [
            first_half * cos_wide - second_half * sin_wide,
            first_half * sin_wide + second_half * cos_wide,
        ],
        axis=-1,
    )


def attend_forward(queries, key_rows, value_rows):
    full_len = queries.shape[0]
    block_rows = min(512, full_len)
    score_scale = HEAD_DIM ** (-0.5)
    query_blocks = queries.reshape(
        full_len // block_rows, block_rows, queries.shape[1], queries.shape[2]
    )

    def one_block(query_block):
        scores = (
            jnp.einsum("qhd,khd->hqk", query_block, key_rows, preferred_element_type=jnp.float32)
            * score_scale
        )
        row_max = jnp.max(scores, axis=-1, keepdims=True)
        exponent = jnp.exp(scores - row_max)
        row_total = jnp.sum(exponent, axis=-1, keepdims=True)
        prob_low = (exponent / row_total).astype(jnp.bfloat16)
        mixed_rows = jnp.einsum(
            "hqk,khd->qhd", prob_low, value_rows, preferred_element_type=jnp.float32
        )
        return (mixed_rows, row_max[..., 0] + jnp.log(row_total[..., 0]))

    mixed_rows, log_sums = lax.map(one_block, query_blocks)
    return (mixed_rows.reshape(queries.shape), log_sums)


def attend_backward(queries, key_rows, value_rows, log_sums, head_grad):
    full_len = queries.shape[0]
    block_rows = min(512, full_len)
    score_scale = HEAD_DIM ** (-0.5)
    block_shape = (full_len // block_rows, block_rows, queries.shape[1], queries.shape[2])

    def one_block(carry, block_in):
        key_grad, value_grad = carry
        query_block, grad_block, lse_block = block_in
        scores = (
            jnp.einsum("qhd,khd->hqk", query_block, key_rows, preferred_element_type=jnp.float32)
            * score_scale
        )
        prob_rows = jnp.exp(scores - lse_block[..., None])
        prob_low = prob_rows.astype(jnp.bfloat16)
        value_grad = value_grad + jnp.einsum(
            "hqk,qhd->khd", prob_low, grad_block, preferred_element_type=jnp.float32
        )
        prob_grad = jnp.einsum(
            "qhd,khd->hqk", grad_block, value_rows, preferred_element_type=jnp.float32
        )
        score_grad = prob_rows * (
            prob_grad - jnp.sum(prob_rows * prob_grad, axis=-1, keepdims=True)
        )
        score_low = (score_grad * score_scale).astype(jnp.bfloat16)
        query_grad = jnp.einsum(
            "hqk,khd->qhd", score_low, key_rows, preferred_element_type=jnp.float32
        )
        key_grad = key_grad + jnp.einsum(
            "hqk,qhd->khd", score_low, query_block, preferred_element_type=jnp.float32
        )
        return ((key_grad, value_grad), query_grad)

    zero_heads = jnp.zeros(queries.shape, jnp.float32)
    (key_grad, value_grad), query_grad = lax.scan(
        one_block,
        (zero_heads, zero_heads),
        (queries.reshape(block_shape), head_grad.reshape(block_shape), log_sums),
    )
    return (query_grad.reshape(queries.shape), key_grad, value_grad)


def layer_forward(hidden, cosine, sine_table, weights, seq_parts):
    vector_low, qkv_w, proj_w, up_w, down_w = weights
    gain_one, shift_one, gain_two, shift_two, proj_bias, down_bias, qkv_bias, up_bias = pieces(
        vector_low.astype(jnp.float32)
    )
    row_count = hidden.shape[0]
    local_heads = HEADS // seq_parts
    normed = layer_norm(hidden, gain_one, shift_one).astype(jnp.bfloat16)
    qkv_all = jnp.dot(normed, qkv_w, preferred_element_type=jnp.float32) + qkv_bias
    split_qkv = qkv_all.reshape(row_count, 3, HEADS, HEAD_DIM)
    stacked = jnp.stack(
        [
            rotate(split_qkv[:, 0], cosine, sine_table),
            rotate(split_qkv[:, 1], cosine, sine_table),
            split_qkv[:, 2],
        ],
        axis=1,
    ).astype(jnp.bfloat16)
    packed = stacked.reshape(row_count, 3, seq_parts, local_heads * HEAD_DIM)
    by_heads = lax.all_to_all(packed, "seq", split_axis=2, concat_axis=0, tiled=True)
    full_len = by_heads.shape[0]
    by_heads = by_heads.reshape(full_len, 3, local_heads, HEAD_DIM)
    mixed_rows, log_sums = attend_forward(by_heads[:, 0], by_heads[:, 1], by_heads[:, 2])
    mixed_low = mixed_rows.astype(jnp.bfloat16).reshape(full_len, 1, local_heads * HEAD_DIM)
    by_tokens = lax.all_to_all(mixed_low, "seq", split_axis=0, concat_axis=1, tiled=True).reshape(
        row_count, D
    )
    after_attn = hidden + jnp.dot(by_tokens, proj_w, preferred_element_type=jnp.float32) + proj_bias
    normed_two = layer_norm(after_attn, gain_two, shift_two).astype(jnp.bfloat16)
    upward = jnp.dot(normed_two, up_w, preferred_element_type=jnp.float32) + up_bias
    active = gelu_exact(upward).astype(jnp.bfloat16)
    result = after_attn + jnp.dot(active, down_w, preferred_element_type=jnp.float32) + down_bias
    saved_state = (
        hidden,
        normed,
        by_heads,
        log_sums,
        by_tokens,
        after_attn,
        normed_two,
        upward,
        active,
    )
    return (result, saved_state)


def layer_backward(grad_out, saved_state, weights, cosine, sine_table, seq_parts):
    vector_low, qkv_w, proj_w, up_w, down_w = weights
    gain_one, shift_one, gain_two, shift_two, proj_bias, down_bias, qkv_bias, up_bias = pieces(
        vector_low.astype(jnp.float32)
    )
    hidden, normed, by_heads, log_sums, by_tokens, after_attn, normed_two, upward, active = (
        saved_state
    )
    row_count = hidden.shape[0]
    local_heads = HEADS // seq_parts
    down_bias_grad = jnp.sum(grad_out, axis=0)
    grad_low = grad_out.astype(jnp.bfloat16)
    down_grad = jnp.dot(active.T, grad_low, preferred_element_type=jnp.float32)
    active_grad = jnp.dot(grad_low, down_w.T, preferred_element_type=jnp.float32)
    gelu_value, gelu_pull = jax.vjp(gelu_exact, upward)
    upward_grad = gelu_pull(active_grad)[0]
    up_bias_grad = jnp.sum(upward_grad, axis=0)
    upward_low = upward_grad.astype(jnp.bfloat16)
    up_grad = jnp.dot(normed_two.T, upward_low, preferred_element_type=jnp.float32)
    normed_two_grad = jnp.dot(upward_low, up_w.T, preferred_element_type=jnp.float32)
    norm_value_two, norm_pull_two = jax.vjp(layer_norm, after_attn, gain_two, shift_two)
    attn_in_grad, gain_two_grad, shift_two_grad = norm_pull_two(normed_two_grad)
    after_grad = grad_out + attn_in_grad
    proj_bias_grad = jnp.sum(after_grad, axis=0)
    after_low = after_grad.astype(jnp.bfloat16)
    proj_grad = jnp.dot(by_tokens.T, after_low, preferred_element_type=jnp.float32)
    mixed_grad = jnp.dot(after_low, proj_w.T, preferred_element_type=jnp.float32).astype(
        jnp.bfloat16
    )
    head_grad = lax.all_to_all(
        mixed_grad.reshape(row_count, seq_parts, local_heads * HEAD_DIM),
        "seq",
        split_axis=1,
        concat_axis=0,
        tiled=True,
    )
    full_len = head_grad.shape[0]
    head_grad = head_grad.reshape(full_len, local_heads, HEAD_DIM)
    query_grad, key_grad, value_grad = attend_backward(
        by_heads[:, 0], by_heads[:, 1], by_heads[:, 2], log_sums, head_grad
    )
    stacked_grad = (
        jnp.stack([query_grad, key_grad, value_grad], axis=1)
        .astype(jnp.bfloat16)
        .reshape(full_len, 3, 1, local_heads * HEAD_DIM)
    )
    token_grad = (
        lax.all_to_all(stacked_grad, "seq", split_axis=0, concat_axis=2, tiled=True)
        .reshape(row_count, 3, HEADS, HEAD_DIM)
        .astype(jnp.float32)
    )
    pair_grad_in = token_grad[:, :2].reshape(row_count, 2 * HEADS, HEAD_DIM)
    rotated_value, rotate_pull = jax.vjp(
        partial(rotate, cosine=cosine, sine_table=sine_table), pair_grad_in
    )
    pair_grad = rotate_pull(pair_grad_in)[0].reshape(row_count, 2, HEADS, HEAD_DIM)
    qkv_grad = jnp.concatenate([pair_grad, token_grad[:, 2:]], axis=1).reshape(row_count, 3 * D)
    qkv_bias_grad = jnp.sum(qkv_grad, axis=0)
    qkv_low = qkv_grad.astype(jnp.bfloat16)
    qkv_w_grad = jnp.dot(normed.T, qkv_low, preferred_element_type=jnp.float32)
    normed_grad = jnp.dot(qkv_low, qkv_w.T, preferred_element_type=jnp.float32)
    norm_value_one, norm_pull_one = jax.vjp(layer_norm, hidden, gain_one, shift_one)
    in_grad, gain_one_grad, shift_one_grad = norm_pull_one(normed_grad)
    input_grad = after_grad + in_grad
    vector_grad = jnp.concatenate(
        [
            gain_one_grad,
            shift_one_grad,
            gain_two_grad,
            shift_two_grad,
            proj_bias_grad,
            down_bias_grad,
            qkv_bias_grad,
            up_bias_grad,
        ]
    )
    return (input_grad, (vector_grad, qkv_w_grad, proj_grad, up_grad, down_grad))


def adam_update(master, grad_item, first_old, second_old, factor):
    clipped = grad_item * factor
    first_new = BETA_ONE * first_old + (1.0 - BETA_ONE) * clipped
    second_new = BETA_TWO * second_old + (1.0 - BETA_TWO) * clipped * clipped
    updated = master - LEARN_RATE * (
        first_new / (jnp.sqrt(second_new) + ADAM_EPS) + DECAY_RATE * master
    )
    return (first_new, second_new, updated)


def general_device(
    clip_tokens,
    patch_coords,
    out_cotangent,
    vector_params,
    qkv_weight,
    proj_weight,
    up_weight,
    down_weight,
    first_vector,
    first_qkv,
    first_proj,
    first_up,
    first_down,
    second_vector,
    second_qkv,
    second_proj,
    second_up,
    second_down,
):
    masters = (vector_params, qkv_weight, proj_weight, up_weight, down_weight)
    firsts = (first_vector, first_qkv, first_proj, first_up, first_down)
    seconds = (second_vector, second_qkv, second_proj, second_up, second_down)
    lowered = tuple((master.astype(jnp.bfloat16) for master in masters))
    layer_count = vector_params.shape[0]
    batch_local = clip_tokens.shape[0]
    seq_parts = lax.axis_size("seq")
    fsdp_parts = lax.axis_size("fsdp")
    grad_accum = tuple(
        (
            jnp.zeros((layer_count, master.shape[1] * fsdp_parts) + master.shape[2:], jnp.float32)
            for master in masters
        )
    )
    output_rows = []
    input_rows = []
    for batch_idx in range(batch_local):
        cosine, sine_table = rotary_tables(patch_coords[:, batch_idx], HEAD_DIM // 2)
        hidden = clip_tokens[batch_idx]
        saved_layers = []
        for layer_idx in range(layer_count):
            weights = (
                lax.all_gather(lowered[0][layer_idx], "fsdp", axis=0, tiled=True),
                lax.all_gather(lowered[1][layer_idx], "fsdp", axis=0, tiled=True),
                lax.all_gather(lowered[2][layer_idx], "fsdp", axis=0, tiled=True),
                lax.all_gather(lowered[3][layer_idx], "fsdp", axis=0, tiled=True),
                lax.all_gather(lowered[4][layer_idx], "fsdp", axis=0, tiled=True),
            )
            hidden, saved_state = layer_forward(hidden, cosine, sine_table, weights, seq_parts)
            saved_layers.append(saved_state)
        output_rows.append(hidden)
        grad_rows = out_cotangent[batch_idx]
        for layer_idx in reversed(range(layer_count)):
            weights = (
                lax.all_gather(lowered[0][layer_idx], "fsdp", axis=0, tiled=True),
                lax.all_gather(lowered[1][layer_idx], "fsdp", axis=0, tiled=True),
                lax.all_gather(lowered[2][layer_idx], "fsdp", axis=0, tiled=True),
                lax.all_gather(lowered[3][layer_idx], "fsdp", axis=0, tiled=True),
                lax.all_gather(lowered[4][layer_idx], "fsdp", axis=0, tiled=True),
            )
            grad_rows, layer_grads = layer_backward(
                grad_rows, saved_layers[layer_idx], weights, cosine, sine_table, seq_parts
            )
            grad_accum = tuple(
                (
                    accum_item.at[layer_idx].add(grad_item)
                    for accum_item, grad_item in zip(grad_accum, layer_grads)
                )
            )
        input_rows.append(grad_rows)
    shard_sums = (
        lax.psum_scatter(grad_accum[0], "fsdp", scatter_dimension=1, tiled=True),
        lax.psum_scatter(grad_accum[1], "fsdp", scatter_dimension=1, tiled=True),
        lax.psum_scatter(grad_accum[2], "fsdp", scatter_dimension=1, tiled=True),
        lax.psum_scatter(grad_accum[3], "fsdp", scatter_dimension=1, tiled=True),
        lax.psum_scatter(grad_accum[4], "fsdp", scatter_dimension=1, tiled=True),
    )
    seq_sums = lax.psum(
        (shard_sums[0], shard_sums[1], shard_sums[2], shard_sums[3], shard_sums[4]), "seq"
    )
    clip_count = batch_local * fsdp_parts
    grad_shards = tuple((sum_item / clip_count for sum_item in seq_sums))
    local_squares = sum((jnp.sum(grad_item * grad_item) for grad_item in grad_shards))
    squares_total = lax.psum(local_squares, "fsdp")
    norm_value = jnp.sqrt(squares_total)
    param_count = sum((master.size for master in masters)) * fsdp_parts
    factor = jnp.minimum(1.0, CLIP_RATIO * math.sqrt(float(param_count)) / (norm_value + 1e-06))
    updates = [
        adam_update(master, grad_item, first_old, second_old, factor)
        for master, grad_item, first_old, second_old in zip(masters, grad_shards, firsts, seconds)
    ]
    return (
        jnp.stack(output_rows),
        jnp.stack(input_rows),
        grad_shards[0],
        grad_shards[1],
        grad_shards[2],
        grad_shards[3],
        grad_shards[4],
        norm_value.reshape(1),
        updates[0][0],
        updates[1][0],
        updates[2][0],
        updates[3][0],
        updates[4][0],
        updates[0][1],
        updates[1][1],
        updates[2][1],
        updates[3][1],
        updates[4][1],
        updates[0][2],
        updates[1][2],
        updates[2][2],
        updates[3][2],
        updates[4][2],
        updates[0][2].astype(jnp.bfloat16),
        updates[1][2].astype(jnp.bfloat16),
        updates[2][2].astype(jnp.bfloat16),
        updates[3][2].astype(jnp.bfloat16),
        updates[4][2].astype(jnp.bfloat16),
    )


ROWS_Q = 256
PAIR = 2 * HEAD_DIM
BF = jnp.bfloat16
F32 = jnp.float32
VMEM_LIMIT = 56 * 1024 * 1024


def fits_fast(mesh):
    return dict(mesh.shape) == {"seq": 4, "fsdp": 8}


def swap_core(item):
    parts = lax.axis_size("fsdp")
    return lax.ppermute(item, "fsdp", [(idx, idx ^ 1) for idx in range(parts)])


def send_up(item):
    parts = lax.axis_size("fsdp")
    return lax.ppermute(item, "fsdp", [(idx, (idx + 2) % parts) for idx in range(parts)])


def swap_seq(item, mask):
    parts = lax.axis_size("seq")
    return lax.ppermute(item, "seq", [(idx, idx ^ mask) for idx in range(parts)])


def pick(item, index, axis=0):
    return lax.dynamic_index_in_dim(item, index, axis, keepdims=False)


def swap_halves(item):
    lane = lax.broadcasted_iota(jnp.int32, item.shape, 1)
    half = HEAD_DIM // 2
    width = item.shape[1]
    ahead = pltpu.roll(item, width - half, 1)
    behind = pltpu.roll(item, half, 1)
    return jnp.where(lane % HEAD_DIM < half, ahead, behind)


NT = (((1,), (1,)), ((), ()))


def head_mask(item, head):
    lane = lax.broadcasted_iota(jnp.int32, item.shape, 1)
    return jnp.where(lane // HEAD_DIM == head, item, jnp.zeros_like(item))


def attn_fwd_kernel(qkv_ref, cos_ref, sin_ref, mixed_ref, low_ref, lse_ref, qs_ref):
    cosine, sine = cos_ref[...], sin_ref[...]
    queries = qkv_ref[:, 0:PAIR]
    key_rows = qkv_ref[:, PAIR : 2 * PAIR]
    values = qkv_ref[:, 2 * PAIR : 3 * PAIR]
    queries = (queries * cosine + swap_halves(queries) * sine).astype(BF)
    key_rows = (key_rows * cosine + swap_halves(key_rows) * sine).astype(BF)
    low_ref[:, 0:PAIR] = queries
    low_ref[:, PAIR : 2 * PAIR] = key_rows
    low_ref[:, 2 * PAIR : 3 * PAIR] = values.astype(BF)
    qs_ref[...] = queries * jnp.asarray(HEAD_DIM**-0.5, BF)
    values_t = values.T.astype(BF)
    keys_by_head = [head_mask(key_rows, head) for head in range(2)]
    length = qs_ref.shape[0]

    @pl.loop(0, length // ROWS_Q)
    def _(step):
        rows = pl.ds(pl.multiple_of(step * ROWS_Q, ROWS_Q), ROWS_Q)
        block = qs_ref[rows, :]
        outs = []
        for head in range(2):
            scores = lax.dot_general(keys_by_head[head], block, NT, preferred_element_type=F32)
            top = jnp.max(scores, axis=0, keepdims=True)
            exponent = jnp.exp(scores - top)
            total = jnp.sum(exponent, axis=0, keepdims=True)
            lse_ref[0, head : head + 1, rows] = top + jnp.log(total)
            probs = (exponent * (1.0 / total)).astype(BF)
            outs.append(
                jnp.dot(
                    values_t[head * HEAD_DIM : (head + 1) * HEAD_DIM],
                    probs,
                    preferred_element_type=F32,
                )
            )
        mixed_ref[rows, :] = jnp.concatenate(outs, axis=0).T.astype(BF)


def attend(qkv_all, cos_wide, sin_wide):
    length, width = qkv_all.shape
    pairs = width // (3 * PAIR)
    table = pl.BlockSpec((length, PAIR), lambda pair: (0, 0))
    triple = pl.BlockSpec((length, 3 * PAIR), lambda pair: (0, pair))
    return pl.pallas_call(
        attn_fwd_kernel,
        grid=(pairs,),
        in_specs=[triple, table, table],
        out_specs=[
            pl.BlockSpec((length, PAIR), lambda pair: (0, pair)),
            triple,
            pl.BlockSpec((1, 8, length), lambda pair: (pair, 0, 0)),
        ],
        out_shape=[
            jax.ShapeDtypeStruct((length, pairs * PAIR), BF),
            jax.ShapeDtypeStruct((length, width), BF),
            jax.ShapeDtypeStruct((pairs, 8, length), F32),
        ],
        scratch_shapes=[pltpu.VMEM((length, PAIR), BF)],
        compiler_params=pltpu.CompilerParams(vmem_limit_bytes=VMEM_LIMIT),
        cost_estimate=pl.CostEstimate(
            flops=16 * pairs * length * length * PAIR,
            bytes_accessed=length * width * 8,
            transcendentals=2 * pairs * length * length,
        ),
        name="attend",
    )(qkv_all, cos_wide, sin_wide)


def attn_bwd_kernel(
    low_ref, dout_ref, lse_ref, cos_ref, sin_ref, grad_ref, bias_ref, dq_ref, dk_ref, dv_ref
):
    length = low_ref.shape[0]
    key_rows = low_ref[:, PAIR : 2 * PAIR]
    values = low_ref[:, 2 * PAIR : 3 * PAIR]
    keys_t = key_rows.astype(F32).T.astype(BF)
    keys_by_head = [head_mask(key_rows, head) for head in range(2)]
    values_by_head = [head_mask(values, head) for head in range(2)]
    scale = HEAD_DIM**-0.5
    dk_ref[...] = jnp.zeros_like(dk_ref)
    dv_ref[...] = jnp.zeros_like(dv_ref)

    @pl.loop(0, length // ROWS_Q)
    def _(step):
        rows = pl.ds(pl.multiple_of(step * ROWS_Q, ROWS_Q), ROWS_Q)
        block = low_ref[rows, 0:PAIR]
        scaled = block * jnp.asarray(scale, BF)
        dout = dout_ref[rows, :]
        outs = []
        for head in range(2):
            scores = lax.dot_general(keys_by_head[head], scaled, NT, preferred_element_type=F32)
            probs = jnp.exp(scores - lse_ref[0, head : head + 1, rows])
            prob_grad = lax.dot_general(values_by_head[head], dout, NT, preferred_element_type=F32)
            delta = jnp.sum(probs * prob_grad, axis=0, keepdims=True)
            score_low = (probs * (prob_grad - delta) * scale).astype(BF)
            dv_ref[head] += jnp.dot(probs.astype(BF), dout, preferred_element_type=F32)
            dk_ref[head] += jnp.dot(score_low, block, preferred_element_type=F32)
            outs.append(
                jnp.dot(
                    keys_t[head * HEAD_DIM : (head + 1) * HEAD_DIM],
                    score_low,
                    preferred_element_type=F32,
                )
            )
        dq_ref[rows, :] = jnp.concatenate(outs, axis=0).T

    lane = lax.broadcasted_iota(jnp.int32, (length, PAIR), 1)
    first = lane // HEAD_DIM == 0
    cosine, sine = cos_ref[...], sin_ref[...]

    def rounded(item):
        return item.astype(BF).astype(F32)

    def back(item):
        return item * cosine - swap_halves(item) * sine

    parts = [
        back(rounded(dq_ref[...])),
        back(rounded(jnp.where(first, dk_ref[0], dk_ref[1]))),
        rounded(jnp.where(first, dv_ref[0], dv_ref[1])),
    ]
    for idx, part in enumerate(parts):
        cols = slice(idx * PAIR, (idx + 1) * PAIR)
        grad_ref[:, cols] = part.astype(BF)
        bias_ref[:, cols] = jnp.broadcast_to(jnp.sum(part, axis=0, keepdims=True), (8, PAIR))


def attend_grad(low_all, mixed_grad, lse, cos_wide, sin_wide):
    length, width = low_all.shape
    pairs = width // (3 * PAIR)
    table = pl.BlockSpec((length, PAIR), lambda pair: (0, 0))
    triple = pl.BlockSpec((length, 3 * PAIR), lambda pair: (0, pair))
    return pl.pallas_call(
        attn_bwd_kernel,
        grid=(pairs,),
        in_specs=[
            triple,
            pl.BlockSpec((length, PAIR), lambda pair: (0, pair)),
            pl.BlockSpec((1, 8, length), lambda pair: (pair, 0, 0)),
            table,
            table,
        ],
        out_specs=[triple, pl.BlockSpec((8, 3 * PAIR), lambda pair: (0, pair))],
        out_shape=[
            jax.ShapeDtypeStruct((length, width), BF),
            jax.ShapeDtypeStruct((8, width), F32),
        ],
        scratch_shapes=[
            pltpu.VMEM((length, PAIR), F32),
            pltpu.VMEM((2, length, PAIR), F32),
            pltpu.VMEM((2, length, PAIR), F32),
        ],
        compiler_params=pltpu.CompilerParams(vmem_limit_bytes=VMEM_LIMIT),
        cost_estimate=pl.CostEstimate(
            flops=40 * pairs * length * length * PAIR,
            bytes_accessed=length * width * 6,
            transcendentals=2 * pairs * length * length,
        ),
        name="attend_grad",
    )(low_all, mixed_grad, lse, cos_wide, sin_wide)


class Places:
    def __init__(self):
        shard, seq = lax.axis_index("fsdp"), lax.axis_index("seq")
        parts = lax.axis_size("fsdp")
        self.ring = parts // 2
        self.seq = seq
        self.chip, self.core = shard // 2, lax.rem(shard, 2)
        self.at_x, self.at_y = lax.rem(seq, 2), seq // 2
        self.near_x = 2 * self.at_y + 1 - self.at_x
        self.near_y = 2 * (1 - self.at_y) + self.at_x
        self.other = {"fsdp": shard + 1 - 2 * self.core}
        self.up = {"fsdp": lax.rem(shard + 2, parts)}
        self.down = {"fsdp": lax.rem(shard + parts - 2, parts)}
        self.over_x = {"seq": self.near_x}
        self.over_y = {"seq": self.near_y}

    def back(self, hops):
        return lax.rem(self.chip - hops + self.ring, self.ring)


def remote(src, dst, send, recv, target):
    return pltpu.make_async_remote_copy(
        src_ref=src,
        dst_ref=dst,
        send_sem=send,
        recv_sem=recv,
        device_id=target,
        device_id_type=pl.DeviceIdType.MESH,
    )


def greet(targets, waits):
    barrier = pltpu.get_barrier_semaphore()
    for target in targets:
        pl.semaphore_signal(barrier, inc=1, device_id=target, device_id_type=pl.DeviceIdType.MESH)
    pl.semaphore_wait(barrier, waits)


def aligned(start, size, unit=None):
    return pl.ds(pl.multiple_of(start, unit or size), size)


def gather_kernel(
    qkv_in, up_in, down_in, proj_in, clip_in, coord_in, vec_in,
    qkv_out, up_out, down_out, proj_out, clip_out, coord_out, vec_out,
    qkv_full, up_full, down_full, proj_full,
    qkv_away, up_away,
    qkv_slab, up_slab, down_slab, proj_slab, clip_slab,
    z_send, z_recv, p_send, p_recv, d_send, d_recv, c_send, c_recv, l_in, l_out,
    m_send, m_recv, m_load,
):
    at = Places()
    ring, seq, chip, core = at.ring, at.seq, at.chip, at.core
    other, up_chip = at.other, at.up
    over_x, over_y, near_x, near_y = at.over_x, at.over_y, at.near_x, at.near_y
    layers = qkv_in.shape[0]
    loads = {}

    def start_load(name, layer, slot):
        source, full = {
            "qkv": (qkv_in, qkv_full),
            "up": (up_in, up_full),
            "down": (down_in, down_full),
            "proj": (proj_in, proj_full),
        }[name]
        copy = pltpu.make_async_copy(source.at[layer], full.at[layer], l_in.at[slot])
        copy.start()
        loads[name, layer] = copy

    outs = {"qkv": qkv_out, "up": up_out, "down": down_out, "proj": proj_out}
    slabs = {"qkv": qkv_slab, "up": up_slab, "down": down_slab, "proj": proj_slab}
    items = [(name, layer) for layer in range(layers) for name in ("qkv", "proj", "up", "down")]

    def place(name, layer, chip_at, part):
        slab = slabs[name].shape[1]
        if part is None:
            start, size = chip_at * slab, slab
        else:
            size = slab // 4
            start = chip_at * slab + part * size
        rows = pl.ds(pl.multiple_of(start, size), size)
        if name == "proj":
            return outs[name].at[layer, 0, rows, :]
        return outs[name].at[layer, rows, :]

    for idx, (name, layer) in enumerate(items):
        start_load(name, layer, idx)
    clip_load = pltpu.make_async_copy(clip_in.at[lax.rem(seq, 2)], clip_slab, m_load.at[0])
    clip_load.start()
    barrier = pltpu.get_barrier_semaphore()
    for target in (other, up_chip, at.down):
        pl.semaphore_signal(barrier, inc=1, device_id=target, device_id_type=pl.DeviceIdType.MESH)
    for step in range(1, 4):
        for half in range(2):
            pl.semaphore_signal(
                barrier,
                inc=1,
                device_id={"fsdp": 2 * chip + half, "seq": seq ^ step},
                device_id_type=pl.DeviceIdType.MESH,
            )
    pl.semaphore_wait(barrier, 9)

    length = clip_in.shape[1]
    token_core = seq // 2
    token_rows = aligned(seq * length, length)
    stays = core == token_core
    clip_copies = []
    for turn in range(2):
        target = {"seq": 2 * core + turn, "fsdp": 2 * chip + token_core}
        slot = 2 * lax.rem(seq, 2)
        copies = [
            remote(
                clip_in.at[turn], clip_out.at[token_rows, :], m_send.at[2 * turn], m_recv.at[slot], target
            ),
            remote(
                coord_in.at[turn], coord_out.at[seq], m_send.at[2 * turn + 1], m_recv.at[slot + 1], target
            ),
        ]
        away = jnp.logical_not(jnp.logical_and(stays, lax.rem(seq, 2) == turn))
        clip_copies.append((away, copies))

        @pl.when(away)
        def _(copies=copies):
            for copy in copies:
                copy.start()

    clip_load.wait()
    clip_store = pltpu.make_async_copy(clip_slab, clip_out.at[token_rows, :], m_load.at[1])

    @pl.when(stays)
    def _():
        clip_store.start()
        coord_out[seq] = coord_in[lax.rem(seq, 2)]

    vec_out[2 * chip + core] = vec_in[...]
    vec_swap = remote(
        vec_in, vec_out.at[2 * chip + core], m_send.at[8], m_recv.at[8], other
    )
    vec_swap.start()

    def clip_arrived():
        for part in range(2):
            came = jnp.logical_not(jnp.logical_and(stays, lax.rem(seq, 2) == part))

            @pl.when(came)
            def _(part=part):
                rows = aligned((2 * core + part) * length, length)
                remote(
                    clip_in.at[0], clip_out.at[rows, :], m_send.at[0], m_recv.at[2 * part], other
                ).wait_recv()
                remote(
                    coord_in.at[0],
                    coord_out.at[2 * core + part],
                    m_send.at[0],
                    m_recv.at[2 * part + 1],
                    other,
                ).wait_recv()

        @pl.when(stays)
        def _():
            clip_store.wait()

        rows = clip_out.at[aligned(core * 2 * length, 2 * length), :]
        swaps = [remote(rows, rows, m_send.at[4], m_recv.at[4], other)]
        ref = coord_out.at[pl.ds(2 * core, 2)]
        swaps.append(remote(ref, ref, m_send.at[5], m_recv.at[5], other))
        for copy in swaps:
            copy.start()
        return swaps

    vec_copies = []

    def vec_hop(hop):
        (vec_copies[-1] if vec_copies else vec_swap).wait_recv()
        ref = vec_out.at[pl.ds(2 * at.back(hop), 2)]
        copy = remote(ref, ref, m_send.at[9 + hop], m_recv.at[9 + hop], up_chip)
        copy.start()
        vec_copies.append(copy)

    swaps, prepared = {}, []

    def prepare():
        if len(prepared) == len(items):
            return
        idx = len(prepared)
        name, layer = items[idx]
        prepared.append(name)
        slab = slabs[name]
        loads[name, layer].wait()
        swaps[idx] = None
        if name in ("down", "proj"):
            full = down_full if name == "down" else proj_full
            slab[layer] = full[layer].astype(BF)
            return
        full, away, kinds = (
            (qkv_full, qkv_away, 3) if name == "qkv" else (up_full, up_away, 1)
        )
        half, columns = full.shape[1], full.shape[2]
        width = columns // (kinds * 2 * ring)
        rows = aligned(core * half, half)
        for pair in range(ring):
            for kind in range(kinds):
                place = slice((pair * kinds + kind) * width, (pair * kinds + kind + 1) * width)
                for ref, which in ((None, core), (away, 1 - core)):
                    start = (kind * 2 * ring + 2 * pair + which) * width
                    block = full[layer, :, aligned(start, width)].astype(BF)
                    if ref is None:
                        slab[layer, rows, place] = block
                    else:
                        ref[layer, :, place] = block
        swaps[idx] = remote(
            away.at[layer], slab.at[layer, rows, :], c_send.at[idx], c_recv.at[idx], other
        )
        swaps[idx].start()

    hops = ring - 1
    order = []
    for first in range(0, len(items), 2):
        for hop in range(hops):
            order += [(first, hop), (first + 1, hop)]

    stores = []
    z_copies = {}

    def begin(idx):
        name, layer = items[idx]
        if swaps[idx] is not None:
            swaps[idx].wait_recv()
        store = pltpu.make_async_copy(
            slabs[name].at[layer], place(name, layer, chip, None), l_out.at[idx]
        )
        store.start()
        stores.append(store)

    def z_copy(idx, hop):
        name, layer = items[idx]
        part = None if name == "proj" else seq
        source = place(name, layer, lax.rem(chip - hop + ring, ring), part)
        if hop == 0:
            if part is None:
                from_ref = slabs[name].at[layer]
            else:
                size = slabs[name].shape[1] // 4
                from_ref = slabs[name].at[layer, pl.ds(pl.multiple_of(seq * size, size), size), :]
        else:
            from_ref = source
        slot = idx * hops + hop
        copy = remote(from_ref, source, z_send.at[slot], z_recv.at[slot], up_chip)
        copy.start()
        z_copies[idx, hop] = copy

    plane, far = {}, {}

    def plane_copies(idx, hop):
        name, layer = items[idx]
        ref = place(name, layer, lax.rem(chip - hop - 1 + ring, ring), seq)
        slot = 2 * (idx * hops + hop)
        plane[idx, hop] = [
            remote(ref, ref, p_send.at[slot], p_recv.at[slot], over_x),
            remote(ref, ref, p_send.at[slot + 1], p_recv.at[slot + 1], over_y),
        ]
        for copy in plane[idx, hop]:
            copy.start()

    def far_copies(idx, hop):
        name, layer = items[idx]
        slot = 2 * (idx * hops + hop)
        size = slabs[name].shape[1] // 4
        half = size // 2
        base = lax.rem(chip - hop - 1 + ring, ring) * 4 * size
        for copy in plane[idx, hop]:
            copy.wait_recv()
        made = []
        for turn, (origin, target) in enumerate(((near_y, over_x), (near_x, over_y))):
            rows = pl.ds(pl.multiple_of(base + origin * size + turn * half, half), half)
            ref = outs[name].at[layer, rows, :]
            made.append(
                remote(ref, ref, d_send.at[slot + turn], d_recv.at[slot + turn], target)
            )
        far[idx, hop] = made
        for copy in made:
            copy.start()

    pending = []
    proj_swaps = []
    clip_swaps = []
    prepare()
    prepare()
    begin(0)
    z_copy(0, 0)
    begin(1)
    z_copy(1, 0)
    prepare()
    prepare()
    for event, (idx, hop) in enumerate(order):
        if event == 2:
            clip_swaps = clip_arrived()
        if 3 <= event < 3 + hops:
            vec_hop(event - 3)
        if event % 2 == 1:
            prepare()
        z_copies[idx, hop].wait_recv()
        if hop + 1 < hops:
            z_copy(idx, hop + 1)
        elif idx + 2 < len(items):
            begin(idx + 2)
            z_copy(idx + 2, 0)
        name, layer = items[idx]
        if name == "proj":
            if hop + 1 == hops:
                stores[idx].wait()
                slot = len(items) + layer
                swap = remote(
                    proj_out.at[layer, 0],
                    proj_out.at[layer, 1],
                    c_send.at[slot],
                    c_recv.at[slot],
                    other,
                )
                swap.start()
                proj_swaps.append(swap)
        else:
            plane_copies(idx, hop)
            pending.append((idx, hop))
            if len(pending) > 1:
                far_copies(*pending.pop(0))
    while pending:
        far_copies(*pending.pop(0))

    for key, made in far.items():
        for copy in made:
            copy.wait()
    for made in plane.values():
        for copy in made:
            copy.wait_send()
    for copy in z_copies.values():
        copy.wait_send()
    for copy in swaps.values():
        if copy is not None:
            copy.wait_send()
    for copy in proj_swaps + clip_swaps:
        copy.wait()
    vec_copies[-1].wait_recv()
    for copy in [vec_swap] + vec_copies:
        copy.wait_send()
    for away, copies in clip_copies:

        @pl.when(away)
        def _(copies=copies):
            for copy in copies:
                copy.wait_send()

    for idx, store in enumerate(stores):
        if items[idx][0] != "proj":
            store.wait()


def gather_weights(qkv, up, down, proj, clips, coords, vectors):
    layers, rows, width = proj.shape
    parts = lax.axis_size("fsdp")
    ring = parts // 2
    count = 4 * layers
    hops = ring - 1
    anywhere = pl.BlockSpec(memory_space=pl.ANY)
    vmem = pl.BlockSpec(memory_space=pltpu.VMEM)
    dma = pltpu.SemaphoreType.DMA
    down_rows = down.shape[1]
    halves = qkv.shape[2] // 2, up.shape[2] // 2
    shapes = [
        ((layers, parts * rows, halves[0]), BF),
        ((layers, parts * rows, halves[1]), BF),
        ((layers, ring * down_rows, width), BF),
        ((layers, 2, ring * rows, width), BF),
        ((4 * clips.shape[1], width), F32),
        ((4,) + coords.shape[1:], jnp.int32),
        ((parts,) + vectors.shape, F32),
    ]
    return pl.pallas_call(
        gather_kernel,
        in_specs=[anywhere] * 5 + [vmem] * 2,
        out_specs=[anywhere] * 5 + [vmem] * 2,
        out_shape=[jax.ShapeDtypeStruct(*shape) for shape in shapes],
        scratch_shapes=[
            pltpu.VMEM(qkv.shape, F32),
            pltpu.VMEM(up.shape, F32),
            pltpu.VMEM(down.shape, F32),
            pltpu.VMEM(proj.shape, F32),
            pltpu.VMEM((layers, rows, halves[0]), BF),
            pltpu.VMEM((layers, rows, halves[1]), BF),
            pltpu.VMEM((layers, 2 * rows, halves[0]), BF),
            pltpu.VMEM((layers, 2 * rows, halves[1]), BF),
            pltpu.VMEM((layers, down_rows, width), BF),
            pltpu.VMEM((layers, rows, width), BF),
            pltpu.VMEM(clips.shape[1:], F32),
            dma((count * hops,)),
            dma((count * hops,)),
            dma((2 * count * hops,)),
            dma((2 * count * hops,)),
            dma((2 * count * hops,)),
            dma((2 * count * hops,)),
            dma((count + layers,)),
            dma((count + layers,)),
            dma((count,)),
            dma((count,)),
            dma((9 + hops,)),
            dma((9 + hops,)),
            dma((2,)),
        ],
        compiler_params=pltpu.CompilerParams(
            collective_id=0, has_side_effects=True, vmem_limit_bytes=VMEM_LIMIT
        ),
        cost_estimate=pl.CostEstimate(flops=0, bytes_accessed=600_000_000, transcendentals=0),
        name="gather_weights",
    )(qkv, up, down, proj, clips, coords, vectors)


ADD_ROWS = 32


def add_into(target, term):
    rows = target.shape[0]

    @pl.loop(0, rows // ADD_ROWS)
    def _(step):
        at = aligned(step * ADD_ROWS, ADD_ROWS)
        total = target[at, :].astype(F32) + term[at, :].astype(F32)
        target[at, :] = total.astype(BF)


class Sems:
    def __init__(self, ref):
        self.ref, self.used = ref, 0

    def take(self):
        self.used += 1
        return self.ref.at[self.used - 1]


class Sum:
    def __init__(self, at, sems, grad, own, one, two, three, z_first, x_first, stage, layer):
        self.at, self.sems = at, sems
        self.grad, self.own, self.one, self.two, self.three = grad, own, one, two, three
        self.z_first, self.x_first = z_first, x_first
        self.stage, self.layer = stage, layer
        self.rows = grad.shape[0] // (4 * at.ring)
        self.sends, self.loads = [], {}
        self.first, self.second, self.hop = {}, {}, {}

    def make(self, src, dst, target):
        copy = remote(src, dst, self.sems[0].take(), self.sems[1].take(), target)
        copy.start()
        self.sends.append(copy)
        return copy

    def load(self, src, dst):
        copy = pltpu.make_async_copy(src, dst, self.sems[2].take())
        copy.start()
        return copy

    def kept(self):
        at = self.at
        if self.x_first:
            return [(at.at_x, 1), (2 + at.at_x, 1)]
        return [(2 * at.at_y, 2)]

    def given(self):
        at = self.at
        if self.x_first:
            return [(1 - at.at_x, 1), (3 - at.at_x, 1)]
        return [(2 * (1 - at.at_y), 2)]

    def fetch_own(self, tile):
        base = self.at.back(tile + 1) * 4 * self.rows
        copies = []
        if self.z_first:
            copies.append(
                self.load(self.grad.at[aligned(base, 4 * self.rows), :], self.own.at[tile])
            )
        else:
            place = 0
            for first, count in self.kept():
                size = count * self.rows
                copies.append(
                    self.load(
                        self.grad.at[aligned(base + first * self.rows, size, self.rows), :],
                        self.own.at[tile, pl.ds(place, size), :],
                    )
                )
                place += size
        self.loads[tile] = copies

    def own_ready(self, tile):
        for copy in self.loads[tile]:
            copy.wait()

    def plane_one(self, tile, source, base):
        target = self.at.over_x if self.x_first else self.at.over_y
        place, made = 0, []
        for first, count in self.given():
            size = count * self.rows
            made.append(
                self.make(
                    source.at[aligned(base + first * self.rows, size, self.rows), :],
                    self.one.at[tile, pl.ds(place, size), :],
                    target,
                )
            )
            place += size
        self.first[tile] = made

    def plane_two(self, tile, kept_ref):
        for copy in self.first[tile]:
            copy.wait_recv()
        place = 0
        for ref in kept_ref:
            size = ref.shape[0]
            add_into(self.one.at[tile, pl.ds(place, size), :], ref)
            place += size
        at = self.at
        target = at.over_y if self.x_first else at.over_x
        keep = at.at_y if self.x_first else at.at_x
        self.keep_ref = lambda: self.one.at[tile, aligned(keep * self.rows, self.rows), :]
        self.second[tile] = self.make(
            self.one.at[tile, aligned((1 - keep) * self.rows, self.rows), :],
            self.two.at[tile],
            target,
        )

    def plane_three(self, tile):
        at = self.at
        keep = at.at_y if self.x_first else at.at_x
        self.second[tile].wait_recv()
        add_into(self.two.at[tile], self.one.at[tile, aligned(keep * self.rows, self.rows), :])

    def start(self, tile):
        base = self.at.back(tile + 1) * 4 * self.rows
        if self.z_first:
            self.own_ready(tile)
            self.hop[0] = self.make(self.own.at[0], self.three.at[0], self.at.up)
        else:
            self.plane_one(tile, self.grad, base)

    def middle(self, tile):
        self.own_ready(tile)
        self.plane_two(tile, [self.own.at[tile]])

    def finish(self, tile):
        self.plane_three(tile)
        if tile > 0:
            self.hop[tile - 1].wait_recv()
            add_into(self.two.at[tile], self.three.at[tile - 1])
        if tile < self.at.ring - 1:
            self.hop[tile] = self.make(self.two.at[tile], self.three.at[tile], self.at.up)

    def ring_step(self, tile):
        last = tile == self.at.ring - 1
        self.hop[tile - 1].wait_recv()
        self.own_ready(tile)
        total = self.three.at[tile - 1]
        add_into(total, self.own.at[tile])
        if last:
            self.plane_one(0, total, 0)
        else:
            self.hop[tile] = self.make(total, self.three.at[tile], self.at.up)

    def slab_middle(self):
        total = self.three.at[self.at.ring - 2]
        refs = [
            total.at[aligned(first * self.rows, count * self.rows, self.rows), :]
            for first, count in self.kept()
        ]
        self.plane_two(0, refs)

    def slab_finish(self):
        self.plane_three(0)

    def total(self):
        return self.two.at[0 if self.z_first else self.at.ring - 1]

    def place(self, quarter, turn=0, size=None):
        size = size or self.rows
        return self.stage.at[aligned(quarter * self.rows + turn * size, size), :]

    def gather(self):
        at = self.at
        self.kept_store = self.load(self.total(), self.place(at.seq))
        self.near = [
            self.make(self.total(), self.place(at.seq), at.over_x),
            self.make(self.total(), self.place(at.seq), at.over_y),
        ]

    def gather_far(self):
        at = self.at
        for copy in self.near:
            copy.wait_recv()
        half = self.rows // 2
        self.far = []
        for turn, (origin, target) in enumerate(((at.near_y, at.over_x), (at.near_x, at.over_y))):
            ref = self.place(origin, turn, half)
            self.far.append(self.make(ref, ref, target))

    def gather_end(self, arrive):
        at = self.at
        self.kept_store.wait()
        for copy in self.far:
            copy.wait_recv()
        self.swap = None
        if arrive is not None:
            half = 2 * self.rows
            self.swap = self.make(
                self.stage.at[aligned((1 - at.core) * half, half), :], arrive, at.other
            )

    def drain(self):
        if self.swap is not None:
            self.swap.wait_recv()
        for copy in self.sends:
            copy.wait_send()


def reduce_kernel(
    last,
    qkv_grad, proj_grad, up_grad, down_grad, vec_in, square_in,
    qkv_stage, qkv_arrive, proj_stage, up_stage, up_arrive, down_stage, vec_out, square_out,
    qkv_own, qkv_one, qkv_two, qkv_three,
    proj_own, proj_one, proj_two, proj_three,
    up_own, up_one, up_two, up_three,
    down_own, down_one, down_two, down_three,
    vec_got, vec_hop, vec_sum, square_got, square_sum,
    send_sem, recv_sem, load_sem,
):
    at = Places()
    ring = at.ring
    sems = (Sems(send_sem), Sems(recv_sem), Sems(load_sem))
    greet((at.other, at.over_x, at.over_y, at.down), 4)
    qkv = Sum(at, sems, qkv_grad, qkv_own, qkv_one, qkv_two, qkv_three, True, True, qkv_stage, 0)
    proj = Sum(
        at, sems, proj_grad, proj_own, proj_one, proj_two, proj_three, True, False, proj_stage, 0
    )
    up = Sum(at, sems, up_grad, up_own, up_one, up_two, up_three, False, True, up_stage, 0)
    down = Sum(
        at, sems, down_grad, down_own, down_one, down_two, down_three, False, False, down_stage, 0
    )
    wide, slabs = (up, down), (qkv, proj)

    vec_copies = []

    def vec_copy(src, dst, target):
        copy = remote(src, dst, sems[0].take(), sems[1].take(), target)
        copy.start()
        vec_copies.append(copy)
        return copy

    partners = (at.other, at.over_x, at.over_y)
    vec_sum[0] = vec_in[...]

    for item in slabs:
        item.fetch_own(0)
    for item in wide:
        item.start(0)
    for item in slabs:
        item.start(0)
    for item in wide:
        item.start(1)
    for tile in range(ring):
        for item in wide:
            item.fetch_own(tile)
        if tile > 0:
            for item in slabs:
                item.fetch_own(tile)
    vec_state = {"copy": vec_copy(vec_sum.at[0], vec_got.at[0], partners[0])}

    def vec_step(idx):
        vec_state["copy"].wait_recv()
        if idx <= 3:
            vec_sum[idx] = vec_sum[idx - 1] + vec_got[idx - 1]
            if idx < 3:
                vec_state["copy"] = vec_copy(vec_sum.at[idx], vec_got.at[idx], partners[idx])
            else:
                vec_state["copy"] = vec_copy(
                    vec_sum.at[3, at.back(1)], vec_hop.at[0], at.up
                )
        else:
            hop = idx - 3
            vec_hop[hop - 1] = vec_hop[hop - 1] + vec_sum[3, at.back(hop + 1)]
            if hop < ring - 1:
                vec_state["copy"] = vec_copy(vec_hop.at[hop - 1], vec_hop.at[hop], at.up)

    for tile in range(ring):
        for item in wide:
            item.middle(tile)
        if tile + 2 < ring:
            for item in wide:
                item.start(tile + 2)
        if tile > 0:
            for item in wide:
                item.finish(tile - 1)
        if tile + 1 < ring:
            for item in slabs:
                item.ring_step(tile + 1)
        vec_step(tile + 1)
    for item in slabs:
        item.slab_middle()
    vec_step(5)
    for item in wide:
        item.finish(ring - 1)
        item.gather()
    vec_step(6)
    vec_total = vec_hop[ring - 2]
    vec_out[...] = vec_total
    for item in slabs:
        item.slab_finish()
        item.gather()

    def squares(ref):
        rows, columns = ref.shape
        total = jnp.zeros((8, 128), F32)

        def body(step, total):
            part = ref[aligned(step * 16, 16), :].astype(F32)
            part = part * part
            part = part[0:8] + part[8:16]
            for column in range(0, columns, 128):
                total = total + part[:, column : column + 128]
            return total

        return lax.fori_loop(0, rows // 16, body, total)

    total = square_in[...]
    for item in (*wide, *slabs):
        total = total + squares(item.total())
    vec_square = vec_total * vec_total * 0.125
    for column in range(0, vec_square.shape[1], 128):
        total = total + vec_square[:, column : column + 128]
    square_sum[0] = total
    if last:
        for idx, target in enumerate(partners):
            copy = vec_copy(square_sum.at[idx], square_got.at[idx], target)
            if idx == 0:
                for item in wide:
                    item.gather_far()
            if idx == 1:
                for item in slabs:
                    item.gather_far()
            copy.wait_recv()
            square_sum[idx + 1] = square_sum[idx] + square_got[idx]
        total = square_sum[3]
        for hop in range(ring - 1):
            source = square_sum.at[3] if hop == 0 else square_got.at[2 + hop]
            copy = vec_copy(source, square_got.at[3 + hop], at.up)
            if hop == 0:
                for item in wide:
                    item.gather_end(up_arrive if item is up else None)
            copy.wait_recv()
            total = total + square_got[3 + hop]
        square_out[...] = total
    else:
        square_out[...] = total
        for item in (*wide, *slabs):
            item.gather_far()
        for item in wide:
            item.gather_end(up_arrive if item is up else None)
    for item in slabs:
        item.gather_end(qkv_arrive if item is qkv else None)
    for item in (*wide, *slabs):
        item.drain()
    for copy in vec_copies:
        copy.wait_send()


def reduce_grads(grads, vec, squares, last, call_id):
    ring = lax.axis_size("fsdp") // 2
    anywhere = pl.BlockSpec(memory_space=pl.ANY)
    vmem = pl.BlockSpec(memory_space=pltpu.VMEM)
    dma = pltpu.SemaphoreType.DMA
    scratch, slab_shapes = [], []
    for idx, grad in enumerate(grads):
        slab, width = grad.shape[0] // ring, grad.shape[1]
        quarter = slab // 4
        slab_shapes.append(jax.ShapeDtypeStruct((slab, width), BF))
        z_first = idx < 2
        tiles = 1 if z_first else ring
        scratch += [
            pltpu.VMEM((ring, slab if z_first else 2 * quarter, width), BF),
            pltpu.VMEM((tiles, 2 * quarter, width), BF),
            pltpu.VMEM((tiles, quarter, width), BF),
            pltpu.VMEM((ring - 1, slab if z_first else quarter, width), BF),
        ]
    half = [
        jax.ShapeDtypeStruct((shape.shape[0] // 2, shape.shape[1]), BF) for shape in slab_shapes
    ]
    return pl.pallas_call(
        partial(reduce_kernel, last),
        in_specs=[anywhere] * 4 + [vmem] * 2,
        out_specs=[anywhere] * 6 + [vmem] * 2,
        out_shape=[
            slab_shapes[0],
            half[0],
            slab_shapes[1],
            slab_shapes[2],
            half[2],
            slab_shapes[3],
            jax.ShapeDtypeStruct(vec.shape[1:], F32),
            jax.ShapeDtypeStruct((8, 128), F32),
        ],
        scratch_shapes=[
            *scratch,
            pltpu.VMEM((3,) + vec.shape, F32),
            pltpu.VMEM((ring - 1,) + vec.shape[1:], F32),
            pltpu.VMEM((4,) + vec.shape, F32),
            pltpu.VMEM((3 + ring - 1, 8, 128), F32),
            pltpu.VMEM((4, 8, 128), F32),
            dma((120,)),
            dma((120,)),
            dma((120,)),
        ],
        compiler_params=pltpu.CompilerParams(
            collective_id=call_id, has_side_effects=True, vmem_limit_bytes=VMEM_LIMIT
        ),
        cost_estimate=pl.CostEstimate(flops=0, bytes_accessed=300_000_000, transcendentals=0),
        name="reduce_grads",
    )(*grads, vec, squares)


def adam_kernel(
    kinds, ring, count, core_ref, factor_ref, *refs
):
    n_grads = len(refs) - 8
    grads = refs[:n_grads]
    master, first, second, grad_out, first_out, second_out, new_out, copy_out = refs[n_grads:]
    layer = pl.program_id(0)
    factor = factor_ref[0]
    scale = 1.0 / count
    columns = master.shape[2]
    per_layer = n_grads // 2
    width = columns // (kinds * ring * 2) if per_layer == 2 else 512

    def update(at, total):
        grad = total.astype(F32) * scale
        first_new, second_new, new = [], [], []
        first_new, second_new, new = adam_update(
            master[0, :, at], grad, first[0, :, at], second[0, :, at], factor
        )
        grad_out[0, :, at] = grad
        first_out[0, :, at] = first_new
        second_out[0, :, at] = second_new
        new_out[0, :, at] = new
        copy_out[0, :, at] = new.astype(BF)

    def choose(which, at):
        values = [grads[idx * per_layer + which][:, at] for idx in range(2)]
        return jnp.where(layer == 0, values[0], values[1])

    if per_layer == 1:
        for start in range(0, columns, width):
            update(slice(start, start + width), choose(0, slice(start, start + width)))
        return
    core = core_ref[0]
    for pair in range(ring):
        for kind in range(kinds):
            source = (pair * kinds + kind) * width
            mine, arrive = [choose(which, slice(source, source + width)) for which in range(2)]
            for which in range(2):
                start = (kind * ring * 2 + 2 * pair + which) * width
                update(slice(start, start + width), jnp.where(core == which, mine, arrive))


def adam_matrix(grads, master, first, second, factor, core, kinds, count):
    layers, rows, columns = master.shape
    ring = lax.axis_size("fsdp") // 2
    block = 32 if columns > 1024 else 64
    steps = rows // block
    per_layer = len(grads) // layers

    def grad_spec(idx):
        layer, which = divmod(idx, per_layer)
        lift = steps if per_layer == 2 and which == 0 else 0

        def where(at_layer, step, core_ref, layer=layer, lift=lift):
            held = 0 if layer > 0 else steps - 1
            row = jnp.where(at_layer == layer, step, held)
            return (row + lift * core_ref[0], 0)

        return pl.BlockSpec((block, grads[idx].shape[1]), where)

    whole = pl.BlockSpec((1, block, columns), lambda layer, step, core_ref: (layer, step, 0))
    shape = jax.ShapeDtypeStruct(master.shape, F32)
    return pl.pallas_call(
        partial(adam_kernel, kinds, ring, count),
        grid_spec=pltpu.PrefetchScalarGridSpec(
            num_scalar_prefetch=1,
            grid=(layers, steps),
            in_specs=[pl.BlockSpec(memory_space=pltpu.SMEM)]
            + [grad_spec(idx) for idx in range(len(grads))]
            + [whole] * 3,
            out_specs=[whole] * 5,
        ),
        out_shape=[shape] * 4 + [jax.ShapeDtypeStruct(master.shape, BF)],
        compiler_params=pltpu.CompilerParams(vmem_limit_bytes=VMEM_LIMIT),
        cost_estimate=pl.CostEstimate(
            flops=20 * master.size, bytes_accessed=32 * master.size, transcendentals=master.size
        ),
        name="update",
    )(core.reshape(1).astype(jnp.int32), factor.reshape(1), *grads, master, first, second)


def norm_parts(hidden):
    center = hidden - jnp.mean(hidden, axis=-1, keepdims=True)
    spread = jnp.mean(center * center, axis=-1, keepdims=True)
    inverse = lax.rsqrt(spread + 1e-06)
    return center * inverse, inverse


def norm_forward(hidden, gain, shift):
    scaled, _ = norm_parts(hidden)
    return (scaled * gain + shift).astype(BF)


def norm_backward(hidden, gain, grad):
    scaled, inverse = norm_parts(hidden)
    entry = grad * gain
    mean_one = jnp.mean(entry, axis=-1, keepdims=True)
    mean_two = jnp.mean(entry * scaled, axis=-1, keepdims=True)
    result = inverse * (entry - mean_one - scaled * mean_two)
    return result, jnp.sum(grad * scaled, axis=0), jnp.sum(grad, axis=0)


def gelu_and_slope(upward):
    erf_part = 0.5 * (1.0 + lax.erf(upward * (1.0 / math.sqrt(2.0))))
    density = jnp.exp(-0.5 * upward * upward) * (1.0 / math.sqrt(2.0 * math.pi))
    return upward * erf_part, erf_part + upward * density


def dot(left, right):
    return jnp.dot(left, right, preferred_element_type=F32)


def dot_nt(left, right):
    return lax.dot_general(left, right, NT, preferred_element_type=F32)


def dot_tn(left, right):
    return lax.dot_general(left, right, (((0,), (0,)), ((), ())), preferred_element_type=F32)


def own_bias(bias, core, fsdp_parts, kinds):
    width = bias.shape[0] // (kinds * fsdp_parts)
    view = bias.reshape(kinds, fsdp_parts // 2, 2, width)
    mine = pick(view, core, 2)
    return mine.transpose(1, 0, 2).reshape(-1)


def spread_bias(grad, core, fsdp_parts, kinds):
    width = grad.shape[0] // (kinds * (fsdp_parts // 2))
    view = grad.reshape(fsdp_parts // 2, kinds, width).transpose(1, 0, 2)
    zero = jnp.zeros_like(view)
    first = jnp.where(core == 0, view, zero)
    second = jnp.where(core == 0, zero, view)
    return jnp.stack([first, second], axis=2).reshape(-1)


def fast_device(
    clip_tokens,
    patch_coords,
    out_cotangent,
    vector_params,
    qkv_weight,
    proj_weight,
    up_weight,
    down_weight,
    first_vector,
    first_qkv,
    first_proj,
    first_up,
    first_down,
    second_vector,
    second_qkv,
    second_proj,
    second_up,
    second_down,
):
    masters = (vector_params, qkv_weight, proj_weight, up_weight, down_weight)
    firsts = (first_vector, first_qkv, first_proj, first_up, first_down)
    seconds = (second_vector, second_qkv, second_proj, second_up, second_down)
    layer_count = vector_params.shape[0]
    batch_local, chunk_len = clip_tokens.shape[:2]
    seq_parts = lax.axis_size("seq")
    parts = lax.axis_size("fsdp")
    ring = parts // 2
    seq = lax.axis_index("seq")
    shard = lax.axis_index("fsdp")
    core = lax.rem(shard, 2)
    even = lax.rem(seq, 2) == 0

    def to_clips(item):
        halves = []
        for turn in range(2):
            piece = jnp.where(even, item[turn], item[1 - turn])
            pairs = []
            for src_seq in range(seq_parts):
                for src in range(parts):
                    dst_seq = 2 * (src % 2) + (src_seq + turn) % 2
                    dst = src - src % 2 + src_seq // 2
                    pairs.append((src_seq * parts + src, dst_seq * parts + dst))
            halves.append(lax.ppermute(piece, ("seq", "fsdp"), pairs))
        mine = jnp.where(
            even, jnp.stack([halves[0], halves[1]]), jnp.stack([halves[1], halves[0]])
        )
        other = swap_core(mine)
        both = jnp.where(core == 0, jnp.stack([mine, other]), jnp.stack([other, mine]))
        return both.reshape((4,) + item.shape[1:])

    def from_clips(item):
        mine = pick(item.reshape((2, 2, chunk_len) + item.shape[1:]), core)
        pieces = [None, None]
        for turn in range(2):
            piece = jnp.where(even, mine[turn], mine[1 - turn])
            pairs = []
            for src_seq in range(seq_parts):
                for src in range(parts):
                    dst_seq = 2 * (src % 2) + (src_seq + turn) % 2
                    dst = src - src % 2 + src_seq // 2
                    pairs.append((dst_seq * parts + dst, src_seq * parts + src))
            pieces[turn] = lax.ppermute(piece, ("seq", "fsdp"), pairs)
        return jnp.where(
            even, jnp.stack([pieces[0], pieces[1]]), jnp.stack([pieces[1], pieces[0]])
        )

    coord_rows = jnp.pad(jnp.swapaxes(patch_coords, 0, 1), ((0, 0), (0, 5), (0, 0)))
    vector_rows = vector_params.astype(BF).astype(F32).reshape(-1)
    vector_rows = jnp.pad(vector_rows, (0, -vector_rows.shape[0] % 1024)).reshape(8, -1)
    qkv_all_w, up_all_w, down_all_w, proj_all_w, hidden, coords, vector_got = gather_weights(
        qkv_weight, up_weight, down_weight, proj_weight, clip_tokens, coord_rows, vector_rows
    )
    layers = [
        (qkv_all_w[idx], proj_all_w[idx, 0], proj_all_w[idx, 1], up_all_w[idx], down_all_w[idx])
        for idx in range(layer_count)
    ]
    coords = jnp.swapaxes(coords[:, :3], 0, 1).reshape(3, 4 * chunk_len)
    cosine, sine = rotary_tables(coords, HEAD_DIM // 2)
    cos_wide = jnp.concatenate([cosine] * 4, axis=1)
    sin_wide = jnp.concatenate([-sine, sine, -sine, sine], axis=1)
    vector_all = vector_got.reshape(parts, -1)[:, : vector_params.size]
    vector_all = vector_all.reshape(parts, layer_count, -1).transpose(1, 0, 2)
    vector_all = vector_all.reshape(layer_count, -1)

    saved = []
    for idx in range(layer_count):
        qkv_w, proj_w, proj_other, up_w, down_w = layers[idx]
        gain_one, shift_one, gain_two, shift_two, proj_bias, down_bias, qkv_bias, up_bias = pieces(
            vector_all[idx]
        )
        qkv_bias = own_bias(qkv_bias, core, parts, 3)
        up_bias = own_bias(up_bias, core, parts, 1)
        normed = norm_forward(hidden, gain_one, shift_one)
        qkv_all = dot(normed, qkv_w) + qkv_bias
        mixed, low_all, lse = attend(qkv_all, cos_wide, sin_wide)
        mixed_other = swap_core(mixed)
        after_attn = hidden + (dot(mixed, proj_w) + dot(mixed_other, proj_other)) + proj_bias
        normed_two = norm_forward(after_attn, gain_two, shift_two)
        upward = dot(normed_two, up_w) + up_bias
        active, slope = gelu_and_slope(upward)
        active, slope = active.astype(BF), slope.astype(BF)
        part = dot(active, down_w)
        other = swap_core(part.astype(BF))
        result = after_attn + (part + other.astype(F32)) + down_bias
        saved.append((hidden, normed, low_all, lse, mixed, after_attn, normed_two, active, slope))
        hidden = result
    block_output = from_clips(hidden)

    grad = to_clips(out_cotangent).reshape(4 * chunk_len, D)
    sums = [None] * layer_count
    vector_sums = [None] * layer_count
    squares = jnp.zeros((8, 128), F32)
    for idx in reversed(range(layer_count)):
        qkv_w, proj_w, proj_other, up_w, down_w = layers[idx]
        entry, normed, low_all, lse, mixed, after_attn, normed_two, active, slope = saved[idx]
        gain_one, shift_one, gain_two, shift_two, proj_bias, down_bias, qkv_bias, up_bias = pieces(
            vector_all[idx]
        )
        down_bias_grad = jnp.sum(grad, axis=0)
        grad_low = grad.astype(BF)
        upward_grad = dot_nt(grad_low, down_w) * slope.astype(F32)
        up_bias_grad = jnp.sum(upward_grad, axis=0)
        upward_low = upward_grad.astype(BF)
        part = dot_nt(upward_low, up_w)
        other = swap_core(part.astype(BF))
        down_grad = dot_tn(active, grad_low).astype(BF)
        up_grad = dot_tn(normed_two, upward_low).astype(BF)
        attn_in, gain_two_grad, shift_two_grad = norm_backward(
            after_attn, gain_two, part + other.astype(F32)
        )
        after_grad = grad + attn_in
        proj_bias_grad = jnp.sum(after_grad, axis=0)
        after_low = after_grad.astype(BF)
        mixed_grad = dot_nt(after_low, proj_w).astype(BF)
        proj_grad = dot_tn(mixed, after_low).astype(BF)
        qkv_low, bias_rows = attend_grad(low_all, mixed_grad, lse, cos_wide, sin_wide)
        part = dot_nt(qkv_low, qkv_w)
        other = swap_core(part.astype(BF))
        qkv_grad = dot_tn(normed, qkv_low).astype(BF)
        attn_in, gain_one_grad, shift_one_grad = norm_backward(
            entry, gain_one, part + other.astype(F32)
        )
        grad = after_grad + attn_in

        shared = jnp.concatenate(
            [
                gain_one_grad,
                shift_one_grad,
                gain_two_grad,
                shift_two_grad,
                proj_bias_grad,
                down_bias_grad,
            ]
        )
        vector_sums[idx] = jnp.concatenate(
            [
                jnp.where(core == 0, shared, jnp.zeros_like(shared)),
                spread_bias(bias_rows[0], core, parts, 3),
                spread_bias(up_bias_grad, core, parts, 1),
            ]
        )

        total_vec = vector_sums[idx].reshape(ring, -1)
        pad = -total_vec.shape[1] % 1024
        total_vec = jnp.pad(total_vec, ((0, 0), (0, pad))).reshape(ring, 8, -1)
        sums[idx] = reduce_grads(
            (qkv_grad, proj_grad, up_grad, down_grad),
            total_vec,
            squares,
            idx == 0,
            1 + idx,
        )
        squares = sums[idx][7]
    input_grad = from_clips(grad)

    clip_count = batch_local * parts
    norm_value = jnp.sqrt(jnp.sum(squares)) / clip_count
    param_count = sum(master.size for master in masters) * parts
    factor = jnp.minimum(1.0, CLIP_RATIO * math.sqrt(float(param_count)) / (norm_value + 1e-06))

    share = vector_params.shape[1]
    vector_total = jnp.stack([item[6].reshape(-1)[: 2 * share] for item in sums])
    vector_grad = lax.dynamic_slice_in_dim(vector_total, core * share, share, 1) / clip_count
    vector_new = adam_update(vector_params, vector_grad, first_vector, second_vector, factor)
    updates = [(vector_grad, *vector_new, vector_new[2].astype(BF))]
    for kind, keys in enumerate(((0, 1), (2,), (3, 4), (5,))):
        updates.append(
            adam_matrix(
                [item[key] for item in sums for key in keys],
                masters[kind + 1],
                firsts[kind + 1],
                seconds[kind + 1],
                factor,
                core,
                3 if kind == 0 else 1,
                clip_count,
            )
        )
    return (
        block_output,
        input_grad,
        *[item[0] for item in updates],
        norm_value.reshape(1),
        *[item[1] for item in updates],
        *[item[2] for item in updates],
        *[item[3] for item in updates],
        *[item[4] for item in updates],
    )


def solution(mesh):
    in_specs = (
        P("fsdp", "seq", None),
        P(None, "fsdp", "seq"),
        P("fsdp", "seq", None),
        P(None, "fsdp"),
        P(None, "fsdp", None),
        P(None, "fsdp", None),
        P(None, "fsdp", None),
        P(None, "fsdp", None),
        P(None, "fsdp"),
        P(None, "fsdp", None),
        P(None, "fsdp", None),
        P(None, "fsdp", None),
        P(None, "fsdp", None),
        P(None, "fsdp"),
        P(None, "fsdp", None),
        P(None, "fsdp", None),
        P(None, "fsdp", None),
        P(None, "fsdp", None),
    )
    out_specs = (
        P("fsdp", "seq", None),
        P("fsdp", "seq", None),
        P(None, "fsdp"),
        P(None, "fsdp", None),
        P(None, "fsdp", None),
        P(None, "fsdp", None),
        P(None, "fsdp", None),
        P(),
        P(None, "fsdp"),
        P(None, "fsdp", None),
        P(None, "fsdp", None),
        P(None, "fsdp", None),
        P(None, "fsdp", None),
        P(None, "fsdp"),
        P(None, "fsdp", None),
        P(None, "fsdp", None),
        P(None, "fsdp", None),
        P(None, "fsdp", None),
        P(None, "fsdp"),
        P(None, "fsdp", None),
        P(None, "fsdp", None),
        P(None, "fsdp", None),
        P(None, "fsdp", None),
        P(None, "fsdp"),
        P(None, "fsdp", None),
        P(None, "fsdp", None),
        P(None, "fsdp", None),
        P(None, "fsdp", None),
    )
    body = fast_device if fits_fast(mesh) else general_device
    return jax.shard_map(
        body, mesh=mesh, in_specs=in_specs, out_specs=out_specs, check_vma=False
    )
```

```python
from functools import partial
import math
from types import SimpleNamespace

import jax
import jax.numpy as jnp
from jax import lax
from jax.experimental import pallas as pl
from jax.experimental.pallas import tpu as pltpu
from jax.sharding import PartitionSpec as P

D = 1024
HEADS = 16
HEAD_DIM = 64


BETA_ONE = 0.5
BETA_TWO = 0.75
LEARN_RATE = 0.1
DECAY_RATE = 0.1
CLIP_RATIO = 0.2
ADAM_EPS = 1e-08
ROPE_BASE = 10000.0


def pieces(vector):
    return (
        vector[0:D],
        vector[D : 2 * D],
        vector[2 * D : 3 * D],
        vector[3 * D : 4 * D],
        vector[4 * D : 5 * D],
        vector[5 * D : 6 * D],
        vector[6 * D : 9 * D],
        vector[9 * D :],
    )


def layer_norm(hidden, ln_gain, ln_shift):
    center = hidden - jnp.mean(hidden, axis=-1, keepdims=True)
    spread = jnp.mean(center * center, axis=-1, keepdims=True)
    return center * lax.rsqrt(spread + 1e-06) * ln_gain + ln_shift


def gelu_exact(upward):
    return 0.5 * upward * (1.0 + jax.scipy.special.erf(upward * (1.0 / math.sqrt(2.0))))


def rotary_tables(coords_clip, pair_count):
    pair_index = jnp.arange(pair_count, dtype=jnp.int32)
    side_pairs = pair_count // 3
    time_pairs = pair_count - 2 * side_pairs
    in_time = pair_index < time_pairs
    in_height = jnp.logical_and(pair_index >= time_pairs, pair_index < time_pairs + side_pairs)
    offset = jnp.where(in_time, 0, jnp.where(in_height, time_pairs, time_pairs + side_pairs))
    seg_span = jnp.where(in_time, time_pairs, side_pairs)
    local_rank = (pair_index - offset).astype(jnp.float32)
    frequency = jnp.exp(-math.log(ROPE_BASE) * local_rank / seg_span.astype(jnp.float32))
    positions = coords_clip.astype(jnp.float32)
    chosen = jnp.where(
        in_time[None, :],
        positions[0][:, None],
        jnp.where(in_height[None, :], positions[1][:, None], positions[2][:, None]),
    )
    angles = chosen * frequency[None, :]
    return (jnp.cos(angles), jnp.sin(angles))


def rotate(values_in, cosine, sine_table):
    half_width = values_in.shape[-1] // 2
    first_half = values_in[..., :half_width]
    second_half = values_in[..., half_width:]
    cos_wide = cosine[:, None, :]
    sin_wide = sine_table[:, None, :]
    return jnp.concatenate(
        [
            first_half * cos_wide - second_half * sin_wide,
            first_half * sin_wide + second_half * cos_wide,
        ],
        axis=-1,
    )


def attend_forward(queries, key_rows, value_rows):
    full_len = queries.shape[0]
    block_rows = min(512, full_len)
    score_scale = HEAD_DIM ** (-0.5)
    query_blocks = queries.reshape(
        full_len // block_rows, block_rows, queries.shape[1], queries.shape[2]
    )

    def one_block(query_block):
        scores = (
            jnp.einsum("qhd,khd->hqk", query_block, key_rows, preferred_element_type=jnp.float32)
            * score_scale
        )
        row_max = jnp.max(scores, axis=-1, keepdims=True)
        exponent = jnp.exp(scores - row_max)
        row_total = jnp.sum(exponent, axis=-1, keepdims=True)
        prob_low = (exponent / row_total).astype(jnp.bfloat16)
        mixed_rows = jnp.einsum(
            "hqk,khd->qhd", prob_low, value_rows, preferred_element_type=jnp.float32
        )
        return (mixed_rows, row_max[..., 0] + jnp.log(row_total[..., 0]))

    mixed_rows, log_sums = lax.map(one_block, query_blocks)
    return (mixed_rows.reshape(queries.shape), log_sums)


def attend_backward(queries, key_rows, value_rows, log_sums, head_grad):
    full_len = queries.shape[0]
    block_rows = min(512, full_len)
    score_scale = HEAD_DIM ** (-0.5)
    block_shape = (full_len // block_rows, block_rows, queries.shape[1], queries.shape[2])

    def one_block(carry, block_in):
        key_grad, value_grad = carry
        query_block, grad_block, lse_block = block_in
        scores = (
            jnp.einsum("qhd,khd->hqk", query_block, key_rows, preferred_element_type=jnp.float32)
            * score_scale
        )
        prob_rows = jnp.exp(scores - lse_block[..., None])
        prob_low = prob_rows.astype(jnp.bfloat16)
        value_grad = value_grad + jnp.einsum(
            "hqk,qhd->khd", prob_low, grad_block, preferred_element_type=jnp.float32
        )
        prob_grad = jnp.einsum(
            "qhd,khd->hqk", grad_block, value_rows, preferred_element_type=jnp.float32
        )
        score_grad = prob_rows * (
            prob_grad - jnp.sum(prob_rows * prob_grad, axis=-1, keepdims=True)
        )
        score_low = (score_grad * score_scale).astype(jnp.bfloat16)
        query_grad = jnp.einsum(
            "hqk,khd->qhd", score_low, key_rows, preferred_element_type=jnp.float32
        )
        key_grad = key_grad + jnp.einsum(
            "hqk,qhd->khd", score_low, query_block, preferred_element_type=jnp.float32
        )
        return ((key_grad, value_grad), query_grad)

    zero_heads = jnp.zeros(queries.shape, jnp.float32)
    (key_grad, value_grad), query_grad = lax.scan(
        one_block,
        (zero_heads, zero_heads),
        (queries.reshape(block_shape), head_grad.reshape(block_shape), log_sums),
    )
    return (query_grad.reshape(queries.shape), key_grad, value_grad)


def layer_forward(hidden, cosine, sine_table, weights, seq_parts):
    vector_low, qkv_w, proj_w, up_w, down_w = weights
    gain_one, shift_one, gain_two, shift_two, proj_bias, down_bias, qkv_bias, up_bias = pieces(
        vector_low.astype(jnp.float32)
    )
    row_count = hidden.shape[0]
    local_heads = HEADS // seq_parts
    normed = layer_norm(hidden, gain_one, shift_one).astype(jnp.bfloat16)
    qkv_all = jnp.dot(normed, qkv_w, preferred_element_type=jnp.float32) + qkv_bias
    split_qkv = qkv_all.reshape(row_count, 3, HEADS, HEAD_DIM)
    stacked = jnp.stack(
        [
            rotate(split_qkv[:, 0], cosine, sine_table),
            rotate(split_qkv[:, 1], cosine, sine_table),
            split_qkv[:, 2],
        ],
        axis=1,
    ).astype(jnp.bfloat16)
    packed = stacked.reshape(row_count, 3, seq_parts, local_heads * HEAD_DIM)
    by_heads = lax.all_to_all(packed, "seq", split_axis=2, concat_axis=0, tiled=True)
    full_len = by_heads.shape[0]
    by_heads = by_heads.reshape(full_len, 3, local_heads, HEAD_DIM)
    mixed_rows, log_sums = attend_forward(by_heads[:, 0], by_heads[:, 1], by_heads[:, 2])
    mixed_low = mixed_rows.astype(jnp.bfloat16).reshape(full_len, 1, local_heads * HEAD_DIM)
    by_tokens = lax.all_to_all(mixed_low, "seq", split_axis=0, concat_axis=1, tiled=True).reshape(
        row_count, D
    )
    after_attn = hidden + jnp.dot(by_tokens, proj_w, preferred_element_type=jnp.float32) + proj_bias
    normed_two = layer_norm(after_attn, gain_two, shift_two).astype(jnp.bfloat16)
    upward = jnp.dot(normed_two, up_w, preferred_element_type=jnp.float32) + up_bias
    active = gelu_exact(upward).astype(jnp.bfloat16)
    result = after_attn + jnp.dot(active, down_w, preferred_element_type=jnp.float32) + down_bias
    saved_state = (
        hidden,
        normed,
        by_heads,
        log_sums,
        by_tokens,
        after_attn,
        normed_two,
        upward,
        active,
    )
    return (result, saved_state)


def layer_backward(grad_out, saved_state, weights, cosine, sine_table, seq_parts):
    vector_low, qkv_w, proj_w, up_w, down_w = weights
    gain_one, shift_one, gain_two, shift_two, proj_bias, down_bias, qkv_bias, up_bias = pieces(
        vector_low.astype(jnp.float32)
    )
    hidden, normed, by_heads, log_sums, by_tokens, after_attn, normed_two, upward, active = (
        saved_state
    )
    row_count = hidden.shape[0]
    local_heads = HEADS // seq_parts
    down_bias_grad = jnp.sum(grad_out, axis=0)
    grad_low = grad_out.astype(jnp.bfloat16)
    down_grad = jnp.dot(active.T, grad_low, preferred_element_type=jnp.float32)
    active_grad = jnp.dot(grad_low, down_w.T, preferred_element_type=jnp.float32)
    gelu_value, gelu_pull = jax.vjp(gelu_exact, upward)
    upward_grad = gelu_pull(active_grad)[0]
    up_bias_grad = jnp.sum(upward_grad, axis=0)
    upward_low = upward_grad.astype(jnp.bfloat16)
    up_grad = jnp.dot(normed_two.T, upward_low, preferred_element_type=jnp.float32)
    normed_two_grad = jnp.dot(upward_low, up_w.T, preferred_element_type=jnp.float32)
    norm_value_two, norm_pull_two = jax.vjp(layer_norm, after_attn, gain_two, shift_two)
    attn_in_grad, gain_two_grad, shift_two_grad = norm_pull_two(normed_two_grad)
    after_grad = grad_out + attn_in_grad
    proj_bias_grad = jnp.sum(after_grad, axis=0)
    after_low = after_grad.astype(jnp.bfloat16)
    proj_grad = jnp.dot(by_tokens.T, after_low, preferred_element_type=jnp.float32)
    mixed_grad = jnp.dot(after_low, proj_w.T, preferred_element_type=jnp.float32).astype(
        jnp.bfloat16
    )
    head_grad = lax.all_to_all(
        mixed_grad.reshape(row_count, seq_parts, local_heads * HEAD_DIM),
        "seq",
        split_axis=1,
        concat_axis=0,
        tiled=True,
    )
    full_len = head_grad.shape[0]
    head_grad = head_grad.reshape(full_len, local_heads, HEAD_DIM)
    query_grad, key_grad, value_grad = attend_backward(
        by_heads[:, 0], by_heads[:, 1], by_heads[:, 2], log_sums, head_grad
    )
    stacked_grad = (
        jnp.stack([query_grad, key_grad, value_grad], axis=1)
        .astype(jnp.bfloat16)
        .reshape(full_len, 3, 1, local_heads * HEAD_DIM)
    )
    token_grad = (
        lax.all_to_all(stacked_grad, "seq", split_axis=0, concat_axis=2, tiled=True)
        .reshape(row_count, 3, HEADS, HEAD_DIM)
        .astype(jnp.float32)
    )
    pair_grad_in = token_grad[:, :2].reshape(row_count, 2 * HEADS, HEAD_DIM)
    rotated_value, rotate_pull = jax.vjp(
        partial(rotate, cosine=cosine, sine_table=sine_table), pair_grad_in
    )
    pair_grad = rotate_pull(pair_grad_in)[0].reshape(row_count, 2, HEADS, HEAD_DIM)
    qkv_grad = jnp.concatenate([pair_grad, token_grad[:, 2:]], axis=1).reshape(row_count, 3 * D)
    qkv_bias_grad = jnp.sum(qkv_grad, axis=0)
    qkv_low = qkv_grad.astype(jnp.bfloat16)
    qkv_w_grad = jnp.dot(normed.T, qkv_low, preferred_element_type=jnp.float32)
    normed_grad = jnp.dot(qkv_low, qkv_w.T, preferred_element_type=jnp.float32)
    norm_value_one, norm_pull_one = jax.vjp(layer_norm, hidden, gain_one, shift_one)
    in_grad, gain_one_grad, shift_one_grad = norm_pull_one(normed_grad)
    input_grad = after_grad + in_grad
    vector_grad = jnp.concatenate(
        [
            gain_one_grad,
            shift_one_grad,
            gain_two_grad,
            shift_two_grad,
            proj_bias_grad,
            down_bias_grad,
            qkv_bias_grad,
            up_bias_grad,
        ]
    )
    return (input_grad, (vector_grad, qkv_w_grad, proj_grad, up_grad, down_grad))


def adam_update(master, grad_item, first_old, second_old, factor):
    clipped = grad_item * factor
    first_new = BETA_ONE * first_old + (1.0 - BETA_ONE) * clipped
    second_new = BETA_TWO * second_old + (1.0 - BETA_TWO) * clipped * clipped
    updated = master - LEARN_RATE * (
        first_new / (jnp.sqrt(second_new) + ADAM_EPS) + DECAY_RATE * master
    )
    return (first_new, second_new, updated)


def general_device(
    clip_tokens,
    patch_coords,
    out_cotangent,
    vector_params,
    qkv_weight,
    proj_weight,
    up_weight,
    down_weight,
    first_vector,
    first_qkv,
    first_proj,
    first_up,
    first_down,
    second_vector,
    second_qkv,
    second_proj,
    second_up,
    second_down,
):
    masters = (vector_params, qkv_weight, proj_weight, up_weight, down_weight)
    firsts = (first_vector, first_qkv, first_proj, first_up, first_down)
    seconds = (second_vector, second_qkv, second_proj, second_up, second_down)
    lowered = tuple((master.astype(jnp.bfloat16) for master in masters))
    layer_count = vector_params.shape[0]
    batch_local = clip_tokens.shape[0]
    seq_parts = lax.axis_size("seq")
    fsdp_parts = lax.axis_size("fsdp")
    grad_accum = tuple(
        (
            jnp.zeros((layer_count, master.shape[1] * fsdp_parts) + master.shape[2:], jnp.float32)
            for master in masters
        )
    )
    output_rows = []
    input_rows = []
    for batch_idx in range(batch_local):
        cosine, sine_table = rotary_tables(patch_coords[:, batch_idx], HEAD_DIM // 2)
        hidden = clip_tokens[batch_idx]
        saved_layers = []
        for layer_idx in range(layer_count):
            weights = (
                lax.all_gather(lowered[0][layer_idx], "fsdp", axis=0, tiled=True),
                lax.all_gather(lowered[1][layer_idx], "fsdp", axis=0, tiled=True),
                lax.all_gather(lowered[2][layer_idx], "fsdp", axis=0, tiled=True),
                lax.all_gather(lowered[3][layer_idx], "fsdp", axis=0, tiled=True),
                lax.all_gather(lowered[4][layer_idx], "fsdp", axis=0, tiled=True),
            )
            hidden, saved_state = layer_forward(hidden, cosine, sine_table, weights, seq_parts)
            saved_layers.append(saved_state)
        output_rows.append(hidden)
        grad_rows = out_cotangent[batch_idx]
        for layer_idx in reversed(range(layer_count)):
            weights = (
                lax.all_gather(lowered[0][layer_idx], "fsdp", axis=0, tiled=True),
                lax.all_gather(lowered[1][layer_idx], "fsdp", axis=0, tiled=True),
                lax.all_gather(lowered[2][layer_idx], "fsdp", axis=0, tiled=True),
                lax.all_gather(lowered[3][layer_idx], "fsdp", axis=0, tiled=True),
                lax.all_gather(lowered[4][layer_idx], "fsdp", axis=0, tiled=True),
            )
            grad_rows, layer_grads = layer_backward(
                grad_rows, saved_layers[layer_idx], weights, cosine, sine_table, seq_parts
            )
            grad_accum = tuple(
                (
                    accum_item.at[layer_idx].add(grad_item)
                    for accum_item, grad_item in zip(grad_accum, layer_grads)
                )
            )
        input_rows.append(grad_rows)
    shard_sums = (
        lax.psum_scatter(grad_accum[0], "fsdp", scatter_dimension=1, tiled=True),
        lax.psum_scatter(grad_accum[1], "fsdp", scatter_dimension=1, tiled=True),
        lax.psum_scatter(grad_accum[2], "fsdp", scatter_dimension=1, tiled=True),
        lax.psum_scatter(grad_accum[3], "fsdp", scatter_dimension=1, tiled=True),
        lax.psum_scatter(grad_accum[4], "fsdp", scatter_dimension=1, tiled=True),
    )
    seq_sums = lax.psum(
        (shard_sums[0], shard_sums[1], shard_sums[2], shard_sums[3], shard_sums[4]), "seq"
    )
    clip_count = batch_local * fsdp_parts
    grad_shards = tuple((sum_item / clip_count for sum_item in seq_sums))
    local_squares = sum((jnp.sum(grad_item * grad_item) for grad_item in grad_shards))
    squares_total = lax.psum(local_squares, "fsdp")
    norm_value = jnp.sqrt(squares_total)
    param_count = sum((master.size for master in masters)) * fsdp_parts
    factor = jnp.minimum(1.0, CLIP_RATIO * math.sqrt(float(param_count)) / (norm_value + 1e-06))
    updates = [
        adam_update(master, grad_item, first_old, second_old, factor)
        for master, grad_item, first_old, second_old in zip(masters, grad_shards, firsts, seconds)
    ]
    return (
        jnp.stack(output_rows),
        jnp.stack(input_rows),
        grad_shards[0],
        grad_shards[1],
        grad_shards[2],
        grad_shards[3],
        grad_shards[4],
        norm_value.reshape(1),
        updates[0][0],
        updates[1][0],
        updates[2][0],
        updates[3][0],
        updates[4][0],
        updates[0][1],
        updates[1][1],
        updates[2][1],
        updates[3][1],
        updates[4][1],
        updates[0][2],
        updates[1][2],
        updates[2][2],
        updates[3][2],
        updates[4][2],
        updates[0][2].astype(jnp.bfloat16),
        updates[1][2].astype(jnp.bfloat16),
        updates[2][2].astype(jnp.bfloat16),
        updates[3][2].astype(jnp.bfloat16),
        updates[4][2].astype(jnp.bfloat16),
    )


ROWS_Q = 256
PAIR = 2 * HEAD_DIM
BF = jnp.bfloat16
F32 = jnp.float32
VMEM_LIMIT = 56 * 1024 * 1024


def fits_fast(mesh):
    return dict(mesh.shape) == {"seq": 4, "fsdp": 8}


def swap_core(item):
    parts = lax.axis_size("fsdp")
    return lax.ppermute(item, "fsdp", [(idx, idx ^ 1) for idx in range(parts)])


def send_up(item):
    parts = lax.axis_size("fsdp")
    return lax.ppermute(item, "fsdp", [(idx, (idx + 2) % parts) for idx in range(parts)])


def swap_seq(item, mask):
    parts = lax.axis_size("seq")
    return lax.ppermute(item, "seq", [(idx, idx ^ mask) for idx in range(parts)])


def pick(item, index, axis=0):
    return lax.dynamic_index_in_dim(item, index, axis, keepdims=False)


def swap_halves(item):
    lane = lax.broadcasted_iota(jnp.int32, item.shape, 1)
    half = HEAD_DIM // 2
    width = item.shape[1]
    ahead = pltpu.roll(item, width - half, 1)
    behind = pltpu.roll(item, half, 1)
    return jnp.where(lane % HEAD_DIM < half, ahead, behind)


NT = (((1,), (1,)), ((), ()))


def head_mask(item, head):
    lane = lax.broadcasted_iota(jnp.int32, item.shape, 1)
    return jnp.where(lane // HEAD_DIM == head, item, jnp.zeros_like(item))


def attn_bwd_kernel(
    low_ref, dout_ref, lse_ref, cos_ref, sin_ref, grad_ref, bias_ref, dq_ref, dk_ref, dv_ref
):
    length = low_ref.shape[0]
    key_rows = low_ref[:, PAIR : 2 * PAIR]
    values = low_ref[:, 2 * PAIR : 3 * PAIR]
    keys_t = key_rows.astype(F32).T.astype(BF)
    keys_by_head = [head_mask(key_rows, head) for head in range(2)]
    values_by_head = [head_mask(values, head) for head in range(2)]
    scale = HEAD_DIM**-0.5
    dk_ref[...] = jnp.zeros_like(dk_ref)
    dv_ref[...] = jnp.zeros_like(dv_ref)

    @pl.loop(0, length // ROWS_Q)
    def _(step):
        rows = pl.ds(pl.multiple_of(step * ROWS_Q, ROWS_Q), ROWS_Q)
        block = low_ref[rows, 0:PAIR]
        scaled = block * jnp.asarray(scale, BF)
        dout = dout_ref[rows, :]
        outs = []
        for head in range(2):
            scores = lax.dot_general(keys_by_head[head], scaled, NT, preferred_element_type=F32)
            probs = jnp.exp(scores - lse_ref[0, head : head + 1, rows])
            prob_grad = lax.dot_general(values_by_head[head], dout, NT, preferred_element_type=F32)
            delta = jnp.sum(probs * prob_grad, axis=0, keepdims=True)
            score_low = (probs * (prob_grad - delta) * scale).astype(BF)
            dv_ref[head] += jnp.dot(probs.astype(BF), dout, preferred_element_type=F32)
            dk_ref[head] += jnp.dot(score_low, block, preferred_element_type=F32)
            outs.append(
                jnp.dot(
                    keys_t[head * HEAD_DIM : (head + 1) * HEAD_DIM],
                    score_low,
                    preferred_element_type=F32,
                )
            )
        dq_ref[rows, :] = jnp.concatenate(outs, axis=0).T

    lane = lax.broadcasted_iota(jnp.int32, (length, PAIR), 1)
    first = lane // HEAD_DIM == 0
    cosine, sine = cos_ref[...], sin_ref[...]

    def rounded(item):
        return item.astype(BF).astype(F32)

    def back(item):
        return item * cosine - swap_halves(item) * sine

    parts = [
        back(rounded(dq_ref[...])),
        back(rounded(jnp.where(first, dk_ref[0], dk_ref[1]))),
        rounded(jnp.where(first, dv_ref[0], dv_ref[1])),
    ]
    for idx, part in enumerate(parts):
        cols = slice(idx * PAIR, (idx + 1) * PAIR)
        grad_ref[:, cols] = part.astype(BF)
        bias_ref[:, cols] = jnp.broadcast_to(jnp.sum(part, axis=0, keepdims=True), (8, PAIR))


def attend_grad(low_all, mixed_grad, lse, cos_wide, sin_wide):
    length, width = low_all.shape
    pairs = width // (3 * PAIR)
    table = pl.BlockSpec((length, PAIR), lambda pair: (0, 0))
    triple = pl.BlockSpec((length, 3 * PAIR), lambda pair: (0, pair))
    return pl.pallas_call(
        attn_bwd_kernel,
        grid=(pairs,),
        in_specs=[
            triple,
            pl.BlockSpec((length, PAIR), lambda pair: (0, pair)),
            pl.BlockSpec((1, 8, length), lambda pair: (pair, 0, 0)),
            table,
            table,
        ],
        out_specs=[triple, pl.BlockSpec((8, 3 * PAIR), lambda pair: (0, pair))],
        out_shape=[
            jax.ShapeDtypeStruct((length, width), BF),
            jax.ShapeDtypeStruct((8, width), F32),
        ],
        scratch_shapes=[
            pltpu.VMEM((length, PAIR), F32),
            pltpu.VMEM((2, length, PAIR), F32),
            pltpu.VMEM((2, length, PAIR), F32),
        ],
        compiler_params=pltpu.CompilerParams(vmem_limit_bytes=VMEM_LIMIT),
        cost_estimate=pl.CostEstimate(
            flops=40 * pairs * length * length * PAIR,
            bytes_accessed=length * width * 6,
            transcendentals=2 * pairs * length * length,
        ),
        name="attend_grad",
    )(low_all, mixed_grad, lse, cos_wide, sin_wide)


class Places:
    def __init__(self):
        shard, seq = lax.axis_index("fsdp"), lax.axis_index("seq")
        parts = lax.axis_size("fsdp")
        self.ring = parts // 2
        self.seq = seq
        self.chip, self.core = shard // 2, lax.rem(shard, 2)
        self.at_x, self.at_y = lax.rem(seq, 2), seq // 2
        self.near_x = 2 * self.at_y + 1 - self.at_x
        self.near_y = 2 * (1 - self.at_y) + self.at_x
        self.other = {"fsdp": shard + 1 - 2 * self.core}
        self.up = {"fsdp": lax.rem(shard + 2, parts)}
        self.down = {"fsdp": lax.rem(shard + parts - 2, parts)}
        self.over_x = {"seq": self.near_x}
        self.over_y = {"seq": self.near_y}

    def back(self, hops):
        return lax.rem(self.chip - hops + self.ring, self.ring)


def remote(src, dst, send, recv, target):
    return pltpu.make_async_remote_copy(
        src_ref=src,
        dst_ref=dst,
        send_sem=send,
        recv_sem=recv,
        device_id=target,
        device_id_type=pl.DeviceIdType.MESH,
    )


def greet(targets, waits):
    barrier = pltpu.get_barrier_semaphore()
    for target in targets:
        pl.semaphore_signal(barrier, inc=1, device_id=target, device_id_type=pl.DeviceIdType.MESH)
    pl.semaphore_wait(barrier, waits)


def aligned(start, size, unit=None):
    return pl.ds(pl.multiple_of(start, unit or size), size)


ADD_ROWS = 32


def add_into(target, term):
    rows = target.shape[0]

    @pl.loop(0, rows // ADD_ROWS)
    def _(step):
        at = aligned(step * ADD_ROWS, ADD_ROWS)
        total = target[at, :].astype(F32) + term[at, :].astype(F32)
        target[at, :] = total.astype(BF)


class Sems:
    def __init__(self, ref):
        self.ref, self.used = ref, 0

    def take(self):
        self.used += 1
        return self.ref.at[self.used - 1]


class Sum:
    def __init__(self, at, sems, grad, own, one, two, three, z_first, x_first, stage, layer):
        self.at, self.sems = at, sems
        self.grad, self.own, self.one, self.two, self.three = grad, own, one, two, three
        self.z_first, self.x_first = z_first, x_first
        self.stage, self.layer = stage, layer
        self.rows = grad.shape[0] // (4 * at.ring)
        self.sends, self.loads = [], {}
        self.first, self.second, self.hop = {}, {}, {}

    def make(self, src, dst, target):
        copy = remote(src, dst, self.sems[0].take(), self.sems[1].take(), target)
        copy.start()
        self.sends.append(copy)
        return copy

    def load(self, src, dst):
        copy = pltpu.make_async_copy(src, dst, self.sems[2].take())
        copy.start()
        return copy

    def kept(self):
        at = self.at
        if self.x_first:
            return [(at.at_x, 1), (2 + at.at_x, 1)]
        return [(2 * at.at_y, 2)]

    def given(self):
        at = self.at
        if self.x_first:
            return [(1 - at.at_x, 1), (3 - at.at_x, 1)]
        return [(2 * (1 - at.at_y), 2)]

    def fetch_own(self, tile):
        base = self.at.back(tile + 1) * 4 * self.rows
        copies = []
        if self.z_first:
            copies.append(
                self.load(self.grad.at[aligned(base, 4 * self.rows), :], self.own.at[tile])
            )
        else:
            place = 0
            for first, count in self.kept():
                size = count * self.rows
                copies.append(
                    self.load(
                        self.grad.at[aligned(base + first * self.rows, size, self.rows), :],
                        self.own.at[tile, pl.ds(place, size), :],
                    )
                )
                place += size
        self.loads[tile] = copies

    def own_ready(self, tile):
        for copy in self.loads[tile]:
            copy.wait()

    def plane_one(self, tile, source, base):
        target = self.at.over_x if self.x_first else self.at.over_y
        place, made = 0, []
        for first, count in self.given():
            size = count * self.rows
            made.append(
                self.make(
                    source.at[aligned(base + first * self.rows, size, self.rows), :],
                    self.one.at[tile, pl.ds(place, size), :],
                    target,
                )
            )
            place += size
        self.first[tile] = made

    def plane_two(self, tile, kept_ref):
        for copy in self.first[tile]:
            copy.wait_recv()
        place = 0
        for ref in kept_ref:
            size = ref.shape[0]
            add_into(self.one.at[tile, pl.ds(place, size), :], ref)
            place += size
        at = self.at
        target = at.over_y if self.x_first else at.over_x
        keep = at.at_y if self.x_first else at.at_x
        self.keep_ref = lambda: self.one.at[tile, aligned(keep * self.rows, self.rows), :]
        self.second[tile] = self.make(
            self.one.at[tile, aligned((1 - keep) * self.rows, self.rows), :],
            self.two.at[tile],
            target,
        )

    def plane_three(self, tile):
        at = self.at
        keep = at.at_y if self.x_first else at.at_x
        self.second[tile].wait_recv()
        add_into(self.two.at[tile], self.one.at[tile, aligned(keep * self.rows, self.rows), :])

    def start(self, tile):
        base = self.at.back(tile + 1) * 4 * self.rows
        if self.z_first:
            self.own_ready(tile)
            self.hop[0] = self.make(self.own.at[0], self.three.at[0], self.at.up)
        else:
            self.plane_one(tile, self.grad, base)

    def middle(self, tile):
        self.own_ready(tile)
        self.plane_two(tile, [self.own.at[tile]])

    def finish(self, tile):
        self.plane_three(tile)
        if tile > 0:
            self.hop[tile - 1].wait_recv()
            add_into(self.two.at[tile], self.three.at[tile - 1])
        if tile < self.at.ring - 1:
            self.hop[tile] = self.make(self.two.at[tile], self.three.at[tile], self.at.up)

    def ring_step(self, tile):
        last = tile == self.at.ring - 1
        self.hop[tile - 1].wait_recv()
        self.own_ready(tile)
        total = self.three.at[tile - 1]
        add_into(total, self.own.at[tile])
        if last:
            self.plane_one(0, total, 0)
        else:
            self.hop[tile] = self.make(total, self.three.at[tile], self.at.up)

    def slab_middle(self):
        total = self.three.at[self.at.ring - 2]
        refs = [
            total.at[aligned(first * self.rows, count * self.rows, self.rows), :]
            for first, count in self.kept()
        ]
        self.plane_two(0, refs)

    def slab_finish(self):
        self.plane_three(0)

    def total(self):
        return self.two.at[0 if self.z_first else self.at.ring - 1]

    def place(self, quarter, turn=0, size=None):
        size = size or self.rows
        return self.stage.at[aligned(quarter * self.rows + turn * size, size), :]

    def gather(self):
        at = self.at
        self.kept_store = self.load(self.total(), self.place(at.seq))
        self.near = [
            self.make(self.total(), self.place(at.seq), at.over_x),
            self.make(self.total(), self.place(at.seq), at.over_y),
        ]

    def gather_far(self):
        at = self.at
        for copy in self.near:
            copy.wait_recv()
        half = self.rows // 2
        self.far = []
        for turn, (origin, target) in enumerate(((at.near_y, at.over_x), (at.near_x, at.over_y))):
            ref = self.place(origin, turn, half)
            self.far.append(self.make(ref, ref, target))

    def gather_end(self, arrive):
        at = self.at
        self.kept_store.wait()
        for copy in self.far:
            copy.wait_recv()
        self.swap = None
        if arrive is not None:
            half = 2 * self.rows
            self.swap = self.make(
                self.stage.at[aligned((1 - at.core) * half, half), :], arrive, at.other
            )

    def drain(self):
        if self.swap is not None:
            self.swap.wait_recv()
        for copy in self.sends:
            copy.wait_send()


def reduce_kernel(
    last,
    qkv_grad, proj_grad, up_grad, down_grad, vec_in, square_in,
    qkv_stage, qkv_arrive, proj_stage, up_stage, up_arrive, down_stage, vec_out, square_out,
    qkv_own, qkv_one, qkv_two, qkv_three,
    proj_own, proj_one, proj_two, proj_three,
    up_own, up_one, up_two, up_three,
    down_own, down_one, down_two, down_three,
    vec_got, vec_hop, vec_sum, square_got, square_sum,
    send_sem, recv_sem, load_sem,
):
    at = Places()
    ring = at.ring
    sems = (Sems(send_sem), Sems(recv_sem), Sems(load_sem))
    greet((at.other, at.over_x, at.over_y, at.down), 4)
    qkv = Sum(at, sems, qkv_grad, qkv_own, qkv_one, qkv_two, qkv_three, True, True, qkv_stage, 0)
    proj = Sum(
        at, sems, proj_grad, proj_own, proj_one, proj_two, proj_three, True, False, proj_stage, 0
    )
    up = Sum(at, sems, up_grad, up_own, up_one, up_two, up_three, False, True, up_stage, 0)
    down = Sum(
        at, sems, down_grad, down_own, down_one, down_two, down_three, False, False, down_stage, 0
    )
    wide, slabs = (up, down), (qkv, proj)

    vec_copies = []

    def vec_copy(src, dst, target):
        copy = remote(src, dst, sems[0].take(), sems[1].take(), target)
        copy.start()
        vec_copies.append(copy)
        return copy

    partners = (at.other, at.over_x, at.over_y)
    vec_sum[0] = vec_in[...]

    for item in slabs:
        item.fetch_own(0)
    for item in wide:
        item.start(0)
    for item in slabs:
        item.start(0)
    for item in wide:
        item.start(1)
    for tile in range(ring):
        for item in wide:
            item.fetch_own(tile)
        if tile > 0:
            for item in slabs:
                item.fetch_own(tile)
    vec_state = {"copy": vec_copy(vec_sum.at[0], vec_got.at[0], partners[0])}

    def vec_step(idx):
        vec_state["copy"].wait_recv()
        if idx <= 3:
            vec_sum[idx] = vec_sum[idx - 1] + vec_got[idx - 1]
            if idx < 3:
                vec_state["copy"] = vec_copy(vec_sum.at[idx], vec_got.at[idx], partners[idx])
            else:
                vec_state["copy"] = vec_copy(
                    vec_sum.at[3, at.back(1)], vec_hop.at[0], at.up
                )
        else:
            hop = idx - 3
            vec_hop[hop - 1] = vec_hop[hop - 1] + vec_sum[3, at.back(hop + 1)]
            if hop < ring - 1:
                vec_state["copy"] = vec_copy(vec_hop.at[hop - 1], vec_hop.at[hop], at.up)

    for tile in range(ring):
        for item in wide:
            item.middle(tile)
        if tile + 2 < ring:
            for item in wide:
                item.start(tile + 2)
        if tile > 0:
            for item in wide:
                item.finish(tile - 1)
        if tile + 1 < ring:
            for item in slabs:
                item.ring_step(tile + 1)
        vec_step(tile + 1)
    for item in slabs:
        item.slab_middle()
    vec_step(5)
    for item in wide:
        item.finish(ring - 1)
        item.gather()
    vec_step(6)
    vec_total = vec_hop[ring - 2]
    vec_out[...] = vec_total
    for item in slabs:
        item.slab_finish()
        item.gather()

    def squares(ref):
        rows, columns = ref.shape
        total = jnp.zeros((8, 128), F32)

        def body(step, total):
            part = ref[aligned(step * 16, 16), :].astype(F32)
            part = part * part
            part = part[0:8] + part[8:16]
            for column in range(0, columns, 128):
                total = total + part[:, column : column + 128]
            return total

        return lax.fori_loop(0, rows // 16, body, total)

    total = square_in[...]
    for item in (*wide, *slabs):
        total = total + squares(item.total())
    vec_square = vec_total * vec_total * 0.125
    for column in range(0, vec_square.shape[1], 128):
        total = total + vec_square[:, column : column + 128]
    square_sum[0] = total
    if last:
        for idx, target in enumerate(partners):
            copy = vec_copy(square_sum.at[idx], square_got.at[idx], target)
            if idx == 0:
                for item in wide:
                    item.gather_far()
            if idx == 1:
                for item in slabs:
                    item.gather_far()
            copy.wait_recv()
            square_sum[idx + 1] = square_sum[idx] + square_got[idx]
        total = square_sum[3]
        for hop in range(ring - 1):
            source = square_sum.at[3] if hop == 0 else square_got.at[2 + hop]
            copy = vec_copy(source, square_got.at[3 + hop], at.up)
            if hop == 0:
                for item in wide:
                    item.gather_end(up_arrive if item is up else None)
            copy.wait_recv()
            total = total + square_got[3 + hop]
        square_out[...] = total
    else:
        square_out[...] = total
        for item in (*wide, *slabs):
            item.gather_far()
        for item in wide:
            item.gather_end(up_arrive if item is up else None)
    for item in slabs:
        item.gather_end(qkv_arrive if item is qkv else None)
    for item in (*wide, *slabs):
        item.drain()
    for copy in vec_copies:
        copy.wait_send()


def reduce_grads(grads, vec, squares, last, call_id):
    ring = lax.axis_size("fsdp") // 2
    anywhere = pl.BlockSpec(memory_space=pl.ANY)
    vmem = pl.BlockSpec(memory_space=pltpu.VMEM)
    dma = pltpu.SemaphoreType.DMA
    scratch, slab_shapes = [], []
    for idx, grad in enumerate(grads):
        slab, width = grad.shape[0] // ring, grad.shape[1]
        quarter = slab // 4
        slab_shapes.append(jax.ShapeDtypeStruct((slab, width), BF))
        z_first = idx < 2
        tiles = 1 if z_first else ring
        scratch += [
            pltpu.VMEM((ring, slab if z_first else 2 * quarter, width), BF),
            pltpu.VMEM((tiles, 2 * quarter, width), BF),
            pltpu.VMEM((tiles, quarter, width), BF),
            pltpu.VMEM((ring - 1, slab if z_first else quarter, width), BF),
        ]
    half = [
        jax.ShapeDtypeStruct((shape.shape[0] // 2, shape.shape[1]), BF) for shape in slab_shapes
    ]
    return pl.pallas_call(
        partial(reduce_kernel, last),
        in_specs=[anywhere] * 4 + [vmem] * 2,
        out_specs=[anywhere] * 6 + [vmem] * 2,
        out_shape=[
            slab_shapes[0],
            half[0],
            slab_shapes[1],
            slab_shapes[2],
            half[2],
            slab_shapes[3],
            jax.ShapeDtypeStruct(vec.shape[1:], F32),
            jax.ShapeDtypeStruct((8, 128), F32),
        ],
        scratch_shapes=[
            *scratch,
            pltpu.VMEM((3,) + vec.shape, F32),
            pltpu.VMEM((ring - 1,) + vec.shape[1:], F32),
            pltpu.VMEM((4,) + vec.shape, F32),
            pltpu.VMEM((3 + ring - 1, 8, 128), F32),
            pltpu.VMEM((4, 8, 128), F32),
            dma((120,)),
            dma((120,)),
            dma((120,)),
        ],
        compiler_params=pltpu.CompilerParams(
            collective_id=call_id, has_side_effects=True, vmem_limit_bytes=VMEM_LIMIT
        ),
        cost_estimate=pl.CostEstimate(flops=0, bytes_accessed=300_000_000, transcendentals=0),
        name="reduce_grads",
    )(*grads, vec, squares)


def adam_kernel(
    kinds, ring, count, core_ref, factor_ref, *refs
):
    n_grads = len(refs) - 8
    grads = refs[:n_grads]
    master, first, second, grad_out, first_out, second_out, new_out, copy_out = refs[n_grads:]
    layer = pl.program_id(0)
    factor = factor_ref[0]
    scale = 1.0 / count
    columns = master.shape[2]
    per_layer = n_grads // 2
    width = columns // (kinds * ring * 2) if per_layer == 2 else 512

    def update(at, total):
        grad = total.astype(F32) * scale
        first_new, second_new, new = [], [], []
        first_new, second_new, new = adam_update(
            master[0, :, at], grad, first[0, :, at], second[0, :, at], factor
        )
        grad_out[0, :, at] = grad
        first_out[0, :, at] = first_new
        second_out[0, :, at] = second_new
        new_out[0, :, at] = new
        copy_out[0, :, at] = new.astype(BF)

    def choose(which, at):
        values = [grads[idx * per_layer + which][:, at] for idx in range(2)]
        return jnp.where(layer == 0, values[0], values[1])

    if per_layer == 1:
        for start in range(0, columns, width):
            update(slice(start, start + width), choose(0, slice(start, start + width)))
        return
    core = core_ref[0]
    for pair in range(ring):
        for kind in range(kinds):
            source = (pair * kinds + kind) * width
            mine, arrive = [choose(which, slice(source, source + width)) for which in range(2)]
            for which in range(2):
                start = (kind * ring * 2 + 2 * pair + which) * width
                update(slice(start, start + width), jnp.where(core == which, mine, arrive))


def adam_matrix(grads, master, first, second, factor, core, kinds, count):
    layers, rows, columns = master.shape
    ring = lax.axis_size("fsdp") // 2
    block = 32 if columns > 1024 else 64
    steps = rows // block
    per_layer = len(grads) // layers

    def grad_spec(idx):
        layer, which = divmod(idx, per_layer)
        lift = steps if per_layer == 2 and which == 0 else 0

        def where(at_layer, step, core_ref, layer=layer, lift=lift):
            held = 0 if layer > 0 else steps - 1
            row = jnp.where(at_layer == layer, step, held)
            return (row + lift * core_ref[0], 0)

        return pl.BlockSpec((block, grads[idx].shape[1]), where)

    whole = pl.BlockSpec((1, block, columns), lambda layer, step, core_ref: (layer, step, 0))
    shape = jax.ShapeDtypeStruct(master.shape, F32)
    return pl.pallas_call(
        partial(adam_kernel, kinds, ring, count),
        grid_spec=pltpu.PrefetchScalarGridSpec(
            num_scalar_prefetch=1,
            grid=(layers, steps),
            in_specs=[pl.BlockSpec(memory_space=pltpu.SMEM)]
            + [grad_spec(idx) for idx in range(len(grads))]
            + [whole] * 3,
            out_specs=[whole] * 5,
        ),
        out_shape=[shape] * 4 + [jax.ShapeDtypeStruct(master.shape, BF)],
        compiler_params=pltpu.CompilerParams(vmem_limit_bytes=VMEM_LIMIT),
        cost_estimate=pl.CostEstimate(
            flops=20 * master.size, bytes_accessed=32 * master.size, transcendentals=master.size
        ),
        name="update",
    )(core.reshape(1).astype(jnp.int32), factor.reshape(1), *grads, master, first, second)


def norm_parts(hidden):
    center = hidden - jnp.mean(hidden, axis=-1, keepdims=True)
    spread = jnp.mean(center * center, axis=-1, keepdims=True)
    inverse = lax.rsqrt(spread + 1e-06)
    return center * inverse, inverse


def norm_backward(hidden, gain, grad):
    scaled, inverse = norm_parts(hidden)
    entry = grad * gain
    mean_one = jnp.mean(entry, axis=-1, keepdims=True)
    mean_two = jnp.mean(entry * scaled, axis=-1, keepdims=True)
    result = inverse * (entry - mean_one - scaled * mean_two)
    return result, jnp.sum(grad * scaled, axis=0), jnp.sum(grad, axis=0)


def gelu_and_slope(upward):
    erf_part = 0.5 * (1.0 + lax.erf(upward * (1.0 / math.sqrt(2.0))))
    density = jnp.exp(-0.5 * upward * upward) * (1.0 / math.sqrt(2.0 * math.pi))
    return upward * erf_part, erf_part + upward * density


def dot(left, right):
    return jnp.dot(left, right, preferred_element_type=F32)


def dot_nt(left, right):
    return lax.dot_general(left, right, NT, preferred_element_type=F32)


def dot_tn(left, right):
    return lax.dot_general(left, right, (((0,), (0,)), ((), ())), preferred_element_type=F32)


def rotation_tables(packed):
    lane = lax.broadcasted_iota(jnp.int32, packed.shape, 1)
    first = lane % HEAD_DIM < HEAD_DIM // 2
    turned = pltpu.roll(packed, HEAD_DIM // 2, 1)
    return jnp.where(first, packed, turned), jnp.where(first, -turned, packed)


def each_block(count, body):
    @pl.loop(0, count)
    def _(step):
        body(aligned(step * ROWS_Q, ROWS_Q))


class Forward:
    def __init__(self, at, refs, layers):
        self.at, self.refs, self.layers = at, refs, layers
        self.blocks = refs.res.shape[0] // ROWS_Q
        self.pairs = refs.mixed.shape[1] // PAIR
        self.saves, self.slot = [], 0
        self.mixed_copies, self.part_copies = {}, {}

    def save(self, src, dst):
        copy = pltpu.make_async_copy(src, dst, self.refs.save_sem.at[self.slot])
        self.slot += 1
        copy.start()
        self.saves.append(copy)
        return copy

    def settle(self):
        for copy in self.saves:
            copy.wait()
        self.saves = []

    def bring(self, pairs):
        copies = []
        for src, dst in pairs:
            copies.append(pltpu.make_async_copy(src, dst, self.refs.save_sem.at[self.slot]))
            self.slot += 1
        for copy in copies:
            copy.start()
        for copy in copies:
            copy.wait()

    def vec(self, layer, row, width):
        return self.refs.vecs[layer, row : row + 1, 0:width]

    def unpack_vectors(self):
        refs, at = self.refs, self.at
        ring = at.ring
        per_shard = refs.vec_rows
        for layer in range(self.layers):
            places = [(row, row // 8, row % 8) for row in range(48)]
            for pair in range(ring):
                for kind in range(3):
                    places.append((48 + kind * 8 + 2 * pair + at.core, 6, pair * 3 + kind))
                for part in range(4):
                    places.append((72 + (2 * pair + at.core) * 4 + part, 7, pair * 4 + part))
            for source, row, block in places:
                shard, entry = source // per_shard, layer * per_shard + source % per_shard
                if not isinstance(source, int):
                    shard = lax.div(source, per_shard)
                    entry = layer * per_shard + lax.rem(source, per_shard)
                refs.vecs[layer, row : row + 1, block * 128 : (block + 1) * 128] = refs.vec_out[
                    shard, pl.ds(entry, 1), :
                ]

    def normed(self, rows, layer, first):
        hidden = self.refs.res[rows, :]
        scaled, _ = norm_parts(hidden)
        width = hidden.shape[1]
        return (scaled * self.vec(layer, first, width) + self.vec(layer, first + 1, width)).astype(BF)

    def qkv(self, layer, weight):
        refs = self.refs
        width = weight.shape[1]
        self.settle()
        self.bring([(weight, refs.w_one.at[:, pl.ds(0, width)])])

        def body(rows):
            normed = self.normed(rows, layer, 0)
            refs.norm[rows, :] = normed
            for pair in range(self.pairs):
                cols = slice(pair * 3 * PAIR, (pair + 1) * 3 * PAIR)
                block = dot(normed, refs.w_one[:, cols]) + refs.vecs[layer, 6:7, cols]
                cosine, sine = rotation_tables(refs.tables[rows, :])
                for kind in range(3):
                    part = block[:, kind * PAIR : (kind + 1) * PAIR]
                    if kind < 2:
                        part = part * cosine + swap_halves(part) * sine
                    start = pair * 3 * PAIR + kind * PAIR
                    refs.low[rows, start : start + PAIR] = part.astype(BF)

        each_block(self.blocks, body)
        self.save(refs.norm, refs.normed_out[layer])
        self.save(refs.low, refs.low_out[layer])

    def attend(self, layer, pair):
        refs = self.refs
        base = pair * 3 * PAIR
        key_rows = refs.low[:, base + PAIR : base + 2 * PAIR]
        for head in range(2):
            refs.keys[head] = head_mask(key_rows, head)
        refs.values_t[...] = refs.low[:, base + 2 * PAIR : base + 3 * PAIR].astype(F32).T.astype(BF)

        def body(rows):
            block = refs.low[rows, base : base + PAIR] * jnp.asarray(HEAD_DIM**-0.5, BF)
            outs = []
            for head in range(2):
                scores = lax.dot_general(refs.keys[head], block, NT, preferred_element_type=F32)
                top = jnp.max(scores, axis=0, keepdims=True)
                exponent = jnp.exp(scores - top)
                total = jnp.sum(exponent, axis=0, keepdims=True)
                refs.lse_out[layer, pair, head : head + 1, rows] = top + jnp.log(total)
                probs = (exponent * (1.0 / total)).astype(BF)
                outs.append(dot(refs.values_t[head * HEAD_DIM : (head + 1) * HEAD_DIM], probs))
            refs.mixed[rows, pair * PAIR : (pair + 1) * PAIR] = (
                jnp.concatenate(outs, axis=0).T.astype(BF)
            )

        each_block(self.blocks, body)
        slot = layer * (self.pairs + 2) + pair
        cols = pl.ds(pair * PAIR, PAIR)
        copy = remote(
            refs.mixed.at[:, cols],
            refs.mixed_other.at[:, cols],
            refs.x_send.at[slot],
            refs.x_recv.at[slot],
            self.at.other,
        )
        copy.start()
        self.mixed_copies[layer, pair] = copy

    def project(self, layer, own, other):
        refs = self.refs
        half = own.shape[0]
        self.bring(
            [
                (own, refs.w_two.at[pl.ds(0, half), :]),
                (other, refs.w_two.at[pl.ds(half, half), :]),
            ]
        )
        self.settle()
        for pair in range(self.pairs):
            self.mixed_copies[layer, pair].wait()
        width = refs.res.shape[1]

        def body(rows):
            total = dot(refs.mixed[rows, :], refs.w_two[0:half, :])
            total = total + dot(refs.mixed_other[rows, :], refs.w_two[half : 2 * half, :])
            refs.res[rows, :] = refs.res[rows, :] + total + self.vec(layer, 4, width)
            refs.norm[rows, :] = self.normed(rows, layer, 2)

        each_block(self.blocks, body)
        self.save(refs.mixed, refs.mixed_out[layer])
        self.save(refs.res, refs.after_out[layer])
        self.save(refs.norm, refs.normed_two_out[layer])

    def hidden_units(self, layer, half, up_weight, down_weight):
        refs = self.refs
        if half == 0:
            self.settle()
            self.bring([(up_weight, refs.w_one), (down_weight, refs.w_two)])
        width = refs.res.shape[1]
        tiles = refs.w_one.shape[1] // 512
        blocks = self.blocks // 2

        @pl.loop(half * blocks, (half + 1) * blocks)
        def _(step):
            rows = aligned(step * ROWS_Q, ROWS_Q)

            @pl.loop(0, tiles)
            def _(tile):
                cols = aligned(tile * 512, 512)
                upward = dot(refs.norm[rows, :], refs.w_one[:, cols]) + refs.vecs[layer, 7:8, cols]
                active, slope = gelu_and_slope(upward)
                refs.act[rows, cols] = active.astype(BF)
                refs.slope[rows, cols] = slope.astype(BF)

            part = dot(refs.act[rows, :], refs.w_two[...])
            refs.res[rows, :] = refs.res[rows, :] + part + self.vec(layer, 5, width)
            refs.part[rows, :] = part.astype(BF)

        rows = pl.ds(half * blocks * ROWS_Q, blocks * ROWS_Q)
        slot = layer * (self.pairs + 2) + self.pairs + half
        copy = remote(
            refs.part.at[rows, :],
            refs.part_other.at[rows, :],
            refs.x_send.at[slot],
            refs.x_recv.at[slot],
            self.at.other,
        )
        copy.start()
        self.part_copies[layer, half] = copy
        if half == 1:
            self.save(refs.act, refs.active_out[layer])
            self.save(refs.slope, refs.slope_out[layer])

    def join(self, layer):
        refs = self.refs
        for half in range(2):
            self.part_copies[layer, half].wait()

        def body(rows):
            refs.res[rows, :] = refs.res[rows, :] + refs.part_other[rows, :].astype(F32)

        each_block(self.blocks, body)
        self.save(refs.res, refs.result_out[layer])


WEIGHTS = ("qkv", "proj", "up", "down")


def forward_kernel(names, layers, vec_rows, *operands):
    refs = SimpleNamespace(**dict(zip(names, operands)))
    for name in (*WEIGHTS, "proj_two", "normed", "low", "mixed", "after", "normed_two", "active", "slope", "result"):
        label = name + "_out"
        setattr(refs, label, [getattr(refs, label + str(layer)) for layer in range(layers)])
    refs.vec_rows = vec_rows
    at = Places()
    ring, seq, chip, core = at.ring, at.seq, at.chip, at.core
    full = {name: getattr(refs, name + "_full") for name in WEIGHTS}
    source = {name: getattr(refs, name + "_in") for name in WEIGHTS}
    slabs = {name: getattr(refs, name + "_slab") for name in WEIGHTS}
    outs = {name: getattr(refs, name + "_out") for name in WEIGHTS}
    items = [(name, layer) for layer in range(layers) for name in WEIGHTS]
    loads = {}

    def start_load(name, layer):
        copy = pltpu.make_async_copy(
            source[name].at[layer], full[name], refs.l_in.at[items.index((name, layer))]
        )
        copy.start()
        loads[name, layer] = copy

    for name in WEIGHTS:
        start_load(name, 0)
    barrier = pltpu.get_barrier_semaphore()
    for target in (at.other, at.up, at.down):
        pl.semaphore_signal(barrier, inc=1, device_id=target, device_id_type=pl.DeviceIdType.MESH)
    for step in range(1, 4):
        for half in range(2):
            pl.semaphore_signal(
                barrier,
                inc=1,
                device_id={"fsdp": 2 * chip + half, "seq": seq ^ step},
                device_id_type=pl.DeviceIdType.MESH,
            )
    pl.semaphore_wait(barrier, 9)

    length = refs.clip_in.shape[1]
    token_core = seq // 2
    token_rows = aligned(seq * length, length)
    stays = core == token_core

    class Move:
        def __init__(self, base, pairs):
            self.base, self.pairs, self.copies = base, pairs, []

        def start(self):
            for turn in range(2):
                target = {"seq": 2 * core + turn, "fsdp": 2 * chip + token_core}
                away = jnp.logical_not(jnp.logical_and(stays, lax.rem(seq, 2) == turn))
                copies = [
                    remote(
                        src.at[turn],
                        place(seq),
                        refs.m_send.at[self.base + 2 * turn + idx],
                        refs.m_recv.at[self.base + 2 * lax.rem(seq, 2) + idx],
                        target,
                    )
                    for idx, (src, place) in enumerate(self.pairs)
                ]
                self.copies.append((away, copies))

                @pl.when(away)
                def _(copies=copies):
                    for copy in copies:
                        copy.start()

            @pl.when(stays)
            def _():
                for idx, (src, place) in enumerate(self.pairs):
                    bounce = refs.clip_slab if idx == 0 else refs.table_slab
                    sem = refs.m_load.at[self.base // 6 * 2 + idx]
                    load = pltpu.make_async_copy(src.at[lax.rem(seq, 2)], bounce, sem)
                    load.start()
                    load.wait()
                    store = pltpu.make_async_copy(bounce, place(seq), sem)
                    store.start()
                    store.wait()

        def swap(self):
            for part in range(2):
                came = jnp.logical_not(jnp.logical_and(stays, lax.rem(seq, 2) == part))

                @pl.when(came)
                def _(part=part):
                    for idx, (src, place) in enumerate(self.pairs):
                        remote(
                            src.at[0],
                            place(2 * core + part),
                            refs.m_send.at[self.base],
                            refs.m_recv.at[self.base + 2 * part + idx],
                            at.other,
                        ).wait_recv()

            self.swaps = []
            for idx, (src, place) in enumerate(self.pairs):
                for part in range(2):
                    slot = 24 + self.base // 6 * 4 + 2 * idx + part
                    ref = place(2 * core + part)
                    self.swaps.append(
                        remote(ref, ref, refs.m_send.at[slot], refs.m_recv.at[slot], at.other)
                    )
            for copy in self.swaps:
                copy.start()

        def arrived(self):
            for copy in self.swaps:
                copy.wait_recv()

        def drain(self):
            for copy in self.swaps:
                copy.wait_send()
            for away, copies in self.copies:

                @pl.when(away)
                def _(copies=copies):
                    for copy in copies:
                        copy.wait_send()

    def chunk_of(ref):
        return lambda number: ref.at[aligned(number * length, length), :]

    tokens = Move(0, [(refs.clip_in, chunk_of(refs.clip_out)), (refs.table_in, chunk_of(refs.table_out))])
    cotangents = Move(6, [(refs.cot_in, chunk_of(refs.cot_out))])
    tokens.start()

    refs.vec_out[2 * chip + core] = refs.vec_in[...]
    vec_swap = remote(
        refs.vec_in, refs.vec_out.at[2 * chip + core], refs.m_send.at[16], refs.m_recv.at[16], at.other
    )
    vec_swap.start()
    vec_copies = [vec_swap]

    def vec_hop(hop):
        vec_copies[-1].wait_recv()
        ref = refs.vec_out.at[pl.ds(2 * at.back(hop), 2)]
        slot = 17 + hop
        copy = remote(ref, ref, refs.m_send.at[slot], refs.m_recv.at[slot], at.up)
        copy.start()
        vec_copies.append(copy)

    def place(name, layer, chip_at, part):
        slab = slabs[name].shape[1]
        if part is None:
            return outs[name][layer].at[aligned(chip_at * slab, slab), :]
        size = slab // 4
        return outs[name][layer].at[aligned(chip_at * slab + part * size, size), :]

    swaps, prepared, stores = {}, [], []

    def prepare():
        if len(prepared) == len(items):
            return
        idx = len(prepared)
        name, layer = items[idx]
        prepared.append(name)
        slab = slabs[name]
        loads[name, layer].wait()
        swaps[idx] = None
        if name in ("down", "proj"):
            slab[layer] = full[name][...].astype(BF)
        else:
            away, kinds = (refs.qkv_away, 3) if name == "qkv" else (refs.up_away, 1)
            half, columns = full[name].shape
            width = columns // (kinds * 2 * ring)
            rows = aligned(core * half, half)
            for pair in range(ring):
                for kind in range(kinds):
                    cols = slice((pair * kinds + kind) * width, (pair * kinds + kind + 1) * width)
                    for mine in (True, False):
                        which = core if mine else 1 - core
                        start = (kind * 2 * ring + 2 * pair + which) * width
                        block = full[name][:, aligned(start, width)].astype(BF)
                        if mine:
                            slab[layer, rows, cols] = block
                        else:
                            away[layer, :, cols] = block
            swaps[idx] = remote(
                away.at[layer],
                slab.at[layer, rows, :],
                refs.c_send.at[idx],
                refs.c_recv.at[idx],
                at.other,
            )
            swaps[idx].start()
        if layer + 1 < layers:
            start_load(name, layer + 1)

    hops = ring - 1
    order = []
    for first in range(0, len(items), 2):
        for hop in range(hops):
            order += [(first, hop), (first + 1, hop)]
    z_copies, plane, far, proj_swaps = {}, {}, {}, {}

    def begin(idx):
        name, layer = items[idx]
        if swaps[idx] is not None:
            swaps[idx].wait_recv()
        store = pltpu.make_async_copy(
            slabs[name].at[layer], place(name, layer, chip, None), refs.l_out.at[idx]
        )
        store.start()
        stores.append(store)

    def z_copy(idx, hop):
        name, layer = items[idx]
        part = None if name == "proj" else seq
        target = place(name, layer, at.back(hop), part)
        from_ref = target
        if hop == 0:
            from_ref = slabs[name].at[layer]
            if part is not None:
                size = slabs[name].shape[1] // 4
                from_ref = slabs[name].at[layer, aligned(seq * size, size), :]
        slot = idx * hops + hop
        copy = remote(from_ref, target, refs.z_send.at[slot], refs.z_recv.at[slot], at.up)
        copy.start()
        z_copies[idx, hop] = copy

    def plane_copies(idx, hop):
        name, layer = items[idx]
        ref = place(name, layer, at.back(hop + 1), seq)
        slot = 2 * (idx * hops + hop)
        plane[idx, hop] = [
            remote(ref, ref, refs.p_send.at[slot], refs.p_recv.at[slot], at.over_x),
            remote(ref, ref, refs.p_send.at[slot + 1], refs.p_recv.at[slot + 1], at.over_y),
        ]
        for copy in plane[idx, hop]:
            copy.start()

    def far_copies(idx, hop):
        name, layer = items[idx]
        slot = 2 * (idx * hops + hop)
        size = slabs[name].shape[1] // 4
        half = size // 2
        base = at.back(hop + 1) * 4 * size
        for copy in plane[idx, hop]:
            copy.wait_recv()
        made = []
        for turn, (origin, target) in enumerate(((at.near_y, at.over_x), (at.near_x, at.over_y))):
            ref = outs[name][layer].at[aligned(base + origin * size + turn * half, half), :]
            made.append(
                remote(ref, ref, refs.d_send.at[slot + turn], refs.d_recv.at[slot + turn], target)
            )
        far[idx, hop] = made
        for copy in made:
            copy.start()

    pending = []

    def flush(keep):
        while len(pending) > keep:
            far_copies(*pending.pop(0))

    def event(number):
        idx, hop = order[number]
        z_copies[idx, hop].wait_recv()
        if hop + 1 < hops:
            z_copy(idx, hop + 1)
        elif idx + 2 < len(items):
            begin(idx + 2)
            z_copy(idx + 2, 0)
        name, layer = items[idx]
        if name == "proj":
            if hop + 1 == hops:
                stores[idx].wait()
                slot = len(items) + layer
                proj_swaps[layer] = remote(
                    outs["proj"][layer],
                    refs.proj_two_out[layer],
                    refs.c_send.at[slot],
                    refs.c_recv.at[slot],
                    at.other,
                )
                proj_swaps[layer].start()
        else:
            plane_copies(idx, hop)
            pending.append((idx, hop))
            flush(1)
        prepare()

    def complete(name, layer):
        idx = items.index((name, layer))
        if name == "proj":
            proj_swaps[layer].wait_recv()
            return
        stores[idx].wait()
        flush(0)
        for hop in range(hops):
            for copy in far[idx, hop]:
                copy.wait_recv()

    work = Forward(at, refs, layers)

    def take_tokens():
        tokens.arrived()
        vec_copies[-1].wait_recv()
        work.bring([(refs.clip_out, refs.res), (refs.table_out, refs.tables)])
        work.unpack_vectors()

    def qkv(layer):
        complete("qkv", layer)
        work.qkv(layer, outs["qkv"][layer])

    def project(layer):
        complete("proj", layer)
        work.project(layer, outs["proj"][layer], refs.proj_two_out[layer])

    def hidden_units(layer, half):
        if half == 0:
            complete("up", layer)
            complete("down", layer)
        work.hidden_units(layer, half, outs["up"][layer], outs["down"][layer])

    prepare()
    prepare()
    begin(0)
    z_copy(0, 0)
    begin(1)
    z_copy(1, 0)
    prepare()
    prepare()
    per_layer = 4 * hops
    chunks = []
    for layer in range(layers):
        first = layer * per_layer + 2 * hops
        if layer == 0:
            chunks.append((first, take_tokens))
        chunks.append((first + 1, partial(qkv, layer)))
        for pair in range(work.pairs):
            chunks.append((first + 1 + pair, partial(work.attend, layer, pair)))
        chunks.append((first + 5, partial(project, layer)))
        chunks.append((first + 7, partial(hidden_units, layer, 0)))
        chunks.append((first + 8, partial(hidden_units, layer, 1)))
        chunks.append((first + 9, partial(work.join, layer)))
    for number in range(len(order)):
        while chunks and chunks[0][0] <= number:
            chunks.pop(0)[1]()
        if number == 2:
            tokens.swap()
        if 3 <= number < 3 + hops:
            vec_hop(number - 3)
        if number == per_layer:
            cotangents.start()
        if number == per_layer + 6:
            cotangents.swap()
        event(number)
    flush(0)
    for _, chunk in chunks:
        chunk()

    work.settle()
    cotangents.arrived()
    for made in plane.values():
        for copy in made:
            copy.wait_send()
    for made in far.values():
        for copy in made:
            copy.wait_send()
    for copy in z_copies.values():
        copy.wait_send()
    for copy in swaps.values():
        if copy is not None:
            copy.wait_send()
    for copy in proj_swaps.values():
        copy.wait_send()
    for copy in vec_copies:
        copy.wait_send()
    tokens.drain()
    cotangents.drain()


def forward(qkv, up, down, proj, clips, cots, tables, vectors, vec_rows):
    layers, rows, width = proj.shape
    parts = lax.axis_size("fsdp")
    ring = parts // 2
    count, hops = 4 * layers, ring - 1
    length = 4 * clips.shape[1]
    down_rows = down.shape[1]
    qkv_half, up_half = qkv.shape[2] // 2, up.shape[2] // 2
    pairs = qkv_half // (3 * PAIR)
    inputs = {
        "qkv_in": qkv, "up_in": up, "down_in": down, "proj_in": proj, "clip_in": clips, "cot_in": cots,
        "table_in": tables, "vec_in": vectors,
    }
    outputs = {}
    for layer in range(layers):
        for name, shape, dtype in (
            ("qkv", (parts * rows, qkv_half), BF),
            ("up", (parts * rows, up_half), BF),
            ("down", (ring * down_rows, width), BF),
            ("proj", (ring * rows, width), BF),
            ("proj_two", (ring * rows, width), BF),
            ("normed", (length, width), BF),
            ("low", (length, qkv_half), BF),
            ("mixed", (length, pairs * PAIR), BF),
            ("after", (length, width), F32),
            ("normed_two", (length, width), BF),
            ("active", (length, up_half), BF),
            ("slope", (length, up_half), BF),
            ("result", (length, width), F32),
        ):
            outputs[name + "_out" + str(layer)] = (shape, dtype)
    outputs["clip_out"] = ((length, width), F32)
    outputs["cot_out"] = ((length, width), F32)
    outputs["table_out"] = ((length, PAIR), F32)
    outputs["vec_out"] = ((parts,) + vectors.shape, F32)
    outputs["lse_out"] = ((layers, pairs, 8, length), F32)
    in_vmem = ("vec_in", "vec_out", "lse_out")
    anywhere = pl.BlockSpec(memory_space=pl.ANY)
    vmem = pl.BlockSpec(memory_space=pltpu.VMEM)
    dma = pltpu.SemaphoreType.DMA
    scratch = {
        "qkv_full": pltpu.VMEM(qkv.shape[1:], F32),
        "up_full": pltpu.VMEM(up.shape[1:], F32),
        "down_full": pltpu.VMEM(down.shape[1:], F32),
        "proj_full": pltpu.VMEM(proj.shape[1:], F32),
        "qkv_away": pltpu.VMEM((layers, rows, qkv_half), BF),
        "up_away": pltpu.VMEM((layers, rows, up_half), BF),
        "qkv_slab": pltpu.VMEM((layers, 2 * rows, qkv_half), BF),
        "up_slab": pltpu.VMEM((layers, 2 * rows, up_half), BF),
        "down_slab": pltpu.VMEM((layers, down_rows, width), BF),
        "proj_slab": pltpu.VMEM((layers, rows, width), BF),
        "clip_slab": pltpu.VMEM(clips.shape[1:], F32),
        "table_slab": pltpu.VMEM(tables.shape[1:], F32),
        "res": pltpu.VMEM((length, width), F32),
        "tables": pltpu.VMEM((length, PAIR), F32),
        "vecs": pltpu.VMEM((layers, 8, up_half), F32),
        "norm": pltpu.VMEM((length, width), BF),
        "low": pltpu.VMEM((length, qkv_half), BF),
        "keys": pltpu.VMEM((2, length, PAIR), BF),
        "values_t": pltpu.VMEM((PAIR, length), BF),
        "mixed": pltpu.VMEM((length, pairs * PAIR), BF),
        "mixed_other": pltpu.VMEM((length, pairs * PAIR), BF),
        "w_one": pltpu.VMEM((width, up_half), BF),
        "w_two": pltpu.VMEM((ring * down_rows, width), BF),
        "act": pltpu.VMEM((length, up_half), BF),
        "slope": pltpu.VMEM((length, up_half), BF),
        "part": pltpu.VMEM((length, width), BF),
        "part_other": pltpu.VMEM((length, width), BF),
        "z_send": dma((count * hops,)), "z_recv": dma((count * hops,)),
        "p_send": dma((2 * count * hops,)), "p_recv": dma((2 * count * hops,)),
        "d_send": dma((2 * count * hops,)), "d_recv": dma((2 * count * hops,)),
        "c_send": dma((count + layers,)), "c_recv": dma((count + layers,)),
        "l_in": dma((count,)), "l_out": dma((count,)),
        "m_send": dma((32,)), "m_recv": dma((32,)), "m_load": dma((4,)),
        "x_send": dma((layers * (pairs + 2),)), "x_recv": dma((layers * (pairs + 2),)),
        "save_sem": dma((16 * layers,)),
    }
    names = [*inputs, *outputs, *scratch]
    results = pl.pallas_call(
        partial(forward_kernel, names, layers, vec_rows),
        in_specs=[vmem if name in in_vmem else anywhere for name in inputs],
        out_specs=[vmem if name in in_vmem else anywhere for name in outputs],
        out_shape=[jax.ShapeDtypeStruct(*shape) for shape in outputs.values()],
        scratch_shapes=list(scratch.values()),
        compiler_params=pltpu.CompilerParams(
            collective_id=0, has_side_effects=True, vmem_limit_bytes=62 * 1024 * 1024
        ),
        cost_estimate=pl.CostEstimate(
            flops=60_000_000_000, bytes_accessed=600_000_000, transcendentals=0
        ),
        name="forward",
    )(*inputs.values())
    return SimpleNamespace(**dict(zip(outputs, results)))


def spread_bias(grad, core, fsdp_parts, kinds):
    width = grad.shape[0] // (kinds * (fsdp_parts // 2))
    view = grad.reshape(fsdp_parts // 2, kinds, width).transpose(1, 0, 2)
    zero = jnp.zeros_like(view)
    first = jnp.where(core == 0, view, zero)
    second = jnp.where(core == 0, zero, view)
    return jnp.stack([first, second], axis=2).reshape(-1)


def fast_device(
    clip_tokens,
    patch_coords,
    out_cotangent,
    vector_params,
    qkv_weight,
    proj_weight,
    up_weight,
    down_weight,
    first_vector,
    first_qkv,
    first_proj,
    first_up,
    first_down,
    second_vector,
    second_qkv,
    second_proj,
    second_up,
    second_down,
):
    masters = (vector_params, qkv_weight, proj_weight, up_weight, down_weight)
    firsts = (first_vector, first_qkv, first_proj, first_up, first_down)
    seconds = (second_vector, second_qkv, second_proj, second_up, second_down)
    layer_count = vector_params.shape[0]
    batch_local, chunk_len = clip_tokens.shape[:2]
    seq_parts = lax.axis_size("seq")
    parts = lax.axis_size("fsdp")
    ring = parts // 2
    seq = lax.axis_index("seq")
    shard = lax.axis_index("fsdp")
    core = lax.rem(shard, 2)
    even = lax.rem(seq, 2) == 0

    def from_clips(item):
        mine = pick(item.reshape((2, 2, chunk_len) + item.shape[1:]), core)
        pieces = [None, None]
        for turn in range(2):
            piece = jnp.where(even, mine[turn], mine[1 - turn])
            pairs = []
            for src_seq in range(seq_parts):
                for src in range(parts):
                    dst_seq = 2 * (src % 2) + (src_seq + turn) % 2
                    dst = src - src % 2 + src_seq // 2
                    pairs.append((dst_seq * parts + dst, src_seq * parts + src))
            pieces[turn] = lax.ppermute(piece, ("seq", "fsdp"), pairs)
        return jnp.where(
            even, jnp.stack([pieces[0], pieces[1]]), jnp.stack([pieces[1], pieces[0]])
        )

    tables = []
    for idx in range(batch_local):
        cosine, sine = rotary_tables(patch_coords[:, idx], HEAD_DIM // 2)
        tables.append(jnp.concatenate([cosine, sine, cosine, sine], axis=1))
    share = vector_params.shape[1]
    vector_rows = vector_params.astype(BF).astype(F32).reshape(-1, 128)
    vector_rows = jnp.pad(vector_rows, ((0, -vector_rows.shape[0] % 8), (0, 0)))
    kept = forward(
        qkv_weight,
        up_weight,
        down_weight,
        proj_weight,
        clip_tokens,
        out_cotangent,
        jnp.stack(tables),
        vector_rows,
        share // 128,
    )
    vector_all = kept.vec_out.reshape(parts, -1)[:, : vector_params.size]
    vector_all = vector_all.reshape(parts, layer_count, share).transpose(1, 0, 2)
    vector_all = vector_all.reshape(layer_count, -1)
    cosine, sine = kept.table_out[:, : HEAD_DIM // 2], kept.table_out[:, HEAD_DIM // 2 : HEAD_DIM]
    cos_wide = jnp.concatenate([cosine] * 4, axis=1)
    sin_wide = jnp.concatenate([-sine, sine, -sine, sine], axis=1)
    block_output = from_clips(getattr(kept, "result_out" + str(layer_count - 1)))

    grad = kept.cot_out
    sums = [None] * layer_count
    vector_sums = [None] * layer_count
    squares = jnp.zeros((8, 128), F32)
    for idx in reversed(range(layer_count)):
        qkv_w, proj_w, up_w, down_w, normed, low_all, mixed, after_attn, normed_two, active, slope = [
            getattr(kept, name + "_out" + str(idx))
            for name in (*WEIGHTS, "normed", "low", "mixed", "after", "normed_two", "active", "slope")
        ]
        entry = kept.clip_out if idx == 0 else getattr(kept, "result_out" + str(idx - 1))
        lse = kept.lse_out[idx]
        gain_one, shift_one, gain_two, shift_two, proj_bias, down_bias, qkv_bias, up_bias = pieces(
            vector_all[idx]
        )
        down_bias_grad = jnp.sum(grad, axis=0)
        grad_low = grad.astype(BF)
        upward_grad = dot_nt(grad_low, down_w) * slope.astype(F32)
        up_bias_grad = jnp.sum(upward_grad, axis=0)
        upward_low = upward_grad.astype(BF)
        part = dot_nt(upward_low, up_w)
        other = swap_core(part.astype(BF))
        down_grad = dot_tn(active, grad_low).astype(BF)
        up_grad = dot_tn(normed_two, upward_low).astype(BF)
        attn_in, gain_two_grad, shift_two_grad = norm_backward(
            after_attn, gain_two, part + other.astype(F32)
        )
        after_grad = grad + attn_in
        proj_bias_grad = jnp.sum(after_grad, axis=0)
        after_low = after_grad.astype(BF)
        mixed_grad = dot_nt(after_low, proj_w).astype(BF)
        proj_grad = dot_tn(mixed, after_low).astype(BF)
        qkv_low, bias_rows = attend_grad(low_all, mixed_grad, lse, cos_wide, sin_wide)
        part = dot_nt(qkv_low, qkv_w)
        other = swap_core(part.astype(BF))
        qkv_grad = dot_tn(normed, qkv_low).astype(BF)
        attn_in, gain_one_grad, shift_one_grad = norm_backward(
            entry, gain_one, part + other.astype(F32)
        )
        grad = after_grad + attn_in

        shared = jnp.concatenate(
            [
                gain_one_grad,
                shift_one_grad,
                gain_two_grad,
                shift_two_grad,
                proj_bias_grad,
                down_bias_grad,
            ]
        )
        vector_sums[idx] = jnp.concatenate(
            [
                jnp.where(core == 0, shared, jnp.zeros_like(shared)),
                spread_bias(bias_rows[0], core, parts, 3),
                spread_bias(up_bias_grad, core, parts, 1),
            ]
        )

        total_vec = vector_sums[idx].reshape(ring, -1)
        pad = -total_vec.shape[1] % 1024
        total_vec = jnp.pad(total_vec, ((0, 0), (0, pad))).reshape(ring, 8, -1)
        sums[idx] = reduce_grads(
            (qkv_grad, proj_grad, up_grad, down_grad),
            total_vec,
            squares,
            idx == 0,
            1 + idx,
        )
        squares = sums[idx][7]
    input_grad = from_clips(grad)

    clip_count = batch_local * parts
    norm_value = jnp.sqrt(jnp.sum(squares)) / clip_count
    param_count = sum(master.size for master in masters) * parts
    factor = jnp.minimum(1.0, CLIP_RATIO * math.sqrt(float(param_count)) / (norm_value + 1e-06))

    vector_total = jnp.stack([item[6].reshape(-1)[: 2 * share] for item in sums])
    vector_grad = lax.dynamic_slice_in_dim(vector_total, core * share, share, 1) / clip_count
    vector_new = adam_update(vector_params, vector_grad, first_vector, second_vector, factor)
    updates = [(vector_grad, *vector_new, vector_new[2].astype(BF))]
    for kind, keys in enumerate(((0, 1), (2,), (3, 4), (5,))):
        updates.append(
            adam_matrix(
                [item[key] for item in sums for key in keys],
                masters[kind + 1],
                firsts[kind + 1],
                seconds[kind + 1],
                factor,
                core,
                3 if kind == 0 else 1,
                clip_count,
            )
        )
    return (
        block_output,
        input_grad,
        *[item[0] for item in updates],
        norm_value.reshape(1),
        *[item[1] for item in updates],
        *[item[2] for item in updates],
        *[item[3] for item in updates],
        *[item[4] for item in updates],
    )


def solution(mesh):
    in_specs = (
        P("fsdp", "seq", None),
        P(None, "fsdp", "seq"),
        P("fsdp", "seq", None),
        P(None, "fsdp"),
        P(None, "fsdp", None),
        P(None, "fsdp", None),
        P(None, "fsdp", None),
        P(None, "fsdp", None),
        P(None, "fsdp"),
        P(None, "fsdp", None),
        P(None, "fsdp", None),
        P(None, "fsdp", None),
        P(None, "fsdp", None),
        P(None, "fsdp"),
        P(None, "fsdp", None),
        P(None, "fsdp", None),
        P(None, "fsdp", None),
        P(None, "fsdp", None),
    )
    out_specs = (
        P("fsdp", "seq", None),
        P("fsdp", "seq", None),
        P(None, "fsdp"),
        P(None, "fsdp", None),
        P(None, "fsdp", None),
        P(None, "fsdp", None),
        P(None, "fsdp", None),
        P(),
        P(None, "fsdp"),
        P(None, "fsdp", None),
        P(None, "fsdp", None),
        P(None, "fsdp", None),
        P(None, "fsdp", None),
        P(None, "fsdp"),
        P(None, "fsdp", None),
        P(None, "fsdp", None),
        P(None, "fsdp", None),
        P(None, "fsdp", None),
        P(None, "fsdp"),
        P(None, "fsdp", None),
        P(None, "fsdp", None),
        P(None, "fsdp", None),
        P(None, "fsdp", None),
        P(None, "fsdp"),
        P(None, "fsdp", None),
        P(None, "fsdp", None),
        P(None, "fsdp", None),
        P(None, "fsdp", None),
    )
    body = fast_device if fits_fast(mesh) else general_device
    return jax.shard_map(
        body, mesh=mesh, in_specs=in_specs, out_specs=out_specs, check_vma=False
    )
```

```python
from functools import partial
import math
from types import SimpleNamespace

import jax
import jax.numpy as jnp
from jax import lax
from jax.experimental import pallas as pl
from jax.experimental.pallas import tpu as pltpu
from jax.sharding import PartitionSpec as P

D = 1024
HEADS = 16
HEAD_DIM = 64


BETA_ONE = 0.5
BETA_TWO = 0.75
LEARN_RATE = 0.1
DECAY_RATE = 0.1
CLIP_RATIO = 0.2
ADAM_EPS = 1e-08
ROPE_BASE = 10000.0


def pieces(vector):
    return (
        vector[0:D],
        vector[D : 2 * D],
        vector[2 * D : 3 * D],
        vector[3 * D : 4 * D],
        vector[4 * D : 5 * D],
        vector[5 * D : 6 * D],
        vector[6 * D : 9 * D],
        vector[9 * D :],
    )


def layer_norm(hidden, ln_gain, ln_shift):
    center = hidden - jnp.mean(hidden, axis=-1, keepdims=True)
    spread = jnp.mean(center * center, axis=-1, keepdims=True)
    return center * lax.rsqrt(spread + 1e-06) * ln_gain + ln_shift


def gelu_exact(upward):
    return 0.5 * upward * (1.0 + jax.scipy.special.erf(upward * (1.0 / math.sqrt(2.0))))


def rotary_tables(coords_clip, pair_count):
    pair_index = jnp.arange(pair_count, dtype=jnp.int32)
    side_pairs = pair_count // 3
    time_pairs = pair_count - 2 * side_pairs
    in_time = pair_index < time_pairs
    in_height = jnp.logical_and(pair_index >= time_pairs, pair_index < time_pairs + side_pairs)
    offset = jnp.where(in_time, 0, jnp.where(in_height, time_pairs, time_pairs + side_pairs))
    seg_span = jnp.where(in_time, time_pairs, side_pairs)
    local_rank = (pair_index - offset).astype(jnp.float32)
    frequency = jnp.exp(-math.log(ROPE_BASE) * local_rank / seg_span.astype(jnp.float32))
    positions = coords_clip.astype(jnp.float32)
    chosen = jnp.where(
        in_time[None, :],
        positions[0][:, None],
        jnp.where(in_height[None, :], positions[1][:, None], positions[2][:, None]),
    )
    angles = chosen * frequency[None, :]
    return (jnp.cos(angles), jnp.sin(angles))


def rotate(values_in, cosine, sine_table):
    half_width = values_in.shape[-1] // 2
    first_half = values_in[..., :half_width]
    second_half = values_in[..., half_width:]
    cos_wide = cosine[:, None, :]
    sin_wide = sine_table[:, None, :]
    return jnp.concatenate(
        [
            first_half * cos_wide - second_half * sin_wide,
            first_half * sin_wide + second_half * cos_wide,
        ],
        axis=-1,
    )


def attend_forward(queries, key_rows, value_rows):
    full_len = queries.shape[0]
    block_rows = min(512, full_len)
    score_scale = HEAD_DIM ** (-0.5)
    query_blocks = queries.reshape(
        full_len // block_rows, block_rows, queries.shape[1], queries.shape[2]
    )

    def one_block(query_block):
        scores = (
            jnp.einsum("qhd,khd->hqk", query_block, key_rows, preferred_element_type=jnp.float32)
            * score_scale
        )
        row_max = jnp.max(scores, axis=-1, keepdims=True)
        exponent = jnp.exp(scores - row_max)
        row_total = jnp.sum(exponent, axis=-1, keepdims=True)
        prob_low = (exponent / row_total).astype(jnp.bfloat16)
        mixed_rows = jnp.einsum(
            "hqk,khd->qhd", prob_low, value_rows, preferred_element_type=jnp.float32
        )
        return (mixed_rows, row_max[..., 0] + jnp.log(row_total[..., 0]))

    mixed_rows, log_sums = lax.map(one_block, query_blocks)
    return (mixed_rows.reshape(queries.shape), log_sums)


def attend_backward(queries, key_rows, value_rows, log_sums, head_grad):
    full_len = queries.shape[0]
    block_rows = min(512, full_len)
    score_scale = HEAD_DIM ** (-0.5)
    block_shape = (full_len // block_rows, block_rows, queries.shape[1], queries.shape[2])

    def one_block(carry, block_in):
        key_grad, value_grad = carry
        query_block, grad_block, lse_block = block_in
        scores = (
            jnp.einsum("qhd,khd->hqk", query_block, key_rows, preferred_element_type=jnp.float32)
            * score_scale
        )
        prob_rows = jnp.exp(scores - lse_block[..., None])
        prob_low = prob_rows.astype(jnp.bfloat16)
        value_grad = value_grad + jnp.einsum(
            "hqk,qhd->khd", prob_low, grad_block, preferred_element_type=jnp.float32
        )
        prob_grad = jnp.einsum(
            "qhd,khd->hqk", grad_block, value_rows, preferred_element_type=jnp.float32
        )
        score_grad = prob_rows * (
            prob_grad - jnp.sum(prob_rows * prob_grad, axis=-1, keepdims=True)
        )
        score_low = (score_grad * score_scale).astype(jnp.bfloat16)
        query_grad = jnp.einsum(
            "hqk,khd->qhd", score_low, key_rows, preferred_element_type=jnp.float32
        )
        key_grad = key_grad + jnp.einsum(
            "hqk,qhd->khd", score_low, query_block, preferred_element_type=jnp.float32
        )
        return ((key_grad, value_grad), query_grad)

    zero_heads = jnp.zeros(queries.shape, jnp.float32)
    (key_grad, value_grad), query_grad = lax.scan(
        one_block,
        (zero_heads, zero_heads),
        (queries.reshape(block_shape), head_grad.reshape(block_shape), log_sums),
    )
    return (query_grad.reshape(queries.shape), key_grad, value_grad)


def layer_forward(hidden, cosine, sine_table, weights, seq_parts):
    vector_low, qkv_w, proj_w, up_w, down_w = weights
    gain_one, shift_one, gain_two, shift_two, proj_bias, down_bias, qkv_bias, up_bias = pieces(
        vector_low.astype(jnp.float32)
    )
    row_count = hidden.shape[0]
    local_heads = HEADS // seq_parts
    normed = layer_norm(hidden, gain_one, shift_one).astype(jnp.bfloat16)
    qkv_all = jnp.dot(normed, qkv_w, preferred_element_type=jnp.float32) + qkv_bias
    split_qkv = qkv_all.reshape(row_count, 3, HEADS, HEAD_DIM)
    stacked = jnp.stack(
        [
            rotate(split_qkv[:, 0], cosine, sine_table),
            rotate(split_qkv[:, 1], cosine, sine_table),
            split_qkv[:, 2],
        ],
        axis=1,
    ).astype(jnp.bfloat16)
    packed = stacked.reshape(row_count, 3, seq_parts, local_heads * HEAD_DIM)
    by_heads = lax.all_to_all(packed, "seq", split_axis=2, concat_axis=0, tiled=True)
    full_len = by_heads.shape[0]
    by_heads = by_heads.reshape(full_len, 3, local_heads, HEAD_DIM)
    mixed_rows, log_sums = attend_forward(by_heads[:, 0], by_heads[:, 1], by_heads[:, 2])
    mixed_low = mixed_rows.astype(jnp.bfloat16).reshape(full_len, 1, local_heads * HEAD_DIM)
    by_tokens = lax.all_to_all(mixed_low, "seq", split_axis=0, concat_axis=1, tiled=True).reshape(
        row_count, D
    )
    after_attn = hidden + jnp.dot(by_tokens, proj_w, preferred_element_type=jnp.float32) + proj_bias
    normed_two = layer_norm(after_attn, gain_two, shift_two).astype(jnp.bfloat16)
    upward = jnp.dot(normed_two, up_w, preferred_element_type=jnp.float32) + up_bias
    active = gelu_exact(upward).astype(jnp.bfloat16)
    result = after_attn + jnp.dot(active, down_w, preferred_element_type=jnp.float32) + down_bias
    saved_state = (
        hidden,
        normed,
        by_heads,
        log_sums,
        by_tokens,
        after_attn,
        normed_two,
        upward,
        active,
    )
    return (result, saved_state)


def layer_backward(grad_out, saved_state, weights, cosine, sine_table, seq_parts):
    vector_low, qkv_w, proj_w, up_w, down_w = weights
    gain_one, shift_one, gain_two, shift_two, proj_bias, down_bias, qkv_bias, up_bias = pieces(
        vector_low.astype(jnp.float32)
    )
    hidden, normed, by_heads, log_sums, by_tokens, after_attn, normed_two, upward, active = (
        saved_state
    )
    row_count = hidden.shape[0]
    local_heads = HEADS // seq_parts
    down_bias_grad = jnp.sum(grad_out, axis=0)
    grad_low = grad_out.astype(jnp.bfloat16)
    down_grad = jnp.dot(active.T, grad_low, preferred_element_type=jnp.float32)
    active_grad = jnp.dot(grad_low, down_w.T, preferred_element_type=jnp.float32)
    gelu_value, gelu_pull = jax.vjp(gelu_exact, upward)
    upward_grad = gelu_pull(active_grad)[0]
    up_bias_grad = jnp.sum(upward_grad, axis=0)
    upward_low = upward_grad.astype(jnp.bfloat16)
    up_grad = jnp.dot(normed_two.T, upward_low, preferred_element_type=jnp.float32)
    normed_two_grad = jnp.dot(upward_low, up_w.T, preferred_element_type=jnp.float32)
    norm_value_two, norm_pull_two = jax.vjp(layer_norm, after_attn, gain_two, shift_two)
    attn_in_grad, gain_two_grad, shift_two_grad = norm_pull_two(normed_two_grad)
    after_grad = grad_out + attn_in_grad
    proj_bias_grad = jnp.sum(after_grad, axis=0)
    after_low = after_grad.astype(jnp.bfloat16)
    proj_grad = jnp.dot(by_tokens.T, after_low, preferred_element_type=jnp.float32)
    mixed_grad = jnp.dot(after_low, proj_w.T, preferred_element_type=jnp.float32).astype(
        jnp.bfloat16
    )
    head_grad = lax.all_to_all(
        mixed_grad.reshape(row_count, seq_parts, local_heads * HEAD_DIM),
        "seq",
        split_axis=1,
        concat_axis=0,
        tiled=True,
    )
    full_len = head_grad.shape[0]
    head_grad = head_grad.reshape(full_len, local_heads, HEAD_DIM)
    query_grad, key_grad, value_grad = attend_backward(
        by_heads[:, 0], by_heads[:, 1], by_heads[:, 2], log_sums, head_grad
    )
    stacked_grad = (
        jnp.stack([query_grad, key_grad, value_grad], axis=1)
        .astype(jnp.bfloat16)
        .reshape(full_len, 3, 1, local_heads * HEAD_DIM)
    )
    token_grad = (
        lax.all_to_all(stacked_grad, "seq", split_axis=0, concat_axis=2, tiled=True)
        .reshape(row_count, 3, HEADS, HEAD_DIM)
        .astype(jnp.float32)
    )
    pair_grad_in = token_grad[:, :2].reshape(row_count, 2 * HEADS, HEAD_DIM)
    rotated_value, rotate_pull = jax.vjp(
        partial(rotate, cosine=cosine, sine_table=sine_table), pair_grad_in
    )
    pair_grad = rotate_pull(pair_grad_in)[0].reshape(row_count, 2, HEADS, HEAD_DIM)
    qkv_grad = jnp.concatenate([pair_grad, token_grad[:, 2:]], axis=1).reshape(row_count, 3 * D)
    qkv_bias_grad = jnp.sum(qkv_grad, axis=0)
    qkv_low = qkv_grad.astype(jnp.bfloat16)
    qkv_w_grad = jnp.dot(normed.T, qkv_low, preferred_element_type=jnp.float32)
    normed_grad = jnp.dot(qkv_low, qkv_w.T, preferred_element_type=jnp.float32)
    norm_value_one, norm_pull_one = jax.vjp(layer_norm, hidden, gain_one, shift_one)
    in_grad, gain_one_grad, shift_one_grad = norm_pull_one(normed_grad)
    input_grad = after_grad + in_grad
    vector_grad = jnp.concatenate(
        [
            gain_one_grad,
            shift_one_grad,
            gain_two_grad,
            shift_two_grad,
            proj_bias_grad,
            down_bias_grad,
            qkv_bias_grad,
            up_bias_grad,
        ]
    )
    return (input_grad, (vector_grad, qkv_w_grad, proj_grad, up_grad, down_grad))


def adam_update(master, grad_item, first_old, second_old, factor):
    clipped = grad_item * factor
    first_new = BETA_ONE * first_old + (1.0 - BETA_ONE) * clipped
    second_new = BETA_TWO * second_old + (1.0 - BETA_TWO) * clipped * clipped
    updated = master - LEARN_RATE * (
        first_new / (jnp.sqrt(second_new) + ADAM_EPS) + DECAY_RATE * master
    )
    return (first_new, second_new, updated)


def general_device(
    clip_tokens,
    patch_coords,
    out_cotangent,
    vector_params,
    qkv_weight,
    proj_weight,
    up_weight,
    down_weight,
    first_vector,
    first_qkv,
    first_proj,
    first_up,
    first_down,
    second_vector,
    second_qkv,
    second_proj,
    second_up,
    second_down,
):
    masters = (vector_params, qkv_weight, proj_weight, up_weight, down_weight)
    firsts = (first_vector, first_qkv, first_proj, first_up, first_down)
    seconds = (second_vector, second_qkv, second_proj, second_up, second_down)
    lowered = tuple((master.astype(jnp.bfloat16) for master in masters))
    layer_count = vector_params.shape[0]
    batch_local = clip_tokens.shape[0]
    seq_parts = lax.axis_size("seq")
    fsdp_parts = lax.axis_size("fsdp")
    grad_accum = tuple(
        (
            jnp.zeros((layer_count, master.shape[1] * fsdp_parts) + master.shape[2:], jnp.float32)
            for master in masters
        )
    )
    output_rows = []
    input_rows = []
    for batch_idx in range(batch_local):
        cosine, sine_table = rotary_tables(patch_coords[:, batch_idx], HEAD_DIM // 2)
        hidden = clip_tokens[batch_idx]
        saved_layers = []
        for layer_idx in range(layer_count):
            weights = (
                lax.all_gather(lowered[0][layer_idx], "fsdp", axis=0, tiled=True),
                lax.all_gather(lowered[1][layer_idx], "fsdp", axis=0, tiled=True),
                lax.all_gather(lowered[2][layer_idx], "fsdp", axis=0, tiled=True),
                lax.all_gather(lowered[3][layer_idx], "fsdp", axis=0, tiled=True),
                lax.all_gather(lowered[4][layer_idx], "fsdp", axis=0, tiled=True),
            )
            hidden, saved_state = layer_forward(hidden, cosine, sine_table, weights, seq_parts)
            saved_layers.append(saved_state)
        output_rows.append(hidden)
        grad_rows = out_cotangent[batch_idx]
        for layer_idx in reversed(range(layer_count)):
            weights = (
                lax.all_gather(lowered[0][layer_idx], "fsdp", axis=0, tiled=True),
                lax.all_gather(lowered[1][layer_idx], "fsdp", axis=0, tiled=True),
                lax.all_gather(lowered[2][layer_idx], "fsdp", axis=0, tiled=True),
                lax.all_gather(lowered[3][layer_idx], "fsdp", axis=0, tiled=True),
                lax.all_gather(lowered[4][layer_idx], "fsdp", axis=0, tiled=True),
            )
            grad_rows, layer_grads = layer_backward(
                grad_rows, saved_layers[layer_idx], weights, cosine, sine_table, seq_parts
            )
            grad_accum = tuple(
                (
                    accum_item.at[layer_idx].add(grad_item)
                    for accum_item, grad_item in zip(grad_accum, layer_grads)
                )
            )
        input_rows.append(grad_rows)
    shard_sums = (
        lax.psum_scatter(grad_accum[0], "fsdp", scatter_dimension=1, tiled=True),
        lax.psum_scatter(grad_accum[1], "fsdp", scatter_dimension=1, tiled=True),
        lax.psum_scatter(grad_accum[2], "fsdp", scatter_dimension=1, tiled=True),
        lax.psum_scatter(grad_accum[3], "fsdp", scatter_dimension=1, tiled=True),
        lax.psum_scatter(grad_accum[4], "fsdp", scatter_dimension=1, tiled=True),
    )
    seq_sums = lax.psum(
        (shard_sums[0], shard_sums[1], shard_sums[2], shard_sums[3], shard_sums[4]), "seq"
    )
    clip_count = batch_local * fsdp_parts
    grad_shards = tuple((sum_item / clip_count for sum_item in seq_sums))
    local_squares = sum((jnp.sum(grad_item * grad_item) for grad_item in grad_shards))
    squares_total = lax.psum(local_squares, "fsdp")
    norm_value = jnp.sqrt(squares_total)
    param_count = sum((master.size for master in masters)) * fsdp_parts
    factor = jnp.minimum(1.0, CLIP_RATIO * math.sqrt(float(param_count)) / (norm_value + 1e-06))
    updates = [
        adam_update(master, grad_item, first_old, second_old, factor)
        for master, grad_item, first_old, second_old in zip(masters, grad_shards, firsts, seconds)
    ]
    return (
        jnp.stack(output_rows),
        jnp.stack(input_rows),
        grad_shards[0],
        grad_shards[1],
        grad_shards[2],
        grad_shards[3],
        grad_shards[4],
        norm_value.reshape(1),
        updates[0][0],
        updates[1][0],
        updates[2][0],
        updates[3][0],
        updates[4][0],
        updates[0][1],
        updates[1][1],
        updates[2][1],
        updates[3][1],
        updates[4][1],
        updates[0][2],
        updates[1][2],
        updates[2][2],
        updates[3][2],
        updates[4][2],
        updates[0][2].astype(jnp.bfloat16),
        updates[1][2].astype(jnp.bfloat16),
        updates[2][2].astype(jnp.bfloat16),
        updates[3][2].astype(jnp.bfloat16),
        updates[4][2].astype(jnp.bfloat16),
    )


ROWS_Q = 256
ADD_ROWS = 32
PAIR = 2 * HEAD_DIM
BF = jnp.bfloat16
F32 = jnp.float32
VMEM_LIMIT = 56 * 1024 * 1024


def fits_fast(mesh):
    return dict(mesh.shape) == {"seq": 4, "fsdp": 8}


def swap_core(item):
    parts = lax.axis_size("fsdp")
    return lax.ppermute(item, "fsdp", [(idx, idx ^ 1) for idx in range(parts)])


def send_up(item):
    parts = lax.axis_size("fsdp")
    return lax.ppermute(item, "fsdp", [(idx, (idx + 2) % parts) for idx in range(parts)])


def swap_seq(item, mask):
    parts = lax.axis_size("seq")
    return lax.ppermute(item, "seq", [(idx, idx ^ mask) for idx in range(parts)])


def pick(item, index, axis=0):
    return lax.dynamic_index_in_dim(item, index, axis, keepdims=False)


def swap_halves(item):
    lane = lax.broadcasted_iota(jnp.int32, item.shape, 1)
    half = HEAD_DIM // 2
    width = item.shape[1]
    ahead = pltpu.roll(item, width - half, 1)
    behind = pltpu.roll(item, half, 1)
    return jnp.where(lane % HEAD_DIM < half, ahead, behind)


NT = (((1,), (1,)), ((), ()))


def head_mask(item, head):
    lane = lax.broadcasted_iota(jnp.int32, item.shape, 1)
    return jnp.where(lane // HEAD_DIM == head, item, jnp.zeros_like(item))


class Places:
    def __init__(self):
        shard, seq = lax.axis_index("fsdp"), lax.axis_index("seq")
        parts = lax.axis_size("fsdp")
        self.ring = parts // 2
        self.seq = seq
        self.chip, self.core = shard // 2, lax.rem(shard, 2)
        self.at_x, self.at_y = lax.rem(seq, 2), seq // 2
        self.near_x = 2 * self.at_y + 1 - self.at_x
        self.near_y = 2 * (1 - self.at_y) + self.at_x
        self.other = {"fsdp": shard + 1 - 2 * self.core}
        self.up = {"fsdp": lax.rem(shard + 2, parts)}
        self.down = {"fsdp": lax.rem(shard + parts - 2, parts)}
        self.over_x = {"seq": self.near_x}
        self.over_y = {"seq": self.near_y}

    def back(self, hops):
        return lax.rem(self.chip - hops + self.ring, self.ring)


def remote(src, dst, send, recv, target):
    return pltpu.make_async_remote_copy(
        src_ref=src,
        dst_ref=dst,
        send_sem=send,
        recv_sem=recv,
        device_id=target,
        device_id_type=pl.DeviceIdType.MESH,
    )


def greet(targets, waits):
    barrier = pltpu.get_barrier_semaphore()
    for target in targets:
        pl.semaphore_signal(barrier, inc=1, device_id=target, device_id_type=pl.DeviceIdType.MESH)
    pl.semaphore_wait(barrier, waits)


def aligned(start, size, unit=None):
    return pl.ds(pl.multiple_of(start, unit or size), size)


def adam_kernel(
    kinds, ring, count, core_ref, factor_ref, *refs
):
    n_grads = len(refs) - 8
    grads = refs[:n_grads]
    master, first, second, grad_out, first_out, second_out, new_out, copy_out = refs[n_grads:]
    layer = pl.program_id(0)
    factor = factor_ref[0]
    scale = 1.0 / count
    columns = master.shape[2]
    per_layer = n_grads // 2
    width = columns // (kinds * ring * 2) if per_layer == 2 else 512

    def update(at, total):
        grad = total.astype(F32) * scale
        first_new, second_new, new = [], [], []
        first_new, second_new, new = adam_update(
            master[0, :, at], grad, first[0, :, at], second[0, :, at], factor
        )
        grad_out[0, :, at] = grad
        first_out[0, :, at] = first_new
        second_out[0, :, at] = second_new
        new_out[0, :, at] = new
        copy_out[0, :, at] = new.astype(BF)

    def choose(which, at):
        values = [grads[idx * per_layer + which][:, at] for idx in range(2)]
        return jnp.where(layer == 0, values[0], values[1])

    if per_layer == 1:
        for start in range(0, columns, width):
            update(slice(start, start + width), choose(0, slice(start, start + width)))
        return
    core = core_ref[0]
    for pair in range(ring):
        for kind in range(kinds):
            source = (pair * kinds + kind) * width
            mine, arrive = [choose(which, slice(source, source + width)) for which in range(2)]
            for which in range(2):
                start = (kind * ring * 2 + 2 * pair + which) * width
                update(slice(start, start + width), jnp.where(core == which, mine, arrive))


def adam_matrix(grads, master, first, second, factor, core, kinds, count):
    layers, rows, columns = master.shape
    ring = lax.axis_size("fsdp") // 2
    block = 32 if columns > 1024 else 64
    steps = rows // block
    per_layer = len(grads) // layers

    def grad_spec(idx):
        layer, which = divmod(idx, per_layer)
        lift = steps if per_layer == 2 and which == 0 else 0

        def where(at_layer, step, core_ref, layer=layer, lift=lift):
            held = 0 if layer > 0 else steps - 1
            row = jnp.where(at_layer == layer, step, held)
            return (row + lift * core_ref[0], 0)

        return pl.BlockSpec((block, grads[idx].shape[1]), where)

    whole = pl.BlockSpec((1, block, columns), lambda layer, step, core_ref: (layer, step, 0))
    shape = jax.ShapeDtypeStruct(master.shape, F32)
    return pl.pallas_call(
        partial(adam_kernel, kinds, ring, count),
        grid_spec=pltpu.PrefetchScalarGridSpec(
            num_scalar_prefetch=1,
            grid=(layers, steps),
            in_specs=[pl.BlockSpec(memory_space=pltpu.SMEM)]
            + [grad_spec(idx) for idx in range(len(grads))]
            + [whole] * 3,
            out_specs=[whole] * 5,
        ),
        out_shape=[shape] * 4 + [jax.ShapeDtypeStruct(master.shape, BF)],
        compiler_params=pltpu.CompilerParams(vmem_limit_bytes=VMEM_LIMIT),
        cost_estimate=pl.CostEstimate(
            flops=20 * master.size, bytes_accessed=32 * master.size, transcendentals=master.size
        ),
        name="update",
    )(core.reshape(1).astype(jnp.int32), factor.reshape(1), *grads, master, first, second)


def norm_parts(hidden):
    center = hidden - jnp.mean(hidden, axis=-1, keepdims=True)
    spread = jnp.mean(center * center, axis=-1, keepdims=True)
    inverse = lax.rsqrt(spread + 1e-06)
    return center * inverse, inverse


def gelu_and_slope(upward):
    erf_part = 0.5 * (1.0 + lax.erf(upward * (1.0 / math.sqrt(2.0))))
    density = jnp.exp(-0.5 * upward * upward) * (1.0 / math.sqrt(2.0 * math.pi))
    return upward * erf_part, erf_part + upward * density


def dot(left, right):
    return jnp.dot(left, right, preferred_element_type=F32)


def dot_nt(left, right):
    return lax.dot_general(left, right, NT, preferred_element_type=F32)


def dot_tn(left, right):
    return lax.dot_general(left, right, (((0,), (0,)), ((), ())), preferred_element_type=F32)


def rotation_tables(packed):
    lane = lax.broadcasted_iota(jnp.int32, packed.shape, 1)
    first = lane % HEAD_DIM < HEAD_DIM // 2
    turned = pltpu.roll(packed, HEAD_DIM // 2, 1)
    return jnp.where(first, packed, turned), jnp.where(first, -turned, packed)


def each_block(count, body):
    @pl.loop(0, count)
    def _(step):
        body(aligned(step * ROWS_Q, ROWS_Q))


class Forward:
    def __init__(self, at, refs, layers):
        self.at, self.refs, self.layers = at, refs, layers
        self.blocks = refs.res.shape[0] // ROWS_Q
        self.pairs = refs.mixed.shape[1] // PAIR
        self.saves, self.slot = [], 0
        self.mixed_copies, self.part_copies = {}, {}

    def save(self, src, dst):
        copy = pltpu.make_async_copy(src, dst, self.refs.save_sem.at[self.slot])
        self.slot += 1
        copy.start()
        self.saves.append(copy)
        return copy

    def settle(self):
        for copy in self.saves:
            copy.wait()
        self.saves = []

    def bring(self, pairs):
        copies = []
        for src, dst in pairs:
            copies.append(pltpu.make_async_copy(src, dst, self.refs.save_sem.at[self.slot]))
            self.slot += 1
        for copy in copies:
            copy.start()
        for copy in copies:
            copy.wait()

    def vec(self, layer, row, width):
        return self.refs.vecs[layer, row : row + 1, 0:width]

    def unpack_vectors(self):
        refs, at = self.refs, self.at
        ring = at.ring
        per_shard = refs.vec_rows
        for layer in range(self.layers):
            places = [(row, row // 8, row % 8) for row in range(48)]
            for pair in range(ring):
                for kind in range(3):
                    places.append((48 + kind * 8 + 2 * pair + at.core, 6, pair * 3 + kind))
                for part in range(4):
                    places.append((72 + (2 * pair + at.core) * 4 + part, 7, pair * 4 + part))
            for source, row, block in places:
                shard, entry = source // per_shard, layer * per_shard + source % per_shard
                if not isinstance(source, int):
                    shard = lax.div(source, per_shard)
                    entry = layer * per_shard + lax.rem(source, per_shard)
                refs.vecs[layer, row : row + 1, block * 128 : (block + 1) * 128] = refs.vec_out[
                    shard, pl.ds(entry, 1), :
                ]

    def normed(self, rows, layer, first):
        hidden = self.refs.res[rows, :]
        scaled, _ = norm_parts(hidden)
        width = hidden.shape[1]
        return (scaled * self.vec(layer, first, width) + self.vec(layer, first + 1, width)).astype(BF)

    def qkv(self, layer, weight):
        refs = self.refs
        width = weight.shape[1]
        self.settle()
        self.bring([(weight, refs.w_one.at[:, pl.ds(0, width)])])

        def body(rows):
            normed = self.normed(rows, layer, 0)
            refs.norm[rows, :] = normed
            for pair in range(self.pairs):
                cols = slice(pair * 3 * PAIR, (pair + 1) * 3 * PAIR)
                block = dot(normed, refs.w_one[:, cols]) + refs.vecs[layer, 6:7, cols]
                cosine, sine = rotation_tables(refs.tables[rows, :])
                for kind in range(3):
                    part = block[:, kind * PAIR : (kind + 1) * PAIR]
                    if kind < 2:
                        part = part * cosine + swap_halves(part) * sine
                    start = pair * 3 * PAIR + kind * PAIR
                    refs.low[rows, start : start + PAIR] = part.astype(BF)

        each_block(self.blocks, body)
        self.save(refs.norm, refs.normed_out[layer])
        self.save(refs.low, refs.low_out[layer])

    def attend(self, layer, pair):
        refs = self.refs
        base = pair * 3 * PAIR
        key_rows = refs.low[:, base + PAIR : base + 2 * PAIR]
        for head in range(2):
            refs.keys[head] = head_mask(key_rows, head)
        refs.values_t[...] = refs.low[:, base + 2 * PAIR : base + 3 * PAIR].astype(F32).T.astype(BF)

        def body(rows):
            block = refs.low[rows, base : base + PAIR] * jnp.asarray(HEAD_DIM**-0.5, BF)
            outs = []
            for head in range(2):
                scores = lax.dot_general(refs.keys[head], block, NT, preferred_element_type=F32)
                top = jnp.max(scores, axis=0, keepdims=True)
                exponent = jnp.exp(scores - top)
                total = jnp.sum(exponent, axis=0, keepdims=True)
                refs.lse_out[layer, pair, head : head + 1, rows] = top + jnp.log(total)
                probs = (exponent * (1.0 / total)).astype(BF)
                outs.append(dot(refs.values_t[head * HEAD_DIM : (head + 1) * HEAD_DIM], probs))
            refs.mixed[rows, pair * PAIR : (pair + 1) * PAIR] = (
                jnp.concatenate(outs, axis=0).T.astype(BF)
            )

        each_block(self.blocks, body)
        slot = layer * (self.pairs + 2) + pair
        cols = pl.ds(pair * PAIR, PAIR)
        copy = remote(
            refs.mixed.at[:, cols],
            refs.mixed_other.at[:, cols],
            refs.x_send.at[slot],
            refs.x_recv.at[slot],
            self.at.other,
        )
        copy.start()
        self.mixed_copies[layer, pair] = copy

    def project(self, layer, own, other):
        refs = self.refs
        half = own.shape[0]
        self.bring(
            [
                (own, refs.w_two.at[pl.ds(0, half), :]),
                (other, refs.w_two.at[pl.ds(half, half), :]),
            ]
        )
        self.settle()
        for pair in range(self.pairs):
            self.mixed_copies[layer, pair].wait()
        width = refs.res.shape[1]

        def body(rows):
            total = dot(refs.mixed[rows, :], refs.w_two[0:half, :])
            total = total + dot(refs.mixed_other[rows, :], refs.w_two[half : 2 * half, :])
            refs.res[rows, :] = refs.res[rows, :] + total + self.vec(layer, 4, width)
            refs.norm[rows, :] = self.normed(rows, layer, 2)

        each_block(self.blocks, body)
        self.save(refs.mixed, refs.mixed_out[layer])
        self.save(refs.res, refs.after_out[layer])
        self.save(refs.norm, refs.normed_two_out[layer])

    def hidden_units(self, layer, half, up_weight, down_weight):
        refs = self.refs
        if half == 0:
            self.settle()
            self.bring([(up_weight, refs.w_one), (down_weight, refs.w_two)])
        width = refs.res.shape[1]
        tiles = refs.w_one.shape[1] // 512
        blocks = self.blocks // 2

        @pl.loop(half * blocks, (half + 1) * blocks)
        def _(step):
            rows = aligned(step * ROWS_Q, ROWS_Q)

            @pl.loop(0, tiles)
            def _(tile):
                cols = aligned(tile * 512, 512)
                upward = dot(refs.norm[rows, :], refs.w_one[:, cols]) + refs.vecs[layer, 7:8, cols]
                active, slope = gelu_and_slope(upward)
                refs.act[rows, cols] = active.astype(BF)
                refs.slope[rows, cols] = slope.astype(BF)

            part = dot(refs.act[rows, :], refs.w_two[...])
            refs.res[rows, :] = refs.res[rows, :] + part + self.vec(layer, 5, width)
            refs.part[rows, :] = part.astype(BF)

        rows = pl.ds(half * blocks * ROWS_Q, blocks * ROWS_Q)
        slot = layer * (self.pairs + 2) + self.pairs + half
        copy = remote(
            refs.part.at[rows, :],
            refs.part_other.at[rows, :],
            refs.x_send.at[slot],
            refs.x_recv.at[slot],
            self.at.other,
        )
        copy.start()
        self.part_copies[layer, half] = copy
        if half == 1:
            self.save(refs.act, refs.active_out[layer])
            self.save(refs.slope, refs.slope_out[layer])

    def join(self, layer):
        refs = self.refs
        for half in range(2):
            self.part_copies[layer, half].wait()

        def body(rows):
            refs.res[rows, :] = refs.res[rows, :] + refs.part_other[rows, :].astype(F32)

        each_block(self.blocks, body)
        self.save(refs.res, refs.result_out[layer])


WEIGHTS = ("qkv", "proj", "up", "down")


def forward_kernel(names, layers, vec_rows, *operands):
    refs = SimpleNamespace(**dict(zip(names, operands)))
    for name in (*WEIGHTS, "proj_two", "normed", "low", "mixed", "after", "normed_two", "active", "slope", "result"):
        label = name + "_out"
        setattr(refs, label, [getattr(refs, label + str(layer)) for layer in range(layers)])
    refs.vec_rows = vec_rows
    at = Places()
    ring, seq, chip, core = at.ring, at.seq, at.chip, at.core
    full = {name: getattr(refs, name + "_full") for name in WEIGHTS}
    source = {name: getattr(refs, name + "_in") for name in WEIGHTS}
    slabs = {name: getattr(refs, name + "_slab") for name in WEIGHTS}
    outs = {name: getattr(refs, name + "_out") for name in WEIGHTS}
    items = [(name, layer) for layer in range(layers) for name in WEIGHTS]
    loads = {}

    def start_load(name, layer):
        copy = pltpu.make_async_copy(
            source[name].at[layer], full[name], refs.l_in.at[items.index((name, layer))]
        )
        copy.start()
        loads[name, layer] = copy

    for name in WEIGHTS:
        start_load(name, 0)
    barrier = pltpu.get_barrier_semaphore()
    for target in (at.other, at.up, at.down):
        pl.semaphore_signal(barrier, inc=1, device_id=target, device_id_type=pl.DeviceIdType.MESH)
    for step in range(1, 4):
        for half in range(2):
            pl.semaphore_signal(
                barrier,
                inc=1,
                device_id={"fsdp": 2 * chip + half, "seq": seq ^ step},
                device_id_type=pl.DeviceIdType.MESH,
            )
    pl.semaphore_wait(barrier, 9)

    length = refs.clip_in.shape[1]
    token_core = seq // 2
    token_rows = aligned(seq * length, length)
    stays = core == token_core

    class Move:
        def __init__(self, base, pairs):
            self.base, self.pairs, self.copies = base, pairs, []

        def start(self):
            for turn in range(2):
                target = {"seq": 2 * core + turn, "fsdp": 2 * chip + token_core}
                away = jnp.logical_not(jnp.logical_and(stays, lax.rem(seq, 2) == turn))
                copies = [
                    remote(
                        src.at[turn],
                        place(seq),
                        refs.m_send.at[self.base + 2 * turn + idx],
                        refs.m_recv.at[self.base + 2 * lax.rem(seq, 2) + idx],
                        target,
                    )
                    for idx, (src, place) in enumerate(self.pairs)
                ]
                self.copies.append((away, copies))

                @pl.when(away)
                def _(copies=copies):
                    for copy in copies:
                        copy.start()

            @pl.when(stays)
            def _():
                for idx, (src, place) in enumerate(self.pairs):
                    bounce = refs.clip_slab if idx == 0 else refs.table_slab
                    sem = refs.m_load.at[self.base // 6 * 2 + idx]
                    load = pltpu.make_async_copy(src.at[lax.rem(seq, 2)], bounce, sem)
                    load.start()
                    load.wait()
                    store = pltpu.make_async_copy(bounce, place(seq), sem)
                    store.start()
                    store.wait()

        def swap(self):
            for part in range(2):
                came = jnp.logical_not(jnp.logical_and(stays, lax.rem(seq, 2) == part))

                @pl.when(came)
                def _(part=part):
                    for idx, (src, place) in enumerate(self.pairs):
                        remote(
                            src.at[0],
                            place(2 * core + part),
                            refs.m_send.at[self.base],
                            refs.m_recv.at[self.base + 2 * part + idx],
                            at.other,
                        ).wait_recv()

            self.swaps = []
            for idx, (src, place) in enumerate(self.pairs):
                for part in range(2):
                    slot = 24 + self.base // 6 * 4 + 2 * idx + part
                    ref = place(2 * core + part)
                    self.swaps.append(
                        remote(ref, ref, refs.m_send.at[slot], refs.m_recv.at[slot], at.other)
                    )
            for copy in self.swaps:
                copy.start()

        def arrived(self):
            for copy in self.swaps:
                copy.wait_recv()

        def drain(self):
            for copy in self.swaps:
                copy.wait_send()
            for away, copies in self.copies:

                @pl.when(away)
                def _(copies=copies):
                    for copy in copies:
                        copy.wait_send()

    def chunk_of(ref):
        return lambda number: ref.at[aligned(number * length, length), :]

    tokens = Move(0, [(refs.clip_in, chunk_of(refs.clip_out)), (refs.table_in, chunk_of(refs.table_out))])
    cotangents = Move(6, [(refs.cot_in, chunk_of(refs.cot_out))])
    tokens.start()

    refs.vec_out[2 * chip + core] = refs.vec_in[...]
    vec_swap = remote(
        refs.vec_in, refs.vec_out.at[2 * chip + core], refs.m_send.at[16], refs.m_recv.at[16], at.other
    )
    vec_swap.start()
    vec_copies = [vec_swap]

    def vec_hop(hop):
        vec_copies[-1].wait_recv()
        ref = refs.vec_out.at[pl.ds(2 * at.back(hop), 2)]
        slot = 17 + hop
        copy = remote(ref, ref, refs.m_send.at[slot], refs.m_recv.at[slot], at.up)
        copy.start()
        vec_copies.append(copy)

    def place(name, layer, chip_at, part):
        slab = slabs[name].shape[1]
        if part is None:
            return outs[name][layer].at[aligned(chip_at * slab, slab), :]
        size = slab // 4
        return outs[name][layer].at[aligned(chip_at * slab + part * size, size), :]

    swaps, prepared, stores = {}, [], []

    def prepare():
        if len(prepared) == len(items):
            return
        idx = len(prepared)
        name, layer = items[idx]
        prepared.append(name)
        slab = slabs[name]
        loads[name, layer].wait()
        swaps[idx] = None
        if name in ("down", "proj"):
            slab[layer] = full[name][...].astype(BF)
        else:
            away, kinds = (refs.qkv_away, 3) if name == "qkv" else (refs.up_away, 1)
            half, columns = full[name].shape
            width = columns // (kinds * 2 * ring)
            rows = aligned(core * half, half)
            for pair in range(ring):
                for kind in range(kinds):
                    cols = slice((pair * kinds + kind) * width, (pair * kinds + kind + 1) * width)
                    for mine in (True, False):
                        which = core if mine else 1 - core
                        start = (kind * 2 * ring + 2 * pair + which) * width
                        block = full[name][:, aligned(start, width)].astype(BF)
                        if mine:
                            slab[layer, rows, cols] = block
                        else:
                            away[layer, :, cols] = block
            swaps[idx] = remote(
                away.at[layer],
                slab.at[layer, rows, :],
                refs.c_send.at[idx],
                refs.c_recv.at[idx],
                at.other,
            )
            swaps[idx].start()
        if layer + 1 < layers:
            start_load(name, layer + 1)

    hops = ring - 1
    order = []
    for first in range(0, len(items), 2):
        for hop in range(hops):
            order += [(first, hop), (first + 1, hop)]
    z_copies, plane, far, proj_swaps = {}, {}, {}, {}

    def begin(idx):
        name, layer = items[idx]
        if swaps[idx] is not None:
            swaps[idx].wait_recv()
        store = pltpu.make_async_copy(
            slabs[name].at[layer], place(name, layer, chip, None), refs.l_out.at[idx]
        )
        store.start()
        stores.append(store)

    def z_copy(idx, hop):
        name, layer = items[idx]
        part = None if name == "proj" else seq
        target = place(name, layer, at.back(hop), part)
        from_ref = target
        if hop == 0:
            from_ref = slabs[name].at[layer]
            if part is not None:
                size = slabs[name].shape[1] // 4
                from_ref = slabs[name].at[layer, aligned(seq * size, size), :]
        slot = idx * hops + hop
        copy = remote(from_ref, target, refs.z_send.at[slot], refs.z_recv.at[slot], at.up)
        copy.start()
        z_copies[idx, hop] = copy

    def plane_copies(idx, hop):
        name, layer = items[idx]
        ref = place(name, layer, at.back(hop + 1), seq)
        slot = 2 * (idx * hops + hop)
        plane[idx, hop] = [
            remote(ref, ref, refs.p_send.at[slot], refs.p_recv.at[slot], at.over_x),
            remote(ref, ref, refs.p_send.at[slot + 1], refs.p_recv.at[slot + 1], at.over_y),
        ]
        for copy in plane[idx, hop]:
            copy.start()

    def far_copies(idx, hop):
        name, layer = items[idx]
        slot = 2 * (idx * hops + hop)
        size = slabs[name].shape[1] // 4
        half = size // 2
        base = at.back(hop + 1) * 4 * size
        for copy in plane[idx, hop]:
            copy.wait_recv()
        made = []
        for turn, (origin, target) in enumerate(((at.near_y, at.over_x), (at.near_x, at.over_y))):
            ref = outs[name][layer].at[aligned(base + origin * size + turn * half, half), :]
            made.append(
                remote(ref, ref, refs.d_send.at[slot + turn], refs.d_recv.at[slot + turn], target)
            )
        far[idx, hop] = made
        for copy in made:
            copy.start()

    pending = []

    def flush(keep):
        while len(pending) > keep:
            far_copies(*pending.pop(0))

    def event(number):
        idx, hop = order[number]
        z_copies[idx, hop].wait_recv()
        if hop + 1 < hops:
            z_copy(idx, hop + 1)
        elif idx + 2 < len(items):
            begin(idx + 2)
            z_copy(idx + 2, 0)
        name, layer = items[idx]
        if name == "proj":
            if hop + 1 == hops:
                stores[idx].wait()
                slot = len(items) + layer
                proj_swaps[layer] = remote(
                    outs["proj"][layer],
                    refs.proj_two_out[layer],
                    refs.c_send.at[slot],
                    refs.c_recv.at[slot],
                    at.other,
                )
                proj_swaps[layer].start()
        else:
            plane_copies(idx, hop)
            pending.append((idx, hop))
            flush(1)
        prepare()

    def complete(name, layer):
        idx = items.index((name, layer))
        if name == "proj":
            proj_swaps[layer].wait_recv()
            return
        stores[idx].wait()
        flush(0)
        for hop in range(hops):
            for copy in far[idx, hop]:
                copy.wait_recv()

    work = Forward(at, refs, layers)

    def take_tokens():
        tokens.arrived()
        vec_copies[-1].wait_recv()
        work.bring([(refs.clip_out, refs.res), (refs.table_out, refs.tables)])
        work.unpack_vectors()

    def qkv(layer):
        complete("qkv", layer)
        work.qkv(layer, outs["qkv"][layer])

    def project(layer):
        complete("proj", layer)
        work.project(layer, outs["proj"][layer], refs.proj_two_out[layer])

    def hidden_units(layer, half):
        if half == 0:
            complete("up", layer)
            complete("down", layer)
        work.hidden_units(layer, half, outs["up"][layer], outs["down"][layer])

    prepare()
    prepare()
    begin(0)
    z_copy(0, 0)
    begin(1)
    z_copy(1, 0)
    prepare()
    prepare()
    per_layer = 4 * hops
    chunks = []
    for layer in range(layers):
        first = layer * per_layer + 2 * hops
        if layer == 0:
            chunks.append((first, take_tokens))
        chunks.append((first + 1, partial(qkv, layer)))
        for pair in range(work.pairs):
            chunks.append((first + 1 + pair, partial(work.attend, layer, pair)))
        chunks.append((first + 5, partial(project, layer)))
        chunks.append((first + 7, partial(hidden_units, layer, 0)))
        chunks.append((first + 8, partial(hidden_units, layer, 1)))
        chunks.append((first + 9, partial(work.join, layer)))
    for number in range(len(order)):
        while chunks and chunks[0][0] <= number:
            chunks.pop(0)[1]()
        if number == 2:
            tokens.swap()
        if 3 <= number < 3 + hops:
            vec_hop(number - 3)
        if number == per_layer:
            cotangents.start()
        if number == per_layer + 6:
            cotangents.swap()
        event(number)
    flush(0)
    for _, chunk in chunks:
        chunk()

    work.settle()
    cotangents.arrived()
    for made in plane.values():
        for copy in made:
            copy.wait_send()
    for made in far.values():
        for copy in made:
            copy.wait_send()
    for copy in z_copies.values():
        copy.wait_send()
    for copy in swaps.values():
        if copy is not None:
            copy.wait_send()
    for copy in proj_swaps.values():
        copy.wait_send()
    for copy in vec_copies:
        copy.wait_send()
    tokens.drain()
    cotangents.drain()


def forward(qkv, up, down, proj, clips, cots, tables, vectors, vec_rows):
    layers, rows, width = proj.shape
    parts = lax.axis_size("fsdp")
    ring = parts // 2
    count, hops = 4 * layers, ring - 1
    length = 4 * clips.shape[1]
    down_rows = down.shape[1]
    qkv_half, up_half = qkv.shape[2] // 2, up.shape[2] // 2
    pairs = qkv_half // (3 * PAIR)
    inputs = {
        "qkv_in": qkv, "up_in": up, "down_in": down, "proj_in": proj, "clip_in": clips, "cot_in": cots,
        "table_in": tables, "vec_in": vectors,
    }
    outputs = {}
    for layer in range(layers):
        for name, shape, dtype in (
            ("qkv", (parts * rows, qkv_half), BF),
            ("up", (parts * rows, up_half), BF),
            ("down", (ring * down_rows, width), BF),
            ("proj", (ring * rows, width), BF),
            ("proj_two", (ring * rows, width), BF),
            ("normed", (length, width), BF),
            ("low", (length, qkv_half), BF),
            ("mixed", (length, pairs * PAIR), BF),
            ("after", (length, width), F32),
            ("normed_two", (length, width), BF),
            ("active", (length, up_half), BF),
            ("slope", (length, up_half), BF),
            ("result", (length, width), F32),
        ):
            outputs[name + "_out" + str(layer)] = (shape, dtype)
    outputs["clip_out"] = ((length, width), F32)
    outputs["cot_out"] = ((length, width), F32)
    outputs["table_out"] = ((length, PAIR), F32)
    outputs["vec_out"] = ((parts,) + vectors.shape, F32)
    outputs["vecs"] = ((layers, 8, up_half), F32)
    outputs["lse_out"] = ((layers, pairs, 8, length), F32)
    in_vmem = ("vec_in", "vec_out", "vecs", "lse_out")
    anywhere = pl.BlockSpec(memory_space=pl.ANY)
    vmem = pl.BlockSpec(memory_space=pltpu.VMEM)
    dma = pltpu.SemaphoreType.DMA
    scratch = {
        "qkv_full": pltpu.VMEM(qkv.shape[1:], F32),
        "up_full": pltpu.VMEM(up.shape[1:], F32),
        "down_full": pltpu.VMEM(down.shape[1:], F32),
        "proj_full": pltpu.VMEM(proj.shape[1:], F32),
        "qkv_away": pltpu.VMEM((layers, rows, qkv_half), BF),
        "up_away": pltpu.VMEM((layers, rows, up_half), BF),
        "qkv_slab": pltpu.VMEM((layers, 2 * rows, qkv_half), BF),
        "up_slab": pltpu.VMEM((layers, 2 * rows, up_half), BF),
        "down_slab": pltpu.VMEM((layers, down_rows, width), BF),
        "proj_slab": pltpu.VMEM((layers, rows, width), BF),
        "clip_slab": pltpu.VMEM(clips.shape[1:], F32),
        "table_slab": pltpu.VMEM(tables.shape[1:], F32),
        "res": pltpu.VMEM((length, width), F32),
        "tables": pltpu.VMEM((length, PAIR), F32),
        "norm": pltpu.VMEM((length, width), BF),
        "low": pltpu.VMEM((length, qkv_half), BF),
        "keys": pltpu.VMEM((2, length, PAIR), BF),
        "values_t": pltpu.VMEM((PAIR, length), BF),
        "mixed": pltpu.VMEM((length, pairs * PAIR), BF),
        "mixed_other": pltpu.VMEM((length, pairs * PAIR), BF),
        "w_one": pltpu.VMEM((width, up_half), BF),
        "w_two": pltpu.VMEM((ring * down_rows, width), BF),
        "act": pltpu.VMEM((length, up_half), BF),
        "slope": pltpu.VMEM((length, up_half), BF),
        "part": pltpu.VMEM((length, width), BF),
        "part_other": pltpu.VMEM((length, width), BF),
        "z_send": dma((count * hops,)), "z_recv": dma((count * hops,)),
        "p_send": dma((2 * count * hops,)), "p_recv": dma((2 * count * hops,)),
        "d_send": dma((2 * count * hops,)), "d_recv": dma((2 * count * hops,)),
        "c_send": dma((count + layers,)), "c_recv": dma((count + layers,)),
        "l_in": dma((count,)), "l_out": dma((count,)),
        "m_send": dma((32,)), "m_recv": dma((32,)), "m_load": dma((4,)),
        "x_send": dma((layers * (pairs + 2),)), "x_recv": dma((layers * (pairs + 2),)),
        "save_sem": dma((16 * layers,)),
    }
    names = [*inputs, *outputs, *scratch]
    results = pl.pallas_call(
        partial(forward_kernel, names, layers, vec_rows),
        in_specs=[vmem if name in in_vmem else anywhere for name in inputs],
        out_specs=[vmem if name in in_vmem else anywhere for name in outputs],
        out_shape=[jax.ShapeDtypeStruct(*shape) for shape in outputs.values()],
        scratch_shapes=list(scratch.values()),
        compiler_params=pltpu.CompilerParams(
            collective_id=0, has_side_effects=True, vmem_limit_bytes=62 * 1024 * 1024
        ),
        cost_estimate=pl.CostEstimate(
            flops=60_000_000_000, bytes_accessed=600_000_000, transcendentals=0
        ),
        name="forward",
    )(*inputs.values())
    return SimpleNamespace(**dict(zip(outputs, results)))


def add_into(target, term):
    @pl.loop(0, target.shape[0] // ADD_ROWS)
    def _(step):
        at = aligned(step * ADD_ROWS, ADD_ROWS)
        target[at, :] = (target[at, :].astype(F32) + term[at, :].astype(F32)).astype(BF)


class Sems:
    def __init__(self, ref):
        self.ref, self.used = ref, 0

    def take(self):
        self.used += 1
        return self.ref.at[self.used - 1]


class Sum:
    def __init__(self, at, sems, refs, name, layer, z_first, x_first, compute):
        self.at, self.sems = at, sems
        self.own, self.one, self.two, self.three = [
            getattr(refs, name + part) for part in ("_own", "_one", "_two", "_three")
        ]
        self.stage = getattr(refs, name + "_stage" + str(layer))
        self.arrive = getattr(refs, name + "_arrive" + str(layer), None)
        self.z_first, self.x_first, self.compute = z_first, x_first, compute
        self.rows = self.two.shape[1]
        self.sends, self.slot_sends = [], [[], []]
        self.first, self.second, self.hop = {}, {}, {}
        self.swap = None

    def make(self, src, dst, target, slot=None):
        copy = remote(src, dst, self.sems[0].take(), self.sems[1].take(), target)
        copy.start()
        (self.sends if slot is None else self.slot_sends[slot]).append(copy)
        return copy

    def pieces(self, mine):
        at = self.at
        if self.x_first:
            side = at.at_x if mine else 1 - at.at_x
            return [(side, 1), (2 + side, 1)]
        return [(2 * (at.at_y if mine else 1 - at.at_y), 2)]

    def tile(self, tile):
        slot = tile % 2
        for copy in self.slot_sends[slot]:
            copy.wait_send()
        self.slot_sends[slot] = []
        self.compute(tile, self.own.at[slot])

    def start(self, tile):
        self.tile(tile)
        slot = tile % 2
        if self.z_first:
            self.hop[0] = self.make(self.own.at[slot], self.three.at[0], self.at.up, slot)
        else:
            self.plane_one(tile, self.own.at[slot], slot)

    def plane_one(self, tile, source, slot=None):
        target = self.at.over_x if self.x_first else self.at.over_y
        place, made = 0, []
        for first, count in self.pieces(False):
            size = count * self.rows
            made.append(
                self.make(
                    source.at[aligned(first * self.rows, size, self.rows), :],
                    self.one.at[tile, pl.ds(place, size), :],
                    target,
                    slot,
                )
            )
            place += size
        self.first[tile] = made

    def plane_two(self, tile, source):
        for copy in self.first[tile]:
            copy.wait_recv()
        place = 0
        for first, count in self.pieces(True):
            size = count * self.rows
            add_into(
                self.one.at[tile, pl.ds(place, size), :],
                source.at[aligned(first * self.rows, size, self.rows), :],
            )
            place += size
        at = self.at
        target, keep = (at.over_y, at.at_y) if self.x_first else (at.over_x, at.at_x)
        self.second[tile] = self.make(
            self.one.at[tile, aligned((1 - keep) * self.rows, self.rows), :],
            self.two.at[tile],
            target,
        )

    def plane_three(self, tile):
        keep = self.at.at_y if self.x_first else self.at.at_x
        self.second[tile].wait_recv()
        add_into(self.two.at[tile], self.one.at[tile, aligned(keep * self.rows, self.rows), :])

    def middle(self, tile):
        self.plane_two(tile, self.own.at[tile % 2])

    def finish(self, tile):
        self.plane_three(tile)
        if tile > 0:
            self.hop[tile - 1].wait_recv()
            add_into(self.two.at[tile], self.three.at[tile - 1])
        if tile < self.at.ring - 1:
            self.hop[tile] = self.make(self.two.at[tile], self.three.at[tile], self.at.up)
        else:
            self.gather()

    def ring_step(self, tile):
        self.tile(tile)
        self.hop[tile - 1].wait_recv()
        total = self.three.at[tile - 1]
        add_into(total, self.own.at[tile % 2])
        if tile == self.at.ring - 1:
            self.plane_one(0, total)
        else:
            self.hop[tile] = self.make(total, self.three.at[tile], self.at.up)

    def slab_middle(self):
        self.plane_two(0, self.three.at[self.at.ring - 2])

    def slab_finish(self):
        self.plane_three(0)
        self.gather()

    def total(self):
        return self.two.at[0 if self.z_first else self.at.ring - 1]

    def place(self, quarter, turn=0, size=None):
        size = size or self.rows
        return self.stage.at[aligned(quarter * self.rows + turn * size, size), :]

    def gather(self):
        at = self.at
        self.store = pltpu.make_async_copy(self.total(), self.place(at.seq), self.sems[2].take())
        self.store.start()
        self.near = [
            self.make(self.total(), self.place(at.seq), at.over_x),
            self.make(self.total(), self.place(at.seq), at.over_y),
        ]

    def gather_far(self):
        at = self.at
        for copy in self.near:
            copy.wait_recv()
        half = self.rows // 2
        self.far = []
        for turn, (origin, target) in enumerate(((at.near_y, at.over_x), (at.near_x, at.over_y))):
            ref = self.place(origin, turn, half)
            self.far.append(self.make(ref, ref, target))

    def gather_end(self):
        at = self.at
        self.store.wait()
        for copy in self.far:
            copy.wait_recv()
        if self.arrive is not None:
            half = 2 * self.rows
            self.swap = self.make(
                self.stage.at[aligned((1 - at.core) * half, half), :], self.arrive, at.other
            )

    def drain(self):
        if self.swap is not None:
            self.swap.wait_recv()
        for copy in self.sends + self.slot_sends[0] + self.slot_sends[1]:
            copy.wait_send()
        self.sends, self.slot_sends = [], [[], []]


class VectorSum:
    def __init__(self, at, sems, source, got, hop, total):
        self.at, self.sems = at, sems
        self.got, self.hop, self.total = got, hop, total
        self.copies, self.step = [], 0
        self.partners = (at.other, at.over_x, at.over_y)

    def send(self, src, dst, target):
        copy = remote(src, dst, self.sems[0].take(), self.sems[1].take(), target)
        copy.start()
        self.copies.append(copy)

    def advance(self):
        idx, at = self.step, self.at
        self.step += 1
        if idx == 0:
            self.send(self.total.at[0], self.got.at[0], self.partners[0])
            return
        self.copies[-1].wait_recv()
        if idx <= 3:
            self.total[idx] = self.total[idx - 1] + self.got[idx - 1]
            if idx < 3:
                self.send(self.total.at[idx], self.got.at[idx], self.partners[idx])
            else:
                self.send(self.total.at[3, at.back(1)], self.hop.at[0], at.up)
            return
        hop = idx - 3
        self.hop[hop - 1] = self.hop[hop - 1] + self.total[3, at.back(hop + 1)]
        if hop < at.ring - 1:
            self.send(self.hop.at[hop - 1], self.hop.at[hop], at.up)


class Backward:
    def __init__(self, at, refs, layers):
        self.at, self.refs, self.layers = at, refs, layers
        self.blocks = refs.grad.shape[0] // ROWS_Q
        self.pairs = refs.low.shape[1] // (3 * PAIR)
        self.slot = 0
        self.part_copies = {}

    def bring(self, pairs):
        copies = []
        for src, dst in pairs:
            copies.append(pltpu.make_async_copy(src, dst, self.refs.load_sem.at[self.slot]))
            self.slot += 1
        for copy in copies:
            copy.start()
        return copies

    def bring_now(self, pairs):
        for copy in self.bring(pairs):
            copy.wait()

    def saved(self, name, layer):
        return getattr(self.refs, name + "_in" + str(layer))

    def add_vec(self, row, value):
        total = jnp.sum(value, axis=0, keepdims=True)
        width = value.shape[1]
        self.refs.vgrad[row : row + 1, 0:width] = self.refs.vgrad[row : row + 1, 0:width] + total

    def send_part(self, key, landing):
        refs = self.refs
        slot = len(self.part_copies)
        copy = remote(
            refs.part, landing, refs.x_send.at[slot], refs.x_recv.at[slot], self.at.other
        )
        copy.start()
        self.part_copies[key] = copy

    def units(self, layer):
        refs = self.refs
        if layer == self.layers - 1:
            self.bring_now([(refs.cot_in, refs.grad)])
        self.bring_now(
            [
                (self.saved("down", layer), refs.w_one),
                (self.saved("up", layer), refs.w_two),
                (self.saved("slope", layer), refs.ups),
            ]
        )
        refs.vgrad[...] = jnp.zeros_like(refs.vgrad)
        tiles = refs.w_one.shape[0] // 512

        def body(rows):
            grad = refs.grad[rows, :]
            self.add_vec(5, grad)
            refs.grad_low[rows, :] = grad.astype(BF)

            @pl.loop(0, tiles)
            def _(tile):
                cols = aligned(tile * 512, 512)
                value = dot_nt(refs.grad_low[rows, :], refs.w_one[cols, :])
                value = value * refs.ups[rows, cols].astype(F32)
                total = jnp.sum(value, axis=0, keepdims=True)
                refs.vgrad[7:8, cols] = refs.vgrad[7:8, cols] + total
                refs.ups[rows, cols] = value.astype(BF)

            part = dot_nt(refs.ups[rows, :], refs.w_two[...])
            refs.part_f[rows, :] = part
            refs.part[rows, :] = part.astype(BF)

        each_block(self.blocks, body)
        self.send_part((layer, 0), refs.got_one)

    def vec(self, layer, row, width):
        return self.refs.vecs[layer, row : row + 1, 0:width]

    def norm_blocks(self, layer, first, landing, source, use):
        refs = self.refs

        def copy_of(step):
            slot = lax.rem(step, 2)
            rows = aligned(step * ROWS_Q, ROWS_Q)
            return pltpu.make_async_copy(
                source.at[rows, :], refs.aux.at[slot], refs.aux_sem.at[slot]
            )

        copy_of(0).start()

        @pl.loop(0, self.blocks)
        def _(step):
            @pl.when(step + 1 < self.blocks)
            def _():
                copy_of(step + 1).start()

            copy_of(step).wait()
            rows = aligned(step * ROWS_Q, ROWS_Q)
            use(rows, self.norm_back(rows, layer, first, landing, refs.aux[lax.rem(step, 2)]))

    def norm_back(self, rows, layer, first, landing, hidden):
        refs = self.refs
        width = refs.grad.shape[1]
        part = refs.part_f[rows, :] + landing[rows, :].astype(F32)
        scaled, inverse = norm_parts(hidden)
        entry = part * self.vec(layer, first, width)
        mean_one = jnp.mean(entry, axis=-1, keepdims=True)
        mean_two = jnp.mean(entry * scaled, axis=-1, keepdims=True)
        self.add_vec(first, part * scaled)
        self.add_vec(first + 1, part)
        grad = refs.grad[rows, :] + inverse * (entry - mean_one - scaled * mean_two)
        refs.grad[rows, :] = grad
        return grad

    def after(self, layer):
        refs = self.refs
        half = refs.mixed_grad.shape[1]
        weight = refs.w_one.at[pl.ds(0, half), :]
        self.bring_now([(self.saved("proj", layer), weight)])
        self.part_copies[layer, 0].wait()

        def body(rows, grad):
            self.add_vec(4, grad)
            low = grad.astype(BF)
            refs.after_low[rows, :] = low
            refs.mixed_grad[rows, :] = dot_nt(low, refs.w_one[0:half, :]).astype(BF)

        self.norm_blocks(layer, 2, refs.got_one, self.saved("after", layer), body)
        self.entry_load = self.bring(
            [(self.saved("qkv", layer), refs.w_two.at[:, pl.ds(0, refs.low.shape[1])])]
        )

    def attend(self, layer, pair):
        refs = self.refs
        if pair == 0:
            self.bring_now([(self.saved("low", layer), refs.low)])
        base = pair * 3 * PAIR
        query_cols, key_cols, value_cols = [
            slice(base + kind * PAIR, base + (kind + 1) * PAIR) for kind in range(3)
        ]
        refs.keys_t[...] = refs.low[:, key_cols].astype(F32).T.astype(BF)
        scale = HEAD_DIM**-0.5
        refs.dk[...] = jnp.zeros_like(refs.dk)
        refs.dv[...] = jnp.zeros_like(refs.dv)

        def body(rows):
            block = refs.low[rows, query_cols]
            dout = refs.mixed_grad[rows, pair * PAIR : (pair + 1) * PAIR]
            outs = []
            for head in range(2):
                mine, dmine = head_mask(block, head), head_mask(dout, head)
                scores = dot_nt(refs.low[:, key_cols], mine * jnp.asarray(scale, BF))
                probs = jnp.exp(scores - refs.lse_in[layer, pair, head : head + 1, rows])
                prob_grad = dot_nt(refs.low[:, value_cols], dmine)
                delta = jnp.sum(probs * prob_grad, axis=0, keepdims=True)
                score_low = (probs * (prob_grad - delta) * scale).astype(BF)
                refs.dv[...] += dot(probs.astype(BF), dmine)
                refs.dk[...] += dot(score_low, mine)
                outs.append(dot(refs.keys_t[head * HEAD_DIM : (head + 1) * HEAD_DIM], score_low))
            refs.dq[rows, :] = jnp.concatenate(outs, axis=0).T

        each_block(self.blocks, body)

        def last(rows):
            cosine, sine = rotation_tables(refs.tables[rows, :])

            def back(item):
                item = item.astype(BF).astype(F32)
                return item * cosine - swap_halves(item) * sine

            parts = (
                back(refs.dq[rows, :]),
                back(refs.dk[rows, :]),
                refs.dv[rows, :].astype(BF).astype(F32),
            )
            for kind, part in enumerate(parts):
                cols = slice(base + kind * PAIR, base + (kind + 1) * PAIR)
                refs.vgrad[6:7, cols] = refs.vgrad[6:7, cols] + jnp.sum(part, axis=0, keepdims=True)
                refs.low[rows, cols] = part.astype(BF)

        each_block(self.blocks, last)

    def heads(self, layer):
        refs = self.refs
        width = refs.low.shape[1]
        for copy in self.entry_load:
            copy.wait()

        def body(rows):
            part = dot_nt(refs.low[rows, :], refs.w_two[:, 0:width])
            refs.part_f[rows, :] = part
            refs.part[rows, :] = part.astype(BF)

        each_block(self.blocks, body)
        self.send_part((layer, 1), refs.got_two)

    def entry(self, layer):
        refs = self.refs
        self.part_copies[layer, 1].wait()
        source = self.saved("entry", layer)
        self.norm_blocks(layer, 0, refs.got_two, source, lambda rows, grad: None)

    def weight_tile(self, name, layer):
        refs = self.refs
        source, right = {
            "down": ("active", refs.grad_low),
            "up": ("normed_two", refs.ups),
            "proj": ("mixed", refs.after_low),
            "qkv": ("normed", refs.low),
        }[name]
        saved = self.saved(source, layer)

        def compute(tile, out):
            rows, columns = out.shape
            held = refs.stream.at[:, pl.ds(0, rows)]
            self.bring_now([(saved.at[:, aligned(self.at.back(tile + 1) * rows, rows)], held)])
            high, wide = min(rows, 256), min(columns, 512)

            @pl.loop(0, rows // high)
            def _(row):
                at_rows = aligned(row * high, high)

                @pl.loop(0, columns // wide)
                def _(column):
                    cols = aligned(column * wide, wide)
                    out[at_rows, cols] = dot_tn(refs.stream[:, at_rows], right[:, cols]).astype(BF)

        return compute

    def vector_rows(self, target):
        refs, at = self.refs, self.at
        target[...] = jnp.zeros_like(target)
        per_chip = refs.vec_rows * 2
        keep = (at.core == 0).astype(F32)
        for row in range(48):
            source = refs.vgrad[row // 8 : row // 8 + 1, row % 8 * 128 : (row % 8 + 1) * 128]
            place = row % per_chip
            target[row // per_chip, place : place + 1, :] = source * keep
        places = []
        for pair in range(at.ring):
            for kind in range(3):
                places.append((48 + kind * 8 + 2 * pair + at.core, 6, pair * 3 + kind))
            for part in range(4):
                places.append((72 + (2 * pair + at.core) * 4 + part, 7, pair * 4 + part))
        for place, row, block in places:
            target[lax.div(place, per_chip), pl.ds(lax.rem(place, per_chip), 1), :] = refs.vgrad[
                row : row + 1, block * 128 : (block + 1) * 128
            ]


def squares_of(ref):
    rows, columns = ref.shape

    def body(step, total):
        part = ref[aligned(step * 16, 16), :].astype(F32)
        part = part * part
        part = part[0:8] + part[8:16]
        for column in range(0, columns, 128):
            total = total + part[:, column : column + 128]
        return total

    return lax.fori_loop(0, rows // 16, body, jnp.zeros((8, 128), F32))


def backward_kernel(names, layers, vec_rows, *operands):
    refs = SimpleNamespace(**dict(zip(names, operands)))
    refs.vec_rows = vec_rows
    at = Places()
    ring = at.ring
    sems = (Sems(refs.send_sem), Sems(refs.recv_sem), Sems(refs.store_sem))
    greet((at.other, at.over_x, at.over_y, at.down), 4)
    work = Backward(at, refs, layers)
    sums = {}
    for layer in range(layers):
        for name, z_first, x_first in (
            ("qkv", True, True),
            ("proj", True, False),
            ("up", False, True),
            ("down", False, False),
        ):
            sums[name, layer] = Sum(
                at, sems, refs, name, layer, z_first, x_first, work.weight_tile(name, layer)
            )
    vectors = [
        VectorSum(at, sems, None, refs.vec_got.at[layer], refs.vec_hop.at[layer], refs.vec_sum.at[layer])
        for layer in range(layers)
    ]
    refs.square_sum[0] = jnp.zeros((8, 128), F32)
    steps = []

    def free(sem):
        for target in (at.over_x, at.over_y, at.down):
            pl.semaphore_signal(sem, inc=1, device_id=target, device_id_type=pl.DeviceIdType.MESH)

    def wide_steps(layer):
        items = [sums["down", layer], sums["up", layer]]

        def turn(tile):
            for item in items:
                item.middle(tile)
            if tile + 2 < ring:
                for item in items:
                    item.start(tile + 2)
            if tile > 0:
                for item in items:
                    item.finish(tile - 1)

        def begin(tile):
            if tile == 0 and layer + 1 < layers:
                pl.semaphore_wait(refs.free_wide, 3)
            for item in items:
                item.start(tile)

        def end():
            for item in items:
                item.finish(ring - 1)

        def far():
            for item in items:
                item.gather_far()

        def close():
            for item in items:
                item.gather_end()
                refs.square_sum[0] = refs.square_sum[0] + squares_of(item.total())
            if layer > 0:
                for item in items:
                    item.drain()
                free(refs.free_wide)

        turns = [partial(begin, 0), partial(begin, 1)]
        turns += [partial(turn, tile) for tile in range(ring)]
        return turns + [end, far, close]

    def slab_steps(name, layer):
        item = sums[name, layer]

        def begin():
            item.start(0)

        def close():
            item.gather_end()
            refs.square_sum[0] = refs.square_sum[0] + squares_of(item.total())
            if layer > 0:
                item.drain()

        turns = [begin] + [partial(item.ring_step, tile) for tile in range(1, ring)]
        return turns + [item.slab_middle, item.slab_finish, item.gather_far, close]

    def run(steps, count=1):
        for _ in range(count):
            if steps:
                steps.pop(0)()

    late = []
    for layer in reversed(range(layers)):
        last = layer == 0
        wide, proj, qkv = wide_steps(layer), slab_steps("proj", layer), slab_steps("qkv", layer)
        work.units(layer)
        run(late, 3)
        run(wide, 2)
        run(late, 2)
        work.after(layer)
        run(late, 2)
        if layer + 1 == layers:
            run(proj)
        for pair in range(work.pairs):
            work.attend(layer, pair)
            run(wide)
            run(late, 3)
            if layer + 1 == layers and pair > 0:
                run(proj)
        while late:
            run(late)
        if layer + 1 < layers:
            free(refs.free_slab)
            pl.semaphore_wait(refs.free_slab, 3)
            run(proj)
        work.heads(layer)
        run(wide)
        run(proj)
        run(qkv)
        work.entry(layer)
        if last:
            save = pltpu.make_async_copy(refs.grad, refs.input_grad, sems[2].take())
            save.start()
        work.vector_rows(refs.vec_sum.at[layer, 0])
        run(qkv)
        run(wide)
        run(proj)
        vector = [vectors[layer].advance] * 7
        while proj or qkv or vector:
            late += wide[:1] + qkv[:1] + proj[:1] + vector[:1]
            qkv, proj, vector, wide = qkv[1:], proj[1:], vector[1:], wide[1:]
        late = late + wide
        wide = []
    while late:
        run(late)
    save.wait()
    total = refs.square_sum[0]
    for layer in range(layers):
        vec_total = refs.vec_hop[layer, ring - 2]
        refs.vec_out[layer] = vec_total
        part = vec_total * vec_total * 0.125
        for row in range(0, part.shape[0], 8):
            total = total + part[row : row + 8]
    refs.square_sum[0] = total
    copies = []

    def square_copy(src, dst, target):
        copy = remote(src, dst, sems[0].take(), sems[1].take(), target)
        copy.start()
        copies.append(copy)
        copy.wait_recv()

    for idx, target in enumerate((at.other, at.over_x, at.over_y)):
        square_copy(refs.square_sum.at[idx], refs.square_got.at[idx], target)
        refs.square_sum[idx + 1] = refs.square_sum[idx] + refs.square_got[idx]
    total = refs.square_sum[3]
    for hop in range(ring - 1):
        source = refs.square_sum.at[3] if hop == 0 else refs.square_got.at[2 + hop]
        square_copy(source, refs.square_got.at[3 + hop], at.up)
        total = total + refs.square_got[3 + hop]
    refs.square_out[...] = total
    for name in WEIGHTS:
        sums[name, 0].drain()
    for vector in vectors:
        for copy in vector.copies:
            copy.wait_send()
    for copy in copies:
        copy.wait_send()


def backward(kept, layers, vec_rows):
    ring = lax.axis_size("fsdp") // 2
    length, width = kept.cot_out.shape
    qkv_half, up_half = kept.low_out0.shape[1], kept.slope_out0.shape[1]
    half = kept.mixed_out0.shape[1]
    inputs = {
        "cot_in": kept.cot_out,
        "tables": kept.table_out,
        "vecs": kept.vecs,
        "lse_in": kept.lse_out,
    }
    for layer in range(layers):
        for name in (*WEIGHTS, "normed", "low", "mixed", "after", "normed_two", "active", "slope"):
            inputs[name + "_in" + str(layer)] = getattr(kept, name + "_out" + str(layer))
        entry = kept.clip_out if layer == 0 else getattr(kept, "result_out" + str(layer - 1))
        inputs["entry_in" + str(layer)] = entry
    slabs = {
        "qkv": (width // ring, qkv_half),
        "proj": (half // ring, width),
        "up": (width // ring, up_half),
        "down": (up_half // ring, width),
    }
    outputs, scratch = {}, {}
    dma, regular = pltpu.SemaphoreType.DMA, pltpu.SemaphoreType.REGULAR
    for name, (rows, columns) in slabs.items():
        for layer in range(layers):
            outputs[name + "_stage" + str(layer)] = ((rows, columns), BF)
            if name in ("qkv", "up"):
                outputs[name + "_arrive" + str(layer)] = ((rows // 2, columns), BF)
        z_first = name in ("qkv", "proj")
        tiles, quarter = 1 if z_first else ring, rows // 4
        scratch[name + "_own"] = pltpu.VMEM((2, rows, columns), BF)
        scratch[name + "_one"] = pltpu.VMEM((tiles, 2 * quarter, columns), BF)
        scratch[name + "_two"] = pltpu.VMEM((tiles, quarter, columns), BF)
        scratch[name + "_three"] = pltpu.VMEM(
            (ring - 1, rows if z_first else quarter, columns), BF
        )
    outputs["input_grad"] = ((length, width), F32)
    outputs["vec_out"] = ((layers, 32, 128), F32)
    outputs["square_out"] = ((8, 128), F32)
    scratch |= {
        "grad": pltpu.VMEM((length, width), F32),
        "aux": pltpu.VMEM((2, ROWS_Q, width), F32),
        "aux_sem": dma((2,)),
        "part_f": pltpu.VMEM((length, width), F32),
        "grad_low": pltpu.VMEM((length, width), BF),
        "after_low": pltpu.VMEM((length, width), BF),
        "part": pltpu.VMEM((length, width), BF),
        "got_one": pltpu.VMEM((length, width), BF),
        "got_two": pltpu.VMEM((length, width), BF),
        "ups": pltpu.VMEM((length, up_half), BF),
        "w_one": pltpu.VMEM((up_half, width), BF),
        "w_two": pltpu.VMEM((width, up_half), BF),
        "low": pltpu.VMEM((length, qkv_half), BF),
        "mixed_grad": pltpu.VMEM((length, half), BF),
        "stream": pltpu.VMEM((length, up_half // ring), BF),
        "keys_t": pltpu.VMEM((PAIR, length), BF),
        "dq": pltpu.VMEM((length, PAIR), F32),
        "dk": pltpu.VMEM((length, PAIR), F32),
        "dv": pltpu.VMEM((length, PAIR), F32),
        "vgrad": pltpu.VMEM((8, up_half), F32),
        "vec_got": pltpu.VMEM((layers, 3, ring, 32, 128), F32),
        "vec_hop": pltpu.VMEM((layers, ring - 1, 32, 128), F32),
        "vec_sum": pltpu.VMEM((layers, 4, ring, 32, 128), F32),
        "square_got": pltpu.VMEM((3 + ring - 1, 8, 128), F32),
        "square_sum": pltpu.VMEM((4, 8, 128), F32),
        "send_sem": dma((120 * layers,)),
        "recv_sem": dma((120 * layers,)),
        "store_sem": dma((8 * layers,)),
        "load_sem": dma((32 * layers,)),
        "x_send": dma((2 * layers,)),
        "x_recv": dma((2 * layers,)),
        "free_wide": regular,
        "free_slab": regular,
    }
    in_vmem = ("tables", "vecs", "lse_in", "vec_out", "square_out")
    anywhere = pl.BlockSpec(memory_space=pl.ANY)
    vmem = pl.BlockSpec(memory_space=pltpu.VMEM)
    names = [*inputs, *outputs, *scratch]
    results = pl.pallas_call(
        partial(backward_kernel, names, layers, vec_rows),
        in_specs=[vmem if name in in_vmem else anywhere for name in inputs],
        out_specs=[vmem if name in in_vmem else anywhere for name in outputs],
        out_shape=[jax.ShapeDtypeStruct(*shape) for shape in outputs.values()],
        scratch_shapes=list(scratch.values()),
        compiler_params=pltpu.CompilerParams(
            collective_id=1, has_side_effects=True, vmem_limit_bytes=63 * 1024 * 1024
        ),
        cost_estimate=pl.CostEstimate(
            flops=100_000_000_000, bytes_accessed=600_000_000, transcendentals=0
        ),
        name="backward",
    )(*inputs.values())
    return SimpleNamespace(**dict(zip(outputs, results)))


def fast_device(
    clip_tokens,
    patch_coords,
    out_cotangent,
    vector_params,
    qkv_weight,
    proj_weight,
    up_weight,
    down_weight,
    first_vector,
    first_qkv,
    first_proj,
    first_up,
    first_down,
    second_vector,
    second_qkv,
    second_proj,
    second_up,
    second_down,
):
    masters = (vector_params, qkv_weight, proj_weight, up_weight, down_weight)
    firsts = (first_vector, first_qkv, first_proj, first_up, first_down)
    seconds = (second_vector, second_qkv, second_proj, second_up, second_down)
    layer_count = vector_params.shape[0]
    batch_local, chunk_len = clip_tokens.shape[:2]
    seq_parts = lax.axis_size("seq")
    parts = lax.axis_size("fsdp")
    ring = parts // 2
    seq = lax.axis_index("seq")
    shard = lax.axis_index("fsdp")
    core = lax.rem(shard, 2)
    even = lax.rem(seq, 2) == 0

    def from_clips(item):
        mine = pick(item.reshape((2, 2, chunk_len) + item.shape[1:]), core)
        pieces = [None, None]
        for turn in range(2):
            piece = jnp.where(even, mine[turn], mine[1 - turn])
            pairs = []
            for src_seq in range(seq_parts):
                for src in range(parts):
                    dst_seq = 2 * (src % 2) + (src_seq + turn) % 2
                    dst = src - src % 2 + src_seq // 2
                    pairs.append((dst_seq * parts + dst, src_seq * parts + src))
            pieces[turn] = lax.ppermute(piece, ("seq", "fsdp"), pairs)
        return jnp.where(
            even, jnp.stack([pieces[0], pieces[1]]), jnp.stack([pieces[1], pieces[0]])
        )

    tables = []
    for idx in range(batch_local):
        cosine, sine = rotary_tables(patch_coords[:, idx], HEAD_DIM // 2)
        tables.append(jnp.concatenate([cosine, sine, cosine, sine], axis=1))
    share = vector_params.shape[1]
    vector_rows = vector_params.astype(BF).astype(F32).reshape(-1, 128)
    vector_rows = jnp.pad(vector_rows, ((0, -vector_rows.shape[0] % 8), (0, 0)))
    kept = forward(
        qkv_weight,
        up_weight,
        down_weight,
        proj_weight,
        clip_tokens,
        out_cotangent,
        jnp.stack(tables),
        vector_rows,
        share // 128,
    )
    block_output = from_clips(getattr(kept, "result_out" + str(layer_count - 1)))

    back = backward(kept, layer_count, share // 128)
    input_grad = from_clips(back.input_grad)

    clip_count = batch_local * parts
    norm_value = jnp.sqrt(jnp.sum(back.square_out)) / clip_count
    param_count = sum(master.size for master in masters) * parts
    factor = jnp.minimum(1.0, CLIP_RATIO * math.sqrt(float(param_count)) / (norm_value + 1e-06))

    vector_total = back.vec_out.reshape(layer_count, -1)[:, : 2 * share]
    vector_grad = lax.dynamic_slice_in_dim(vector_total, core * share, share, 1) / clip_count
    vector_new = adam_update(vector_params, vector_grad, first_vector, second_vector, factor)
    updates = [(vector_grad, *vector_new, vector_new[2].astype(BF))]
    for kind, name in enumerate(WEIGHTS):
        parts_of = ("_stage", "_arrive") if name in ("qkv", "up") else ("_stage",)
        updates.append(
            adam_matrix(
                [
                    getattr(back, name + part + str(layer))
                    for layer in range(layer_count)
                    for part in parts_of
                ],
                masters[kind + 1],
                firsts[kind + 1],
                seconds[kind + 1],
                factor,
                core,
                3 if kind == 0 else 1,
                clip_count,
            )
        )
    return (
        block_output,
        input_grad,
        *[item[0] for item in updates],
        norm_value.reshape(1),
        *[item[1] for item in updates],
        *[item[2] for item in updates],
        *[item[3] for item in updates],
        *[item[4] for item in updates],
    )


def solution(mesh):
    in_specs = (
        P("fsdp", "seq", None),
        P(None, "fsdp", "seq"),
        P("fsdp", "seq", None),
        P(None, "fsdp"),
        P(None, "fsdp", None),
        P(None, "fsdp", None),
        P(None, "fsdp", None),
        P(None, "fsdp", None),
        P(None, "fsdp"),
        P(None, "fsdp", None),
        P(None, "fsdp", None),
        P(None, "fsdp", None),
        P(None, "fsdp", None),
        P(None, "fsdp"),
        P(None, "fsdp", None),
        P(None, "fsdp", None),
        P(None, "fsdp", None),
        P(None, "fsdp", None),
    )
    out_specs = (
        P("fsdp", "seq", None),
        P("fsdp", "seq", None),
        P(None, "fsdp"),
        P(None, "fsdp", None),
        P(None, "fsdp", None),
        P(None, "fsdp", None),
        P(None, "fsdp", None),
        P(),
        P(None, "fsdp"),
        P(None, "fsdp", None),
        P(None, "fsdp", None),
        P(None, "fsdp", None),
        P(None, "fsdp", None),
        P(None, "fsdp"),
        P(None, "fsdp", None),
        P(None, "fsdp", None),
        P(None, "fsdp", None),
        P(None, "fsdp", None),
        P(None, "fsdp"),
        P(None, "fsdp", None),
        P(None, "fsdp", None),
        P(None, "fsdp", None),
        P(None, "fsdp", None),
        P(None, "fsdp"),
        P(None, "fsdp", None),
        P(None, "fsdp", None),
        P(None, "fsdp", None),
        P(None, "fsdp", None),
    )
    body = fast_device if fits_fast(mesh) else general_device
    return jax.shard_map(
        body, mesh=mesh, in_specs=in_specs, out_specs=out_specs, check_vma=False
    )
```

```python
from functools import partial
import math
from types import SimpleNamespace

import jax
import jax.numpy as jnp
from jax import lax
from jax.experimental import pallas as pl
from jax.experimental.pallas import tpu as pltpu
from jax.sharding import PartitionSpec as P

D = 1024
HEADS = 16
HEAD_DIM = 64


BETA_ONE = 0.5
BETA_TWO = 0.75
LEARN_RATE = 0.1
DECAY_RATE = 0.1
CLIP_RATIO = 0.2
ADAM_EPS = 1e-08
ROPE_BASE = 10000.0


def pieces(vector):
    return (
        vector[0:D],
        vector[D : 2 * D],
        vector[2 * D : 3 * D],
        vector[3 * D : 4 * D],
        vector[4 * D : 5 * D],
        vector[5 * D : 6 * D],
        vector[6 * D : 9 * D],
        vector[9 * D :],
    )


def layer_norm(hidden, ln_gain, ln_shift):
    center = hidden - jnp.mean(hidden, axis=-1, keepdims=True)
    spread = jnp.mean(center * center, axis=-1, keepdims=True)
    return center * lax.rsqrt(spread + 1e-06) * ln_gain + ln_shift


def gelu_exact(upward):
    return 0.5 * upward * (1.0 + jax.scipy.special.erf(upward * (1.0 / math.sqrt(2.0))))


def rotary_tables(coords_clip, pair_count):
    pair_index = jnp.arange(pair_count, dtype=jnp.int32)
    side_pairs = pair_count // 3
    time_pairs = pair_count - 2 * side_pairs
    in_time = pair_index < time_pairs
    in_height = jnp.logical_and(pair_index >= time_pairs, pair_index < time_pairs + side_pairs)
    offset = jnp.where(in_time, 0, jnp.where(in_height, time_pairs, time_pairs + side_pairs))
    seg_span = jnp.where(in_time, time_pairs, side_pairs)
    local_rank = (pair_index - offset).astype(jnp.float32)
    frequency = jnp.exp(-math.log(ROPE_BASE) * local_rank / seg_span.astype(jnp.float32))
    positions = coords_clip.astype(jnp.float32)
    chosen = jnp.where(
        in_time[None, :],
        positions[0][:, None],
        jnp.where(in_height[None, :], positions[1][:, None], positions[2][:, None]),
    )
    angles = chosen * frequency[None, :]
    return (jnp.cos(angles), jnp.sin(angles))


def rotate(values_in, cosine, sine_table):
    half_width = values_in.shape[-1] // 2
    first_half = values_in[..., :half_width]
    second_half = values_in[..., half_width:]
    cos_wide = cosine[:, None, :]
    sin_wide = sine_table[:, None, :]
    return jnp.concatenate(
        [
            first_half * cos_wide - second_half * sin_wide,
            first_half * sin_wide + second_half * cos_wide,
        ],
        axis=-1,
    )


def attend_forward(queries, key_rows, value_rows):
    full_len = queries.shape[0]
    block_rows = min(512, full_len)
    score_scale = HEAD_DIM ** (-0.5)
    query_blocks = queries.reshape(
        full_len // block_rows, block_rows, queries.shape[1], queries.shape[2]
    )

    def one_block(query_block):
        scores = (
            jnp.einsum("qhd,khd->hqk", query_block, key_rows, preferred_element_type=jnp.float32)
            * score_scale
        )
        row_max = jnp.max(scores, axis=-1, keepdims=True)
        exponent = jnp.exp(scores - row_max)
        row_total = jnp.sum(exponent, axis=-1, keepdims=True)
        prob_low = (exponent / row_total).astype(jnp.bfloat16)
        mixed_rows = jnp.einsum(
            "hqk,khd->qhd", prob_low, value_rows, preferred_element_type=jnp.float32
        )
        return (mixed_rows, row_max[..., 0] + jnp.log(row_total[..., 0]))

    mixed_rows, log_sums = lax.map(one_block, query_blocks)
    return (mixed_rows.reshape(queries.shape), log_sums)


def attend_backward(queries, key_rows, value_rows, log_sums, head_grad):
    full_len = queries.shape[0]
    block_rows = min(512, full_len)
    score_scale = HEAD_DIM ** (-0.5)
    block_shape = (full_len // block_rows, block_rows, queries.shape[1], queries.shape[2])

    def one_block(carry, block_in):
        key_grad, value_grad = carry
        query_block, grad_block, lse_block = block_in
        scores = (
            jnp.einsum("qhd,khd->hqk", query_block, key_rows, preferred_element_type=jnp.float32)
            * score_scale
        )
        prob_rows = jnp.exp(scores - lse_block[..., None])
        prob_low = prob_rows.astype(jnp.bfloat16)
        value_grad = value_grad + jnp.einsum(
            "hqk,qhd->khd", prob_low, grad_block, preferred_element_type=jnp.float32
        )
        prob_grad = jnp.einsum(
            "qhd,khd->hqk", grad_block, value_rows, preferred_element_type=jnp.float32
        )
        score_grad = prob_rows * (
            prob_grad - jnp.sum(prob_rows * prob_grad, axis=-1, keepdims=True)
        )
        score_low = (score_grad * score_scale).astype(jnp.bfloat16)
        query_grad = jnp.einsum(
            "hqk,khd->qhd", score_low, key_rows, preferred_element_type=jnp.float32
        )
        key_grad = key_grad + jnp.einsum(
            "hqk,qhd->khd", score_low, query_block, preferred_element_type=jnp.float32
        )
        return ((key_grad, value_grad), query_grad)

    zero_heads = jnp.zeros(queries.shape, jnp.float32)
    (key_grad, value_grad), query_grad = lax.scan(
        one_block,
        (zero_heads, zero_heads),
        (queries.reshape(block_shape), head_grad.reshape(block_shape), log_sums),
    )
    return (query_grad.reshape(queries.shape), key_grad, value_grad)


def layer_forward(hidden, cosine, sine_table, weights, seq_parts):
    vector_low, qkv_w, proj_w, up_w, down_w = weights
    gain_one, shift_one, gain_two, shift_two, proj_bias, down_bias, qkv_bias, up_bias = pieces(
        vector_low.astype(jnp.float32)
    )
    row_count = hidden.shape[0]
    local_heads = HEADS // seq_parts
    normed = layer_norm(hidden, gain_one, shift_one).astype(jnp.bfloat16)
    qkv_all = jnp.dot(normed, qkv_w, preferred_element_type=jnp.float32) + qkv_bias
    split_qkv = qkv_all.reshape(row_count, 3, HEADS, HEAD_DIM)
    stacked = jnp.stack(
        [
            rotate(split_qkv[:, 0], cosine, sine_table),
            rotate(split_qkv[:, 1], cosine, sine_table),
            split_qkv[:, 2],
        ],
        axis=1,
    ).astype(jnp.bfloat16)
    packed = stacked.reshape(row_count, 3, seq_parts, local_heads * HEAD_DIM)
    by_heads = lax.all_to_all(packed, "seq", split_axis=2, concat_axis=0, tiled=True)
    full_len = by_heads.shape[0]
    by_heads = by_heads.reshape(full_len, 3, local_heads, HEAD_DIM)
    mixed_rows, log_sums = attend_forward(by_heads[:, 0], by_heads[:, 1], by_heads[:, 2])
    mixed_low = mixed_rows.astype(jnp.bfloat16).reshape(full_len, 1, local_heads * HEAD_DIM)
    by_tokens = lax.all_to_all(mixed_low, "seq", split_axis=0, concat_axis=1, tiled=True).reshape(
        row_count, D
    )
    after_attn = hidden + jnp.dot(by_tokens, proj_w, preferred_element_type=jnp.float32) + proj_bias
    normed_two = layer_norm(after_attn, gain_two, shift_two).astype(jnp.bfloat16)
    upward = jnp.dot(normed_two, up_w, preferred_element_type=jnp.float32) + up_bias
    active = gelu_exact(upward).astype(jnp.bfloat16)
    result = after_attn + jnp.dot(active, down_w, preferred_element_type=jnp.float32) + down_bias
    saved_state = (
        hidden,
        normed,
        by_heads,
        log_sums,
        by_tokens,
        after_attn,
        normed_two,
        upward,
        active,
    )
    return (result, saved_state)


def layer_backward(grad_out, saved_state, weights, cosine, sine_table, seq_parts):
    vector_low, qkv_w, proj_w, up_w, down_w = weights
    gain_one, shift_one, gain_two, shift_two, proj_bias, down_bias, qkv_bias, up_bias = pieces(
        vector_low.astype(jnp.float32)
    )
    hidden, normed, by_heads, log_sums, by_tokens, after_attn, normed_two, upward, active = (
        saved_state
    )
    row_count = hidden.shape[0]
    local_heads = HEADS // seq_parts
    down_bias_grad = jnp.sum(grad_out, axis=0)
    grad_low = grad_out.astype(jnp.bfloat16)
    down_grad = jnp.dot(active.T, grad_low, preferred_element_type=jnp.float32)
    active_grad = jnp.dot(grad_low, down_w.T, preferred_element_type=jnp.float32)
    gelu_value, gelu_pull = jax.vjp(gelu_exact, upward)
    upward_grad = gelu_pull(active_grad)[0]
    up_bias_grad = jnp.sum(upward_grad, axis=0)
    upward_low = upward_grad.astype(jnp.bfloat16)
    up_grad = jnp.dot(normed_two.T, upward_low, preferred_element_type=jnp.float32)
    normed_two_grad = jnp.dot(upward_low, up_w.T, preferred_element_type=jnp.float32)
    norm_value_two, norm_pull_two = jax.vjp(layer_norm, after_attn, gain_two, shift_two)
    attn_in_grad, gain_two_grad, shift_two_grad = norm_pull_two(normed_two_grad)
    after_grad = grad_out + attn_in_grad
    proj_bias_grad = jnp.sum(after_grad, axis=0)
    after_low = after_grad.astype(jnp.bfloat16)
    proj_grad = jnp.dot(by_tokens.T, after_low, preferred_element_type=jnp.float32)
    mixed_grad = jnp.dot(after_low, proj_w.T, preferred_element_type=jnp.float32).astype(
        jnp.bfloat16
    )
    head_grad = lax.all_to_all(
        mixed_grad.reshape(row_count, seq_parts, local_heads * HEAD_DIM),
        "seq",
        split_axis=1,
        concat_axis=0,
        tiled=True,
    )
    full_len = head_grad.shape[0]
    head_grad = head_grad.reshape(full_len, local_heads, HEAD_DIM)
    query_grad, key_grad, value_grad = attend_backward(
        by_heads[:, 0], by_heads[:, 1], by_heads[:, 2], log_sums, head_grad
    )
    stacked_grad = (
        jnp.stack([query_grad, key_grad, value_grad], axis=1)
        .astype(jnp.bfloat16)
        .reshape(full_len, 3, 1, local_heads * HEAD_DIM)
    )
    token_grad = (
        lax.all_to_all(stacked_grad, "seq", split_axis=0, concat_axis=2, tiled=True)
        .reshape(row_count, 3, HEADS, HEAD_DIM)
        .astype(jnp.float32)
    )
    pair_grad_in = token_grad[:, :2].reshape(row_count, 2 * HEADS, HEAD_DIM)
    rotated_value, rotate_pull = jax.vjp(
        partial(rotate, cosine=cosine, sine_table=sine_table), pair_grad_in
    )
    pair_grad = rotate_pull(pair_grad_in)[0].reshape(row_count, 2, HEADS, HEAD_DIM)
    qkv_grad = jnp.concatenate([pair_grad, token_grad[:, 2:]], axis=1).reshape(row_count, 3 * D)
    qkv_bias_grad = jnp.sum(qkv_grad, axis=0)
    qkv_low = qkv_grad.astype(jnp.bfloat16)
    qkv_w_grad = jnp.dot(normed.T, qkv_low, preferred_element_type=jnp.float32)
    normed_grad = jnp.dot(qkv_low, qkv_w.T, preferred_element_type=jnp.float32)
    norm_value_one, norm_pull_one = jax.vjp(layer_norm, hidden, gain_one, shift_one)
    in_grad, gain_one_grad, shift_one_grad = norm_pull_one(normed_grad)
    input_grad = after_grad + in_grad
    vector_grad = jnp.concatenate(
        [
            gain_one_grad,
            shift_one_grad,
            gain_two_grad,
            shift_two_grad,
            proj_bias_grad,
            down_bias_grad,
            qkv_bias_grad,
            up_bias_grad,
        ]
    )
    return (input_grad, (vector_grad, qkv_w_grad, proj_grad, up_grad, down_grad))


def adam_update(master, grad_item, first_old, second_old, factor):
    clipped = grad_item * factor
    first_new = BETA_ONE * first_old + (1.0 - BETA_ONE) * clipped
    second_new = BETA_TWO * second_old + (1.0 - BETA_TWO) * clipped * clipped
    updated = master - LEARN_RATE * (
        first_new / (jnp.sqrt(second_new) + ADAM_EPS) + DECAY_RATE * master
    )
    return (first_new, second_new, updated)


def general_device(
    clip_tokens,
    patch_coords,
    out_cotangent,
    vector_params,
    qkv_weight,
    proj_weight,
    up_weight,
    down_weight,
    first_vector,
    first_qkv,
    first_proj,
    first_up,
    first_down,
    second_vector,
    second_qkv,
    second_proj,
    second_up,
    second_down,
):
    masters = (vector_params, qkv_weight, proj_weight, up_weight, down_weight)
    firsts = (first_vector, first_qkv, first_proj, first_up, first_down)
    seconds = (second_vector, second_qkv, second_proj, second_up, second_down)
    lowered = tuple((master.astype(jnp.bfloat16) for master in masters))
    layer_count = vector_params.shape[0]
    batch_local = clip_tokens.shape[0]
    seq_parts = lax.axis_size("seq")
    fsdp_parts = lax.axis_size("fsdp")
    grad_accum = tuple(
        (
            jnp.zeros((layer_count, master.shape[1] * fsdp_parts) + master.shape[2:], jnp.float32)
            for master in masters
        )
    )
    output_rows = []
    input_rows = []
    for batch_idx in range(batch_local):
        cosine, sine_table = rotary_tables(patch_coords[:, batch_idx], HEAD_DIM // 2)
        hidden = clip_tokens[batch_idx]
        saved_layers = []
        for layer_idx in range(layer_count):
            weights = (
                lax.all_gather(lowered[0][layer_idx], "fsdp", axis=0, tiled=True),
                lax.all_gather(lowered[1][layer_idx], "fsdp", axis=0, tiled=True),
                lax.all_gather(lowered[2][layer_idx], "fsdp", axis=0, tiled=True),
                lax.all_gather(lowered[3][layer_idx], "fsdp", axis=0, tiled=True),
                lax.all_gather(lowered[4][layer_idx], "fsdp", axis=0, tiled=True),
            )
            hidden, saved_state = layer_forward(hidden, cosine, sine_table, weights, seq_parts)
            saved_layers.append(saved_state)
        output_rows.append(hidden)
        grad_rows = out_cotangent[batch_idx]
        for layer_idx in reversed(range(layer_count)):
            weights = (
                lax.all_gather(lowered[0][layer_idx], "fsdp", axis=0, tiled=True),
                lax.all_gather(lowered[1][layer_idx], "fsdp", axis=0, tiled=True),
                lax.all_gather(lowered[2][layer_idx], "fsdp", axis=0, tiled=True),
                lax.all_gather(lowered[3][layer_idx], "fsdp", axis=0, tiled=True),
                lax.all_gather(lowered[4][layer_idx], "fsdp", axis=0, tiled=True),
            )
            grad_rows, layer_grads = layer_backward(
                grad_rows, saved_layers[layer_idx], weights, cosine, sine_table, seq_parts
            )
            grad_accum = tuple(
                (
                    accum_item.at[layer_idx].add(grad_item)
                    for accum_item, grad_item in zip(grad_accum, layer_grads)
                )
            )
        input_rows.append(grad_rows)
    shard_sums = (
        lax.psum_scatter(grad_accum[0], "fsdp", scatter_dimension=1, tiled=True),
        lax.psum_scatter(grad_accum[1], "fsdp", scatter_dimension=1, tiled=True),
        lax.psum_scatter(grad_accum[2], "fsdp", scatter_dimension=1, tiled=True),
        lax.psum_scatter(grad_accum[3], "fsdp", scatter_dimension=1, tiled=True),
        lax.psum_scatter(grad_accum[4], "fsdp", scatter_dimension=1, tiled=True),
    )
    seq_sums = lax.psum(
        (shard_sums[0], shard_sums[1], shard_sums[2], shard_sums[3], shard_sums[4]), "seq"
    )
    clip_count = batch_local * fsdp_parts
    grad_shards = tuple((sum_item / clip_count for sum_item in seq_sums))
    local_squares = sum((jnp.sum(grad_item * grad_item) for grad_item in grad_shards))
    squares_total = lax.psum(local_squares, "fsdp")
    norm_value = jnp.sqrt(squares_total)
    param_count = sum((master.size for master in masters)) * fsdp_parts
    factor = jnp.minimum(1.0, CLIP_RATIO * math.sqrt(float(param_count)) / (norm_value + 1e-06))
    updates = [
        adam_update(master, grad_item, first_old, second_old, factor)
        for master, grad_item, first_old, second_old in zip(masters, grad_shards, firsts, seconds)
    ]
    return (
        jnp.stack(output_rows),
        jnp.stack(input_rows),
        grad_shards[0],
        grad_shards[1],
        grad_shards[2],
        grad_shards[3],
        grad_shards[4],
        norm_value.reshape(1),
        updates[0][0],
        updates[1][0],
        updates[2][0],
        updates[3][0],
        updates[4][0],
        updates[0][1],
        updates[1][1],
        updates[2][1],
        updates[3][1],
        updates[4][1],
        updates[0][2],
        updates[1][2],
        updates[2][2],
        updates[3][2],
        updates[4][2],
        updates[0][2].astype(jnp.bfloat16),
        updates[1][2].astype(jnp.bfloat16),
        updates[2][2].astype(jnp.bfloat16),
        updates[3][2].astype(jnp.bfloat16),
        updates[4][2].astype(jnp.bfloat16),
    )


ROWS_Q = 256
ADD_ROWS = 32
PAIR = 2 * HEAD_DIM
BF = jnp.bfloat16
F32 = jnp.float32
VMEM_LIMIT = 56 * 1024 * 1024


def fits_fast(mesh):
    return dict(mesh.shape) == {"seq": 4, "fsdp": 8}


def swap_core(item):
    parts = lax.axis_size("fsdp")
    return lax.ppermute(item, "fsdp", [(idx, idx ^ 1) for idx in range(parts)])


def send_up(item):
    parts = lax.axis_size("fsdp")
    return lax.ppermute(item, "fsdp", [(idx, (idx + 2) % parts) for idx in range(parts)])


def swap_seq(item, mask):
    parts = lax.axis_size("seq")
    return lax.ppermute(item, "seq", [(idx, idx ^ mask) for idx in range(parts)])


def pick(item, index, axis=0):
    return lax.dynamic_index_in_dim(item, index, axis, keepdims=False)


def swap_halves(item):
    lane = lax.broadcasted_iota(jnp.int32, item.shape, 1)
    half = HEAD_DIM // 2
    width = item.shape[1]
    ahead = pltpu.roll(item, width - half, 1)
    behind = pltpu.roll(item, half, 1)
    return jnp.where(lane % HEAD_DIM < half, ahead, behind)


NT = (((1,), (1,)), ((), ()))


def head_mask(item, head):
    lane = lax.broadcasted_iota(jnp.int32, item.shape, 1)
    return jnp.where(lane // HEAD_DIM == head, item, jnp.zeros_like(item))


class Places:
    def __init__(self):
        shard, seq = lax.axis_index("fsdp"), lax.axis_index("seq")
        parts = lax.axis_size("fsdp")
        self.ring = parts // 2
        self.seq = seq
        self.chip, self.core = shard // 2, lax.rem(shard, 2)
        self.at_x, self.at_y = lax.rem(seq, 2), seq // 2
        self.near_x = 2 * self.at_y + 1 - self.at_x
        self.near_y = 2 * (1 - self.at_y) + self.at_x
        self.other = {"fsdp": shard + 1 - 2 * self.core}
        self.up = {"fsdp": lax.rem(shard + 2, parts)}
        self.down = {"fsdp": lax.rem(shard + parts - 2, parts)}
        self.over_x = {"seq": self.near_x}
        self.over_y = {"seq": self.near_y}

    def back(self, hops):
        return lax.rem(self.chip - hops + self.ring, self.ring)


def remote(src, dst, send, recv, target):
    return pltpu.make_async_remote_copy(
        src_ref=src,
        dst_ref=dst,
        send_sem=send,
        recv_sem=recv,
        device_id=target,
        device_id_type=pl.DeviceIdType.MESH,
    )


def greet(targets, waits):
    barrier = pltpu.get_barrier_semaphore()
    for target in targets:
        pl.semaphore_signal(barrier, inc=1, device_id=target, device_id_type=pl.DeviceIdType.MESH)
    pl.semaphore_wait(barrier, waits)


def aligned(start, size, unit=None):
    return pl.ds(pl.multiple_of(start, unit or size), size)


def adam_kernel(
    kinds, ring, count, core_ref, factor_ref, *refs
):
    n_grads = len(refs) - 8
    grads = refs[:n_grads]
    master, first, second, grad_out, first_out, second_out, new_out, copy_out = refs[n_grads:]
    layer = pl.program_id(0)
    factor = factor_ref[0]
    scale = 1.0 / count
    columns = master.shape[2]
    per_layer = n_grads // 2
    width = columns // (kinds * ring * 2) if per_layer == 2 else 512

    def update(at, total):
        grad = total.astype(F32) * scale
        first_new, second_new, new = [], [], []
        first_new, second_new, new = adam_update(
            master[0, :, at], grad, first[0, :, at], second[0, :, at], factor
        )
        grad_out[0, :, at] = grad
        first_out[0, :, at] = first_new
        second_out[0, :, at] = second_new
        new_out[0, :, at] = new
        copy_out[0, :, at] = new.astype(BF)

    def choose(which, at):
        values = [grads[idx * per_layer + which][:, at] for idx in range(2)]
        return jnp.where(layer == 0, values[0], values[1])

    if per_layer == 1:
        for start in range(0, columns, width):
            update(slice(start, start + width), choose(0, slice(start, start + width)))
        return
    core = core_ref[0]
    for pair in range(ring):
        for kind in range(kinds):
            source = (pair * kinds + kind) * width
            mine, arrive = [choose(which, slice(source, source + width)) for which in range(2)]
            for which in range(2):
                start = (kind * ring * 2 + 2 * pair + which) * width
                update(slice(start, start + width), jnp.where(core == which, mine, arrive))


def adam_matrix(grads, master, first, second, factor, core, kinds, count):
    layers, rows, columns = master.shape
    ring = lax.axis_size("fsdp") // 2
    block = 32 if columns > 1024 else 64
    steps = rows // block
    per_layer = len(grads) // layers

    def grad_spec(idx):
        layer, which = divmod(idx, per_layer)
        lift = steps if per_layer == 2 and which == 0 else 0

        def where(at_layer, step, core_ref, layer=layer, lift=lift):
            held = 0 if layer > 0 else steps - 1
            row = jnp.where(at_layer == layer, step, held)
            return (row + lift * core_ref[0], 0)

        return pl.BlockSpec((block, grads[idx].shape[1]), where)

    whole = pl.BlockSpec((1, block, columns), lambda layer, step, core_ref: (layer, step, 0))
    shape = jax.ShapeDtypeStruct(master.shape, F32)
    return pl.pallas_call(
        partial(adam_kernel, kinds, ring, count),
        grid_spec=pltpu.PrefetchScalarGridSpec(
            num_scalar_prefetch=1,
            grid=(layers, steps),
            in_specs=[pl.BlockSpec(memory_space=pltpu.SMEM)]
            + [grad_spec(idx) for idx in range(len(grads))]
            + [whole] * 3,
            out_specs=[whole] * 5,
        ),
        out_shape=[shape] * 4 + [jax.ShapeDtypeStruct(master.shape, BF)],
        compiler_params=pltpu.CompilerParams(vmem_limit_bytes=VMEM_LIMIT),
        cost_estimate=pl.CostEstimate(
            flops=20 * master.size, bytes_accessed=32 * master.size, transcendentals=master.size
        ),
        name="update",
    )(core.reshape(1).astype(jnp.int32), factor.reshape(1), *grads, master, first, second)


def norm_parts(hidden):
    center = hidden - jnp.mean(hidden, axis=-1, keepdims=True)
    spread = jnp.mean(center * center, axis=-1, keepdims=True)
    inverse = lax.rsqrt(spread + 1e-06)
    return center * inverse, inverse


def gelu_and_slope(upward):
    erf_part = 0.5 * (1.0 + lax.erf(upward * (1.0 / math.sqrt(2.0))))
    density = jnp.exp(-0.5 * upward * upward) * (1.0 / math.sqrt(2.0 * math.pi))
    return upward * erf_part, erf_part + upward * density


def dot(left, right):
    return jnp.dot(left, right, preferred_element_type=F32)


def dot_nt(left, right):
    return lax.dot_general(left, right, NT, preferred_element_type=F32)


def dot_tn(left, right):
    return lax.dot_general(left, right, (((0,), (0,)), ((), ())), preferred_element_type=F32)


def rotation_tables(packed):
    lane = lax.broadcasted_iota(jnp.int32, packed.shape, 1)
    first = lane % HEAD_DIM < HEAD_DIM // 2
    turned = pltpu.roll(packed, HEAD_DIM // 2, 1)
    return jnp.where(first, packed, turned), jnp.where(first, -turned, packed)


def each_block(count, body):
    @pl.loop(0, count)
    def _(step):
        body(aligned(step * ROWS_Q, ROWS_Q))


class Forward:
    def __init__(self, at, refs, layers):
        self.at, self.refs, self.layers = at, refs, layers
        self.blocks = refs.res.shape[0] // ROWS_Q
        self.pairs = refs.mixed.shape[1] // PAIR
        self.saves, self.loads, self.slot = [], [], 0
        self.mixed_copies, self.part_copies = {}, {}

    def save(self, src, dst):
        copy = pltpu.make_async_copy(src, dst, self.refs.save_sem.at[self.slot])
        self.slot += 1
        copy.start()
        self.saves.append(copy)
        return copy

    def settle(self):
        for copy in self.saves:
            copy.wait()
        self.saves = []

    def bring(self, pairs):
        for src, dst in pairs:
            copy = pltpu.make_async_copy(src, dst, self.refs.save_sem.at[self.slot])
            self.slot += 1
            copy.start()
            self.loads.append(copy)

    def arrive(self):
        for copy in self.loads:
            copy.wait()
        self.loads = []

    def vec(self, layer, row, width):
        return self.refs.vecs[layer, row : row + 1, 0:width]

    def unpack_vectors(self):
        refs, at = self.refs, self.at
        ring = at.ring
        per_shard = refs.vec_rows
        for layer in range(self.layers):
            places = [(row, row // 8, row % 8) for row in range(48)]
            for pair in range(ring):
                for kind in range(3):
                    places.append((48 + kind * 8 + 2 * pair + at.core, 6, pair * 3 + kind))
                for part in range(4):
                    places.append((72 + (2 * pair + at.core) * 4 + part, 7, pair * 4 + part))
            for source, row, block in places:
                shard, entry = source // per_shard, layer * per_shard + source % per_shard
                if not isinstance(source, int):
                    shard = lax.div(source, per_shard)
                    entry = layer * per_shard + lax.rem(source, per_shard)
                refs.vecs[layer, row : row + 1, block * 128 : (block + 1) * 128] = refs.vec_out[
                    shard, pl.ds(entry, 1), :
                ]

    def normed(self, rows, layer, first):
        hidden = self.refs.res[rows, :]
        scaled, _ = norm_parts(hidden)
        width = hidden.shape[1]
        return (scaled * self.vec(layer, first, width) + self.vec(layer, first + 1, width)).astype(BF)

    def load_qkv(self, weight):
        self.bring([(weight, self.refs.w_one.at[:, pl.ds(0, weight.shape[1])])])

    def load_proj(self, own, other):
        half, target = own.shape[0], self.refs.w_two
        self.bring([(own, target.at[pl.ds(0, half), :]), (other, target.at[pl.ds(half, half), :])])

    def load_units(self, up_weight, down_weight):
        self.bring([(up_weight, self.refs.w_one), (down_weight, self.refs.w_two)])

    def qkv(self, layer):
        refs = self.refs
        self.settle()
        self.arrive()

        def body(rows):
            normed = self.normed(rows, layer, 0)
            refs.norm[rows, :] = normed
            for pair in range(self.pairs):
                cols = slice(pair * 3 * PAIR, (pair + 1) * 3 * PAIR)
                block = dot(normed, refs.w_one[:, cols]) + refs.vecs[layer, 6:7, cols]
                cosine, sine = rotation_tables(refs.tables[rows, :])
                for kind in range(3):
                    part = block[:, kind * PAIR : (kind + 1) * PAIR]
                    if kind < 2:
                        part = part * cosine + swap_halves(part) * sine
                    start = pair * 3 * PAIR + kind * PAIR
                    refs.low[rows, start : start + PAIR] = part.astype(BF)

        each_block(self.blocks, body)
        self.save(refs.norm, refs.normed_out[layer])
        self.save(refs.low, refs.low_out[layer])

    def attend(self, layer, pair):
        refs = self.refs
        base = pair * 3 * PAIR
        key_cols, value_cols = [
            slice(base + kind * PAIR, base + (kind + 1) * PAIR) for kind in (1, 2)
        ]

        def body(rows):
            block = refs.low[rows, base : base + PAIR] * jnp.asarray(HEAD_DIM**-0.5, BF)
            outs = []
            for head in range(2):
                scores = dot_nt(head_mask(block, head), refs.low[:, key_cols])
                top = jnp.max(scores, axis=1, keepdims=True)
                exponent = jnp.exp(scores - top)
                total = jnp.sum(exponent, axis=1, keepdims=True)
                sums = jnp.broadcast_to(top + jnp.log(total), (ROWS_Q, PAIR)).T
                refs.lse_out[layer, pair, head : head + 1, rows] = sums[0:1]
                probs = (exponent * (1.0 / total)).astype(BF)
                outs.append(dot(probs, refs.low[:, value_cols]))
            lane = lax.broadcasted_iota(jnp.int32, outs[0].shape, 1)
            refs.mixed[rows, pair * PAIR : (pair + 1) * PAIR] = jnp.where(
                lane < HEAD_DIM, outs[0], outs[1]
            ).astype(BF)

        each_block(self.blocks, body)
        slot = layer * (self.pairs + 2) + pair
        cols = pl.ds(pair * PAIR, PAIR)
        copy = remote(
            refs.mixed.at[:, cols],
            refs.mixed_other.at[:, cols],
            refs.x_send.at[slot],
            refs.x_recv.at[slot],
            self.at.other,
        )
        copy.start()
        self.mixed_copies[layer, pair] = copy

    def project(self, layer):
        refs = self.refs
        half = refs.mixed.shape[1]
        self.arrive()
        self.settle()
        for pair in range(self.pairs):
            self.mixed_copies[layer, pair].wait()
        width = refs.res.shape[1]

        def body(rows):
            total = dot(refs.mixed[rows, :], refs.w_two[0:half, :])
            total = total + dot(refs.mixed_other[rows, :], refs.w_two[half : 2 * half, :])
            refs.res[rows, :] = refs.res[rows, :] + total + self.vec(layer, 4, width)
            refs.norm[rows, :] = self.normed(rows, layer, 2)

        each_block(self.blocks, body)
        self.save(refs.mixed, refs.mixed_out[layer])
        self.save(refs.res, refs.after_out[layer])
        self.save(refs.norm, refs.normed_two_out[layer])

    def hidden_units(self, layer, half):
        refs = self.refs
        if half == 0:
            self.settle()
            self.arrive()
        width = refs.res.shape[1]
        tiles = refs.w_one.shape[1] // 512
        blocks = self.blocks // 2

        @pl.loop(half * blocks, (half + 1) * blocks)
        def _(step):
            rows = aligned(step * ROWS_Q, ROWS_Q)

            @pl.loop(0, tiles)
            def _(tile):
                cols = aligned(tile * 512, 512)
                upward = dot(refs.norm[rows, :], refs.w_one[:, cols]) + refs.vecs[layer, 7:8, cols]
                active, slope = gelu_and_slope(upward)
                refs.act[rows, cols] = active.astype(BF)
                refs.slope[rows, cols] = slope.astype(BF)

            part = dot(refs.act[rows, :], refs.w_two[...])
            refs.res[rows, :] = refs.res[rows, :] + part + self.vec(layer, 5, width)
            refs.part[rows, :] = part.astype(BF)

        rows = pl.ds(half * blocks * ROWS_Q, blocks * ROWS_Q)
        slot = layer * (self.pairs + 2) + self.pairs + half
        copy = remote(
            refs.part.at[rows, :],
            refs.part_other.at[rows, :],
            refs.x_send.at[slot],
            refs.x_recv.at[slot],
            self.at.other,
        )
        copy.start()
        self.part_copies[layer, half] = copy
        if half == 1:
            self.save(refs.act, refs.active_out[layer])
            self.save(refs.slope, refs.slope_out[layer])

    def join(self, layer):
        refs = self.refs
        for half in range(2):
            self.part_copies[layer, half].wait()

        def body(rows):
            refs.res[rows, :] = refs.res[rows, :] + refs.part_other[rows, :].astype(F32)

        each_block(self.blocks, body)
        self.save(refs.res, refs.result_out[layer])


WEIGHTS = ("qkv", "proj", "up", "down")


def forward_kernel(names, layers, vec_rows, *operands):
    refs = SimpleNamespace(**dict(zip(names, operands)))
    for name in (*WEIGHTS, "proj_two", "normed", "low", "mixed", "after", "normed_two", "active", "slope", "result"):
        label = name + "_out"
        setattr(refs, label, [getattr(refs, label + str(layer)) for layer in range(layers)])
    refs.vec_rows = vec_rows
    at = Places()
    ring, seq, chip, core = at.ring, at.seq, at.chip, at.core
    full = {name: getattr(refs, name + "_full") for name in WEIGHTS}
    source = {name: getattr(refs, name + "_in") for name in WEIGHTS}
    slabs = {name: getattr(refs, name + "_slab") for name in WEIGHTS}
    outs = {name: getattr(refs, name + "_out") for name in WEIGHTS}
    items = [(name, layer) for layer in range(layers) for name in WEIGHTS]
    loads = {}

    def start_load(name, layer):
        copy = pltpu.make_async_copy(
            source[name].at[layer], full[name], refs.l_in.at[items.index((name, layer))]
        )
        copy.start()
        loads[name, layer] = copy

    for name in WEIGHTS:
        start_load(name, 0)
    barrier = pltpu.get_barrier_semaphore()
    for target in (at.other, at.up, at.down):
        pl.semaphore_signal(barrier, inc=1, device_id=target, device_id_type=pl.DeviceIdType.MESH)
    for step in range(1, 4):
        for half in range(2):
            pl.semaphore_signal(
                barrier,
                inc=1,
                device_id={"fsdp": 2 * chip + half, "seq": seq ^ step},
                device_id_type=pl.DeviceIdType.MESH,
            )
    pl.semaphore_wait(barrier, 9)

    length = refs.clip_in.shape[1]
    token_core = seq // 2
    token_rows = aligned(seq * length, length)
    stays = core == token_core

    class Move:
        def __init__(self, base, pairs):
            self.base, self.pairs, self.copies = base, pairs, []

        def start(self):
            for turn in range(2):
                target = {"seq": 2 * core + turn, "fsdp": 2 * chip + token_core}
                away = jnp.logical_not(jnp.logical_and(stays, lax.rem(seq, 2) == turn))
                copies = [
                    remote(
                        src.at[turn],
                        place(seq),
                        refs.m_send.at[self.base + 2 * turn + idx],
                        refs.m_recv.at[self.base + 2 * lax.rem(seq, 2) + idx],
                        target,
                    )
                    for idx, (src, place) in enumerate(self.pairs)
                ]
                self.copies.append((away, copies))

                @pl.when(away)
                def _(copies=copies):
                    for copy in copies:
                        copy.start()

            @pl.when(stays)
            def _():
                for idx, (src, place) in enumerate(self.pairs):
                    bounce = refs.clip_slab if idx == 0 else refs.table_slab
                    sem = refs.m_load.at[self.base // 6 * 2 + idx]
                    load = pltpu.make_async_copy(src.at[lax.rem(seq, 2)], bounce, sem)
                    load.start()
                    load.wait()
                    store = pltpu.make_async_copy(bounce, place(seq), sem)
                    store.start()
                    store.wait()

        def swap(self):
            for part in range(2):
                came = jnp.logical_not(jnp.logical_and(stays, lax.rem(seq, 2) == part))

                @pl.when(came)
                def _(part=part):
                    for idx, (src, place) in enumerate(self.pairs):
                        remote(
                            src.at[0],
                            place(2 * core + part),
                            refs.m_send.at[self.base],
                            refs.m_recv.at[self.base + 2 * part + idx],
                            at.other,
                        ).wait_recv()

            self.swaps = []
            for idx, (src, place) in enumerate(self.pairs):
                for part in range(2):
                    slot = 24 + self.base // 6 * 4 + 2 * idx + part
                    ref = place(2 * core + part)
                    self.swaps.append(
                        remote(ref, ref, refs.m_send.at[slot], refs.m_recv.at[slot], at.other)
                    )
            for copy in self.swaps:
                copy.start()

        def arrived(self):
            for copy in self.swaps:
                copy.wait_recv()

        def drain(self):
            for copy in self.swaps:
                copy.wait_send()
            for away, copies in self.copies:

                @pl.when(away)
                def _(copies=copies):
                    for copy in copies:
                        copy.wait_send()

    def chunk_of(ref):
        return lambda number: ref.at[aligned(number * length, length), :]

    tokens = Move(0, [(refs.clip_in, chunk_of(refs.clip_out)), (refs.table_in, chunk_of(refs.table_out))])
    cotangents = Move(6, [(refs.cot_in, chunk_of(refs.cot_out))])
    tokens.start()

    refs.vec_out[2 * chip + core] = refs.vec_in[...]
    vec_swap = remote(
        refs.vec_in, refs.vec_out.at[2 * chip + core], refs.m_send.at[16], refs.m_recv.at[16], at.other
    )
    vec_swap.start()
    vec_copies = [vec_swap]

    def vec_hop(hop):
        vec_copies[-1].wait_recv()
        ref = refs.vec_out.at[pl.ds(2 * at.back(hop), 2)]
        slot = 17 + hop
        copy = remote(ref, ref, refs.m_send.at[slot], refs.m_recv.at[slot], at.up)
        copy.start()
        vec_copies.append(copy)

    def place(name, layer, chip_at, part):
        slab = slabs[name].shape[1]
        if part is None:
            return outs[name][layer].at[aligned(chip_at * slab, slab), :]
        size = slab // 4
        return outs[name][layer].at[aligned(chip_at * slab + part * size, size), :]

    swaps, prepared, stores = {}, [], []

    def prepare():
        if len(prepared) == len(items):
            return
        idx = len(prepared)
        name, layer = items[idx]
        prepared.append(name)
        slab = slabs[name]
        loads[name, layer].wait()
        swaps[idx] = None
        if name in ("down", "proj"):
            slab[layer] = full[name][...].astype(BF)
        else:
            away, kinds = (refs.qkv_away, 3) if name == "qkv" else (refs.up_away, 1)
            half, columns = full[name].shape
            width = columns // (kinds * 2 * ring)
            rows = aligned(core * half, half)
            for pair in range(ring):
                for kind in range(kinds):
                    cols = slice((pair * kinds + kind) * width, (pair * kinds + kind + 1) * width)
                    for mine in (True, False):
                        which = core if mine else 1 - core
                        start = (kind * 2 * ring + 2 * pair + which) * width
                        block = full[name][:, aligned(start, width)].astype(BF)
                        if mine:
                            slab[layer, rows, cols] = block
                        else:
                            away[layer, :, cols] = block
            swaps[idx] = remote(
                away.at[layer],
                slab.at[layer, rows, :],
                refs.c_send.at[idx],
                refs.c_recv.at[idx],
                at.other,
            )
            swaps[idx].start()
        if layer + 1 < layers:
            start_load(name, layer + 1)

    hops = ring - 1
    order = []
    for first in range(0, len(items), 2):
        for hop in range(hops):
            order += [(first, hop), (first + 1, hop)]
    z_copies, plane, far, proj_swaps = {}, {}, {}, {}

    def begin(idx):
        name, layer = items[idx]
        if swaps[idx] is not None:
            swaps[idx].wait_recv()
        store = pltpu.make_async_copy(
            slabs[name].at[layer], place(name, layer, chip, None), refs.l_out.at[idx]
        )
        store.start()
        stores.append(store)

    def z_copy(idx, hop):
        name, layer = items[idx]
        part = None if name == "proj" else seq
        target = place(name, layer, at.back(hop), part)
        from_ref = target
        if hop == 0:
            from_ref = slabs[name].at[layer]
            if part is not None:
                size = slabs[name].shape[1] // 4
                from_ref = slabs[name].at[layer, aligned(seq * size, size), :]
        slot = idx * hops + hop
        copy = remote(from_ref, target, refs.z_send.at[slot], refs.z_recv.at[slot], at.up)
        copy.start()
        z_copies[idx, hop] = copy

    def plane_copies(idx, hop):
        name, layer = items[idx]
        ref = place(name, layer, at.back(hop + 1), seq)
        slot = 2 * (idx * hops + hop)
        plane[idx, hop] = [
            remote(ref, ref, refs.p_send.at[slot], refs.p_recv.at[slot], at.over_x),
            remote(ref, ref, refs.p_send.at[slot + 1], refs.p_recv.at[slot + 1], at.over_y),
        ]
        for copy in plane[idx, hop]:
            copy.start()

    def far_copies(idx, hop):
        name, layer = items[idx]
        slot = 2 * (idx * hops + hop)
        size = slabs[name].shape[1] // 4
        half = size // 2
        base = at.back(hop + 1) * 4 * size
        for copy in plane[idx, hop]:
            copy.wait_recv()
        made = []
        for turn, (origin, target) in enumerate(((at.near_y, at.over_x), (at.near_x, at.over_y))):
            ref = outs[name][layer].at[aligned(base + origin * size + turn * half, half), :]
            made.append(
                remote(ref, ref, refs.d_send.at[slot + turn], refs.d_recv.at[slot + turn], target)
            )
        far[idx, hop] = made
        for copy in made:
            copy.start()

    pending = []

    def flush(keep):
        while len(pending) > keep:
            far_copies(*pending.pop(0))

    def event(number):
        idx, hop = order[number]
        z_copies[idx, hop].wait_recv()
        if hop + 1 < hops:
            z_copy(idx, hop + 1)
        elif idx + 2 < len(items):
            begin(idx + 2)
            z_copy(idx + 2, 0)
        name, layer = items[idx]
        if name == "proj":
            flush(0)
            if hop + 1 == hops:
                stores[idx].wait()
                slot = len(items) + layer
                proj_swaps[layer] = remote(
                    outs["proj"][layer],
                    refs.proj_two_out[layer],
                    refs.c_send.at[slot],
                    refs.c_recv.at[slot],
                    at.other,
                )
                proj_swaps[layer].start()
        else:
            plane_copies(idx, hop)
            pending.append((idx, hop))
            flush(1)
        prepare()

    def complete(name, layer):
        idx = items.index((name, layer))
        if name == "proj":
            proj_swaps[layer].wait_recv()
            return
        stores[idx].wait()
        flush(0)
        for hop in range(hops):
            for copy in far[idx, hop]:
                copy.wait_recv()

    work = Forward(at, refs, layers)

    def take_tokens():
        tokens.arrived()
        vec_copies[-1].wait_recv()
        work.bring([(refs.clip_out, refs.res), (refs.table_out, refs.tables)])
        work.unpack_vectors()

    def load_qkv(layer):
        complete("qkv", layer)
        work.load_qkv(outs["qkv"][layer])

    def load_proj(layer):
        complete("proj", layer)
        work.load_proj(outs["proj"][layer], refs.proj_two_out[layer])

    def load_units(layer):
        complete("up", layer)
        complete("down", layer)
        work.load_units(outs["up"][layer], outs["down"][layer])

    prepare()
    prepare()
    begin(0)
    z_copy(0, 0)
    begin(1)
    z_copy(1, 0)
    prepare()
    prepare()
    per_layer = 4 * hops
    chunks = []
    for layer in range(layers):
        first = layer * per_layer + 2 * hops
        if layer == 0:
            chunks.append((first, take_tokens))
        chunks.append((first + 1, partial(load_qkv, layer)))
        chunks.append((first + 2, partial(work.qkv, layer)))
        chunks.append((first + 2, partial(load_proj, layer)))
        for pair in range(work.pairs):
            chunks.append((first + 2 + pair, partial(work.attend, layer, pair)))
        chunks.append((first + 7, partial(work.project, layer)))
        chunks.append((first + 7, partial(load_units, layer)))
        chunks.append((first + 8, partial(work.hidden_units, layer, 0)))
        chunks.append((first + 9, partial(work.hidden_units, layer, 1)))
        chunks.append((first + 10, partial(work.join, layer)))
    for number in range(len(order)):
        while chunks and chunks[0][0] <= number:
            chunks.pop(0)[1]()
        if number == 2:
            tokens.swap()
        if 3 <= number < 3 + hops:
            vec_hop(number - 3)
        if number == per_layer:
            cotangents.start()
        if number == per_layer + 6:
            cotangents.swap()
        event(number)
    flush(0)
    for _, chunk in chunks:
        chunk()

    work.settle()
    cotangents.arrived()
    for made in plane.values():
        for copy in made:
            copy.wait_send()
    for made in far.values():
        for copy in made:
            copy.wait_send()
    for copy in z_copies.values():
        copy.wait_send()
    for copy in swaps.values():
        if copy is not None:
            copy.wait_send()
    for copy in proj_swaps.values():
        copy.wait_send()
    for copy in vec_copies:
        copy.wait_send()
    tokens.drain()
    cotangents.drain()


def forward(qkv, up, down, proj, clips, cots, tables, vectors, vec_rows):
    layers, rows, width = proj.shape
    parts = lax.axis_size("fsdp")
    ring = parts // 2
    count, hops = 4 * layers, ring - 1
    length = 4 * clips.shape[1]
    down_rows = down.shape[1]
    qkv_half, up_half = qkv.shape[2] // 2, up.shape[2] // 2
    pairs = qkv_half // (3 * PAIR)
    inputs = {
        "qkv_in": qkv, "up_in": up, "down_in": down, "proj_in": proj, "clip_in": clips, "cot_in": cots,
        "table_in": tables, "vec_in": vectors,
    }
    outputs = {}
    for layer in range(layers):
        for name, shape, dtype in (
            ("qkv", (parts * rows, qkv_half), BF),
            ("up", (parts * rows, up_half), BF),
            ("down", (ring * down_rows, width), BF),
            ("proj", (ring * rows, width), BF),
            ("proj_two", (ring * rows, width), BF),
            ("normed", (length, width), BF),
            ("low", (length, qkv_half), BF),
            ("mixed", (length, pairs * PAIR), BF),
            ("after", (length, width), F32),
            ("normed_two", (length, width), BF),
            ("active", (length, up_half), BF),
            ("slope", (length, up_half), BF),
            ("result", (length, width), F32),
        ):
            outputs[name + "_out" + str(layer)] = (shape, dtype)
    outputs["clip_out"] = ((length, width), F32)
    outputs["cot_out"] = ((length, width), F32)
    outputs["table_out"] = ((length, PAIR), F32)
    outputs["vec_out"] = ((parts,) + vectors.shape, F32)
    outputs["vecs"] = ((layers, 8, up_half), F32)
    outputs["lse_out"] = ((layers, pairs, 8, length), F32)
    in_vmem = ("vec_in", "vec_out", "vecs", "lse_out")
    anywhere = pl.BlockSpec(memory_space=pl.ANY)
    vmem = pl.BlockSpec(memory_space=pltpu.VMEM)
    dma = pltpu.SemaphoreType.DMA
    scratch = {
        "qkv_full": pltpu.VMEM(qkv.shape[1:], F32),
        "up_full": pltpu.VMEM(up.shape[1:], F32),
        "down_full": pltpu.VMEM(down.shape[1:], F32),
        "proj_full": pltpu.VMEM(proj.shape[1:], F32),
        "qkv_away": pltpu.VMEM((layers, rows, qkv_half), BF),
        "up_away": pltpu.VMEM((layers, rows, up_half), BF),
        "qkv_slab": pltpu.VMEM((layers, 2 * rows, qkv_half), BF),
        "up_slab": pltpu.VMEM((layers, 2 * rows, up_half), BF),
        "down_slab": pltpu.VMEM((layers, down_rows, width), BF),
        "proj_slab": pltpu.VMEM((layers, rows, width), BF),
        "clip_slab": pltpu.VMEM(clips.shape[1:], F32),
        "table_slab": pltpu.VMEM(tables.shape[1:], F32),
        "res": pltpu.VMEM((length, width), F32),
        "tables": pltpu.VMEM((length, PAIR), F32),
        "norm": pltpu.VMEM((length, width), BF),
        "low": pltpu.VMEM((length, qkv_half), BF),
        "mixed": pltpu.VMEM((length, pairs * PAIR), BF),
        "mixed_other": pltpu.VMEM((length, pairs * PAIR), BF),
        "w_one": pltpu.VMEM((width, up_half), BF),
        "w_two": pltpu.VMEM((ring * down_rows, width), BF),
        "act": pltpu.VMEM((length, up_half), BF),
        "slope": pltpu.VMEM((length, up_half), BF),
        "part": pltpu.VMEM((length, width), BF),
        "part_other": pltpu.VMEM((length, width), BF),
        "z_send": dma((count * hops,)), "z_recv": dma((count * hops,)),
        "p_send": dma((2 * count * hops,)), "p_recv": dma((2 * count * hops,)),
        "d_send": dma((2 * count * hops,)), "d_recv": dma((2 * count * hops,)),
        "c_send": dma((count + layers,)), "c_recv": dma((count + layers,)),
        "l_in": dma((count,)), "l_out": dma((count,)),
        "m_send": dma((32,)), "m_recv": dma((32,)), "m_load": dma((4,)),
        "x_send": dma((layers * (pairs + 2),)), "x_recv": dma((layers * (pairs + 2),)),
        "save_sem": dma((16 * layers,)),
    }
    names = [*inputs, *outputs, *scratch]
    results = pl.pallas_call(
        partial(forward_kernel, names, layers, vec_rows),
        in_specs=[vmem if name in in_vmem else anywhere for name in inputs],
        out_specs=[vmem if name in in_vmem else anywhere for name in outputs],
        out_shape=[jax.ShapeDtypeStruct(*shape) for shape in outputs.values()],
        scratch_shapes=list(scratch.values()),
        compiler_params=pltpu.CompilerParams(
            collective_id=0, has_side_effects=True, vmem_limit_bytes=62 * 1024 * 1024
        ),
        cost_estimate=pl.CostEstimate(
            flops=60_000_000_000, bytes_accessed=600_000_000, transcendentals=0
        ),
        name="forward",
    )(*inputs.values())
    return SimpleNamespace(**dict(zip(outputs, results)))


def add_into(target, term):
    @pl.loop(0, target.shape[0] // ADD_ROWS)
    def _(step):
        at = aligned(step * ADD_ROWS, ADD_ROWS)
        target[at, :] = (target[at, :].astype(F32) + term[at, :].astype(F32)).astype(BF)


class Sems:
    def __init__(self, ref):
        self.ref, self.used = ref, 0

    def take(self):
        self.used += 1
        return self.ref.at[self.used - 1]


class Sum:
    def __init__(self, at, sems, refs, name, layer, z_first, x_first, compute):
        self.at, self.sems = at, sems
        self.own, self.one, self.two, self.three = [
            getattr(refs, name + part) for part in ("_own", "_one", "_two", "_three")
        ]
        self.stage = getattr(refs, name + "_stage" + str(layer))
        self.arrive = getattr(refs, name + "_arrive" + str(layer), None)
        self.z_first, self.x_first, self.compute = z_first, x_first, compute
        self.rows = self.two.shape[1]
        self.sends, self.slot_sends = [], [[], []]
        self.first, self.second, self.hop = {}, {}, {}
        self.swap = None

    def make(self, src, dst, target, slot=None):
        copy = remote(src, dst, self.sems[0].take(), self.sems[1].take(), target)
        copy.start()
        (self.sends if slot is None else self.slot_sends[slot]).append(copy)
        return copy

    def pieces(self, mine):
        at = self.at
        if self.x_first:
            side = at.at_x if mine else 1 - at.at_x
            return [(side, 1), (2 + side, 1)]
        return [(2 * (at.at_y if mine else 1 - at.at_y), 2)]

    def tile(self, tile):
        slot = tile % 2
        for copy in self.slot_sends[slot]:
            copy.wait_send()
        self.slot_sends[slot] = []
        self.compute(tile, self.own.at[slot])

    def start(self, tile):
        self.tile(tile)
        slot = tile % 2
        if self.z_first:
            self.hop[0] = self.make(self.own.at[slot], self.three.at[0], self.at.up, slot)
        else:
            self.plane_one(tile, self.own.at[slot], slot)

    def plane_one(self, tile, source, slot=None):
        target = self.at.over_x if self.x_first else self.at.over_y
        place, made = 0, []
        for first, count in self.pieces(False):
            size = count * self.rows
            made.append(
                self.make(
                    source.at[aligned(first * self.rows, size, self.rows), :],
                    self.one.at[tile, pl.ds(place, size), :],
                    target,
                    slot,
                )
            )
            place += size
        self.first[tile] = made

    def plane_two(self, tile, source):
        for copy in self.first[tile]:
            copy.wait_recv()
        place = 0
        for first, count in self.pieces(True):
            size = count * self.rows
            add_into(
                self.one.at[tile, pl.ds(place, size), :],
                source.at[aligned(first * self.rows, size, self.rows), :],
            )
            place += size
        at = self.at
        target, keep = (at.over_y, at.at_y) if self.x_first else (at.over_x, at.at_x)
        self.second[tile] = self.make(
            self.one.at[tile, aligned((1 - keep) * self.rows, self.rows), :],
            self.two.at[tile],
            target,
        )

    def plane_three(self, tile):
        keep = self.at.at_y if self.x_first else self.at.at_x
        self.second[tile].wait_recv()
        add_into(self.two.at[tile], self.one.at[tile, aligned(keep * self.rows, self.rows), :])

    def middle(self, tile):
        self.plane_two(tile, self.own.at[tile % 2])

    def finish(self, tile):
        self.plane_three(tile)
        if tile > 0:
            self.hop[tile - 1].wait_recv()
            add_into(self.two.at[tile], self.three.at[tile - 1])
        if tile < self.at.ring - 1:
            self.hop[tile] = self.make(self.two.at[tile], self.three.at[tile], self.at.up)
        else:
            self.gather()

    def ring_step(self, tile):
        self.tile(tile)
        self.hop[tile - 1].wait_recv()
        total = self.three.at[tile - 1]
        add_into(total, self.own.at[tile % 2])
        if tile == self.at.ring - 1:
            self.plane_one(0, total)
        else:
            self.hop[tile] = self.make(total, self.three.at[tile], self.at.up)

    def slab_middle(self):
        self.plane_two(0, self.three.at[self.at.ring - 2])

    def slab_finish(self):
        self.plane_three(0)
        self.gather()

    def total(self):
        return self.two.at[0 if self.z_first else self.at.ring - 1]

    def place(self, quarter, turn=0, size=None):
        size = size or self.rows
        return self.stage.at[aligned(quarter * self.rows + turn * size, size), :]

    def gather(self):
        at = self.at
        self.store = pltpu.make_async_copy(self.total(), self.place(at.seq), self.sems[2].take())
        self.store.start()
        self.near = [
            self.make(self.total(), self.place(at.seq), at.over_x),
            self.make(self.total(), self.place(at.seq), at.over_y),
        ]

    def gather_far(self):
        at = self.at
        for copy in self.near:
            copy.wait_recv()
        half = self.rows // 2
        self.far = []
        for turn, (origin, target) in enumerate(((at.near_y, at.over_x), (at.near_x, at.over_y))):
            ref = self.place(origin, turn, half)
            self.far.append(self.make(ref, ref, target))

    def gather_end(self):
        at = self.at
        self.store.wait()
        for copy in self.far:
            copy.wait_recv()
        if self.arrive is not None:
            half = 2 * self.rows
            self.swap = self.make(
                self.stage.at[aligned((1 - at.core) * half, half), :], self.arrive, at.other
            )

    def drain(self):
        if self.swap is not None:
            self.swap.wait_recv()
        for copy in self.sends + self.slot_sends[0] + self.slot_sends[1]:
            copy.wait_send()
        self.sends, self.slot_sends = [], [[], []]


class VectorSum:
    def __init__(self, at, sems, source, got, hop, total):
        self.at, self.sems = at, sems
        self.got, self.hop, self.total = got, hop, total
        self.copies, self.step = [], 0
        self.partners = (at.other, at.over_x, at.over_y)

    def send(self, src, dst, target):
        copy = remote(src, dst, self.sems[0].take(), self.sems[1].take(), target)
        copy.start()
        self.copies.append(copy)

    def advance(self):
        idx, at = self.step, self.at
        self.step += 1
        if idx == 0:
            self.send(self.total.at[0], self.got.at[0], self.partners[0])
            return
        self.copies[-1].wait_recv()
        if idx <= 3:
            self.total[idx] = self.total[idx - 1] + self.got[idx - 1]
            if idx < 3:
                self.send(self.total.at[idx], self.got.at[idx], self.partners[idx])
            else:
                self.send(self.total.at[3, at.back(1)], self.hop.at[0], at.up)
            return
        hop = idx - 3
        self.hop[hop - 1] = self.hop[hop - 1] + self.total[3, at.back(hop + 1)]
        if hop < at.ring - 1:
            self.send(self.hop.at[hop - 1], self.hop.at[hop], at.up)


class Backward:
    def __init__(self, at, refs, layers):
        self.at, self.refs, self.layers = at, refs, layers
        self.blocks = refs.grad.shape[0] // ROWS_Q
        self.pairs = refs.low.shape[1] // (3 * PAIR)
        self.slot = 0
        self.part_copies, self.loads = {}, {}

    def prefetch(self, key, pairs):
        self.loads[key] = self.bring(pairs)

    def arrive(self, key):
        for copy in self.loads.pop(key):
            copy.wait()

    def prefetch_units(self, layer, which):
        refs = self.refs
        targets = {"down": refs.w_one, "up": refs.w_two, "slope": refs.ups}
        for name in which:
            self.prefetch((name, layer), [(self.saved(name, layer), targets[name])])

    def bring(self, pairs):
        copies = []
        for src, dst in pairs:
            copies.append(pltpu.make_async_copy(src, dst, self.refs.load_sem.at[self.slot]))
            self.slot += 1
        for copy in copies:
            copy.start()
        return copies

    def saved(self, name, layer):
        return getattr(self.refs, name + "_in" + str(layer))

    def add_vec(self, row, value):
        total = jnp.sum(value, axis=0, keepdims=True)
        width = value.shape[1]
        self.refs.vgrad[row : row + 1, 0:width] = self.refs.vgrad[row : row + 1, 0:width] + total

    def send_part(self, key, landing):
        refs = self.refs
        slot = len(self.part_copies)
        copy = remote(
            refs.part, landing, refs.x_send.at[slot], refs.x_recv.at[slot], self.at.other
        )
        copy.start()
        self.part_copies[key] = copy

    def units(self, layer):
        refs = self.refs
        if layer == self.layers - 1:
            self.arrive(("cot", 0))
        for name in ("down", "slope", "up"):
            self.arrive((name, layer))
        refs.vgrad[...] = jnp.zeros_like(refs.vgrad)
        tiles = refs.w_one.shape[0] // 512

        def body(rows):
            grad = refs.grad[rows, :]
            self.add_vec(5, grad)
            refs.grad_low[rows, :] = grad.astype(BF)

            @pl.loop(0, tiles)
            def _(tile):
                cols = aligned(tile * 512, 512)
                value = dot_nt(refs.grad_low[rows, :], refs.w_one[cols, :])
                value = value * refs.ups[rows, cols].astype(F32)
                total = jnp.sum(value, axis=0, keepdims=True)
                refs.vgrad[7:8, cols] = refs.vgrad[7:8, cols] + total
                refs.ups[rows, cols] = value.astype(BF)

            part = dot_nt(refs.ups[rows, :], refs.w_two[...])
            refs.part_f[rows, :] = part
            refs.part[rows, :] = part.astype(BF)

        each_block(self.blocks, body)
        self.send_part((layer, 0), refs.got_one)
        weight = refs.w_one.at[pl.ds(0, refs.mixed_grad.shape[1]), :]
        self.prefetch(("proj", layer), [(self.saved("proj", layer), weight)])

    def vec(self, layer, row, width):
        return self.refs.vecs[layer, row : row + 1, 0:width]

    def norm_blocks(self, layer, first, landing, source, use):
        refs = self.refs

        def copy_of(step):
            slot = lax.rem(step, 2)
            rows = aligned(step * ROWS_Q, ROWS_Q)
            return pltpu.make_async_copy(
                source.at[rows, :], refs.aux.at[slot], refs.aux_sem.at[slot]
            )

        copy_of(0).start()

        @pl.loop(0, self.blocks)
        def _(step):
            @pl.when(step + 1 < self.blocks)
            def _():
                copy_of(step + 1).start()

            copy_of(step).wait()
            rows = aligned(step * ROWS_Q, ROWS_Q)
            use(rows, self.norm_back(rows, layer, first, landing, refs.aux[lax.rem(step, 2)]))

    def norm_back(self, rows, layer, first, landing, hidden):
        refs = self.refs
        width = refs.grad.shape[1]
        part = refs.part_f[rows, :] + landing[rows, :].astype(F32)
        scaled, inverse = norm_parts(hidden)
        entry = part * self.vec(layer, first, width)
        mean_one = jnp.mean(entry, axis=-1, keepdims=True)
        mean_two = jnp.mean(entry * scaled, axis=-1, keepdims=True)
        self.add_vec(first, part * scaled)
        self.add_vec(first + 1, part)
        grad = refs.grad[rows, :] + inverse * (entry - mean_one - scaled * mean_two)
        refs.grad[rows, :] = grad
        return grad

    def after(self, layer):
        refs = self.refs
        half = refs.mixed_grad.shape[1]
        self.prefetch(("low", layer), [(self.saved("low", layer), refs.low)])
        self.arrive(("proj", layer))
        self.part_copies[layer, 0].wait()

        def body(rows, grad):
            self.add_vec(4, grad)
            low = grad.astype(BF)
            refs.after_low[rows, :] = low
            refs.mixed_grad[rows, :] = dot_nt(low, refs.w_one[0:half, :]).astype(BF)

        self.norm_blocks(layer, 2, refs.got_one, self.saved("after", layer), body)
        weight = refs.w_two.at[:, pl.ds(0, refs.low.shape[1])]
        self.prefetch(("qkv", layer), [(self.saved("qkv", layer), weight)])
        if layer > 0:
            self.prefetch_units(layer - 1, ("down",))

    def attend(self, layer, pair):
        refs = self.refs
        if pair == 0:
            self.arrive(("low", layer))
        base = pair * 3 * PAIR
        query_cols, key_cols, value_cols = [
            slice(base + kind * PAIR, base + (kind + 1) * PAIR) for kind in range(3)
        ]
        refs.keys_t[...] = refs.low[:, key_cols].astype(F32).T.astype(BF)
        scale = HEAD_DIM**-0.5
        refs.dk[...] = jnp.zeros_like(refs.dk)
        refs.dv[...] = jnp.zeros_like(refs.dv)

        def body(rows):
            block = refs.low[rows, query_cols]
            dout = refs.mixed_grad[rows, pair * PAIR : (pair + 1) * PAIR]
            outs = []
            for head in range(2):
                mine, dmine = head_mask(block, head), head_mask(dout, head)
                scores = dot_nt(refs.low[:, key_cols], mine * jnp.asarray(scale, BF))
                probs = jnp.exp(scores - refs.lse_in[layer, pair, head : head + 1, rows])
                prob_grad = dot_nt(refs.low[:, value_cols], dmine)
                delta = jnp.sum(probs * prob_grad, axis=0, keepdims=True)
                score_low = (probs * (prob_grad - delta) * scale).astype(BF)
                refs.dv[...] += dot(probs.astype(BF), dmine)
                refs.dk[...] += dot(score_low, mine)
                outs.append(dot(refs.keys_t[head * HEAD_DIM : (head + 1) * HEAD_DIM], score_low))
            refs.dq[rows, :] = jnp.concatenate(outs, axis=0).T

        each_block(self.blocks, body)

        def last(rows):
            cosine, sine = rotation_tables(refs.tables[rows, :])

            def back(item):
                item = item.astype(BF).astype(F32)
                return item * cosine - swap_halves(item) * sine

            parts = (
                back(refs.dq[rows, :]),
                back(refs.dk[rows, :]),
                refs.dv[rows, :].astype(BF).astype(F32),
            )
            for kind, part in enumerate(parts):
                cols = slice(base + kind * PAIR, base + (kind + 1) * PAIR)
                refs.vgrad[6:7, cols] = refs.vgrad[6:7, cols] + jnp.sum(part, axis=0, keepdims=True)
                refs.low[rows, cols] = part.astype(BF)

        each_block(self.blocks, last)

    def heads(self, layer):
        refs = self.refs
        width = refs.low.shape[1]
        self.arrive(("qkv", layer))

        def body(rows):
            part = dot_nt(refs.low[rows, :], refs.w_two[:, 0:width])
            refs.part_f[rows, :] = part
            refs.part[rows, :] = part.astype(BF)

        each_block(self.blocks, body)
        self.send_part((layer, 1), refs.got_two)
        if layer > 0:
            self.prefetch_units(layer - 1, ("up", "slope"))

    def entry(self, layer):
        refs = self.refs
        self.part_copies[layer, 1].wait()
        source = self.saved("entry", layer)
        self.norm_blocks(layer, 0, refs.got_two, source, lambda rows, grad: None)

    def weight_tile(self, name, layer):
        refs = self.refs
        stream = getattr(refs, name + "_stream")
        source, right = {
            "down": ("active", refs.grad_low),
            "up": ("normed_two", refs.ups),
            "proj": ("mixed", refs.after_low),
            "qkv": ("normed", refs.low),
        }[name]
        def fetch(tile, layer):
            rows = stream.shape[1]
            cols = aligned(self.at.back(tile + 1) * rows, rows)
            self.prefetch((name, "tile"), [(self.saved(source, layer).at[:, cols], stream)])

        def compute(tile, out):
            rows, columns = out.shape
            if (name, "tile") not in self.loads:
                fetch(tile, layer)
            self.arrive((name, "tile"))
            high, wide = min(rows, 256), min(columns, 512)

            @pl.loop(0, rows // high)
            def _(row):
                at_rows = aligned(row * high, high)

                @pl.loop(0, columns // wide)
                def _(column):
                    cols = aligned(column * wide, wide)
                    out[at_rows, cols] = dot_tn(stream[:, at_rows], right[:, cols]).astype(BF)

            if tile + 1 < self.at.ring:
                fetch(tile + 1, layer)
            elif layer > 0:
                fetch(0, layer - 1)

        return compute

    def vector_rows(self, target):
        refs, at = self.refs, self.at
        target[...] = jnp.zeros_like(target)
        per_chip = refs.vec_rows * 2
        keep = (at.core == 0).astype(F32)
        for row in range(48):
            source = refs.vgrad[row // 8 : row // 8 + 1, row % 8 * 128 : (row % 8 + 1) * 128]
            place = row % per_chip
            target[row // per_chip, place : place + 1, :] = source * keep
        places = []
        for pair in range(at.ring):
            for kind in range(3):
                places.append((48 + kind * 8 + 2 * pair + at.core, 6, pair * 3 + kind))
            for part in range(4):
                places.append((72 + (2 * pair + at.core) * 4 + part, 7, pair * 4 + part))
        for place, row, block in places:
            target[lax.div(place, per_chip), pl.ds(lax.rem(place, per_chip), 1), :] = refs.vgrad[
                row : row + 1, block * 128 : (block + 1) * 128
            ]


def squares_of(ref):
    rows, columns = ref.shape

    def body(step, total):
        part = ref[aligned(step * 16, 16), :].astype(F32)
        part = part * part
        part = part[0:8] + part[8:16]
        for column in range(0, columns, 128):
            total = total + part[:, column : column + 128]
        return total

    return lax.fori_loop(0, rows // 16, body, jnp.zeros((8, 128), F32))


def backward_kernel(names, layers, vec_rows, *operands):
    refs = SimpleNamespace(**dict(zip(names, operands)))
    refs.vec_rows = vec_rows
    at = Places()
    ring = at.ring
    sems = (Sems(refs.send_sem), Sems(refs.recv_sem), Sems(refs.store_sem))
    greet((at.other, at.over_x, at.over_y, at.down), 4)
    work = Backward(at, refs, layers)
    work.prefetch(("cot", 0), [(refs.cot_in, refs.grad)])
    work.prefetch_units(layers - 1, ("down", "slope", "up"))
    sums = {}
    for layer in range(layers):
        for name, z_first, x_first in (
            ("qkv", True, True),
            ("proj", True, False),
            ("up", False, True),
            ("down", False, False),
        ):
            sums[name, layer] = Sum(
                at, sems, refs, name, layer, z_first, x_first, work.weight_tile(name, layer)
            )
    vectors = [
        VectorSum(at, sems, None, refs.vec_got.at[layer], refs.vec_hop.at[layer], refs.vec_sum.at[layer])
        for layer in range(layers)
    ]
    refs.square_sum[0] = jnp.zeros((8, 128), F32)
    steps = []

    def free(sem):
        for target in (at.over_x, at.over_y, at.down):
            pl.semaphore_signal(sem, inc=1, device_id=target, device_id_type=pl.DeviceIdType.MESH)

    def wide_steps(layer):
        items = [sums["down", layer], sums["up", layer]]

        def turn(tile):
            for item in items:
                item.middle(tile)
            if tile + 2 < ring:
                for item in items:
                    item.start(tile + 2)
            if tile > 0:
                for item in items:
                    item.finish(tile - 1)

        def begin(tile):
            if tile == 0 and layer + 1 < layers:
                pl.semaphore_wait(refs.free_wide, 3)
            for item in items:
                item.start(tile)

        def end():
            for item in items:
                item.finish(ring - 1)

        def far():
            for item in items:
                item.gather_far()

        def close():
            for item in items:
                item.gather_end()
                refs.square_sum[0] = refs.square_sum[0] + squares_of(item.total())
            if layer > 0:
                for item in items:
                    item.drain()
                free(refs.free_wide)

        turns = [partial(begin, 0), partial(begin, 1)]
        turns += [partial(turn, tile) for tile in range(ring)]
        return turns + [end, far, close]

    def slab_steps(name, layer):
        item = sums[name, layer]

        def begin():
            item.start(0)

        def close():
            item.gather_end()
            refs.square_sum[0] = refs.square_sum[0] + squares_of(item.total())
            if layer > 0:
                item.drain()

        turns = [begin] + [partial(item.ring_step, tile) for tile in range(1, ring)]
        return turns + [item.slab_middle, item.slab_finish, item.gather_far, close]

    def run(steps, count=1):
        for _ in range(count):
            if steps:
                steps.pop(0)()

    late = []
    for layer in reversed(range(layers)):
        last = layer == 0
        wide, proj, qkv = wide_steps(layer), slab_steps("proj", layer), slab_steps("qkv", layer)
        work.units(layer)
        run(late, 3)
        run(wide, 2)
        run(late, 2)
        work.after(layer)
        run(late, 2)
        if layer + 1 == layers:
            run(proj)
        for pair in range(work.pairs):
            work.attend(layer, pair)
            run(wide)
            run(late, 3)
            if layer + 1 == layers and pair > 0:
                run(proj)
        while late:
            run(late)
        if layer + 1 < layers:
            free(refs.free_slab)
            pl.semaphore_wait(refs.free_slab, 3)
            run(proj)
        work.heads(layer)
        run(wide)
        run(proj)
        run(qkv)
        work.entry(layer)
        if last:
            save = pltpu.make_async_copy(refs.grad, refs.input_grad, sems[2].take())
            save.start()
        work.vector_rows(refs.vec_sum.at[layer, 0])
        run(qkv)
        run(wide)
        run(proj)
        vector = [vectors[layer].advance] * 7
        while proj or qkv or vector:
            late += wide[:1] + qkv[:1] + proj[:1] + vector[:1]
            qkv, proj, vector, wide = qkv[1:], proj[1:], vector[1:], wide[1:]
        late = late + wide
        wide = []
    while late:
        run(late)
    save.wait()
    total = refs.square_sum[0]
    for layer in range(layers):
        vec_total = refs.vec_hop[layer, ring - 2]
        refs.vec_out[layer] = vec_total
        part = vec_total * vec_total * 0.125
        for row in range(0, part.shape[0], 8):
            total = total + part[row : row + 8]
    refs.square_sum[0] = total
    copies = []

    def square_copy(src, dst, target):
        copy = remote(src, dst, sems[0].take(), sems[1].take(), target)
        copy.start()
        copies.append(copy)
        copy.wait_recv()

    for idx, target in enumerate((at.other, at.over_x, at.over_y)):
        square_copy(refs.square_sum.at[idx], refs.square_got.at[idx], target)
        refs.square_sum[idx + 1] = refs.square_sum[idx] + refs.square_got[idx]
    total = refs.square_sum[3]
    for hop in range(ring - 1):
        source = refs.square_sum.at[3] if hop == 0 else refs.square_got.at[2 + hop]
        square_copy(source, refs.square_got.at[3 + hop], at.up)
        total = total + refs.square_got[3 + hop]
    refs.square_out[...] = total
    for name in WEIGHTS:
        sums[name, 0].drain()
    for vector in vectors:
        for copy in vector.copies:
            copy.wait_send()
    for copy in copies:
        copy.wait_send()


def backward(kept, layers, vec_rows):
    ring = lax.axis_size("fsdp") // 2
    length, width = kept.cot_out.shape
    qkv_half, up_half = kept.low_out0.shape[1], kept.slope_out0.shape[1]
    half = kept.mixed_out0.shape[1]
    inputs = {
        "cot_in": kept.cot_out,
        "tables": kept.table_out,
        "vecs": kept.vecs,
        "lse_in": kept.lse_out,
    }
    for layer in range(layers):
        for name in (*WEIGHTS, "normed", "low", "mixed", "after", "normed_two", "active", "slope"):
            inputs[name + "_in" + str(layer)] = getattr(kept, name + "_out" + str(layer))
        entry = kept.clip_out if layer == 0 else getattr(kept, "result_out" + str(layer - 1))
        inputs["entry_in" + str(layer)] = entry
    slabs = {
        "qkv": (width // ring, qkv_half),
        "proj": (half // ring, width),
        "up": (width // ring, up_half),
        "down": (up_half // ring, width),
    }
    outputs, scratch = {}, {}
    dma, regular = pltpu.SemaphoreType.DMA, pltpu.SemaphoreType.REGULAR
    for name, (rows, columns) in slabs.items():
        for layer in range(layers):
            outputs[name + "_stage" + str(layer)] = ((rows, columns), BF)
            if name in ("qkv", "up"):
                outputs[name + "_arrive" + str(layer)] = ((rows // 2, columns), BF)
        z_first = name in ("qkv", "proj")
        tiles, quarter = 1 if z_first else ring, rows // 4
        scratch[name + "_stream"] = pltpu.VMEM((length, rows), BF)
        scratch[name + "_own"] = pltpu.VMEM((2, rows, columns), BF)
        scratch[name + "_one"] = pltpu.VMEM((tiles, 2 * quarter, columns), BF)
        scratch[name + "_two"] = pltpu.VMEM((tiles, quarter, columns), BF)
        scratch[name + "_three"] = pltpu.VMEM(
            (ring - 1, rows if z_first else quarter, columns), BF
        )
    outputs["input_grad"] = ((length, width), F32)
    outputs["vec_out"] = ((layers, 32, 128), F32)
    outputs["square_out"] = ((8, 128), F32)
    scratch |= {
        "grad": pltpu.VMEM((length, width), F32),
        "aux": pltpu.VMEM((2, ROWS_Q, width), F32),
        "aux_sem": dma((2,)),
        "part_f": pltpu.VMEM((length, width), F32),
        "grad_low": pltpu.VMEM((length, width), BF),
        "after_low": pltpu.VMEM((length, width), BF),
        "part": pltpu.VMEM((length, width), BF),
        "got_one": pltpu.VMEM((length, width), BF),
        "got_two": pltpu.VMEM((length, width), BF),
        "ups": pltpu.VMEM((length, up_half), BF),
        "w_one": pltpu.VMEM((up_half, width), BF),
        "w_two": pltpu.VMEM((width, up_half), BF),
        "low": pltpu.VMEM((length, qkv_half), BF),
        "mixed_grad": pltpu.VMEM((length, half), BF),
        "keys_t": pltpu.VMEM((PAIR, length), BF),
        "dq": pltpu.VMEM((length, PAIR), F32),
        "dk": pltpu.VMEM((length, PAIR), F32),
        "dv": pltpu.VMEM((length, PAIR), F32),
        "vgrad": pltpu.VMEM((8, up_half), F32),
        "vec_got": pltpu.VMEM((layers, 3, ring, 32, 128), F32),
        "vec_hop": pltpu.VMEM((layers, ring - 1, 32, 128), F32),
        "vec_sum": pltpu.VMEM((layers, 4, ring, 32, 128), F32),
        "square_got": pltpu.VMEM((3 + ring - 1, 8, 128), F32),
        "square_sum": pltpu.VMEM((4, 8, 128), F32),
        "send_sem": dma((120 * layers,)),
        "recv_sem": dma((120 * layers,)),
        "store_sem": dma((8 * layers,)),
        "load_sem": dma((32 * layers,)),
        "x_send": dma((2 * layers,)),
        "x_recv": dma((2 * layers,)),
        "free_wide": regular,
        "free_slab": regular,
    }
    in_vmem = ("tables", "vecs", "lse_in", "vec_out", "square_out")
    anywhere = pl.BlockSpec(memory_space=pl.ANY)
    vmem = pl.BlockSpec(memory_space=pltpu.VMEM)
    names = [*inputs, *outputs, *scratch]
    results = pl.pallas_call(
        partial(backward_kernel, names, layers, vec_rows),
        in_specs=[vmem if name in in_vmem else anywhere for name in inputs],
        out_specs=[vmem if name in in_vmem else anywhere for name in outputs],
        out_shape=[jax.ShapeDtypeStruct(*shape) for shape in outputs.values()],
        scratch_shapes=list(scratch.values()),
        compiler_params=pltpu.CompilerParams(
            collective_id=1, has_side_effects=True, vmem_limit_bytes=63 * 1024 * 1024
        ),
        cost_estimate=pl.CostEstimate(
            flops=100_000_000_000, bytes_accessed=600_000_000, transcendentals=0
        ),
        name="backward",
    )(*inputs.values())
    return SimpleNamespace(**dict(zip(outputs, results)))


def fast_device(
    clip_tokens,
    patch_coords,
    out_cotangent,
    vector_params,
    qkv_weight,
    proj_weight,
    up_weight,
    down_weight,
    first_vector,
    first_qkv,
    first_proj,
    first_up,
    first_down,
    second_vector,
    second_qkv,
    second_proj,
    second_up,
    second_down,
):
    masters = (vector_params, qkv_weight, proj_weight, up_weight, down_weight)
    firsts = (first_vector, first_qkv, first_proj, first_up, first_down)
    seconds = (second_vector, second_qkv, second_proj, second_up, second_down)
    layer_count = vector_params.shape[0]
    batch_local, chunk_len = clip_tokens.shape[:2]
    seq_parts = lax.axis_size("seq")
    parts = lax.axis_size("fsdp")
    ring = parts // 2
    seq = lax.axis_index("seq")
    shard = lax.axis_index("fsdp")
    core = lax.rem(shard, 2)
    even = lax.rem(seq, 2) == 0

    def from_clips(item):
        mine = pick(item.reshape((2, 2, chunk_len) + item.shape[1:]), core)
        pieces = [None, None]
        for turn in range(2):
            piece = jnp.where(even, mine[turn], mine[1 - turn])
            pairs = []
            for src_seq in range(seq_parts):
                for src in range(parts):
                    dst_seq = 2 * (src % 2) + (src_seq + turn) % 2
                    dst = src - src % 2 + src_seq // 2
                    pairs.append((dst_seq * parts + dst, src_seq * parts + src))
            pieces[turn] = lax.ppermute(piece, ("seq", "fsdp"), pairs)
        return jnp.where(
            even, jnp.stack([pieces[0], pieces[1]]), jnp.stack([pieces[1], pieces[0]])
        )

    tables = []
    for idx in range(batch_local):
        cosine, sine = rotary_tables(patch_coords[:, idx], HEAD_DIM // 2)
        tables.append(jnp.concatenate([cosine, sine, cosine, sine], axis=1))
    share = vector_params.shape[1]
    vector_rows = vector_params.astype(BF).astype(F32).reshape(-1, 128)
    vector_rows = jnp.pad(vector_rows, ((0, -vector_rows.shape[0] % 8), (0, 0)))
    kept = forward(
        qkv_weight,
        up_weight,
        down_weight,
        proj_weight,
        clip_tokens,
        out_cotangent,
        jnp.stack(tables),
        vector_rows,
        share // 128,
    )
    block_output = from_clips(getattr(kept, "result_out" + str(layer_count - 1)))

    back = backward(kept, layer_count, share // 128)
    input_grad = from_clips(back.input_grad)

    clip_count = batch_local * parts
    norm_value = jnp.sqrt(jnp.sum(back.square_out)) / clip_count
    param_count = sum(master.size for master in masters) * parts
    factor = jnp.minimum(1.0, CLIP_RATIO * math.sqrt(float(param_count)) / (norm_value + 1e-06))

    vector_total = back.vec_out.reshape(layer_count, -1)[:, : 2 * share]
    vector_grad = lax.dynamic_slice_in_dim(vector_total, core * share, share, 1) / clip_count
    vector_new = adam_update(vector_params, vector_grad, first_vector, second_vector, factor)
    updates = [(vector_grad, *vector_new, vector_new[2].astype(BF))]
    for kind, name in enumerate(WEIGHTS):
        parts_of = ("_stage", "_arrive") if name in ("qkv", "up") else ("_stage",)
        updates.append(
            adam_matrix(
                [
                    getattr(back, name + part + str(layer))
                    for layer in range(layer_count)
                    for part in parts_of
                ],
                masters[kind + 1],
                firsts[kind + 1],
                seconds[kind + 1],
                factor,
                core,
                3 if kind == 0 else 1,
                clip_count,
            )
        )
    return (
        block_output,
        input_grad,
        *[item[0] for item in updates],
        norm_value.reshape(1),
        *[item[1] for item in updates],
        *[item[2] for item in updates],
        *[item[3] for item in updates],
        *[item[4] for item in updates],
    )


def solution(mesh):
    in_specs = (
        P("fsdp", "seq", None),
        P(None, "fsdp", "seq"),
        P("fsdp", "seq", None),
        P(None, "fsdp"),
        P(None, "fsdp", None),
        P(None, "fsdp", None),
        P(None, "fsdp", None),
        P(None, "fsdp", None),
        P(None, "fsdp"),
        P(None, "fsdp", None),
        P(None, "fsdp", None),
        P(None, "fsdp", None),
        P(None, "fsdp", None),
        P(None, "fsdp"),
        P(None, "fsdp", None),
        P(None, "fsdp", None),
        P(None, "fsdp", None),
        P(None, "fsdp", None),
    )
    out_specs = (
        P("fsdp", "seq", None),
        P("fsdp", "seq", None),
        P(None, "fsdp"),
        P(None, "fsdp", None),
        P(None, "fsdp", None),
        P(None, "fsdp", None),
        P(None, "fsdp", None),
        P(),
        P(None, "fsdp"),
        P(None, "fsdp", None),
        P(None, "fsdp", None),
        P(None, "fsdp", None),
        P(None, "fsdp", None),
        P(None, "fsdp"),
        P(None, "fsdp", None),
        P(None, "fsdp", None),
        P(None, "fsdp", None),
        P(None, "fsdp", None),
        P(None, "fsdp"),
        P(None, "fsdp", None),
        P(None, "fsdp", None),
        P(None, "fsdp", None),
        P(None, "fsdp", None),
        P(None, "fsdp"),
        P(None, "fsdp", None),
        P(None, "fsdp", None),
        P(None, "fsdp", None),
        P(None, "fsdp", None),
    )
    body = fast_device if fits_fast(mesh) else general_device
    return jax.shard_map(
        body, mesh=mesh, in_specs=in_specs, out_specs=out_specs, check_vma=False
    )
```

```python
from functools import partial
import math
from types import SimpleNamespace

import jax
import jax.numpy as jnp
from jax import lax
from jax.experimental import pallas as pl
from jax.experimental.pallas import tpu as pltpu
from jax.sharding import PartitionSpec as P

FSDP = "fsdp"
SEQ = "seq"
D = 1024
HEADS = 16
HEAD_DIM = 64


BETA_ONE = 0.5
BETA_TWO = 0.75
LEARN_RATE = 0.1
DECAY_RATE = 0.1
CLIP_RATIO = 0.2
ADAM_EPS = 1e-08
ROPE_BASE = 10000.0


def pieces(vector):
    return (
        vector[0:D],
        vector[D : 2 * D],
        vector[2 * D : 3 * D],
        vector[3 * D : 4 * D],
        vector[4 * D : 5 * D],
        vector[5 * D : 6 * D],
        vector[6 * D : 9 * D],
        vector[9 * D :],
    )


def layer_norm(hidden, ln_gain, ln_shift):
    center = hidden - jnp.mean(hidden, axis=-1, keepdims=True)
    spread = jnp.mean(center * center, axis=-1, keepdims=True)
    return center * lax.rsqrt(spread + 1e-06) * ln_gain + ln_shift


def gelu_exact(upward):
    return 0.5 * upward * (1.0 + jax.scipy.special.erf(upward * (1.0 / math.sqrt(2.0))))


def rotary_tables(coords_clip, pair_count):
    pair_index = jnp.arange(pair_count, dtype=jnp.int32)
    side_pairs = pair_count // 3
    time_pairs = pair_count - 2 * side_pairs
    in_time = pair_index < time_pairs
    in_height = jnp.logical_and(pair_index >= time_pairs, pair_index < time_pairs + side_pairs)
    offset = jnp.where(in_time, 0, jnp.where(in_height, time_pairs, time_pairs + side_pairs))
    seg_span = jnp.where(in_time, time_pairs, side_pairs)
    local_rank = (pair_index - offset).astype(jnp.float32)
    frequency = jnp.exp(-math.log(ROPE_BASE) * local_rank / seg_span.astype(jnp.float32))
    positions = coords_clip.astype(jnp.float32)
    chosen = jnp.where(
        in_time[None, :],
        positions[0][:, None],
        jnp.where(in_height[None, :], positions[1][:, None], positions[2][:, None]),
    )
    angles = chosen * frequency[None, :]
    return (jnp.cos(angles), jnp.sin(angles))


def rotate(values_in, cosine, sine_table):
    half_width = values_in.shape[-1] // 2
    first_half = values_in[..., :half_width]
    second_half = values_in[..., half_width:]
    cos_wide = cosine[:, None, :]
    sin_wide = sine_table[:, None, :]
    return jnp.concatenate(
        [
            first_half * cos_wide - second_half * sin_wide,
            first_half * sin_wide + second_half * cos_wide,
        ],
        axis=-1,
    )


def attend_forward(queries, key_rows, value_rows):
    full_len = queries.shape[0]
    block_rows = min(512, full_len)
    score_scale = HEAD_DIM ** (-0.5)
    query_blocks = queries.reshape(
        full_len // block_rows, block_rows, queries.shape[1], queries.shape[2]
    )

    def one_block(query_block):
        scores = (
            jnp.einsum("qhd,khd->hqk", query_block, key_rows, preferred_element_type=jnp.float32)
            * score_scale
        )
        row_max = jnp.max(scores, axis=-1, keepdims=True)
        exponent = jnp.exp(scores - row_max)
        row_total = jnp.sum(exponent, axis=-1, keepdims=True)
        prob_low = (exponent / row_total).astype(jnp.bfloat16)
        mixed_rows = jnp.einsum(
            "hqk,khd->qhd", prob_low, value_rows, preferred_element_type=jnp.float32
        )
        return (mixed_rows, row_max[..., 0] + jnp.log(row_total[..., 0]))

    mixed_rows, log_sums = lax.map(one_block, query_blocks)
    return (mixed_rows.reshape(queries.shape), log_sums)


def attend_backward(queries, key_rows, value_rows, log_sums, head_grad):
    full_len = queries.shape[0]
    block_rows = min(512, full_len)
    score_scale = HEAD_DIM ** (-0.5)
    block_shape = (full_len // block_rows, block_rows, queries.shape[1], queries.shape[2])

    def one_block(carry, block_in):
        key_grad, value_grad = carry
        query_block, grad_block, lse_block = block_in
        scores = (
            jnp.einsum("qhd,khd->hqk", query_block, key_rows, preferred_element_type=jnp.float32)
            * score_scale
        )
        prob_rows = jnp.exp(scores - lse_block[..., None])
        prob_low = prob_rows.astype(jnp.bfloat16)
        value_grad = value_grad + jnp.einsum(
            "hqk,qhd->khd", prob_low, grad_block, preferred_element_type=jnp.float32
        )
        prob_grad = jnp.einsum(
            "qhd,khd->hqk", grad_block, value_rows, preferred_element_type=jnp.float32
        )
        score_grad = prob_rows * (
            prob_grad - jnp.sum(prob_rows * prob_grad, axis=-1, keepdims=True)
        )
        score_low = (score_grad * score_scale).astype(jnp.bfloat16)
        query_grad = jnp.einsum(
            "hqk,khd->qhd", score_low, key_rows, preferred_element_type=jnp.float32
        )
        key_grad = key_grad + jnp.einsum(
            "hqk,qhd->khd", score_low, query_block, preferred_element_type=jnp.float32
        )
        return ((key_grad, value_grad), query_grad)

    zero_heads = jnp.zeros(queries.shape, jnp.float32)
    (key_grad, value_grad), query_grad = lax.scan(
        one_block,
        (zero_heads, zero_heads),
        (queries.reshape(block_shape), head_grad.reshape(block_shape), log_sums),
    )
    return (query_grad.reshape(queries.shape), key_grad, value_grad)


def layer_forward(hidden, cosine, sine_table, weights, seq_parts):
    vector_low, qkv_w, proj_w, up_w, down_w = weights
    gain_one, shift_one, gain_two, shift_two, proj_bias, down_bias, qkv_bias, up_bias = pieces(
        vector_low.astype(jnp.float32)
    )
    row_count = hidden.shape[0]
    local_heads = HEADS // seq_parts
    normed = layer_norm(hidden, gain_one, shift_one).astype(jnp.bfloat16)
    qkv_all = jnp.dot(normed, qkv_w, preferred_element_type=jnp.float32) + qkv_bias
    split_qkv = qkv_all.reshape(row_count, 3, HEADS, HEAD_DIM)
    stacked = jnp.stack(
        [
            rotate(split_qkv[:, 0], cosine, sine_table),
            rotate(split_qkv[:, 1], cosine, sine_table),
            split_qkv[:, 2],
        ],
        axis=1,
    ).astype(jnp.bfloat16)
    packed = stacked.reshape(row_count, 3, seq_parts, local_heads * HEAD_DIM)
    by_heads = lax.all_to_all(packed, SEQ, split_axis=2, concat_axis=0, tiled=True)
    full_len = by_heads.shape[0]
    by_heads = by_heads.reshape(full_len, 3, local_heads, HEAD_DIM)
    mixed_rows, log_sums = attend_forward(by_heads[:, 0], by_heads[:, 1], by_heads[:, 2])
    mixed_low = mixed_rows.astype(jnp.bfloat16).reshape(full_len, 1, local_heads * HEAD_DIM)
    by_tokens = lax.all_to_all(mixed_low, SEQ, split_axis=0, concat_axis=1, tiled=True).reshape(
        row_count, D
    )
    after_attn = hidden + jnp.dot(by_tokens, proj_w, preferred_element_type=jnp.float32) + proj_bias
    normed_two = layer_norm(after_attn, gain_two, shift_two).astype(jnp.bfloat16)
    upward = jnp.dot(normed_two, up_w, preferred_element_type=jnp.float32) + up_bias
    active = gelu_exact(upward).astype(jnp.bfloat16)
    result = after_attn + jnp.dot(active, down_w, preferred_element_type=jnp.float32) + down_bias
    saved_state = (
        hidden,
        normed,
        by_heads,
        log_sums,
        by_tokens,
        after_attn,
        normed_two,
        upward,
        active,
    )
    return (result, saved_state)


def layer_backward(grad_out, saved_state, weights, cosine, sine_table, seq_parts):
    vector_low, qkv_w, proj_w, up_w, down_w = weights
    gain_one, shift_one, gain_two, shift_two, proj_bias, down_bias, qkv_bias, up_bias = pieces(
        vector_low.astype(jnp.float32)
    )
    hidden, normed, by_heads, log_sums, by_tokens, after_attn, normed_two, upward, active = (
        saved_state
    )
    row_count = hidden.shape[0]
    local_heads = HEADS // seq_parts
    down_bias_grad = jnp.sum(grad_out, axis=0)
    grad_low = grad_out.astype(jnp.bfloat16)
    down_grad = jnp.dot(active.T, grad_low, preferred_element_type=jnp.float32)
    active_grad = jnp.dot(grad_low, down_w.T, preferred_element_type=jnp.float32)
    gelu_value, gelu_pull = jax.vjp(gelu_exact, upward)
    upward_grad = gelu_pull(active_grad)[0]
    up_bias_grad = jnp.sum(upward_grad, axis=0)
    upward_low = upward_grad.astype(jnp.bfloat16)
    up_grad = jnp.dot(normed_two.T, upward_low, preferred_element_type=jnp.float32)
    normed_two_grad = jnp.dot(upward_low, up_w.T, preferred_element_type=jnp.float32)
    norm_value_two, norm_pull_two = jax.vjp(layer_norm, after_attn, gain_two, shift_two)
    attn_in_grad, gain_two_grad, shift_two_grad = norm_pull_two(normed_two_grad)
    after_grad = grad_out + attn_in_grad
    proj_bias_grad = jnp.sum(after_grad, axis=0)
    after_low = after_grad.astype(jnp.bfloat16)
    proj_grad = jnp.dot(by_tokens.T, after_low, preferred_element_type=jnp.float32)
    mixed_grad = jnp.dot(after_low, proj_w.T, preferred_element_type=jnp.float32).astype(
        jnp.bfloat16
    )
    head_grad = lax.all_to_all(
        mixed_grad.reshape(row_count, seq_parts, local_heads * HEAD_DIM),
        SEQ,
        split_axis=1,
        concat_axis=0,
        tiled=True,
    )
    full_len = head_grad.shape[0]
    head_grad = head_grad.reshape(full_len, local_heads, HEAD_DIM)
    query_grad, key_grad, value_grad = attend_backward(
        by_heads[:, 0], by_heads[:, 1], by_heads[:, 2], log_sums, head_grad
    )
    stacked_grad = (
        jnp.stack([query_grad, key_grad, value_grad], axis=1)
        .astype(jnp.bfloat16)
        .reshape(full_len, 3, 1, local_heads * HEAD_DIM)
    )
    token_grad = (
        lax.all_to_all(stacked_grad, SEQ, split_axis=0, concat_axis=2, tiled=True)
        .reshape(row_count, 3, HEADS, HEAD_DIM)
        .astype(jnp.float32)
    )
    pair_grad_in = token_grad[:, :2].reshape(row_count, 2 * HEADS, HEAD_DIM)
    rotated_value, rotate_pull = jax.vjp(
        partial(rotate, cosine=cosine, sine_table=sine_table), pair_grad_in
    )
    pair_grad = rotate_pull(pair_grad_in)[0].reshape(row_count, 2, HEADS, HEAD_DIM)
    qkv_grad = jnp.concatenate([pair_grad, token_grad[:, 2:]], axis=1).reshape(row_count, 3 * D)
    qkv_bias_grad = jnp.sum(qkv_grad, axis=0)
    qkv_low = qkv_grad.astype(jnp.bfloat16)
    qkv_w_grad = jnp.dot(normed.T, qkv_low, preferred_element_type=jnp.float32)
    normed_grad = jnp.dot(qkv_low, qkv_w.T, preferred_element_type=jnp.float32)
    norm_value_one, norm_pull_one = jax.vjp(layer_norm, hidden, gain_one, shift_one)
    in_grad, gain_one_grad, shift_one_grad = norm_pull_one(normed_grad)
    input_grad = after_grad + in_grad
    vector_grad = jnp.concatenate(
        [
            gain_one_grad,
            shift_one_grad,
            gain_two_grad,
            shift_two_grad,
            proj_bias_grad,
            down_bias_grad,
            qkv_bias_grad,
            up_bias_grad,
        ]
    )
    return (input_grad, (vector_grad, qkv_w_grad, proj_grad, up_grad, down_grad))


def adam_update(master, grad_item, first_old, second_old, factor):
    clipped = grad_item * factor
    first_new = BETA_ONE * first_old + (1.0 - BETA_ONE) * clipped
    second_new = BETA_TWO * second_old + (1.0 - BETA_TWO) * clipped * clipped
    updated = master - LEARN_RATE * (
        first_new / (jnp.sqrt(second_new) + ADAM_EPS) + DECAY_RATE * master
    )
    return (first_new, second_new, updated)


def general_device(
    clip_tokens,
    patch_coords,
    out_cotangent,
    vector_params,
    qkv_weight,
    proj_weight,
    up_weight,
    down_weight,
    first_vector,
    first_qkv,
    first_proj,
    first_up,
    first_down,
    second_vector,
    second_qkv,
    second_proj,
    second_up,
    second_down,
):
    masters = (vector_params, qkv_weight, proj_weight, up_weight, down_weight)
    firsts = (first_vector, first_qkv, first_proj, first_up, first_down)
    seconds = (second_vector, second_qkv, second_proj, second_up, second_down)
    lowered = tuple((master.astype(jnp.bfloat16) for master in masters))
    layer_count = vector_params.shape[0]
    batch_local = clip_tokens.shape[0]
    seq_parts = lax.axis_size(SEQ)
    fsdp_parts = lax.axis_size(FSDP)
    grad_accum = tuple(
        (
            jnp.zeros((layer_count, master.shape[1] * fsdp_parts) + master.shape[2:], jnp.float32)
            for master in masters
        )
    )
    output_rows = []
    input_rows = []
    for batch_idx in range(batch_local):
        cosine, sine_table = rotary_tables(patch_coords[:, batch_idx], HEAD_DIM // 2)
        hidden = clip_tokens[batch_idx]
        saved_layers = []
        for layer_idx in range(layer_count):
            weights = (
                lax.all_gather(lowered[0][layer_idx], FSDP, axis=0, tiled=True),
                lax.all_gather(lowered[1][layer_idx], FSDP, axis=0, tiled=True),
                lax.all_gather(lowered[2][layer_idx], FSDP, axis=0, tiled=True),
                lax.all_gather(lowered[3][layer_idx], FSDP, axis=0, tiled=True),
                lax.all_gather(lowered[4][layer_idx], FSDP, axis=0, tiled=True),
            )
            hidden, saved_state = layer_forward(hidden, cosine, sine_table, weights, seq_parts)
            saved_layers.append(saved_state)
        output_rows.append(hidden)
        grad_rows = out_cotangent[batch_idx]
        for layer_idx in reversed(range(layer_count)):
            weights = (
                lax.all_gather(lowered[0][layer_idx], FSDP, axis=0, tiled=True),
                lax.all_gather(lowered[1][layer_idx], FSDP, axis=0, tiled=True),
                lax.all_gather(lowered[2][layer_idx], FSDP, axis=0, tiled=True),
                lax.all_gather(lowered[3][layer_idx], FSDP, axis=0, tiled=True),
                lax.all_gather(lowered[4][layer_idx], FSDP, axis=0, tiled=True),
            )
            grad_rows, layer_grads = layer_backward(
                grad_rows, saved_layers[layer_idx], weights, cosine, sine_table, seq_parts
            )
            grad_accum = tuple(
                (
                    accum_item.at[layer_idx].add(grad_item)
                    for accum_item, grad_item in zip(grad_accum, layer_grads)
                )
            )
        input_rows.append(grad_rows)
    shard_sums = (
        lax.psum_scatter(grad_accum[0], FSDP, scatter_dimension=1, tiled=True),
        lax.psum_scatter(grad_accum[1], FSDP, scatter_dimension=1, tiled=True),
        lax.psum_scatter(grad_accum[2], FSDP, scatter_dimension=1, tiled=True),
        lax.psum_scatter(grad_accum[3], FSDP, scatter_dimension=1, tiled=True),
        lax.psum_scatter(grad_accum[4], FSDP, scatter_dimension=1, tiled=True),
    )
    seq_sums = lax.psum(
        (shard_sums[0], shard_sums[1], shard_sums[2], shard_sums[3], shard_sums[4]), SEQ
    )
    clip_count = batch_local * fsdp_parts
    grad_shards = tuple((sum_item / clip_count for sum_item in seq_sums))
    local_squares = sum((jnp.sum(grad_item * grad_item) for grad_item in grad_shards))
    squares_total = lax.psum(local_squares, FSDP)
    norm_value = jnp.sqrt(squares_total)
    param_count = sum((master.size for master in masters)) * fsdp_parts
    factor = jnp.minimum(1.0, CLIP_RATIO * math.sqrt(float(param_count)) / (norm_value + 1e-06))
    updates = [
        adam_update(master, grad_item, first_old, second_old, factor)
        for master, grad_item, first_old, second_old in zip(masters, grad_shards, firsts, seconds)
    ]
    return (
        jnp.stack(output_rows),
        jnp.stack(input_rows),
        grad_shards[0],
        grad_shards[1],
        grad_shards[2],
        grad_shards[3],
        grad_shards[4],
        norm_value.reshape(1),
        updates[0][0],
        updates[1][0],
        updates[2][0],
        updates[3][0],
        updates[4][0],
        updates[0][1],
        updates[1][1],
        updates[2][1],
        updates[3][1],
        updates[4][1],
        updates[0][2],
        updates[1][2],
        updates[2][2],
        updates[3][2],
        updates[4][2],
        updates[0][2].astype(jnp.bfloat16),
        updates[1][2].astype(jnp.bfloat16),
        updates[2][2].astype(jnp.bfloat16),
        updates[3][2].astype(jnp.bfloat16),
        updates[4][2].astype(jnp.bfloat16),
    )


ROWS_Q = 256
ADD_ROWS = 32
PAIR = 2 * HEAD_DIM
BF = jnp.bfloat16
F32 = jnp.float32
VMEM_LIMIT = 56 * 1024 * 1024


def fits_fast(mesh):
    return dict(mesh.shape) == {"seq": 4, "fsdp": 8}


def swap_core(item):
    parts = lax.axis_size(FSDP)
    return lax.ppermute(item, FSDP, [(idx, idx ^ 1) for idx in range(parts)])


def send_up(item):
    parts = lax.axis_size(FSDP)
    return lax.ppermute(item, FSDP, [(idx, (idx + 2) % parts) for idx in range(parts)])


def swap_seq(item, mask):
    parts = lax.axis_size(SEQ)
    return lax.ppermute(item, SEQ, [(idx, idx ^ mask) for idx in range(parts)])


def pick(item, index, axis=0):
    return lax.dynamic_index_in_dim(item, index, axis, keepdims=False)


def swap_halves(item):
    lane = lax.broadcasted_iota(jnp.int32, item.shape, 1)
    half = HEAD_DIM // 2
    width = item.shape[1]
    ahead = pltpu.roll(item, width - half, 1)
    behind = pltpu.roll(item, half, 1)
    return jnp.where(lane % HEAD_DIM < half, ahead, behind)


NT = (((1,), (1,)), ((), ()))


def head_mask(item, head):
    lane = lax.broadcasted_iota(jnp.int32, item.shape, 1)
    return jnp.where(lane // HEAD_DIM == head, item, jnp.zeros_like(item))


class Places:
    def __init__(self):
        shard, seq = lax.axis_index(FSDP), lax.axis_index(SEQ)
        parts = lax.axis_size(FSDP)
        self.ring = parts // 2
        self.seq = seq
        self.chip, self.core = shard // 2, lax.rem(shard, 2)
        self.at_x, self.at_y = lax.rem(seq, 2), seq // 2
        self.near_x = 2 * self.at_y + 1 - self.at_x
        self.near_y = 2 * (1 - self.at_y) + self.at_x
        self.other = {FSDP: shard + 1 - 2 * self.core}
        self.up = {FSDP: lax.rem(shard + 2, parts)}
        self.down = {FSDP: lax.rem(shard + parts - 2, parts)}
        self.over_x = {SEQ: self.near_x}
        self.over_y = {SEQ: self.near_y}

    def back(self, hops):
        return lax.rem(self.chip - hops + self.ring, self.ring)


def remote(src, dst, send, recv, target):
    return pltpu.make_async_remote_copy(
        src_ref=src,
        dst_ref=dst,
        send_sem=send,
        recv_sem=recv,
        device_id=target,
        device_id_type=pl.DeviceIdType.MESH,
    )


def greet(targets, waits):
    barrier = pltpu.get_barrier_semaphore()
    for target in targets:
        pl.semaphore_signal(barrier, inc=1, device_id=target, device_id_type=pl.DeviceIdType.MESH)
    pl.semaphore_wait(barrier, waits)


def aligned(start, size, unit=None):
    return pl.ds(pl.multiple_of(start, unit or size), size)


def adam_kernel(
    kinds, ring, count, core_ref, factor_ref, *refs
):
    n_grads = len(refs) - 8
    grads = refs[:n_grads]
    master, first, second, grad_out, first_out, second_out, new_out, copy_out = refs[n_grads:]
    layer = pl.program_id(0)
    factor = factor_ref[0]
    scale = 1.0 / count
    columns = master.shape[2]
    per_layer = n_grads // 2
    width = columns // (kinds * ring * 2) if per_layer == 2 else 512

    def update(at, total):
        grad = total.astype(F32) * scale
        first_new, second_new, new = [], [], []
        first_new, second_new, new = adam_update(
            master[0, :, at], grad, first[0, :, at], second[0, :, at], factor
        )
        grad_out[0, :, at] = grad
        first_out[0, :, at] = first_new
        second_out[0, :, at] = second_new
        new_out[0, :, at] = new
        copy_out[0, :, at] = new.astype(BF)

    def choose(which, at):
        values = [grads[idx * per_layer + which][:, at] for idx in range(2)]
        return jnp.where(layer == 0, values[0], values[1])

    if per_layer == 1:
        for start in range(0, columns, width):
            update(slice(start, start + width), choose(0, slice(start, start + width)))
        return
    core = core_ref[0]
    for pair in range(ring):
        for kind in range(kinds):
            source = (pair * kinds + kind) * width
            mine, arrive = [choose(which, slice(source, source + width)) for which in range(2)]
            for which in range(2):
                start = (kind * ring * 2 + 2 * pair + which) * width
                update(slice(start, start + width), jnp.where(core == which, mine, arrive))


def adam_matrix(grads, master, first, second, factor, core, kinds, count):
    layers, rows, columns = master.shape
    ring = lax.axis_size(FSDP) // 2
    block = 16 if columns > 1024 else 64
    steps = rows // block
    per_layer = len(grads) // layers

    def grad_spec(idx):
        layer, which = divmod(idx, per_layer)
        lift = steps if per_layer == 2 and which == 0 else 0

        def where(at_layer, step, core_ref, layer=layer, lift=lift):
            held = 0 if layer > 0 else steps - 1
            row = jnp.where(at_layer == layer, step, held)
            return (row + lift * core_ref[0], 0)

        return pl.BlockSpec((block, grads[idx].shape[1]), where)

    whole = pl.BlockSpec((1, block, columns), lambda layer, step, core_ref: (layer, step, 0))
    shape = jax.ShapeDtypeStruct(master.shape, F32)
    return pl.pallas_call(
        partial(adam_kernel, kinds, ring, count),
        grid_spec=pltpu.PrefetchScalarGridSpec(
            num_scalar_prefetch=1,
            grid=(layers, steps),
            in_specs=[pl.BlockSpec(memory_space=pltpu.SMEM)]
            + [grad_spec(idx) for idx in range(len(grads))]
            + [whole] * 3,
            out_specs=[whole] * 5,
        ),
        out_shape=[shape] * 4 + [jax.ShapeDtypeStruct(master.shape, BF)],
        compiler_params=pltpu.CompilerParams(vmem_limit_bytes=VMEM_LIMIT),
        cost_estimate=pl.CostEstimate(
            flops=20 * master.size, bytes_accessed=32 * master.size, transcendentals=master.size
        ),
        name="update",
    )(core.reshape(1).astype(jnp.int32), factor.reshape(1), *grads, master, first, second)


def norm_parts(hidden):
    center = hidden - jnp.mean(hidden, axis=-1, keepdims=True)
    spread = jnp.mean(center * center, axis=-1, keepdims=True)
    inverse = lax.rsqrt(spread + 1e-06)
    return center * inverse, inverse


def gelu_and_slope(upward):
    erf_part = 0.5 * (1.0 + lax.erf(upward * (1.0 / math.sqrt(2.0))))
    density = jnp.exp(-0.5 * upward * upward) * (1.0 / math.sqrt(2.0 * math.pi))
    return upward * erf_part, erf_part + upward * density


def dot(left, right):
    return jnp.dot(left, right, preferred_element_type=F32)


def dot_nt(left, right):
    return lax.dot_general(left, right, NT, preferred_element_type=F32)


def dot_tn(left, right):
    return lax.dot_general(left, right, (((0,), (0,)), ((), ())), preferred_element_type=F32)


def rotation_tables(packed):
    lane = lax.broadcasted_iota(jnp.int32, packed.shape, 1)
    first = lane % HEAD_DIM < HEAD_DIM // 2
    turned = pltpu.roll(packed, HEAD_DIM // 2, 1)
    return jnp.where(first, packed, turned), jnp.where(first, -turned, packed)


def each_block(count, body):
    @pl.loop(0, count)
    def _(step):
        body(aligned(step * ROWS_Q, ROWS_Q))


class Forward:
    def __init__(self, at, refs, layers):
        self.at, self.refs, self.layers = at, refs, layers
        self.blocks = refs.res.shape[0] // ROWS_Q
        self.pairs = refs.mixed.shape[1] // PAIR
        self.saves, self.loads, self.slot = [], [], 0
        self.mixed_copies, self.part_copies = {}, {}

    def save(self, src, dst):
        copy = pltpu.make_async_copy(src, dst, self.refs.save_sem.at[self.slot])
        self.slot += 1
        copy.start()
        self.saves.append(copy)
        return copy

    def settle(self):
        for copy in self.saves:
            copy.wait()
        self.saves = []

    def bring(self, pairs):
        for src, dst in pairs:
            copy = pltpu.make_async_copy(src, dst, self.refs.save_sem.at[self.slot])
            self.slot += 1
            copy.start()
            self.loads.append(copy)

    def arrive(self):
        for copy in self.loads:
            copy.wait()
        self.loads = []

    def vec(self, layer, row, width):
        return self.refs.vecs[layer, row : row + 1, 0:width]

    def unpack_vectors(self):
        refs, at = self.refs, self.at
        ring = at.ring
        per_shard = refs.vec_rows
        for layer in range(self.layers):
            places = [(row, row // 8, row % 8) for row in range(48)]
            for pair in range(ring):
                for kind in range(3):
                    places.append((48 + kind * 8 + 2 * pair + at.core, 6, pair * 3 + kind))
                for part in range(4):
                    places.append((72 + (2 * pair + at.core) * 4 + part, 7, pair * 4 + part))
            for source, row, block in places:
                shard, entry = source // per_shard, layer * per_shard + source % per_shard
                if not isinstance(source, int):
                    shard = lax.div(source, per_shard)
                    entry = layer * per_shard + lax.rem(source, per_shard)
                refs.vecs[layer, row : row + 1, block * 128 : (block + 1) * 128] = refs.vec_out[
                    shard, pl.ds(entry, 1), :
                ]

    def normed(self, rows, layer, first):
        hidden = self.refs.res[rows, :]
        scaled, _ = norm_parts(hidden)
        width = hidden.shape[1]
        return (scaled * self.vec(layer, first, width) + self.vec(layer, first + 1, width)).astype(BF)

    def load_qkv(self, weight):
        self.bring([(weight, self.refs.w_one.at[:, pl.ds(0, weight.shape[1])])])

    def load_proj(self, own, other):
        half, target = own.shape[0], self.refs.w_two
        self.bring([(own, target.at[pl.ds(0, half), :]), (other, target.at[pl.ds(half, half), :])])

    def load_units(self, up_weight, down_weight):
        self.bring([(up_weight, self.refs.w_one), (down_weight, self.refs.w_two)])

    def qkv(self, layer):
        refs = self.refs
        self.settle()
        self.arrive()

        def body(rows):
            normed = self.normed(rows, layer, 0)
            refs.norm[rows, :] = normed
            for pair in range(self.pairs):
                cols = slice(pair * 3 * PAIR, (pair + 1) * 3 * PAIR)
                block = dot(normed, refs.w_one[:, cols]) + refs.vecs[layer, 6:7, cols]
                cosine, sine = rotation_tables(refs.tables[rows, :])
                for kind in range(3):
                    part = block[:, kind * PAIR : (kind + 1) * PAIR]
                    if kind < 2:
                        part = part * cosine + swap_halves(part) * sine
                    start = pair * 3 * PAIR + kind * PAIR
                    refs.low[rows, start : start + PAIR] = part.astype(BF)

        each_block(self.blocks, body)
        self.save(refs.norm, refs.normed_out[layer])
        self.save(refs.low, refs.low_out[layer])

    def attend(self, layer, pair):
        refs = self.refs
        base = pair * 3 * PAIR
        key_cols, value_cols = [
            slice(base + kind * PAIR, base + (kind + 1) * PAIR) for kind in (1, 2)
        ]

        def body(rows):
            block = refs.low[rows, base : base + PAIR] * jnp.asarray(HEAD_DIM**-0.5, BF)
            outs = []
            for head in range(2):
                scores = dot_nt(head_mask(block, head), refs.low[:, key_cols])
                top = jnp.max(scores, axis=1, keepdims=True)
                exponent = jnp.exp(scores - top)
                total = jnp.sum(exponent, axis=1, keepdims=True)
                sums = jnp.broadcast_to(top + jnp.log(total), (ROWS_Q, PAIR)).T
                refs.lse_out[layer, pair, head : head + 1, rows] = sums[0:1]
                probs = (exponent * (1.0 / total)).astype(BF)
                outs.append(dot(probs, refs.low[:, value_cols]))
            lane = lax.broadcasted_iota(jnp.int32, outs[0].shape, 1)
            refs.mixed[rows, pair * PAIR : (pair + 1) * PAIR] = jnp.where(
                lane < HEAD_DIM, outs[0], outs[1]
            ).astype(BF)

        each_block(self.blocks, body)
        slot = layer * (self.pairs + 2) + pair
        cols = pl.ds(pair * PAIR, PAIR)
        copy = remote(
            refs.mixed.at[:, cols],
            refs.mixed_other.at[:, cols],
            refs.x_send.at[slot],
            refs.x_recv.at[slot],
            self.at.other,
        )
        copy.start()
        self.mixed_copies[layer, pair] = copy

    def project(self, layer):
        refs = self.refs
        half = refs.mixed.shape[1]
        self.arrive()
        self.settle()
        for pair in range(self.pairs):
            self.mixed_copies[layer, pair].wait()
        width = refs.res.shape[1]

        def body(rows):
            total = dot(refs.mixed[rows, :], refs.w_two[0:half, :])
            total = total + dot(refs.mixed_other[rows, :], refs.w_two[half : 2 * half, :])
            refs.res[rows, :] = refs.res[rows, :] + total + self.vec(layer, 4, width)
            refs.norm[rows, :] = self.normed(rows, layer, 2)

        each_block(self.blocks, body)
        self.save(refs.mixed, refs.mixed_out[layer])
        self.save(refs.res, refs.after_out[layer])
        self.save(refs.norm, refs.normed_two_out[layer])

    def hidden_units(self, layer, half):
        refs = self.refs
        if half == 0:
            self.settle()
            self.arrive()
        width = refs.res.shape[1]
        tiles = refs.w_one.shape[1] // 512
        blocks = self.blocks // 2

        @pl.loop(half * blocks, (half + 1) * blocks)
        def _(step):
            rows = aligned(step * ROWS_Q, ROWS_Q)

            @pl.loop(0, tiles)
            def _(tile):
                cols = aligned(tile * 512, 512)
                upward = dot(refs.norm[rows, :], refs.w_one[:, cols]) + refs.vecs[layer, 7:8, cols]
                active, slope = gelu_and_slope(upward)
                refs.act[rows, cols] = active.astype(BF)
                refs.slope[rows, cols] = slope.astype(BF)

            part = dot(refs.act[rows, :], refs.w_two[...])
            refs.res[rows, :] = refs.res[rows, :] + part + self.vec(layer, 5, width)
            refs.part[rows, :] = part.astype(BF)

        rows = pl.ds(half * blocks * ROWS_Q, blocks * ROWS_Q)
        slot = layer * (self.pairs + 2) + self.pairs + half
        copy = remote(
            refs.part.at[rows, :],
            refs.part_other.at[rows, :],
            refs.x_send.at[slot],
            refs.x_recv.at[slot],
            self.at.other,
        )
        copy.start()
        self.part_copies[layer, half] = copy
        if half == 1:
            self.save(refs.act, refs.active_out[layer])
            self.save(refs.slope, refs.slope_out[layer])

    def join(self, layer):
        refs = self.refs
        for half in range(2):
            self.part_copies[layer, half].wait()

        def body(rows):
            refs.res[rows, :] = refs.res[rows, :] + refs.part_other[rows, :].astype(F32)

        each_block(self.blocks, body)
        self.save(refs.res, refs.result_out[layer])


WEIGHTS = ("qkv", "proj", "up", "down")


def forward_kernel(names, layers, vec_rows, *operands):
    refs = SimpleNamespace(**dict(zip(names, operands)))
    for name in (*WEIGHTS, "proj_two", "normed", "low", "mixed", "after", "normed_two", "active", "slope", "result"):
        label = name + "_out"
        setattr(refs, label, [getattr(refs, label + str(layer)) for layer in range(layers)])
    refs.vec_rows = vec_rows
    at = Places()
    ring, seq, chip, core = at.ring, at.seq, at.chip, at.core
    full = {name: getattr(refs, name + "_full") for name in WEIGHTS}
    source = {name: getattr(refs, name + "_in") for name in WEIGHTS}
    slabs = {name: getattr(refs, name + "_slab") for name in WEIGHTS}
    outs = {name: getattr(refs, name + "_out") for name in WEIGHTS}
    items = [(name, layer) for layer in range(layers) for name in WEIGHTS]
    loads = {}

    def start_load(name, layer):
        copy = pltpu.make_async_copy(
            source[name].at[layer], full[name], refs.l_in.at[items.index((name, layer))]
        )
        copy.start()
        loads[name, layer] = copy

    for name in WEIGHTS:
        start_load(name, 0)
    barrier = pltpu.get_barrier_semaphore()
    for target in (at.other, at.up, at.down):
        pl.semaphore_signal(barrier, inc=1, device_id=target, device_id_type=pl.DeviceIdType.MESH)
    for step in range(1, 4):
        for half in range(2):
            pl.semaphore_signal(
                barrier,
                inc=1,
                device_id={FSDP: 2 * chip + half, SEQ: seq ^ step},
                device_id_type=pl.DeviceIdType.MESH,
            )
    pl.semaphore_wait(barrier, 9)

    length = refs.clip_in.shape[1]
    token_core = seq // 2
    token_rows = aligned(seq * length, length)
    stays = core == token_core

    class Move:
        def __init__(self, base, pairs):
            self.base, self.pairs, self.copies = base, pairs, []

        def start(self):
            for turn in range(2):
                target = {SEQ: 2 * core + turn, FSDP: 2 * chip + token_core}
                away = jnp.logical_not(jnp.logical_and(stays, lax.rem(seq, 2) == turn))
                copies = [
                    remote(
                        src.at[turn],
                        place(seq),
                        refs.m_send.at[self.base + 2 * turn + idx],
                        refs.m_recv.at[self.base + 2 * lax.rem(seq, 2) + idx],
                        target,
                    )
                    for idx, (src, place) in enumerate(self.pairs)
                ]
                self.copies.append((away, copies))

                @pl.when(away)
                def _(copies=copies):
                    for copy in copies:
                        copy.start()

            @pl.when(stays)
            def _():
                for idx, (src, place) in enumerate(self.pairs):
                    bounce = refs.clip_slab if idx == 0 else refs.table_slab
                    sem = refs.m_load.at[self.base // 6 * 2 + idx]
                    load = pltpu.make_async_copy(src.at[lax.rem(seq, 2)], bounce, sem)
                    load.start()
                    load.wait()
                    store = pltpu.make_async_copy(bounce, place(seq), sem)
                    store.start()
                    store.wait()

        def swap(self):
            for part in range(2):
                came = jnp.logical_not(jnp.logical_and(stays, lax.rem(seq, 2) == part))

                @pl.when(came)
                def _(part=part):
                    for idx, (src, place) in enumerate(self.pairs):
                        remote(
                            src.at[0],
                            place(2 * core + part),
                            refs.m_send.at[self.base],
                            refs.m_recv.at[self.base + 2 * part + idx],
                            at.other,
                        ).wait_recv()

            self.swaps = []
            for idx, (src, place) in enumerate(self.pairs):
                for part in range(2):
                    slot = 24 + self.base // 6 * 4 + 2 * idx + part
                    ref = place(2 * core + part)
                    self.swaps.append(
                        remote(ref, ref, refs.m_send.at[slot], refs.m_recv.at[slot], at.other)
                    )
            for copy in self.swaps:
                copy.start()

        def arrived(self):
            for copy in self.swaps:
                copy.wait_recv()

        def drain(self):
            for copy in self.swaps:
                copy.wait_send()
            for away, copies in self.copies:

                @pl.when(away)
                def _(copies=copies):
                    for copy in copies:
                        copy.wait_send()

    def chunk_of(ref):
        return lambda number: ref.at[aligned(number * length, length), :]

    tokens = Move(0, [(refs.clip_in, chunk_of(refs.clip_out)), (refs.table_in, chunk_of(refs.table_out))])
    cotangents = Move(6, [(refs.cot_in, chunk_of(refs.cot_out))])
    tokens.start()

    refs.vec_out[2 * chip + core] = refs.vec_in[...]
    vec_swap = remote(
        refs.vec_in, refs.vec_out.at[2 * chip + core], refs.m_send.at[16], refs.m_recv.at[16], at.other
    )
    vec_swap.start()
    vec_copies = [vec_swap]

    def vec_hop(hop):
        vec_copies[-1].wait_recv()
        ref = refs.vec_out.at[pl.ds(2 * at.back(hop), 2)]
        slot = 17 + hop
        copy = remote(ref, ref, refs.m_send.at[slot], refs.m_recv.at[slot], at.up)
        copy.start()
        vec_copies.append(copy)

    def place(name, layer, chip_at, part):
        slab = slabs[name].shape[1]
        if part is None:
            return outs[name][layer].at[aligned(chip_at * slab, slab), :]
        size = slab // 4
        return outs[name][layer].at[aligned(chip_at * slab + part * size, size), :]

    swaps, prepared, stores = {}, [], []

    def prepare():
        if len(prepared) == len(items):
            return
        idx = len(prepared)
        name, layer = items[idx]
        prepared.append(name)
        slab = slabs[name]
        loads[name, layer].wait()
        swaps[idx] = None
        if name in ("down", "proj"):
            slab[layer] = full[name][...].astype(BF)
        else:
            away, kinds = (refs.qkv_away, 3) if name == "qkv" else (refs.up_away, 1)
            half, columns = full[name].shape
            width = columns // (kinds * 2 * ring)
            rows = aligned(core * half, half)
            for pair in range(ring):
                for kind in range(kinds):
                    cols = slice((pair * kinds + kind) * width, (pair * kinds + kind + 1) * width)
                    for mine in (True, False):
                        which = core if mine else 1 - core
                        start = (kind * 2 * ring + 2 * pair + which) * width
                        block = full[name][:, aligned(start, width)].astype(BF)
                        if mine:
                            slab[layer, rows, cols] = block
                        else:
                            away[layer, :, cols] = block
            swaps[idx] = remote(
                away.at[layer],
                slab.at[layer, rows, :],
                refs.c_send.at[idx],
                refs.c_recv.at[idx],
                at.other,
            )
            swaps[idx].start()
        if layer + 1 < layers:
            start_load(name, layer + 1)

    hops = ring - 1
    order = []
    for first in range(0, len(items), 2):
        for hop in range(hops):
            order += [(first, hop), (first + 1, hop)]
    z_copies, plane, far, proj_swaps = {}, {}, {}, {}

    def begin(idx):
        name, layer = items[idx]
        if swaps[idx] is not None:
            swaps[idx].wait_recv()
        store = pltpu.make_async_copy(
            slabs[name].at[layer], place(name, layer, chip, None), refs.l_out.at[idx]
        )
        store.start()
        stores.append(store)

    def z_copy(idx, hop):
        name, layer = items[idx]
        part = None if name == "proj" else seq
        target = place(name, layer, at.back(hop), part)
        from_ref = target
        if hop == 0:
            from_ref = slabs[name].at[layer]
            if part is not None:
                size = slabs[name].shape[1] // 4
                from_ref = slabs[name].at[layer, aligned(seq * size, size), :]
        slot = idx * hops + hop
        copy = remote(from_ref, target, refs.z_send.at[slot], refs.z_recv.at[slot], at.up)
        copy.start()
        z_copies[idx, hop] = copy

    def plane_copies(idx, hop):
        name, layer = items[idx]
        ref = place(name, layer, at.back(hop + 1), seq)
        slot = 2 * (idx * hops + hop)
        plane[idx, hop] = [
            remote(ref, ref, refs.p_send.at[slot], refs.p_recv.at[slot], at.over_x),
            remote(ref, ref, refs.p_send.at[slot + 1], refs.p_recv.at[slot + 1], at.over_y),
        ]
        for copy in plane[idx, hop]:
            copy.start()

    def far_copies(idx, hop):
        name, layer = items[idx]
        slot = 2 * (idx * hops + hop)
        size = slabs[name].shape[1] // 4
        half = size // 2
        base = at.back(hop + 1) * 4 * size
        for copy in plane[idx, hop]:
            copy.wait_recv()
        made = []
        for turn, (origin, target) in enumerate(((at.near_y, at.over_x), (at.near_x, at.over_y))):
            ref = outs[name][layer].at[aligned(base + origin * size + turn * half, half), :]
            made.append(
                remote(ref, ref, refs.d_send.at[slot + turn], refs.d_recv.at[slot + turn], target)
            )
        far[idx, hop] = made
        for copy in made:
            copy.start()

    pending = []

    def flush(keep):
        while len(pending) > keep:
            far_copies(*pending.pop(0))

    def event(number):
        idx, hop = order[number]
        z_copies[idx, hop].wait_recv()
        if hop + 1 < hops:
            z_copy(idx, hop + 1)
        elif idx + 2 < len(items):
            begin(idx + 2)
            z_copy(idx + 2, 0)
        name, layer = items[idx]
        if name == "proj":
            flush(0)
            if hop + 1 == hops:
                stores[idx].wait()
                slot = len(items) + layer
                proj_swaps[layer] = remote(
                    outs["proj"][layer],
                    refs.proj_two_out[layer],
                    refs.c_send.at[slot],
                    refs.c_recv.at[slot],
                    at.other,
                )
                proj_swaps[layer].start()
        else:
            plane_copies(idx, hop)
            pending.append((idx, hop))
            flush(1)
        prepare()

    def complete(name, layer):
        idx = items.index((name, layer))
        if name == "proj":
            proj_swaps[layer].wait_recv()
            return
        stores[idx].wait()
        flush(0)
        for hop in range(hops):
            for copy in far[idx, hop]:
                copy.wait_recv()

    work = Forward(at, refs, layers)

    def take_tokens():
        tokens.arrived()
        vec_copies[-1].wait_recv()
        work.bring([(refs.clip_out, refs.res), (refs.table_out, refs.tables)])
        work.unpack_vectors()

    def load_qkv(layer):
        complete("qkv", layer)
        work.load_qkv(outs["qkv"][layer])

    def load_proj(layer):
        complete("proj", layer)
        work.load_proj(outs["proj"][layer], refs.proj_two_out[layer])

    def load_units(layer):
        complete("up", layer)
        complete("down", layer)
        work.load_units(outs["up"][layer], outs["down"][layer])

    prepare()
    prepare()
    begin(0)
    z_copy(0, 0)
    begin(1)
    z_copy(1, 0)
    prepare()
    prepare()
    per_layer = 4 * hops
    chunks = []
    for layer in range(layers):
        first = layer * per_layer + 2 * hops
        if layer == 0:
            chunks.append((first, take_tokens))
        chunks.append((first + 1, partial(load_qkv, layer)))
        chunks.append((first + 2, partial(work.qkv, layer)))
        chunks.append((first + 2, partial(load_proj, layer)))
        for pair in range(work.pairs):
            chunks.append((first + 2 + pair, partial(work.attend, layer, pair)))
        chunks.append((first + 7, partial(work.project, layer)))
        chunks.append((first + 7, partial(load_units, layer)))
        chunks.append((first + 8, partial(work.hidden_units, layer, 0)))
        chunks.append((first + 9, partial(work.hidden_units, layer, 1)))
        chunks.append((first + 10, partial(work.join, layer)))
    for number in range(len(order)):
        while chunks and chunks[0][0] <= number:
            chunks.pop(0)[1]()
        if number == 2:
            tokens.swap()
        if 3 <= number < 3 + hops:
            vec_hop(number - 3)
        if number == per_layer:
            cotangents.start()
        if number == per_layer + 6:
            cotangents.swap()
        event(number)
    flush(0)
    for _, chunk in chunks:
        chunk()

    work.settle()
    cotangents.arrived()
    for made in plane.values():
        for copy in made:
            copy.wait_send()
    for made in far.values():
        for copy in made:
            copy.wait_send()
    for copy in z_copies.values():
        copy.wait_send()
    for copy in swaps.values():
        if copy is not None:
            copy.wait_send()
    for copy in proj_swaps.values():
        copy.wait_send()
    for copy in vec_copies:
        copy.wait_send()
    tokens.drain()
    cotangents.drain()


def forward(qkv, up, down, proj, clips, cots, tables, vectors, vec_rows):
    layers, rows, width = proj.shape
    parts = lax.axis_size(FSDP)
    ring = parts // 2
    count, hops = 4 * layers, ring - 1
    length = 4 * clips.shape[1]
    down_rows = down.shape[1]
    qkv_half, up_half = qkv.shape[2] // 2, up.shape[2] // 2
    pairs = qkv_half // (3 * PAIR)
    inputs = dict(
        qkv_in=qkv, up_in=up, down_in=down, proj_in=proj, clip_in=clips, cot_in=cots,
        table_in=tables, vec_in=vectors,
    )
    outputs = {}
    for layer in range(layers):
        for name, shape, dtype in (
            ("qkv", (parts * rows, qkv_half), BF),
            ("up", (parts * rows, up_half), BF),
            ("down", (ring * down_rows, width), BF),
            ("proj", (ring * rows, width), BF),
            ("proj_two", (ring * rows, width), BF),
            ("normed", (length, width), BF),
            ("low", (length, qkv_half), BF),
            ("mixed", (length, pairs * PAIR), BF),
            ("after", (length, width), F32),
            ("normed_two", (length, width), BF),
            ("active", (length, up_half), BF),
            ("slope", (length, up_half), BF),
            ("result", (length, width), F32),
        ):
            outputs[name + "_out" + str(layer)] = (shape, dtype)
    outputs["clip_out"] = ((length, width), F32)
    outputs["cot_out"] = ((length, width), F32)
    outputs["table_out"] = ((length, PAIR), F32)
    outputs["vec_out"] = ((parts,) + vectors.shape, F32)
    outputs["vecs"] = ((layers, 8, up_half), F32)
    outputs["lse_out"] = ((layers, pairs, 8, length), F32)
    in_vmem = ("vec_in", "vec_out", "vecs", "lse_out")
    anywhere = pl.BlockSpec(memory_space=pl.ANY)
    vmem = pl.BlockSpec(memory_space=pltpu.VMEM)
    dma = pltpu.SemaphoreType.DMA
    scratch = dict(
        qkv_full=pltpu.VMEM(qkv.shape[1:], F32),
        up_full=pltpu.VMEM(up.shape[1:], F32),
        down_full=pltpu.VMEM(down.shape[1:], F32),
        proj_full=pltpu.VMEM(proj.shape[1:], F32),
        qkv_away=pltpu.VMEM((layers, rows, qkv_half), BF),
        up_away=pltpu.VMEM((layers, rows, up_half), BF),
        qkv_slab=pltpu.VMEM((layers, 2 * rows, qkv_half), BF),
        up_slab=pltpu.VMEM((layers, 2 * rows, up_half), BF),
        down_slab=pltpu.VMEM((layers, down_rows, width), BF),
        proj_slab=pltpu.VMEM((layers, rows, width), BF),
        clip_slab=pltpu.VMEM(clips.shape[1:], F32),
        table_slab=pltpu.VMEM(tables.shape[1:], F32),
        res=pltpu.VMEM((length, width), F32),
        tables=pltpu.VMEM((length, PAIR), F32),
        norm=pltpu.VMEM((length, width), BF),
        low=pltpu.VMEM((length, qkv_half), BF),
        mixed=pltpu.VMEM((length, pairs * PAIR), BF),
        mixed_other=pltpu.VMEM((length, pairs * PAIR), BF),
        w_one=pltpu.VMEM((width, up_half), BF),
        w_two=pltpu.VMEM((ring * down_rows, width), BF),
        act=pltpu.VMEM((length, up_half), BF),
        slope=pltpu.VMEM((length, up_half), BF),
        part=pltpu.VMEM((length, width), BF),
        part_other=pltpu.VMEM((length, width), BF),
        z_send=dma((count * hops,)), z_recv=dma((count * hops,)),
        p_send=dma((2 * count * hops,)), p_recv=dma((2 * count * hops,)),
        d_send=dma((2 * count * hops,)), d_recv=dma((2 * count * hops,)),
        c_send=dma((count + layers,)), c_recv=dma((count + layers,)),
        l_in=dma((count,)), l_out=dma((count,)),
        m_send=dma((32,)), m_recv=dma((32,)), m_load=dma((4,)),
        x_send=dma((layers * (pairs + 2),)), x_recv=dma((layers * (pairs + 2),)),
        save_sem=dma((16 * layers,)),
    )
    names = [*inputs, *outputs, *scratch]
    results = pl.pallas_call(
        partial(forward_kernel, names, layers, vec_rows),
        in_specs=[vmem if name in in_vmem else anywhere for name in inputs],
        out_specs=[vmem if name in in_vmem else anywhere for name in outputs],
        out_shape=[jax.ShapeDtypeStruct(*shape) for shape in outputs.values()],
        scratch_shapes=list(scratch.values()),
        compiler_params=pltpu.CompilerParams(
            collective_id=0, has_side_effects=True, vmem_limit_bytes=62 * 1024 * 1024
        ),
        cost_estimate=pl.CostEstimate(
            flops=60_000_000_000, bytes_accessed=600_000_000, transcendentals=0
        ),
        name="forward",
    )(*inputs.values())
    return SimpleNamespace(**dict(zip(outputs, results)))


def add_into(target, term):
    @pl.loop(0, target.shape[0] // ADD_ROWS)
    def _(step):
        at = aligned(step * ADD_ROWS, ADD_ROWS)
        target[at, :] = (target[at, :].astype(F32) + term[at, :].astype(F32)).astype(BF)


class Sems:
    def __init__(self, ref):
        self.ref, self.used = ref, 0

    def take(self):
        self.used += 1
        return self.ref.at[self.used - 1]


class Sum:
    def __init__(self, at, sems, refs, name, layer, z_first, x_first, compute):
        self.at, self.sems = at, sems
        self.own, self.one, self.two, self.three = [
            getattr(refs, name + part) for part in ("_own", "_one", "_two", "_three")
        ]
        self.stage = getattr(refs, name + "_stage" + str(layer))
        self.arrive = getattr(refs, name + "_arrive" + str(layer), None)
        self.z_first, self.x_first, self.compute = z_first, x_first, compute
        self.rows = self.two.shape[1]
        self.sends, self.slot_sends = [], [[], []]
        self.first, self.second, self.hop = {}, {}, {}
        self.swap = None

    def make(self, src, dst, target, slot=None):
        copy = remote(src, dst, self.sems[0].take(), self.sems[1].take(), target)
        copy.start()
        (self.sends if slot is None else self.slot_sends[slot]).append(copy)
        return copy

    def pieces(self, mine):
        at = self.at
        if self.x_first:
            side = at.at_x if mine else 1 - at.at_x
            return [(side, 1), (2 + side, 1)]
        return [(2 * (at.at_y if mine else 1 - at.at_y), 2)]

    def tile(self, tile):
        slot = tile % 2
        for copy in self.slot_sends[slot]:
            copy.wait_send()
        self.slot_sends[slot] = []
        self.compute(tile, self.own.at[slot])

    def start(self, tile):
        self.tile(tile)
        slot = tile % 2
        if self.z_first:
            self.hop[0] = self.make(self.own.at[slot], self.three.at[0], self.at.up, slot)
        else:
            self.plane_one(tile, self.own.at[slot], slot)

    def plane_one(self, tile, source, slot=None):
        target = self.at.over_x if self.x_first else self.at.over_y
        place, made = 0, []
        for first, count in self.pieces(False):
            size = count * self.rows
            made.append(
                self.make(
                    source.at[aligned(first * self.rows, size, self.rows), :],
                    self.one.at[tile, pl.ds(place, size), :],
                    target,
                    slot,
                )
            )
            place += size
        self.first[tile] = made

    def plane_two(self, tile, source):
        for copy in self.first[tile]:
            copy.wait_recv()
        place = 0
        for first, count in self.pieces(True):
            size = count * self.rows
            add_into(
                self.one.at[tile, pl.ds(place, size), :],
                source.at[aligned(first * self.rows, size, self.rows), :],
            )
            place += size
        at = self.at
        target, keep = (at.over_y, at.at_y) if self.x_first else (at.over_x, at.at_x)
        self.second[tile] = self.make(
            self.one.at[tile, aligned((1 - keep) * self.rows, self.rows), :],
            self.two.at[tile],
            target,
        )

    def plane_three(self, tile):
        keep = self.at.at_y if self.x_first else self.at.at_x
        self.second[tile].wait_recv()
        add_into(self.two.at[tile], self.one.at[tile, aligned(keep * self.rows, self.rows), :])

    def middle(self, tile):
        self.plane_two(tile, self.own.at[tile % 2])

    def finish(self, tile):
        self.plane_three(tile)
        if tile > 0:
            self.hop[tile - 1].wait_recv()
            add_into(self.two.at[tile], self.three.at[tile - 1])
        if tile < self.at.ring - 1:
            self.hop[tile] = self.make(self.two.at[tile], self.three.at[tile], self.at.up)
        else:
            self.gather()

    def ring_step(self, tile):
        self.tile(tile)
        self.hop[tile - 1].wait_recv()
        total = self.three.at[tile - 1]
        add_into(total, self.own.at[tile % 2])
        if tile == self.at.ring - 1:
            self.plane_one(0, total)
        else:
            self.hop[tile] = self.make(total, self.three.at[tile], self.at.up)

    def slab_middle(self):
        self.plane_two(0, self.three.at[self.at.ring - 2])

    def slab_finish(self):
        self.plane_three(0)
        self.gather()

    def total(self):
        return self.two.at[0 if self.z_first else self.at.ring - 1]

    def place(self, quarter, turn=0, size=None):
        size = size or self.rows
        return self.stage.at[aligned(quarter * self.rows + turn * size, size), :]

    def gather(self):
        at = self.at
        self.store = pltpu.make_async_copy(self.total(), self.place(at.seq), self.sems[2].take())
        self.store.start()
        self.near = [
            self.make(self.total(), self.place(at.seq), at.over_x),
            self.make(self.total(), self.place(at.seq), at.over_y),
        ]

    def gather_far(self):
        at = self.at
        for copy in self.near:
            copy.wait_recv()
        half = self.rows // 2
        self.far = []
        for turn, (origin, target) in enumerate(((at.near_y, at.over_x), (at.near_x, at.over_y))):
            ref = self.place(origin, turn, half)
            self.far.append(self.make(ref, ref, target))

    def gather_end(self):
        at = self.at
        self.store.wait()
        for copy in self.far:
            copy.wait_recv()
        if self.arrive is not None:
            half = 2 * self.rows
            self.swap = self.make(
                self.stage.at[aligned((1 - at.core) * half, half), :], self.arrive, at.other
            )

    def drain(self):
        if self.swap is not None:
            self.swap.wait_recv()
        for copy in self.sends + self.slot_sends[0] + self.slot_sends[1]:
            copy.wait_send()
        self.sends, self.slot_sends = [], [[], []]


class VectorSum:
    def __init__(self, at, sems, source, got, hop, total):
        self.at, self.sems = at, sems
        self.got, self.hop, self.total = got, hop, total
        self.copies, self.step = [], 0
        self.partners = (at.other, at.over_x, at.over_y)

    def send(self, src, dst, target):
        copy = remote(src, dst, self.sems[0].take(), self.sems[1].take(), target)
        copy.start()
        self.copies.append(copy)

    def advance(self):
        idx, at = self.step, self.at
        self.step += 1
        if idx == 0:
            self.send(self.total.at[0], self.got.at[0], self.partners[0])
            return
        self.copies[-1].wait_recv()
        if idx <= 3:
            self.total[idx] = self.total[idx - 1] + self.got[idx - 1]
            if idx < 3:
                self.send(self.total.at[idx], self.got.at[idx], self.partners[idx])
            else:
                self.send(self.total.at[3, at.back(1)], self.hop.at[0], at.up)
            return
        hop = idx - 3
        self.hop[hop - 1] = self.hop[hop - 1] + self.total[3, at.back(hop + 1)]
        if hop < at.ring - 1:
            self.send(self.hop.at[hop - 1], self.hop.at[hop], at.up)


class Backward:
    def __init__(self, at, refs, layers):
        self.at, self.refs, self.layers = at, refs, layers
        self.blocks = refs.grad.shape[0] // ROWS_Q
        self.pairs = refs.low.shape[1] // (3 * PAIR)
        self.slot = 0
        self.part_copies, self.loads = {}, {}

    def prefetch(self, key, pairs):
        self.loads[key] = self.bring(pairs)

    def arrive(self, key):
        for copy in self.loads.pop(key):
            copy.wait()

    def prefetch_units(self, layer, which):
        refs = self.refs
        targets = {"down": refs.w_one, "up": refs.w_two, "slope": refs.ups}
        for name in which:
            self.prefetch((name, layer), [(self.saved(name, layer), targets[name])])

    def bring(self, pairs):
        copies = []
        for src, dst in pairs:
            copies.append(pltpu.make_async_copy(src, dst, self.refs.load_sem.at[self.slot]))
            self.slot += 1
        for copy in copies:
            copy.start()
        return copies

    def saved(self, name, layer):
        return getattr(self.refs, name + "_in" + str(layer))

    def add_vec(self, row, value):
        total = jnp.sum(value, axis=0, keepdims=True)
        width = value.shape[1]
        self.refs.vgrad[row : row + 1, 0:width] = self.refs.vgrad[row : row + 1, 0:width] + total

    def send_part(self, key, landing):
        refs = self.refs
        slot = len(self.part_copies)
        copy = remote(
            refs.part, landing, refs.x_send.at[slot], refs.x_recv.at[slot], self.at.other
        )
        copy.start()
        self.part_copies[key] = copy

    def units(self, layer):
        refs = self.refs
        if layer == self.layers - 1:
            self.arrive(("cot", 0))
        for name in ("down", "slope", "up"):
            self.arrive((name, layer))
        refs.vgrad[...] = jnp.zeros_like(refs.vgrad)
        tiles = refs.w_one.shape[0] // 512

        def body(rows):
            grad = refs.grad[rows, :]
            self.add_vec(5, grad)
            refs.grad_low[rows, :] = grad.astype(BF)

            @pl.loop(0, tiles)
            def _(tile):
                cols = aligned(tile * 512, 512)
                value = dot_nt(refs.grad_low[rows, :], refs.w_one[cols, :])
                value = value * refs.ups[rows, cols].astype(F32)
                total = jnp.sum(value, axis=0, keepdims=True)
                refs.vgrad[7:8, cols] = refs.vgrad[7:8, cols] + total
                refs.ups[rows, cols] = value.astype(BF)

            part = dot_nt(refs.ups[rows, :], refs.w_two[...])
            refs.part_f[rows, :] = part
            refs.part[rows, :] = part.astype(BF)

        each_block(self.blocks, body)
        self.send_part((layer, 0), refs.got_one)
        weight = refs.w_one.at[pl.ds(0, refs.mixed_grad.shape[1]), :]
        self.prefetch(("proj", layer), [(self.saved("proj", layer), weight)])

    def vec(self, layer, row, width):
        return self.refs.vecs[layer, row : row + 1, 0:width]

    def norm_blocks(self, layer, first, landing, source, use):
        refs = self.refs

        def copy_of(step):
            slot = lax.rem(step, 2)
            rows = aligned(step * ROWS_Q, ROWS_Q)
            return pltpu.make_async_copy(
                source.at[rows, :], refs.aux.at[slot], refs.aux_sem.at[slot]
            )

        copy_of(0).start()

        @pl.loop(0, self.blocks)
        def _(step):
            @pl.when(step + 1 < self.blocks)
            def _():
                copy_of(step + 1).start()

            copy_of(step).wait()
            rows = aligned(step * ROWS_Q, ROWS_Q)
            use(rows, self.norm_back(rows, layer, first, landing, refs.aux[lax.rem(step, 2)]))

    def norm_back(self, rows, layer, first, landing, hidden):
        refs = self.refs
        width = refs.grad.shape[1]
        part = refs.part_f[rows, :] + landing[rows, :].astype(F32)
        scaled, inverse = norm_parts(hidden)
        entry = part * self.vec(layer, first, width)
        mean_one = jnp.mean(entry, axis=-1, keepdims=True)
        mean_two = jnp.mean(entry * scaled, axis=-1, keepdims=True)
        self.add_vec(first, part * scaled)
        self.add_vec(first + 1, part)
        grad = refs.grad[rows, :] + inverse * (entry - mean_one - scaled * mean_two)
        refs.grad[rows, :] = grad
        return grad

    def after(self, layer):
        refs = self.refs
        half = refs.mixed_grad.shape[1]
        self.prefetch(("low", layer), [(self.saved("low", layer), refs.low)])
        self.arrive(("proj", layer))
        self.part_copies[layer, 0].wait()

        def body(rows, grad):
            self.add_vec(4, grad)
            low = grad.astype(BF)
            refs.after_low[rows, :] = low
            refs.mixed_grad[rows, :] = dot_nt(low, refs.w_one[0:half, :]).astype(BF)

        self.norm_blocks(layer, 2, refs.got_one, self.saved("after", layer), body)
        weight = refs.w_two.at[:, pl.ds(0, refs.low.shape[1])]
        self.prefetch(("qkv", layer), [(self.saved("qkv", layer), weight)])
        if layer > 0:
            self.prefetch_units(layer - 1, ("down",))

    def attend(self, layer, pair):
        refs = self.refs
        if pair == 0:
            self.arrive(("low", layer))
        base = pair * 3 * PAIR
        query_cols, key_cols, value_cols = [
            slice(base + kind * PAIR, base + (kind + 1) * PAIR) for kind in range(3)
        ]
        refs.keys_t[...] = refs.low[:, key_cols].astype(F32).T.astype(BF)
        scale = HEAD_DIM**-0.5
        refs.dk[...] = jnp.zeros_like(refs.dk)
        refs.dv[...] = jnp.zeros_like(refs.dv)

        def body(rows):
            block = refs.low[rows, query_cols]
            dout = refs.mixed_grad[rows, pair * PAIR : (pair + 1) * PAIR]
            outs = []
            for head in range(2):
                mine, dmine = head_mask(block, head), head_mask(dout, head)
                scores = dot_nt(refs.low[:, key_cols], mine * jnp.asarray(scale, BF))
                probs = jnp.exp(scores - refs.lse_in[layer, pair, head : head + 1, rows])
                prob_grad = dot_nt(refs.low[:, value_cols], dmine)
                delta = jnp.sum(probs * prob_grad, axis=0, keepdims=True)
                score_low = (probs * (prob_grad - delta) * scale).astype(BF)
                refs.dv[...] += dot(probs.astype(BF), dmine)
                refs.dk[...] += dot(score_low, mine)
                outs.append(dot(refs.keys_t[head * HEAD_DIM : (head + 1) * HEAD_DIM], score_low))
            refs.dq[rows, :] = jnp.concatenate(outs, axis=0).T

        each_block(self.blocks, body)

        def last(rows):
            cosine, sine = rotation_tables(refs.tables[rows, :])

            def back(item):
                item = item.astype(BF).astype(F32)
                return item * cosine - swap_halves(item) * sine

            parts = (
                back(refs.dq[rows, :]),
                back(refs.dk[rows, :]),
                refs.dv[rows, :].astype(BF).astype(F32),
            )
            for kind, part in enumerate(parts):
                cols = slice(base + kind * PAIR, base + (kind + 1) * PAIR)
                refs.vgrad[6:7, cols] = refs.vgrad[6:7, cols] + jnp.sum(part, axis=0, keepdims=True)
                refs.low[rows, cols] = part.astype(BF)

        each_block(self.blocks, last)

    def heads(self, layer):
        refs = self.refs
        width = refs.low.shape[1]
        self.arrive(("qkv", layer))

        def body(rows):
            part = dot_nt(refs.low[rows, :], refs.w_two[:, 0:width])
            refs.part_f[rows, :] = part
            refs.part[rows, :] = part.astype(BF)

        each_block(self.blocks, body)
        self.send_part((layer, 1), refs.got_two)
        if layer > 0:
            self.prefetch_units(layer - 1, ("up", "slope"))

    def entry(self, layer):
        refs = self.refs
        self.part_copies[layer, 1].wait()
        source = self.saved("entry", layer)
        self.norm_blocks(layer, 0, refs.got_two, source, lambda rows, grad: None)

    def weight_tile(self, name, layer):
        refs = self.refs
        stream = getattr(refs, name + "_stream")
        source, right = {
            "down": ("active", refs.grad_low),
            "up": ("normed_two", refs.ups),
            "proj": ("mixed", refs.after_low),
            "qkv": ("normed", refs.low),
        }[name]
        def fetch(tile, layer):
            rows = stream.shape[1]
            cols = aligned(self.at.back(tile + 1) * rows, rows)
            self.prefetch((name, "tile"), [(self.saved(source, layer).at[:, cols], stream)])

        def compute(tile, out):
            rows, columns = out.shape
            if (name, "tile") not in self.loads:
                fetch(tile, layer)
            self.arrive((name, "tile"))
            high, wide = min(rows, 256), min(columns, 512)

            @pl.loop(0, rows // high)
            def _(row):
                at_rows = aligned(row * high, high)

                @pl.loop(0, columns // wide)
                def _(column):
                    cols = aligned(column * wide, wide)
                    out[at_rows, cols] = dot_tn(stream[:, at_rows], right[:, cols]).astype(BF)

            if tile + 1 < self.at.ring:
                fetch(tile + 1, layer)
            elif layer > 0:
                fetch(0, layer - 1)

        return compute

    def vector_rows(self, target):
        refs, at = self.refs, self.at
        target[...] = jnp.zeros_like(target)
        per_chip = refs.vec_rows * 2
        keep = (at.core == 0).astype(F32)
        for row in range(48):
            source = refs.vgrad[row // 8 : row // 8 + 1, row % 8 * 128 : (row % 8 + 1) * 128]
            place = row % per_chip
            target[row // per_chip, place : place + 1, :] = source * keep
        places = []
        for pair in range(at.ring):
            for kind in range(3):
                places.append((48 + kind * 8 + 2 * pair + at.core, 6, pair * 3 + kind))
            for part in range(4):
                places.append((72 + (2 * pair + at.core) * 4 + part, 7, pair * 4 + part))
        for place, row, block in places:
            target[lax.div(place, per_chip), pl.ds(lax.rem(place, per_chip), 1), :] = refs.vgrad[
                row : row + 1, block * 128 : (block + 1) * 128
            ]


def squares_of(ref):
    rows, columns = ref.shape

    def body(step, total):
        part = ref[aligned(step * 16, 16), :].astype(F32)
        part = part * part
        part = part[0:8] + part[8:16]
        for column in range(0, columns, 128):
            total = total + part[:, column : column + 128]
        return total

    return lax.fori_loop(0, rows // 16, body, jnp.zeros((8, 128), F32))


def backward_kernel(names, layers, vec_rows, *operands):
    refs = SimpleNamespace(**dict(zip(names, operands)))
    refs.vec_rows = vec_rows
    at = Places()
    ring = at.ring
    sems = (Sems(refs.send_sem), Sems(refs.recv_sem), Sems(refs.store_sem))
    greet((at.other, at.over_x, at.over_y, at.down), 4)
    work = Backward(at, refs, layers)
    work.prefetch(("cot", 0), [(refs.cot_in, refs.grad)])
    work.prefetch_units(layers - 1, ("down", "slope", "up"))
    sums = {}
    for layer in range(layers):
        for name, z_first, x_first in (
            ("qkv", True, True),
            ("proj", True, False),
            ("up", False, True),
            ("down", False, False),
        ):
            sums[name, layer] = Sum(
                at, sems, refs, name, layer, z_first, x_first, work.weight_tile(name, layer)
            )
    vectors = [
        VectorSum(at, sems, None, refs.vec_got.at[layer], refs.vec_hop.at[layer], refs.vec_sum.at[layer])
        for layer in range(layers)
    ]
    refs.square_sum[0] = jnp.zeros((8, 128), F32)
    steps = []

    def free(sem):
        for target in (at.over_x, at.over_y, at.down):
            pl.semaphore_signal(sem, inc=1, device_id=target, device_id_type=pl.DeviceIdType.MESH)

    def wide_steps(layer):
        items = [sums["down", layer], sums["up", layer]]

        def turn(tile):
            for item in items:
                item.middle(tile)
            if tile + 2 < ring:
                for item in items:
                    item.start(tile + 2)
            if tile > 0:
                for item in items:
                    item.finish(tile - 1)

        def begin(tile):
            if tile == 0 and layer + 1 < layers:
                pl.semaphore_wait(refs.free_wide, 3)
            for item in items:
                item.start(tile)

        def end():
            for item in items:
                item.finish(ring - 1)

        def far():
            for item in items:
                item.gather_far()

        def close():
            for item in items:
                item.gather_end()
                refs.square_sum[0] = refs.square_sum[0] + squares_of(item.total())
            if layer > 0:
                for item in items:
                    item.drain()
                free(refs.free_wide)

        turns = [partial(begin, 0), partial(begin, 1)]
        turns += [partial(turn, tile) for tile in range(ring)]
        return turns + [end, far, close]

    def slab_steps(name, layer):
        item = sums[name, layer]

        def begin():
            item.start(0)

        def close():
            item.gather_end()
            refs.square_sum[0] = refs.square_sum[0] + squares_of(item.total())
            if layer > 0:
                item.drain()

        turns = [begin] + [partial(item.ring_step, tile) for tile in range(1, ring)]
        return turns + [item.slab_middle, item.slab_finish, item.gather_far, close]

    def run(steps, count=1):
        for _ in range(count):
            if steps:
                steps.pop(0)()

    late = []
    for layer in reversed(range(layers)):
        last = layer == 0
        wide, proj, qkv = wide_steps(layer), slab_steps("proj", layer), slab_steps("qkv", layer)
        work.units(layer)
        run(late, 3)
        run(wide, 2)
        run(late, 2)
        work.after(layer)
        run(late, 2)
        if layer + 1 == layers:
            run(proj)
        for pair in range(work.pairs):
            work.attend(layer, pair)
            run(wide)
            run(late, 3)
            if layer + 1 == layers and pair > 0:
                run(proj)
        while late:
            run(late)
        if layer + 1 < layers:
            free(refs.free_slab)
            pl.semaphore_wait(refs.free_slab, 3)
            run(proj)
        work.heads(layer)
        run(wide)
        run(proj)
        run(qkv)
        work.entry(layer)
        if last:
            save = pltpu.make_async_copy(refs.grad, refs.input_grad, sems[2].take())
            save.start()
        work.vector_rows(refs.vec_sum.at[layer, 0])
        run(qkv)
        run(wide)
        run(proj)
        vector = [vectors[layer].advance] * 7
        while proj or qkv or vector:
            late += wide[:1] + qkv[:1] + proj[:1] + vector[:1]
            qkv, proj, vector, wide = qkv[1:], proj[1:], vector[1:], wide[1:]
        late = late + wide
        wide = []
    while late:
        run(late)
    save.wait()
    total = refs.square_sum[0]
    for layer in range(layers):
        vec_total = refs.vec_hop[layer, ring - 2]
        refs.vec_out[layer] = vec_total
        part = vec_total * vec_total * 0.125
        for row in range(0, part.shape[0], 8):
            total = total + part[row : row + 8]
    refs.square_sum[0] = total
    copies = []

    def square_copy(src, dst, target):
        copy = remote(src, dst, sems[0].take(), sems[1].take(), target)
        copy.start()
        copies.append(copy)
        copy.wait_recv()

    for idx, target in enumerate((at.other, at.over_x, at.over_y)):
        square_copy(refs.square_sum.at[idx], refs.square_got.at[idx], target)
        refs.square_sum[idx + 1] = refs.square_sum[idx] + refs.square_got[idx]
    total = refs.square_sum[3]
    for hop in range(ring - 1):
        source = refs.square_sum.at[3] if hop == 0 else refs.square_got.at[2 + hop]
        square_copy(source, refs.square_got.at[3 + hop], at.up)
        total = total + refs.square_got[3 + hop]
    refs.square_out[...] = total
    for name in WEIGHTS:
        sums[name, 0].drain()
    for vector in vectors:
        for copy in vector.copies:
            copy.wait_send()
    for copy in copies:
        copy.wait_send()


def backward(kept, layers, vec_rows):
    ring = lax.axis_size(FSDP) // 2
    length, width = kept.cot_out.shape
    qkv_half, up_half = kept.low_out0.shape[1], kept.slope_out0.shape[1]
    half = kept.mixed_out0.shape[1]
    inputs = dict(
        cot_in=kept.cot_out,
        tables=kept.table_out,
        vecs=kept.vecs,
        lse_in=kept.lse_out,
    )
    for layer in range(layers):
        for name in (*WEIGHTS, "normed", "low", "mixed", "after", "normed_two", "active", "slope"):
            inputs[name + "_in" + str(layer)] = getattr(kept, name + "_out" + str(layer))
        entry = kept.clip_out if layer == 0 else getattr(kept, "result_out" + str(layer - 1))
        inputs["entry_in" + str(layer)] = entry
    slabs = dict(
        qkv=(width // ring, qkv_half),
        proj=(half // ring, width),
        up=(width // ring, up_half),
        down=(up_half // ring, width),
    )
    outputs, scratch = {}, {}
    dma, regular = pltpu.SemaphoreType.DMA, pltpu.SemaphoreType.REGULAR
    for name, (rows, columns) in slabs.items():
        for layer in range(layers):
            outputs[name + "_stage" + str(layer)] = ((rows, columns), BF)
            if name in ("qkv", "up"):
                outputs[name + "_arrive" + str(layer)] = ((rows // 2, columns), BF)
        z_first = name in ("qkv", "proj")
        tiles, quarter = 1 if z_first else ring, rows // 4
        scratch[name + "_stream"] = pltpu.VMEM((length, rows), BF)
        scratch[name + "_own"] = pltpu.VMEM((2, rows, columns), BF)
        scratch[name + "_one"] = pltpu.VMEM((tiles, 2 * quarter, columns), BF)
        scratch[name + "_two"] = pltpu.VMEM((tiles, quarter, columns), BF)
        scratch[name + "_three"] = pltpu.VMEM(
            (ring - 1, rows if z_first else quarter, columns), BF
        )
    outputs["input_grad"] = ((length, width), F32)
    outputs["vec_out"] = ((layers, 32, 128), F32)
    outputs["square_out"] = ((8, 128), F32)
    scratch |= dict(
        grad=pltpu.VMEM((length, width), F32),
        aux=pltpu.VMEM((2, ROWS_Q, width), F32),
        aux_sem=dma((2,)),
        part_f=pltpu.VMEM((length, width), F32),
        grad_low=pltpu.VMEM((length, width), BF),
        after_low=pltpu.VMEM((length, width), BF),
        part=pltpu.VMEM((length, width), BF),
        got_one=pltpu.VMEM((length, width), BF),
        got_two=pltpu.VMEM((length, width), BF),
        ups=pltpu.VMEM((length, up_half), BF),
        w_one=pltpu.VMEM((up_half, width), BF),
        w_two=pltpu.VMEM((width, up_half), BF),
        low=pltpu.VMEM((length, qkv_half), BF),
        mixed_grad=pltpu.VMEM((length, half), BF),
        keys_t=pltpu.VMEM((PAIR, length), BF),
        dq=pltpu.VMEM((length, PAIR), F32),
        dk=pltpu.VMEM((length, PAIR), F32),
        dv=pltpu.VMEM((length, PAIR), F32),
        vgrad=pltpu.VMEM((8, up_half), F32),
        vec_got=pltpu.VMEM((layers, 3, ring, 32, 128), F32),
        vec_hop=pltpu.VMEM((layers, ring - 1, 32, 128), F32),
        vec_sum=pltpu.VMEM((layers, 4, ring, 32, 128), F32),
        square_got=pltpu.VMEM((3 + ring - 1, 8, 128), F32),
        square_sum=pltpu.VMEM((4, 8, 128), F32),
        send_sem=dma((120 * layers,)),
        recv_sem=dma((120 * layers,)),
        store_sem=dma((8 * layers,)),
        load_sem=dma((32 * layers,)),
        x_send=dma((2 * layers,)),
        x_recv=dma((2 * layers,)),
        free_wide=regular,
        free_slab=regular,
    )
    in_vmem = ("tables", "vecs", "lse_in", "vec_out", "square_out")
    anywhere = pl.BlockSpec(memory_space=pl.ANY)
    vmem = pl.BlockSpec(memory_space=pltpu.VMEM)
    names = [*inputs, *outputs, *scratch]
    results = pl.pallas_call(
        partial(backward_kernel, names, layers, vec_rows),
        in_specs=[vmem if name in in_vmem else anywhere for name in inputs],
        out_specs=[vmem if name in in_vmem else anywhere for name in outputs],
        out_shape=[jax.ShapeDtypeStruct(*shape) for shape in outputs.values()],
        scratch_shapes=list(scratch.values()),
        compiler_params=pltpu.CompilerParams(
            collective_id=1, has_side_effects=True, vmem_limit_bytes=63 * 1024 * 1024
        ),
        cost_estimate=pl.CostEstimate(
            flops=100_000_000_000, bytes_accessed=600_000_000, transcendentals=0
        ),
        name="backward",
    )(*inputs.values())
    return SimpleNamespace(**dict(zip(outputs, results)))


def fast_device(
    clip_tokens,
    patch_coords,
    out_cotangent,
    vector_params,
    qkv_weight,
    proj_weight,
    up_weight,
    down_weight,
    first_vector,
    first_qkv,
    first_proj,
    first_up,
    first_down,
    second_vector,
    second_qkv,
    second_proj,
    second_up,
    second_down,
):
    masters = (vector_params, qkv_weight, proj_weight, up_weight, down_weight)
    firsts = (first_vector, first_qkv, first_proj, first_up, first_down)
    seconds = (second_vector, second_qkv, second_proj, second_up, second_down)
    layer_count = vector_params.shape[0]
    batch_local, chunk_len = clip_tokens.shape[:2]
    seq_parts = lax.axis_size(SEQ)
    parts = lax.axis_size(FSDP)
    ring = parts // 2
    seq = lax.axis_index(SEQ)
    shard = lax.axis_index(FSDP)
    core = lax.rem(shard, 2)
    even = lax.rem(seq, 2) == 0

    def from_clips(item):
        mine = pick(item.reshape((2, 2, chunk_len) + item.shape[1:]), core)
        pieces = [None, None]
        for turn in range(2):
            piece = jnp.where(even, mine[turn], mine[1 - turn])
            pairs = []
            for src_seq in range(seq_parts):
                for src in range(parts):
                    dst_seq = 2 * (src % 2) + (src_seq + turn) % 2
                    dst = src - src % 2 + src_seq // 2
                    pairs.append((dst_seq * parts + dst, src_seq * parts + src))
            pieces[turn] = lax.ppermute(piece, (SEQ, FSDP), pairs)
        return jnp.where(
            even, jnp.stack([pieces[0], pieces[1]]), jnp.stack([pieces[1], pieces[0]])
        )

    tables = []
    for idx in range(batch_local):
        cosine, sine = rotary_tables(patch_coords[:, idx], HEAD_DIM // 2)
        tables.append(jnp.concatenate([cosine, sine, cosine, sine], axis=1))
    share = vector_params.shape[1]
    vector_rows = vector_params.astype(BF).astype(F32).reshape(-1, 128)
    vector_rows = jnp.pad(vector_rows, ((0, -vector_rows.shape[0] % 8), (0, 0)))
    kept = forward(
        qkv_weight,
        up_weight,
        down_weight,
        proj_weight,
        clip_tokens,
        out_cotangent,
        jnp.stack(tables),
        vector_rows,
        share // 128,
    )
    block_output = from_clips(getattr(kept, "result_out" + str(layer_count - 1)))

    back = backward(kept, layer_count, share // 128)
    input_grad = from_clips(back.input_grad)

    clip_count = batch_local * parts
    norm_value = jnp.sqrt(jnp.sum(back.square_out)) / clip_count
    param_count = sum(master.size for master in masters) * parts
    factor = jnp.minimum(1.0, CLIP_RATIO * math.sqrt(float(param_count)) / (norm_value + 1e-06))

    vector_total = back.vec_out.reshape(layer_count, -1)[:, : 2 * share]
    vector_grad = lax.dynamic_slice_in_dim(vector_total, core * share, share, 1) / clip_count
    vector_new = adam_update(vector_params, vector_grad, first_vector, second_vector, factor)
    updates = [(vector_grad, *vector_new, vector_new[2].astype(BF))]
    for kind, name in enumerate(WEIGHTS):
        parts_of = ("_stage", "_arrive") if name in ("qkv", "up") else ("_stage",)
        updates.append(
            adam_matrix(
                [
                    getattr(back, name + part + str(layer))
                    for layer in range(layer_count)
                    for part in parts_of
                ],
                masters[kind + 1],
                firsts[kind + 1],
                seconds[kind + 1],
                factor,
                core,
                3 if kind == 0 else 1,
                clip_count,
            )
        )
    return (
        block_output,
        input_grad,
        *[item[0] for item in updates],
        norm_value.reshape(1),
        *[item[1] for item in updates],
        *[item[2] for item in updates],
        *[item[3] for item in updates],
        *[item[4] for item in updates],
    )


def solution(mesh):
    in_specs = (
        P(FSDP, SEQ, None),
        P(None, FSDP, SEQ),
        P(FSDP, SEQ, None),
        P(None, FSDP),
        P(None, FSDP, None),
        P(None, FSDP, None),
        P(None, FSDP, None),
        P(None, FSDP, None),
        P(None, FSDP),
        P(None, FSDP, None),
        P(None, FSDP, None),
        P(None, FSDP, None),
        P(None, FSDP, None),
        P(None, FSDP),
        P(None, FSDP, None),
        P(None, FSDP, None),
        P(None, FSDP, None),
        P(None, FSDP, None),
    )
    out_specs = (
        P(FSDP, SEQ, None),
        P(FSDP, SEQ, None),
        P(None, FSDP),
        P(None, FSDP, None),
        P(None, FSDP, None),
        P(None, FSDP, None),
        P(None, FSDP, None),
        P(),
        P(None, FSDP),
        P(None, FSDP, None),
        P(None, FSDP, None),
        P(None, FSDP, None),
        P(None, FSDP, None),
        P(None, FSDP),
        P(None, FSDP, None),
        P(None, FSDP, None),
        P(None, FSDP, None),
        P(None, FSDP, None),
        P(None, FSDP),
        P(None, FSDP, None),
        P(None, FSDP, None),
        P(None, FSDP, None),
        P(None, FSDP, None),
        P(None, FSDP),
        P(None, FSDP, None),
        P(None, FSDP, None),
        P(None, FSDP, None),
        P(None, FSDP, None),
    )
    body = fast_device if fits_fast(mesh) else general_device
    return jax.shard_map(
        body, mesh=mesh, in_specs=in_specs, out_specs=out_specs, check_vma=False
    )
```

```python
from functools import partial
import math
from types import SimpleNamespace

import jax
import jax.numpy as jnp
from jax import lax
from jax.experimental import pallas as pl
from jax.experimental.pallas import tpu as pltpu
from jax.sharding import PartitionSpec as P

FSDP = "fsdp"
SEQ = "seq"
D = 1024
HEADS = 16
HEAD_DIM = 64


BETA_ONE = 0.5
BETA_TWO = 0.75
LEARN_RATE = 0.1
DECAY_RATE = 0.1
CLIP_RATIO = 0.2
ADAM_EPS = 1e-08
ROPE_BASE = 10000.0


def pieces(vector):
    return (
        vector[0:D],
        vector[D : 2 * D],
        vector[2 * D : 3 * D],
        vector[3 * D : 4 * D],
        vector[4 * D : 5 * D],
        vector[5 * D : 6 * D],
        vector[6 * D : 9 * D],
        vector[9 * D :],
    )


def layer_norm(hidden, ln_gain, ln_shift):
    center = hidden - jnp.mean(hidden, axis=-1, keepdims=True)
    spread = jnp.mean(center * center, axis=-1, keepdims=True)
    return center * lax.rsqrt(spread + 1e-06) * ln_gain + ln_shift


def gelu_exact(upward):
    return 0.5 * upward * (1.0 + jax.scipy.special.erf(upward * (1.0 / math.sqrt(2.0))))


def rotary_tables(coords_clip, pair_count):
    pair_index = jnp.arange(pair_count, dtype=jnp.int32)
    side_pairs = pair_count // 3
    time_pairs = pair_count - 2 * side_pairs
    in_time = pair_index < time_pairs
    in_height = jnp.logical_and(pair_index >= time_pairs, pair_index < time_pairs + side_pairs)
    offset = jnp.where(in_time, 0, jnp.where(in_height, time_pairs, time_pairs + side_pairs))
    seg_span = jnp.where(in_time, time_pairs, side_pairs)
    local_rank = (pair_index - offset).astype(jnp.float32)
    frequency = jnp.exp(-math.log(ROPE_BASE) * local_rank / seg_span.astype(jnp.float32))
    positions = coords_clip.astype(jnp.float32)
    chosen = jnp.where(
        in_time[None, :],
        positions[0][:, None],
        jnp.where(in_height[None, :], positions[1][:, None], positions[2][:, None]),
    )
    angles = chosen * frequency[None, :]
    return (jnp.cos(angles), jnp.sin(angles))


def rotate(values_in, cosine, sine_table):
    half_width = values_in.shape[-1] // 2
    first_half = values_in[..., :half_width]
    second_half = values_in[..., half_width:]
    cos_wide = cosine[:, None, :]
    sin_wide = sine_table[:, None, :]
    return jnp.concatenate(
        [
            first_half * cos_wide - second_half * sin_wide,
            first_half * sin_wide + second_half * cos_wide,
        ],
        axis=-1,
    )


def attend_forward(queries, key_rows, value_rows):
    full_len = queries.shape[0]
    block_rows = min(512, full_len)
    score_scale = HEAD_DIM ** (-0.5)
    query_blocks = queries.reshape(
        full_len // block_rows, block_rows, queries.shape[1], queries.shape[2]
    )

    def one_block(query_block):
        scores = (
            jnp.einsum("qhd,khd->hqk", query_block, key_rows, preferred_element_type=jnp.float32)
            * score_scale
        )
        row_max = jnp.max(scores, axis=-1, keepdims=True)
        exponent = jnp.exp(scores - row_max)
        row_total = jnp.sum(exponent, axis=-1, keepdims=True)
        prob_low = (exponent / row_total).astype(jnp.bfloat16)
        mixed_rows = jnp.einsum(
            "hqk,khd->qhd", prob_low, value_rows, preferred_element_type=jnp.float32
        )
        return (mixed_rows, row_max[..., 0] + jnp.log(row_total[..., 0]))

    mixed_rows, log_sums = lax.map(one_block, query_blocks)
    return (mixed_rows.reshape(queries.shape), log_sums)


def attend_backward(queries, key_rows, value_rows, log_sums, head_grad):
    full_len = queries.shape[0]
    block_rows = min(512, full_len)
    score_scale = HEAD_DIM ** (-0.5)
    block_shape = (full_len // block_rows, block_rows, queries.shape[1], queries.shape[2])

    def one_block(carry, block_in):
        key_grad, value_grad = carry
        query_block, grad_block, lse_block = block_in
        scores = (
            jnp.einsum("qhd,khd->hqk", query_block, key_rows, preferred_element_type=jnp.float32)
            * score_scale
        )
        prob_rows = jnp.exp(scores - lse_block[..., None])
        prob_low = prob_rows.astype(jnp.bfloat16)
        value_grad = value_grad + jnp.einsum(
            "hqk,qhd->khd", prob_low, grad_block, preferred_element_type=jnp.float32
        )
        prob_grad = jnp.einsum(
            "qhd,khd->hqk", grad_block, value_rows, preferred_element_type=jnp.float32
        )
        score_grad = prob_rows * (
            prob_grad - jnp.sum(prob_rows * prob_grad, axis=-1, keepdims=True)
        )
        score_low = (score_grad * score_scale).astype(jnp.bfloat16)
        query_grad = jnp.einsum(
            "hqk,khd->qhd", score_low, key_rows, preferred_element_type=jnp.float32
        )
        key_grad = key_grad + jnp.einsum(
            "hqk,qhd->khd", score_low, query_block, preferred_element_type=jnp.float32
        )
        return ((key_grad, value_grad), query_grad)

    zero_heads = jnp.zeros(queries.shape, jnp.float32)
    (key_grad, value_grad), query_grad = lax.scan(
        one_block,
        (zero_heads, zero_heads),
        (queries.reshape(block_shape), head_grad.reshape(block_shape), log_sums),
    )
    return (query_grad.reshape(queries.shape), key_grad, value_grad)


def layer_forward(hidden, cosine, sine_table, weights, seq_parts):
    vector_low, qkv_w, proj_w, up_w, down_w = weights
    gain_one, shift_one, gain_two, shift_two, proj_bias, down_bias, qkv_bias, up_bias = pieces(
        vector_low.astype(jnp.float32)
    )
    row_count = hidden.shape[0]
    local_heads = HEADS // seq_parts
    normed = layer_norm(hidden, gain_one, shift_one).astype(jnp.bfloat16)
    qkv_all = jnp.dot(normed, qkv_w, preferred_element_type=jnp.float32) + qkv_bias
    split_qkv = qkv_all.reshape(row_count, 3, HEADS, HEAD_DIM)
    stacked = jnp.stack(
        [
            rotate(split_qkv[:, 0], cosine, sine_table),
            rotate(split_qkv[:, 1], cosine, sine_table),
            split_qkv[:, 2],
        ],
        axis=1,
    ).astype(jnp.bfloat16)
    packed = stacked.reshape(row_count, 3, seq_parts, local_heads * HEAD_DIM)
    by_heads = lax.all_to_all(packed, SEQ, split_axis=2, concat_axis=0, tiled=True)
    full_len = by_heads.shape[0]
    by_heads = by_heads.reshape(full_len, 3, local_heads, HEAD_DIM)
    mixed_rows, log_sums = attend_forward(by_heads[:, 0], by_heads[:, 1], by_heads[:, 2])
    mixed_low = mixed_rows.astype(jnp.bfloat16).reshape(full_len, 1, local_heads * HEAD_DIM)
    by_tokens = lax.all_to_all(mixed_low, SEQ, split_axis=0, concat_axis=1, tiled=True).reshape(
        row_count, D
    )
    after_attn = hidden + jnp.dot(by_tokens, proj_w, preferred_element_type=jnp.float32) + proj_bias
    normed_two = layer_norm(after_attn, gain_two, shift_two).astype(jnp.bfloat16)
    upward = jnp.dot(normed_two, up_w, preferred_element_type=jnp.float32) + up_bias
    active = gelu_exact(upward).astype(jnp.bfloat16)
    result = after_attn + jnp.dot(active, down_w, preferred_element_type=jnp.float32) + down_bias
    saved_state = (
        hidden,
        normed,
        by_heads,
        log_sums,
        by_tokens,
        after_attn,
        normed_two,
        upward,
        active,
    )
    return (result, saved_state)


def layer_backward(grad_out, saved_state, weights, cosine, sine_table, seq_parts):
    vector_low, qkv_w, proj_w, up_w, down_w = weights
    gain_one, shift_one, gain_two, shift_two, proj_bias, down_bias, qkv_bias, up_bias = pieces(
        vector_low.astype(jnp.float32)
    )
    hidden, normed, by_heads, log_sums, by_tokens, after_attn, normed_two, upward, active = (
        saved_state
    )
    row_count = hidden.shape[0]
    local_heads = HEADS // seq_parts
    down_bias_grad = jnp.sum(grad_out, axis=0)
    grad_low = grad_out.astype(jnp.bfloat16)
    down_grad = jnp.dot(active.T, grad_low, preferred_element_type=jnp.float32)
    active_grad = jnp.dot(grad_low, down_w.T, preferred_element_type=jnp.float32)
    gelu_value, gelu_pull = jax.vjp(gelu_exact, upward)
    upward_grad = gelu_pull(active_grad)[0]
    up_bias_grad = jnp.sum(upward_grad, axis=0)
    upward_low = upward_grad.astype(jnp.bfloat16)
    up_grad = jnp.dot(normed_two.T, upward_low, preferred_element_type=jnp.float32)
    normed_two_grad = jnp.dot(upward_low, up_w.T, preferred_element_type=jnp.float32)
    norm_value_two, norm_pull_two = jax.vjp(layer_norm, after_attn, gain_two, shift_two)
    attn_in_grad, gain_two_grad, shift_two_grad = norm_pull_two(normed_two_grad)
    after_grad = grad_out + attn_in_grad
    proj_bias_grad = jnp.sum(after_grad, axis=0)
    after_low = after_grad.astype(jnp.bfloat16)
    proj_grad = jnp.dot(by_tokens.T, after_low, preferred_element_type=jnp.float32)
    mixed_grad = jnp.dot(after_low, proj_w.T, preferred_element_type=jnp.float32).astype(
        jnp.bfloat16
    )
    head_grad = lax.all_to_all(
        mixed_grad.reshape(row_count, seq_parts, local_heads * HEAD_DIM),
        SEQ,
        split_axis=1,
        concat_axis=0,
        tiled=True,
    )
    full_len = head_grad.shape[0]
    head_grad = head_grad.reshape(full_len, local_heads, HEAD_DIM)
    query_grad, key_grad, value_grad = attend_backward(
        by_heads[:, 0], by_heads[:, 1], by_heads[:, 2], log_sums, head_grad
    )
    stacked_grad = (
        jnp.stack([query_grad, key_grad, value_grad], axis=1)
        .astype(jnp.bfloat16)
        .reshape(full_len, 3, 1, local_heads * HEAD_DIM)
    )
    token_grad = (
        lax.all_to_all(stacked_grad, SEQ, split_axis=0, concat_axis=2, tiled=True)
        .reshape(row_count, 3, HEADS, HEAD_DIM)
        .astype(jnp.float32)
    )
    pair_grad_in = token_grad[:, :2].reshape(row_count, 2 * HEADS, HEAD_DIM)
    rotated_value, rotate_pull = jax.vjp(
        partial(rotate, cosine=cosine, sine_table=sine_table), pair_grad_in
    )
    pair_grad = rotate_pull(pair_grad_in)[0].reshape(row_count, 2, HEADS, HEAD_DIM)
    qkv_grad = jnp.concatenate([pair_grad, token_grad[:, 2:]], axis=1).reshape(row_count, 3 * D)
    qkv_bias_grad = jnp.sum(qkv_grad, axis=0)
    qkv_low = qkv_grad.astype(jnp.bfloat16)
    qkv_w_grad = jnp.dot(normed.T, qkv_low, preferred_element_type=jnp.float32)
    normed_grad = jnp.dot(qkv_low, qkv_w.T, preferred_element_type=jnp.float32)
    norm_value_one, norm_pull_one = jax.vjp(layer_norm, hidden, gain_one, shift_one)
    in_grad, gain_one_grad, shift_one_grad = norm_pull_one(normed_grad)
    input_grad = after_grad + in_grad
    vector_grad = jnp.concatenate(
        [
            gain_one_grad,
            shift_one_grad,
            gain_two_grad,
            shift_two_grad,
            proj_bias_grad,
            down_bias_grad,
            qkv_bias_grad,
            up_bias_grad,
        ]
    )
    return (input_grad, (vector_grad, qkv_w_grad, proj_grad, up_grad, down_grad))


def adam_update(master, grad_item, first_old, second_old, factor):
    clipped = grad_item * factor
    first_new = BETA_ONE * first_old + (1.0 - BETA_ONE) * clipped
    second_new = BETA_TWO * second_old + (1.0 - BETA_TWO) * clipped * clipped
    updated = master - LEARN_RATE * (
        first_new / (jnp.sqrt(second_new) + ADAM_EPS) + DECAY_RATE * master
    )
    return (first_new, second_new, updated)


def general_device(
    clip_tokens,
    patch_coords,
    out_cotangent,
    vector_params,
    qkv_weight,
    proj_weight,
    up_weight,
    down_weight,
    first_vector,
    first_qkv,
    first_proj,
    first_up,
    first_down,
    second_vector,
    second_qkv,
    second_proj,
    second_up,
    second_down,
):
    masters = (vector_params, qkv_weight, proj_weight, up_weight, down_weight)
    firsts = (first_vector, first_qkv, first_proj, first_up, first_down)
    seconds = (second_vector, second_qkv, second_proj, second_up, second_down)
    lowered = tuple((master.astype(jnp.bfloat16) for master in masters))
    layer_count = vector_params.shape[0]
    batch_local = clip_tokens.shape[0]
    seq_parts = lax.axis_size(SEQ)
    fsdp_parts = lax.axis_size(FSDP)
    grad_accum = tuple(
        (
            jnp.zeros((layer_count, master.shape[1] * fsdp_parts) + master.shape[2:], jnp.float32)
            for master in masters
        )
    )
    output_rows = []
    input_rows = []
    for batch_idx in range(batch_local):
        cosine, sine_table = rotary_tables(patch_coords[:, batch_idx], HEAD_DIM // 2)
        hidden = clip_tokens[batch_idx]
        saved_layers = []
        for layer_idx in range(layer_count):
            weights = (
                lax.all_gather(lowered[0][layer_idx], FSDP, axis=0, tiled=True),
                lax.all_gather(lowered[1][layer_idx], FSDP, axis=0, tiled=True),
                lax.all_gather(lowered[2][layer_idx], FSDP, axis=0, tiled=True),
                lax.all_gather(lowered[3][layer_idx], FSDP, axis=0, tiled=True),
                lax.all_gather(lowered[4][layer_idx], FSDP, axis=0, tiled=True),
            )
            hidden, saved_state = layer_forward(hidden, cosine, sine_table, weights, seq_parts)
            saved_layers.append(saved_state)
        output_rows.append(hidden)
        grad_rows = out_cotangent[batch_idx]
        for layer_idx in reversed(range(layer_count)):
            weights = (
                lax.all_gather(lowered[0][layer_idx], FSDP, axis=0, tiled=True),
                lax.all_gather(lowered[1][layer_idx], FSDP, axis=0, tiled=True),
                lax.all_gather(lowered[2][layer_idx], FSDP, axis=0, tiled=True),
                lax.all_gather(lowered[3][layer_idx], FSDP, axis=0, tiled=True),
                lax.all_gather(lowered[4][layer_idx], FSDP, axis=0, tiled=True),
            )
            grad_rows, layer_grads = layer_backward(
                grad_rows, saved_layers[layer_idx], weights, cosine, sine_table, seq_parts
            )
            grad_accum = tuple(
                (
                    accum_item.at[layer_idx].add(grad_item)
                    for accum_item, grad_item in zip(grad_accum, layer_grads)
                )
            )
        input_rows.append(grad_rows)
    shard_sums = (
        lax.psum_scatter(grad_accum[0], FSDP, scatter_dimension=1, tiled=True),
        lax.psum_scatter(grad_accum[1], FSDP, scatter_dimension=1, tiled=True),
        lax.psum_scatter(grad_accum[2], FSDP, scatter_dimension=1, tiled=True),
        lax.psum_scatter(grad_accum[3], FSDP, scatter_dimension=1, tiled=True),
        lax.psum_scatter(grad_accum[4], FSDP, scatter_dimension=1, tiled=True),
    )
    seq_sums = lax.psum(
        (shard_sums[0], shard_sums[1], shard_sums[2], shard_sums[3], shard_sums[4]), SEQ
    )
    clip_count = batch_local * fsdp_parts
    grad_shards = tuple((sum_item / clip_count for sum_item in seq_sums))
    local_squares = sum((jnp.sum(grad_item * grad_item) for grad_item in grad_shards))
    squares_total = lax.psum(local_squares, FSDP)
    norm_value = jnp.sqrt(squares_total)
    param_count = sum((master.size for master in masters)) * fsdp_parts
    factor = jnp.minimum(1.0, CLIP_RATIO * math.sqrt(float(param_count)) / (norm_value + 1e-06))
    updates = [
        adam_update(master, grad_item, first_old, second_old, factor)
        for master, grad_item, first_old, second_old in zip(masters, grad_shards, firsts, seconds)
    ]
    return (
        jnp.stack(output_rows),
        jnp.stack(input_rows),
        grad_shards[0],
        grad_shards[1],
        grad_shards[2],
        grad_shards[3],
        grad_shards[4],
        norm_value.reshape(1),
        updates[0][0],
        updates[1][0],
        updates[2][0],
        updates[3][0],
        updates[4][0],
        updates[0][1],
        updates[1][1],
        updates[2][1],
        updates[3][1],
        updates[4][1],
        updates[0][2],
        updates[1][2],
        updates[2][2],
        updates[3][2],
        updates[4][2],
        updates[0][2].astype(jnp.bfloat16),
        updates[1][2].astype(jnp.bfloat16),
        updates[2][2].astype(jnp.bfloat16),
        updates[3][2].astype(jnp.bfloat16),
        updates[4][2].astype(jnp.bfloat16),
    )


ROWS_Q = 256
ADD_ROWS = 32
PAIR = 2 * HEAD_DIM
BF = jnp.bfloat16
F32 = jnp.float32
VMEM_LIMIT = 56 * 1024 * 1024


def fits_fast(mesh):
    return dict(mesh.shape) == {"seq": 4, "fsdp": 8}


def swap_core(item):
    parts = lax.axis_size(FSDP)
    return lax.ppermute(item, FSDP, [(idx, idx ^ 1) for idx in range(parts)])


def send_up(item):
    parts = lax.axis_size(FSDP)
    return lax.ppermute(item, FSDP, [(idx, (idx + 2) % parts) for idx in range(parts)])


def swap_seq(item, mask):
    parts = lax.axis_size(SEQ)
    return lax.ppermute(item, SEQ, [(idx, idx ^ mask) for idx in range(parts)])


def pick(item, index, axis=0):
    return lax.dynamic_index_in_dim(item, index, axis, keepdims=False)


def swap_halves(item):
    lane = lax.broadcasted_iota(jnp.int32, item.shape, 1)
    half = HEAD_DIM // 2
    width = item.shape[1]
    ahead = pltpu.roll(item, width - half, 1)
    behind = pltpu.roll(item, half, 1)
    return jnp.where(lane % HEAD_DIM < half, ahead, behind)


NT = (((1,), (1,)), ((), ()))


def head_mask(item, head):
    lane = lax.broadcasted_iota(jnp.int32, item.shape, 1)
    return jnp.where(lane // HEAD_DIM == head, item, jnp.zeros_like(item))


class Places:
    def __init__(self):
        shard, seq = lax.axis_index(FSDP), lax.axis_index(SEQ)
        parts = lax.axis_size(FSDP)
        self.ring = parts // 2
        self.seq = seq
        self.chip, self.core = shard // 2, lax.rem(shard, 2)
        self.at_x, self.at_y = lax.rem(seq, 2), seq // 2
        self.near_x = 2 * self.at_y + 1 - self.at_x
        self.near_y = 2 * (1 - self.at_y) + self.at_x
        self.other = {FSDP: shard + 1 - 2 * self.core}
        self.up = {FSDP: lax.rem(shard + 2, parts)}
        self.down = {FSDP: lax.rem(shard + parts - 2, parts)}
        self.over_x = {SEQ: self.near_x}
        self.over_y = {SEQ: self.near_y}

    def back(self, hops):
        return lax.rem(self.chip - hops + self.ring, self.ring)


def remote(src, dst, send, recv, target):
    return pltpu.make_async_remote_copy(
        src_ref=src,
        dst_ref=dst,
        send_sem=send,
        recv_sem=recv,
        device_id=target,
        device_id_type=pl.DeviceIdType.MESH,
    )


def greet(targets, waits):
    barrier = pltpu.get_barrier_semaphore()
    for target in targets:
        pl.semaphore_signal(barrier, inc=1, device_id=target, device_id_type=pl.DeviceIdType.MESH)
    pl.semaphore_wait(barrier, waits)


def aligned(start, size, unit=None):
    return pl.ds(pl.multiple_of(start, unit or size), size)


def adam_kernel(
    kinds, ring, count, core_ref, factor_ref, *refs
):
    n_grads = len(refs) - 8
    grads = refs[:n_grads]
    master, first, second, grad_out, first_out, second_out, new_out, copy_out = refs[n_grads:]
    layer = pl.program_id(0)
    factor = factor_ref[0]
    scale = 1.0 / count
    columns = master.shape[2]
    per_layer = n_grads // 2
    width = columns // (kinds * ring * 2) if per_layer == 2 else 512

    def update(at, total):
        grad = total.astype(F32) * scale
        first_new, second_new, new = [], [], []
        first_new, second_new, new = adam_update(
            master[0, :, at], grad, first[0, :, at], second[0, :, at], factor
        )
        grad_out[0, :, at] = grad
        first_out[0, :, at] = first_new
        second_out[0, :, at] = second_new
        new_out[0, :, at] = new
        copy_out[0, :, at] = new.astype(BF)

    def choose(which, at):
        values = [grads[idx * per_layer + which][:, at] for idx in range(2)]
        return jnp.where(layer == 0, values[0], values[1])

    if per_layer == 1:
        for start in range(0, columns, width):
            update(slice(start, start + width), choose(0, slice(start, start + width)))
        return
    core = core_ref[0]
    for pair in range(ring):
        for kind in range(kinds):
            source = (pair * kinds + kind) * width
            mine, arrive = [choose(which, slice(source, source + width)) for which in range(2)]
            for which in range(2):
                start = (kind * ring * 2 + 2 * pair + which) * width
                update(slice(start, start + width), jnp.where(core == which, mine, arrive))


def adam_matrix(grads, master, first, second, factor, core, kinds, count):
    layers, rows, columns = master.shape
    ring = lax.axis_size(FSDP) // 2
    block = 64 if columns > 1024 else min(128, rows)
    steps = rows // block
    per_layer = len(grads) // layers

    def grad_spec(idx):
        layer, which = divmod(idx, per_layer)
        lift = steps if per_layer == 2 and which == 0 else 0

        def where(at_layer, step, core_ref, layer=layer, lift=lift):
            held = 0 if layer > 0 else steps - 1
            row = jnp.where(at_layer == layer, step, held)
            return (row + lift * core_ref[0], 0)

        return pl.BlockSpec((block, grads[idx].shape[1]), where)

    whole = pl.BlockSpec((1, block, columns), lambda layer, step, core_ref: (layer, step, 0))
    shape = jax.ShapeDtypeStruct(master.shape, F32)
    return pl.pallas_call(
        partial(adam_kernel, kinds, ring, count),
        grid_spec=pltpu.PrefetchScalarGridSpec(
            num_scalar_prefetch=1,
            grid=(layers, steps),
            in_specs=[pl.BlockSpec(memory_space=pltpu.SMEM)]
            + [grad_spec(idx) for idx in range(len(grads))]
            + [whole] * 3,
            out_specs=[whole] * 5,
        ),
        out_shape=[shape] * 4 + [jax.ShapeDtypeStruct(master.shape, BF)],
        compiler_params=pltpu.CompilerParams(vmem_limit_bytes=VMEM_LIMIT),
        cost_estimate=pl.CostEstimate(
            flops=20 * master.size, bytes_accessed=32 * master.size, transcendentals=master.size
        ),
        name="update",
    )(core.reshape(1).astype(jnp.int32), factor.reshape(1), *grads, master, first, second)


def norm_parts(hidden):
    center = hidden - jnp.mean(hidden, axis=-1, keepdims=True)
    spread = jnp.mean(center * center, axis=-1, keepdims=True)
    inverse = lax.rsqrt(spread + 1e-06)
    return center * inverse, inverse


def gelu_and_slope(upward):
    erf_part = 0.5 * (1.0 + lax.erf(upward * (1.0 / math.sqrt(2.0))))
    density = jnp.exp(-0.5 * upward * upward) * (1.0 / math.sqrt(2.0 * math.pi))
    return upward * erf_part, erf_part + upward * density


def dot(left, right):
    return jnp.dot(left, right, preferred_element_type=F32)


def dot_nt(left, right):
    return lax.dot_general(left, right, NT, preferred_element_type=F32)


def dot_tn(left, right):
    return lax.dot_general(left, right, (((0,), (0,)), ((), ())), preferred_element_type=F32)


def rotation_tables(packed):
    lane = lax.broadcasted_iota(jnp.int32, packed.shape, 1)
    first = lane % HEAD_DIM < HEAD_DIM // 2
    turned = pltpu.roll(packed, HEAD_DIM // 2, 1)
    return jnp.where(first, packed, turned), jnp.where(first, -turned, packed)


def each_block(count, body):
    @pl.loop(0, count)
    def _(step):
        body(aligned(step * ROWS_Q, ROWS_Q))


class Forward:
    def __init__(self, at, refs, layers):
        self.at, self.refs, self.layers = at, refs, layers
        self.blocks = refs.res.shape[0] // ROWS_Q
        self.pairs = refs.mixed.shape[1] // PAIR
        self.saves, self.loads, self.slot = [], [], 0
        self.mixed_copies, self.part_copies = {}, {}

    def save(self, src, dst):
        copy = pltpu.make_async_copy(src, dst, self.refs.save_sem.at[self.slot])
        self.slot += 1
        copy.start()
        self.saves.append(copy)
        return copy

    def settle(self):
        for copy in self.saves:
            copy.wait()
        self.saves = []

    def bring(self, pairs):
        for src, dst in pairs:
            copy = pltpu.make_async_copy(src, dst, self.refs.save_sem.at[self.slot])
            self.slot += 1
            copy.start()
            self.loads.append(copy)

    def arrive(self):
        for copy in self.loads:
            copy.wait()
        self.loads = []

    def vec(self, layer, row, width):
        return self.refs.vecs[layer, row : row + 1, 0:width]

    def unpack_vectors(self):
        refs, at = self.refs, self.at
        ring = at.ring
        per_shard = refs.vec_rows
        for layer in range(self.layers):
            places = [(row, row // 8, row % 8) for row in range(48)]
            for pair in range(ring):
                for kind in range(3):
                    places.append((48 + kind * 8 + 2 * pair + at.core, 6, pair * 3 + kind))
                for part in range(4):
                    places.append((72 + (2 * pair + at.core) * 4 + part, 7, pair * 4 + part))
            for source, row, block in places:
                shard, entry = source // per_shard, layer * per_shard + source % per_shard
                if not isinstance(source, int):
                    shard = lax.div(source, per_shard)
                    entry = layer * per_shard + lax.rem(source, per_shard)
                refs.vecs[layer, row : row + 1, block * 128 : (block + 1) * 128] = refs.vec_out[
                    shard, pl.ds(entry, 1), :
                ]

    def normed(self, rows, layer, first):
        hidden = self.refs.res[rows, :]
        scaled, _ = norm_parts(hidden)
        width = hidden.shape[1]
        return (scaled * self.vec(layer, first, width) + self.vec(layer, first + 1, width)).astype(BF)

    def load_qkv(self, weight):
        self.bring([(weight, self.refs.w_one.at[:, pl.ds(0, weight.shape[1])])])

    def load_proj(self, own, other):
        half, target = own.shape[0], self.refs.w_two
        self.bring([(own, target.at[pl.ds(0, half), :]), (other, target.at[pl.ds(half, half), :])])

    def load_units(self, up_weight, down_weight):
        self.bring([(up_weight, self.refs.w_one), (down_weight, self.refs.w_two)])

    def qkv(self, layer):
        refs = self.refs
        self.settle()
        self.arrive()

        def body(rows):
            normed = self.normed(rows, layer, 0)
            refs.norm[rows, :] = normed
            for pair in range(self.pairs):
                cols = slice(pair * 3 * PAIR, (pair + 1) * 3 * PAIR)
                block = dot(normed, refs.w_one[:, cols]) + refs.vecs[layer, 6:7, cols]
                cosine, sine = rotation_tables(refs.tables[rows, :])
                for kind in range(3):
                    part = block[:, kind * PAIR : (kind + 1) * PAIR]
                    if kind < 2:
                        part = part * cosine + swap_halves(part) * sine
                    start = pair * 3 * PAIR + kind * PAIR
                    refs.low[rows, start : start + PAIR] = part.astype(BF)

        each_block(self.blocks, body)
        self.save(refs.norm, refs.normed_out[layer])
        self.save(refs.low, refs.low_out[layer])

    def attend(self, layer, pair):
        refs = self.refs
        base = pair * 3 * PAIR
        key_cols, value_cols = [
            slice(base + kind * PAIR, base + (kind + 1) * PAIR) for kind in (1, 2)
        ]

        def body(rows):
            block = refs.low[rows, base : base + PAIR] * jnp.asarray(HEAD_DIM**-0.5, BF)
            outs = []
            for head in range(2):
                scores = dot_nt(head_mask(block, head), refs.low[:, key_cols])
                top = jnp.max(scores, axis=1, keepdims=True)
                exponent = jnp.exp(scores - top)
                total = jnp.sum(exponent, axis=1, keepdims=True)
                sums = jnp.broadcast_to(top + jnp.log(total), (ROWS_Q, PAIR)).T
                refs.lse_out[layer, pair, head : head + 1, rows] = sums[0:1]
                probs = (exponent * (1.0 / total)).astype(BF)
                outs.append(dot(probs, refs.low[:, value_cols]))
            lane = lax.broadcasted_iota(jnp.int32, outs[0].shape, 1)
            refs.mixed[rows, pair * PAIR : (pair + 1) * PAIR] = jnp.where(
                lane < HEAD_DIM, outs[0], outs[1]
            ).astype(BF)

        each_block(self.blocks, body)
        slot = layer * (self.pairs + 2) + pair
        cols = pl.ds(pair * PAIR, PAIR)
        copy = remote(
            refs.mixed.at[:, cols],
            refs.mixed_other.at[:, cols],
            refs.x_send.at[slot],
            refs.x_recv.at[slot],
            self.at.other,
        )
        copy.start()
        self.mixed_copies[layer, pair] = copy

    def project(self, layer):
        refs = self.refs
        half = refs.mixed.shape[1]
        self.arrive()
        self.settle()
        for pair in range(self.pairs):
            self.mixed_copies[layer, pair].wait()
        width = refs.res.shape[1]

        def body(rows):
            total = dot(refs.mixed[rows, :], refs.w_two[0:half, :])
            total = total + dot(refs.mixed_other[rows, :], refs.w_two[half : 2 * half, :])
            refs.res[rows, :] = refs.res[rows, :] + total + self.vec(layer, 4, width)
            refs.norm[rows, :] = self.normed(rows, layer, 2)

        each_block(self.blocks, body)
        self.save(refs.mixed, refs.mixed_out[layer])
        self.save(refs.res, refs.after_out[layer])
        self.save(refs.norm, refs.normed_two_out[layer])

    def hidden_units(self, layer, half):
        refs = self.refs
        if half == 0:
            self.settle()
            self.arrive()
        width = refs.res.shape[1]
        tiles = refs.w_one.shape[1] // 512
        blocks = self.blocks // 2

        @pl.loop(half * blocks, (half + 1) * blocks)
        def _(step):
            rows = aligned(step * ROWS_Q, ROWS_Q)

            @pl.loop(0, tiles)
            def _(tile):
                cols = aligned(tile * 512, 512)
                upward = dot(refs.norm[rows, :], refs.w_one[:, cols]) + refs.vecs[layer, 7:8, cols]
                active, slope = gelu_and_slope(upward)
                refs.act[rows, cols] = active.astype(BF)
                refs.slope[rows, cols] = slope.astype(BF)

            part = dot(refs.act[rows, :], refs.w_two[...])
            refs.res[rows, :] = refs.res[rows, :] + part + self.vec(layer, 5, width)
            refs.part[rows, :] = part.astype(BF)

        rows = pl.ds(half * blocks * ROWS_Q, blocks * ROWS_Q)
        slot = layer * (self.pairs + 2) + self.pairs + half
        copy = remote(
            refs.part.at[rows, :],
            refs.part_other.at[rows, :],
            refs.x_send.at[slot],
            refs.x_recv.at[slot],
            self.at.other,
        )
        copy.start()
        self.part_copies[layer, half] = copy
        if half == 1:
            self.save(refs.act, refs.active_out[layer])
            self.save(refs.slope, refs.slope_out[layer])

    def join(self, layer):
        refs = self.refs
        for half in range(2):
            self.part_copies[layer, half].wait()

        def body(rows):
            refs.res[rows, :] = refs.res[rows, :] + refs.part_other[rows, :].astype(F32)

        each_block(self.blocks, body)
        self.save(refs.res, refs.result_out[layer])


WEIGHTS = ("qkv", "proj", "up", "down")


def forward_kernel(names, layers, vec_rows, *operands):
    refs = SimpleNamespace(**dict(zip(names, operands)))
    for name in (*WEIGHTS, "proj_two", "normed", "low", "mixed", "after", "normed_two", "active", "slope", "result"):
        label = name + "_out"
        setattr(refs, label, [getattr(refs, label + str(layer)) for layer in range(layers)])
    refs.vec_rows = vec_rows
    at = Places()
    ring, seq, chip, core = at.ring, at.seq, at.chip, at.core
    full = {name: getattr(refs, name + "_full") for name in WEIGHTS}
    source = {name: getattr(refs, name + "_in") for name in WEIGHTS}
    slabs = {name: getattr(refs, name + "_slab") for name in WEIGHTS}
    outs = {name: getattr(refs, name + "_out") for name in WEIGHTS}
    items = [(name, layer) for layer in range(layers) for name in WEIGHTS]
    loads = {}

    def start_load(name, layer):
        copy = pltpu.make_async_copy(
            source[name].at[layer], full[name], refs.l_in.at[items.index((name, layer))]
        )
        copy.start()
        loads[name, layer] = copy

    for name in WEIGHTS:
        start_load(name, 0)
    barrier = pltpu.get_barrier_semaphore()
    for target in (at.other, at.up, at.down):
        pl.semaphore_signal(barrier, inc=1, device_id=target, device_id_type=pl.DeviceIdType.MESH)
    for step in range(1, 4):
        for half in range(2):
            pl.semaphore_signal(
                barrier,
                inc=1,
                device_id={FSDP: 2 * chip + half, SEQ: seq ^ step},
                device_id_type=pl.DeviceIdType.MESH,
            )
    pl.semaphore_wait(barrier, 9)

    length = refs.clip_in.shape[1]
    token_core = seq // 2
    token_rows = aligned(seq * length, length)
    stays = core == token_core

    class Move:
        def __init__(self, base, pairs):
            self.base, self.pairs, self.copies = base, pairs, []

        def start(self):
            for turn in range(2):
                target = {SEQ: 2 * core + turn, FSDP: 2 * chip + token_core}
                away = jnp.logical_not(jnp.logical_and(stays, lax.rem(seq, 2) == turn))
                copies = [
                    remote(
                        src.at[turn],
                        place(seq),
                        refs.m_send.at[self.base + 2 * turn + idx],
                        refs.m_recv.at[self.base + 2 * lax.rem(seq, 2) + idx],
                        target,
                    )
                    for idx, (src, place) in enumerate(self.pairs)
                ]
                self.copies.append((away, copies))

                @pl.when(away)
                def _(copies=copies):
                    for copy in copies:
                        copy.start()

            @pl.when(stays)
            def _():
                for idx, (src, place) in enumerate(self.pairs):
                    bounce = refs.clip_slab if idx == 0 else refs.table_slab
                    sem = refs.m_load.at[self.base // 6 * 2 + idx]
                    load = pltpu.make_async_copy(src.at[lax.rem(seq, 2)], bounce, sem)
                    load.start()
                    load.wait()
                    store = pltpu.make_async_copy(bounce, place(seq), sem)
                    store.start()
                    store.wait()

        def swap(self):
            for part in range(2):
                came = jnp.logical_not(jnp.logical_and(stays, lax.rem(seq, 2) == part))

                @pl.when(came)
                def _(part=part):
                    for idx, (src, place) in enumerate(self.pairs):
                        remote(
                            src.at[0],
                            place(2 * core + part),
                            refs.m_send.at[self.base],
                            refs.m_recv.at[self.base + 2 * part + idx],
                            at.other,
                        ).wait_recv()

            self.swaps = []
            for idx, (src, place) in enumerate(self.pairs):
                for part in range(2):
                    slot = 24 + self.base // 6 * 4 + 2 * idx + part
                    ref = place(2 * core + part)
                    self.swaps.append(
                        remote(ref, ref, refs.m_send.at[slot], refs.m_recv.at[slot], at.other)
                    )
            for copy in self.swaps:
                copy.start()

        def arrived(self):
            for copy in self.swaps:
                copy.wait_recv()

        def drain(self):
            for copy in self.swaps:
                copy.wait_send()
            for away, copies in self.copies:

                @pl.when(away)
                def _(copies=copies):
                    for copy in copies:
                        copy.wait_send()

    def chunk_of(ref):
        return lambda number: ref.at[aligned(number * length, length), :]

    tokens = Move(0, [(refs.clip_in, chunk_of(refs.clip_out)), (refs.table_in, chunk_of(refs.table_out))])
    cotangents = Move(6, [(refs.cot_in, chunk_of(refs.cot_out))])
    tokens.start()

    refs.vec_out[2 * chip + core] = refs.vec_in[...]
    vec_swap = remote(
        refs.vec_in, refs.vec_out.at[2 * chip + core], refs.m_send.at[16], refs.m_recv.at[16], at.other
    )
    vec_swap.start()
    vec_copies = [vec_swap]

    def vec_hop(hop):
        vec_copies[-1].wait_recv()
        ref = refs.vec_out.at[pl.ds(2 * at.back(hop), 2)]
        slot = 17 + hop
        copy = remote(ref, ref, refs.m_send.at[slot], refs.m_recv.at[slot], at.up)
        copy.start()
        vec_copies.append(copy)

    def place(name, layer, chip_at, part):
        slab = slabs[name].shape[1]
        if part is None:
            return outs[name][layer].at[aligned(chip_at * slab, slab), :]
        size = slab // 4
        return outs[name][layer].at[aligned(chip_at * slab + part * size, size), :]

    swaps, prepared, stores = {}, [], []

    def prepare():
        if len(prepared) == len(items):
            return
        idx = len(prepared)
        name, layer = items[idx]
        prepared.append(name)
        slab = slabs[name]
        loads[name, layer].wait()
        swaps[idx] = None
        if name in ("down", "proj"):
            slab[layer] = full[name][...].astype(BF)
        else:
            away, kinds = (refs.qkv_away, 3) if name == "qkv" else (refs.up_away, 1)
            half, columns = full[name].shape
            width = columns // (kinds * 2 * ring)
            rows = aligned(core * half, half)
            for pair in range(ring):
                for kind in range(kinds):
                    cols = slice((pair * kinds + kind) * width, (pair * kinds + kind + 1) * width)
                    for mine in (True, False):
                        which = core if mine else 1 - core
                        start = (kind * 2 * ring + 2 * pair + which) * width
                        block = full[name][:, aligned(start, width)].astype(BF)
                        if mine:
                            slab[layer, rows, cols] = block
                        else:
                            away[layer, :, cols] = block
            swaps[idx] = remote(
                away.at[layer],
                slab.at[layer, rows, :],
                refs.c_send.at[idx],
                refs.c_recv.at[idx],
                at.other,
            )
            swaps[idx].start()
        if layer + 1 < layers:
            start_load(name, layer + 1)

    hops = ring - 1
    order = []
    for first in range(0, len(items), 2):
        for hop in range(hops):
            order += [(first, hop), (first + 1, hop)]
    z_copies, plane, far, proj_swaps = {}, {}, {}, {}

    def begin(idx):
        name, layer = items[idx]
        if swaps[idx] is not None:
            swaps[idx].wait_recv()
        store = pltpu.make_async_copy(
            slabs[name].at[layer], place(name, layer, chip, None), refs.l_out.at[idx]
        )
        store.start()
        stores.append(store)

    def z_copy(idx, hop):
        name, layer = items[idx]
        part = None if name == "proj" else seq
        target = place(name, layer, at.back(hop), part)
        from_ref = target
        if hop == 0:
            from_ref = slabs[name].at[layer]
            if part is not None:
                size = slabs[name].shape[1] // 4
                from_ref = slabs[name].at[layer, aligned(seq * size, size), :]
        slot = idx * hops + hop
        copy = remote(from_ref, target, refs.z_send.at[slot], refs.z_recv.at[slot], at.up)
        copy.start()
        z_copies[idx, hop] = copy

    def plane_copies(idx, hop):
        name, layer = items[idx]
        ref = place(name, layer, at.back(hop + 1), seq)
        slot = 2 * (idx * hops + hop)
        plane[idx, hop] = [
            remote(ref, ref, refs.p_send.at[slot], refs.p_recv.at[slot], at.over_x),
            remote(ref, ref, refs.p_send.at[slot + 1], refs.p_recv.at[slot + 1], at.over_y),
        ]
        for copy in plane[idx, hop]:
            copy.start()

    def far_copies(idx, hop):
        name, layer = items[idx]
        slot = 2 * (idx * hops + hop)
        size = slabs[name].shape[1] // 4
        half = size // 2
        base = at.back(hop + 1) * 4 * size
        for copy in plane[idx, hop]:
            copy.wait_recv()
        made = []
        for turn, (origin, target) in enumerate(((at.near_y, at.over_x), (at.near_x, at.over_y))):
            ref = outs[name][layer].at[aligned(base + origin * size + turn * half, half), :]
            made.append(
                remote(ref, ref, refs.d_send.at[slot + turn], refs.d_recv.at[slot + turn], target)
            )
        far[idx, hop] = made
        for copy in made:
            copy.start()

    pending = []

    def flush(keep):
        while len(pending) > keep:
            far_copies(*pending.pop(0))

    def event(number):
        idx, hop = order[number]
        z_copies[idx, hop].wait_recv()
        if hop + 1 < hops:
            z_copy(idx, hop + 1)
        elif idx + 2 < len(items):
            begin(idx + 2)
            z_copy(idx + 2, 0)
        name, layer = items[idx]
        if name == "proj":
            flush(0)
            if hop + 1 == hops:
                stores[idx].wait()
                slot = len(items) + layer
                proj_swaps[layer] = remote(
                    outs["proj"][layer],
                    refs.proj_two_out[layer],
                    refs.c_send.at[slot],
                    refs.c_recv.at[slot],
                    at.other,
                )
                proj_swaps[layer].start()
        else:
            plane_copies(idx, hop)
            pending.append((idx, hop))
            flush(1)
        prepare()

    def complete(name, layer):
        idx = items.index((name, layer))
        if name == "proj":
            proj_swaps[layer].wait_recv()
            return
        stores[idx].wait()
        flush(0)
        for hop in range(hops):
            for copy in far[idx, hop]:
                copy.wait_recv()

    work = Forward(at, refs, layers)

    def take_tokens():
        tokens.arrived()
        vec_copies[-1].wait_recv()
        work.bring([(refs.clip_out, refs.res), (refs.table_out, refs.tables)])
        work.unpack_vectors()

    def load_qkv(layer):
        complete("qkv", layer)
        work.load_qkv(outs["qkv"][layer])

    def load_proj(layer):
        complete("proj", layer)
        work.load_proj(outs["proj"][layer], refs.proj_two_out[layer])

    def load_units(layer):
        complete("up", layer)
        complete("down", layer)
        work.load_units(outs["up"][layer], outs["down"][layer])

    prepare()
    prepare()
    begin(0)
    z_copy(0, 0)
    begin(1)
    z_copy(1, 0)
    prepare()
    prepare()
    per_layer = 4 * hops
    chunks = []
    for layer in range(layers):
        first = layer * per_layer + 2 * hops
        if layer == 0:
            chunks.append((first, take_tokens))
        chunks.append((first + 1, partial(load_qkv, layer)))
        chunks.append((first + 2, partial(work.qkv, layer)))
        chunks.append((first + 2, partial(load_proj, layer)))
        for pair in range(work.pairs):
            chunks.append((first + 2 + pair, partial(work.attend, layer, pair)))
        chunks.append((first + 7, partial(work.project, layer)))
        chunks.append((first + 7, partial(load_units, layer)))
        chunks.append((first + 8, partial(work.hidden_units, layer, 0)))
        chunks.append((first + 9, partial(work.hidden_units, layer, 1)))
        chunks.append((first + 10, partial(work.join, layer)))
    for number in range(len(order)):
        while chunks and chunks[0][0] <= number:
            chunks.pop(0)[1]()
        if number == 2:
            tokens.swap()
        if 3 <= number < 3 + hops:
            vec_hop(number - 3)
        if number == per_layer:
            cotangents.start()
        if number == per_layer + 6:
            cotangents.swap()
        event(number)
    flush(0)
    for _, chunk in chunks:
        chunk()

    work.settle()
    cotangents.arrived()
    for made in plane.values():
        for copy in made:
            copy.wait_send()
    for made in far.values():
        for copy in made:
            copy.wait_send()
    for copy in z_copies.values():
        copy.wait_send()
    for copy in swaps.values():
        if copy is not None:
            copy.wait_send()
    for copy in proj_swaps.values():
        copy.wait_send()
    for copy in vec_copies:
        copy.wait_send()
    tokens.drain()
    cotangents.drain()


def forward(qkv, up, down, proj, clips, cots, tables, vectors, vec_rows):
    layers, rows, width = proj.shape
    parts = lax.axis_size(FSDP)
    ring = parts // 2
    count, hops = 4 * layers, ring - 1
    length = 4 * clips.shape[1]
    down_rows = down.shape[1]
    qkv_half, up_half = qkv.shape[2] // 2, up.shape[2] // 2
    pairs = qkv_half // (3 * PAIR)
    inputs = dict(
        qkv_in=qkv, up_in=up, down_in=down, proj_in=proj, clip_in=clips, cot_in=cots,
        table_in=tables, vec_in=vectors,
    )
    outputs = {}
    for layer in range(layers):
        for name, shape, dtype in (
            ("qkv", (parts * rows, qkv_half), BF),
            ("up", (parts * rows, up_half), BF),
            ("down", (ring * down_rows, width), BF),
            ("proj", (ring * rows, width), BF),
            ("proj_two", (ring * rows, width), BF),
            ("normed", (length, width), BF),
            ("low", (length, qkv_half), BF),
            ("mixed", (length, pairs * PAIR), BF),
            ("after", (length, width), F32),
            ("normed_two", (length, width), BF),
            ("active", (length, up_half), BF),
            ("slope", (length, up_half), BF),
            ("result", (length, width), F32),
        ):
            outputs[name + "_out" + str(layer)] = (shape, dtype)
    outputs["clip_out"] = ((length, width), F32)
    outputs["cot_out"] = ((length, width), F32)
    outputs["table_out"] = ((length, PAIR), F32)
    outputs["vec_out"] = ((parts,) + vectors.shape, F32)
    outputs["vecs"] = ((layers, 8, up_half), F32)
    outputs["lse_out"] = ((layers, pairs, 8, length), F32)
    in_vmem = ("vec_in", "vec_out", "vecs", "lse_out")
    anywhere = pl.BlockSpec(memory_space=pl.ANY)
    vmem = pl.BlockSpec(memory_space=pltpu.VMEM)
    dma = pltpu.SemaphoreType.DMA
    scratch = dict(
        qkv_full=pltpu.VMEM(qkv.shape[1:], F32),
        up_full=pltpu.VMEM(up.shape[1:], F32),
        down_full=pltpu.VMEM(down.shape[1:], F32),
        proj_full=pltpu.VMEM(proj.shape[1:], F32),
        qkv_away=pltpu.VMEM((layers, rows, qkv_half), BF),
        up_away=pltpu.VMEM((layers, rows, up_half), BF),
        qkv_slab=pltpu.VMEM((layers, 2 * rows, qkv_half), BF),
        up_slab=pltpu.VMEM((layers, 2 * rows, up_half), BF),
        down_slab=pltpu.VMEM((layers, down_rows, width), BF),
        proj_slab=pltpu.VMEM((layers, rows, width), BF),
        clip_slab=pltpu.VMEM(clips.shape[1:], F32),
        table_slab=pltpu.VMEM(tables.shape[1:], F32),
        res=pltpu.VMEM((length, width), F32),
        tables=pltpu.VMEM((length, PAIR), F32),
        norm=pltpu.VMEM((length, width), BF),
        low=pltpu.VMEM((length, qkv_half), BF),
        mixed=pltpu.VMEM((length, pairs * PAIR), BF),
        mixed_other=pltpu.VMEM((length, pairs * PAIR), BF),
        w_one=pltpu.VMEM((width, up_half), BF),
        w_two=pltpu.VMEM((ring * down_rows, width), BF),
        act=pltpu.VMEM((length, up_half), BF),
        slope=pltpu.VMEM((length, up_half), BF),
        part=pltpu.VMEM((length, width), BF),
        part_other=pltpu.VMEM((length, width), BF),
        z_send=dma((count * hops,)), z_recv=dma((count * hops,)),
        p_send=dma((2 * count * hops,)), p_recv=dma((2 * count * hops,)),
        d_send=dma((2 * count * hops,)), d_recv=dma((2 * count * hops,)),
        c_send=dma((count + layers,)), c_recv=dma((count + layers,)),
        l_in=dma((count,)), l_out=dma((count,)),
        m_send=dma((32,)), m_recv=dma((32,)), m_load=dma((4,)),
        x_send=dma((layers * (pairs + 2),)), x_recv=dma((layers * (pairs + 2),)),
        save_sem=dma((16 * layers,)),
    )
    names = [*inputs, *outputs, *scratch]
    results = pl.pallas_call(
        partial(forward_kernel, names, layers, vec_rows),
        in_specs=[vmem if name in in_vmem else anywhere for name in inputs],
        out_specs=[vmem if name in in_vmem else anywhere for name in outputs],
        out_shape=[jax.ShapeDtypeStruct(*shape) for shape in outputs.values()],
        scratch_shapes=list(scratch.values()),
        compiler_params=pltpu.CompilerParams(
            collective_id=0, has_side_effects=True, vmem_limit_bytes=62 * 1024 * 1024
        ),
        cost_estimate=pl.CostEstimate(
            flops=60_000_000_000, bytes_accessed=600_000_000, transcendentals=0
        ),
        name="forward",
    )(*inputs.values())
    return SimpleNamespace(**dict(zip(outputs, results)))


def add_into(target, term):
    @pl.loop(0, target.shape[0] // ADD_ROWS)
    def _(step):
        at = aligned(step * ADD_ROWS, ADD_ROWS)
        target[at, :] = (target[at, :].astype(F32) + term[at, :].astype(F32)).astype(BF)


class Sems:
    def __init__(self, ref):
        self.ref, self.used = ref, 0

    def take(self):
        self.used += 1
        return self.ref.at[self.used - 1]


class Sum:
    def __init__(self, at, sems, refs, name, layer, z_first, x_first, compute):
        self.at, self.sems = at, sems
        self.own, self.one, self.two, self.three = [
            getattr(refs, name + part) for part in ("_own", "_one", "_two", "_three")
        ]
        self.stage = getattr(refs, name + "_stage" + str(layer))
        self.arrive = getattr(refs, name + "_arrive" + str(layer), None)
        self.z_first, self.x_first, self.compute = z_first, x_first, compute
        self.rows = self.two.shape[1]
        self.sends, self.slot_sends = [], [[], []]
        self.first, self.second, self.hop = {}, {}, {}
        self.swap = None

    def make(self, src, dst, target, slot=None):
        copy = remote(src, dst, self.sems[0].take(), self.sems[1].take(), target)
        copy.start()
        (self.sends if slot is None else self.slot_sends[slot]).append(copy)
        return copy

    def pieces(self, mine):
        at = self.at
        if self.x_first:
            side = at.at_x if mine else 1 - at.at_x
            return [(side, 1), (2 + side, 1)]
        return [(2 * (at.at_y if mine else 1 - at.at_y), 2)]

    def tile(self, tile):
        slot = tile % 2
        for copy in self.slot_sends[slot]:
            copy.wait_send()
        self.slot_sends[slot] = []
        self.compute(tile, self.own.at[slot])

    def start(self, tile):
        self.tile(tile)
        slot = tile % 2
        if self.z_first:
            self.hop[0] = self.make(self.own.at[slot], self.three.at[0], self.at.up, slot)
        else:
            self.plane_one(tile, self.own.at[slot], slot)

    def plane_one(self, tile, source, slot=None):
        target = self.at.over_x if self.x_first else self.at.over_y
        place, made = 0, []
        for first, count in self.pieces(False):
            size = count * self.rows
            made.append(
                self.make(
                    source.at[aligned(first * self.rows, size, self.rows), :],
                    self.one.at[tile, pl.ds(place, size), :],
                    target,
                    slot,
                )
            )
            place += size
        self.first[tile] = made

    def plane_two(self, tile, source):
        for copy in self.first[tile]:
            copy.wait_recv()
        place = 0
        for first, count in self.pieces(True):
            size = count * self.rows
            add_into(
                self.one.at[tile, pl.ds(place, size), :],
                source.at[aligned(first * self.rows, size, self.rows), :],
            )
            place += size
        at = self.at
        target, keep = (at.over_y, at.at_y) if self.x_first else (at.over_x, at.at_x)
        self.second[tile] = self.make(
            self.one.at[tile, aligned((1 - keep) * self.rows, self.rows), :],
            self.two.at[tile],
            target,
        )

    def plane_three(self, tile):
        keep = self.at.at_y if self.x_first else self.at.at_x
        self.second[tile].wait_recv()
        add_into(self.two.at[tile], self.one.at[tile, aligned(keep * self.rows, self.rows), :])

    def middle(self, tile):
        self.plane_two(tile, self.own.at[tile % 2])

    def finish(self, tile):
        self.plane_three(tile)
        if tile > 0:
            self.hop[tile - 1].wait_recv()
            add_into(self.two.at[tile], self.three.at[tile - 1])
        if tile < self.at.ring - 1:
            self.hop[tile] = self.make(self.two.at[tile], self.three.at[tile], self.at.up)
        else:
            self.gather()

    def ring_step(self, tile):
        self.tile(tile)
        self.hop[tile - 1].wait_recv()
        total = self.three.at[tile - 1]
        add_into(total, self.own.at[tile % 2])
        if tile == self.at.ring - 1:
            self.plane_one(0, total)
        else:
            self.hop[tile] = self.make(total, self.three.at[tile], self.at.up)

    def slab_middle(self):
        self.plane_two(0, self.three.at[self.at.ring - 2])

    def slab_finish(self):
        self.plane_three(0)
        self.gather()

    def total(self):
        return self.two.at[0 if self.z_first else self.at.ring - 1]

    def place(self, quarter, turn=0, size=None):
        size = size or self.rows
        return self.stage.at[aligned(quarter * self.rows + turn * size, size), :]

    def gather(self):
        at = self.at
        self.store = pltpu.make_async_copy(self.total(), self.place(at.seq), self.sems[2].take())
        self.store.start()
        self.near = [
            self.make(self.total(), self.place(at.seq), at.over_x),
            self.make(self.total(), self.place(at.seq), at.over_y),
        ]

    def gather_far(self):
        at = self.at
        for copy in self.near:
            copy.wait_recv()
        half = self.rows // 2
        self.far = []
        for turn, (origin, target) in enumerate(((at.near_y, at.over_x), (at.near_x, at.over_y))):
            ref = self.place(origin, turn, half)
            self.far.append(self.make(ref, ref, target))

    def gather_end(self):
        at = self.at
        self.store.wait()
        for copy in self.far:
            copy.wait_recv()
        if self.arrive is not None:
            half = 2 * self.rows
            self.swap = self.make(
                self.stage.at[aligned((1 - at.core) * half, half), :], self.arrive, at.other
            )

    def drain(self):
        if self.swap is not None:
            self.swap.wait_recv()
        for copy in self.sends + self.slot_sends[0] + self.slot_sends[1]:
            copy.wait_send()
        self.sends, self.slot_sends = [], [[], []]


class VectorSum:
    def __init__(self, at, sems, source, got, hop, total):
        self.at, self.sems = at, sems
        self.got, self.hop, self.total = got, hop, total
        self.copies, self.step = [], 0
        self.partners = (at.other, at.over_x, at.over_y)

    def send(self, src, dst, target):
        copy = remote(src, dst, self.sems[0].take(), self.sems[1].take(), target)
        copy.start()
        self.copies.append(copy)

    def advance(self):
        idx, at = self.step, self.at
        self.step += 1
        if idx == 0:
            self.send(self.total.at[0], self.got.at[0], self.partners[0])
            return
        self.copies[-1].wait_recv()
        if idx <= 3:
            self.total[idx] = self.total[idx - 1] + self.got[idx - 1]
            if idx < 3:
                self.send(self.total.at[idx], self.got.at[idx], self.partners[idx])
            else:
                self.send(self.total.at[3, at.back(1)], self.hop.at[0], at.up)
            return
        hop = idx - 3
        self.hop[hop - 1] = self.hop[hop - 1] + self.total[3, at.back(hop + 1)]
        if hop < at.ring - 1:
            self.send(self.hop.at[hop - 1], self.hop.at[hop], at.up)


class Backward:
    def __init__(self, at, refs, layers):
        self.at, self.refs, self.layers = at, refs, layers
        self.blocks = refs.grad.shape[0] // ROWS_Q
        self.pairs = refs.low.shape[1] // (3 * PAIR)
        self.slot = 0
        self.part_copies, self.loads = {}, {}

    def prefetch(self, key, pairs):
        self.loads[key] = self.bring(pairs)

    def arrive(self, key):
        for copy in self.loads.pop(key):
            copy.wait()

    def prefetch_units(self, layer, which):
        refs = self.refs
        targets = {"down": refs.w_one, "up": refs.w_two, "slope": refs.ups}
        for name in which:
            self.prefetch((name, layer), [(self.saved(name, layer), targets[name])])

    def bring(self, pairs):
        copies = []
        for src, dst in pairs:
            copies.append(pltpu.make_async_copy(src, dst, self.refs.load_sem.at[self.slot]))
            self.slot += 1
        for copy in copies:
            copy.start()
        return copies

    def saved(self, name, layer):
        return getattr(self.refs, name + "_in" + str(layer))

    def add_vec(self, row, value):
        total = jnp.sum(value, axis=0, keepdims=True)
        width = value.shape[1]
        self.refs.vgrad[row : row + 1, 0:width] = self.refs.vgrad[row : row + 1, 0:width] + total

    def send_part(self, key, landing):
        refs = self.refs
        slot = len(self.part_copies)
        copy = remote(
            refs.part, landing, refs.x_send.at[slot], refs.x_recv.at[slot], self.at.other
        )
        copy.start()
        self.part_copies[key] = copy

    def units(self, layer):
        refs = self.refs
        if layer == self.layers - 1:
            self.arrive(("cot", 0))
        for name in ("down", "slope", "up"):
            self.arrive((name, layer))
        refs.vgrad[...] = jnp.zeros_like(refs.vgrad)
        tiles = refs.w_one.shape[0] // 512

        def body(rows):
            grad = refs.grad[rows, :]
            self.add_vec(5, grad)
            refs.grad_low[rows, :] = grad.astype(BF)

            @pl.loop(0, tiles)
            def _(tile):
                cols = aligned(tile * 512, 512)
                value = dot_nt(refs.grad_low[rows, :], refs.w_one[cols, :])
                value = value * refs.ups[rows, cols].astype(F32)
                total = jnp.sum(value, axis=0, keepdims=True)
                refs.vgrad[7:8, cols] = refs.vgrad[7:8, cols] + total
                refs.ups[rows, cols] = value.astype(BF)

            part = dot_nt(refs.ups[rows, :], refs.w_two[...])
            refs.part_f[rows, :] = part
            refs.part[rows, :] = part.astype(BF)

        each_block(self.blocks, body)
        self.send_part((layer, 0), refs.got_one)
        weight = refs.w_one.at[pl.ds(0, refs.mixed_grad.shape[1]), :]
        self.prefetch(("proj", layer), [(self.saved("proj", layer), weight)])

    def vec(self, layer, row, width):
        return self.refs.vecs[layer, row : row + 1, 0:width]

    def norm_blocks(self, layer, first, landing, source, use):
        refs = self.refs

        def copy_of(step):
            slot = lax.rem(step, 2)
            rows = aligned(step * ROWS_Q, ROWS_Q)
            return pltpu.make_async_copy(
                source.at[rows, :], refs.aux.at[slot], refs.aux_sem.at[slot]
            )

        copy_of(0).start()

        @pl.loop(0, self.blocks)
        def _(step):
            @pl.when(step + 1 < self.blocks)
            def _():
                copy_of(step + 1).start()

            copy_of(step).wait()
            rows = aligned(step * ROWS_Q, ROWS_Q)
            use(rows, self.norm_back(rows, layer, first, landing, refs.aux[lax.rem(step, 2)]))

    def norm_back(self, rows, layer, first, landing, hidden):
        refs = self.refs
        width = refs.grad.shape[1]
        part = refs.part_f[rows, :] + landing[rows, :].astype(F32)
        scaled, inverse = norm_parts(hidden)
        entry = part * self.vec(layer, first, width)
        mean_one = jnp.mean(entry, axis=-1, keepdims=True)
        mean_two = jnp.mean(entry * scaled, axis=-1, keepdims=True)
        self.add_vec(first, part * scaled)
        self.add_vec(first + 1, part)
        grad = refs.grad[rows, :] + inverse * (entry - mean_one - scaled * mean_two)
        refs.grad[rows, :] = grad
        return grad

    def after(self, layer):
        refs = self.refs
        half = refs.mixed_grad.shape[1]
        self.prefetch(("low", layer), [(self.saved("low", layer), refs.low)])
        self.arrive(("proj", layer))
        self.part_copies[layer, 0].wait()

        def body(rows, grad):
            self.add_vec(4, grad)
            low = grad.astype(BF)
            refs.after_low[rows, :] = low
            refs.mixed_grad[rows, :] = dot_nt(low, refs.w_one[0:half, :]).astype(BF)

        self.norm_blocks(layer, 2, refs.got_one, self.saved("after", layer), body)
        weight = refs.w_two.at[:, pl.ds(0, refs.low.shape[1])]
        self.prefetch(("qkv", layer), [(self.saved("qkv", layer), weight)])
        if layer > 0:
            self.prefetch_units(layer - 1, ("down",))

    def attend(self, layer, pair):
        refs = self.refs
        if pair == 0:
            self.arrive(("low", layer))
        base = pair * 3 * PAIR
        query_cols, key_cols, value_cols = [
            slice(base + kind * PAIR, base + (kind + 1) * PAIR) for kind in range(3)
        ]
        refs.keys_t[...] = refs.low[:, key_cols].astype(F32).T.astype(BF)
        scale = HEAD_DIM**-0.5
        refs.dk[...] = jnp.zeros_like(refs.dk)
        refs.dv[...] = jnp.zeros_like(refs.dv)

        def body(rows):
            block = refs.low[rows, query_cols]
            dout = refs.mixed_grad[rows, pair * PAIR : (pair + 1) * PAIR]
            outs = []
            for head in range(2):
                mine, dmine = head_mask(block, head), head_mask(dout, head)
                scores = dot_nt(refs.low[:, key_cols], mine * jnp.asarray(scale, BF))
                probs = jnp.exp(scores - refs.lse_in[layer, pair, head : head + 1, rows])
                prob_grad = dot_nt(refs.low[:, value_cols], dmine)
                delta = jnp.sum(probs * prob_grad, axis=0, keepdims=True)
                score_low = (probs * (prob_grad - delta) * scale).astype(BF)
                refs.dv[...] += dot(probs.astype(BF), dmine)
                refs.dk[...] += dot(score_low, mine)
                outs.append(dot(refs.keys_t[head * HEAD_DIM : (head + 1) * HEAD_DIM], score_low))
            refs.dq[rows, :] = jnp.concatenate(outs, axis=0).T

        each_block(self.blocks, body)

        def last(rows):
            cosine, sine = rotation_tables(refs.tables[rows, :])

            def back(item):
                item = item.astype(BF).astype(F32)
                return item * cosine - swap_halves(item) * sine

            parts = (
                back(refs.dq[rows, :]),
                back(refs.dk[rows, :]),
                refs.dv[rows, :].astype(BF).astype(F32),
            )
            for kind, part in enumerate(parts):
                cols = slice(base + kind * PAIR, base + (kind + 1) * PAIR)
                refs.vgrad[6:7, cols] = refs.vgrad[6:7, cols] + jnp.sum(part, axis=0, keepdims=True)
                refs.low[rows, cols] = part.astype(BF)

        each_block(self.blocks, last)

    def heads(self, layer):
        refs = self.refs
        width = refs.low.shape[1]
        self.arrive(("qkv", layer))

        def body(rows):
            part = dot_nt(refs.low[rows, :], refs.w_two[:, 0:width])
            refs.part_f[rows, :] = part
            refs.part[rows, :] = part.astype(BF)

        each_block(self.blocks, body)
        self.send_part((layer, 1), refs.got_two)
        if layer > 0:
            self.prefetch_units(layer - 1, ("up", "slope"))

    def entry(self, layer):
        refs = self.refs
        self.part_copies[layer, 1].wait()
        source = self.saved("entry", layer)
        self.norm_blocks(layer, 0, refs.got_two, source, lambda rows, grad: None)

    def weight_tile(self, name, layer):
        refs = self.refs
        stream = getattr(refs, name + "_stream")
        source, right = {
            "down": ("active", refs.grad_low),
            "up": ("normed_two", refs.ups),
            "proj": ("mixed", refs.after_low),
            "qkv": ("normed", refs.low),
        }[name]
        def fetch(tile, layer):
            rows = stream.shape[1]
            cols = aligned(self.at.back(tile + 1) * rows, rows)
            self.prefetch((name, "tile"), [(self.saved(source, layer).at[:, cols], stream)])

        def compute(tile, out):
            rows, columns = out.shape
            if (name, "tile") not in self.loads:
                fetch(tile, layer)
            self.arrive((name, "tile"))
            high, wide = min(rows, 256), min(columns, 512)

            @pl.loop(0, rows // high)
            def _(row):
                at_rows = aligned(row * high, high)

                @pl.loop(0, columns // wide)
                def _(column):
                    cols = aligned(column * wide, wide)
                    out[at_rows, cols] = dot_tn(stream[:, at_rows], right[:, cols]).astype(BF)

            if tile + 1 < self.at.ring:
                fetch(tile + 1, layer)
            elif layer > 0:
                fetch(0, layer - 1)

        return compute

    def vector_rows(self, target):
        refs, at = self.refs, self.at
        target[...] = jnp.zeros_like(target)
        per_chip = refs.vec_rows * 2
        keep = (at.core == 0).astype(F32)
        for row in range(48):
            source = refs.vgrad[row // 8 : row // 8 + 1, row % 8 * 128 : (row % 8 + 1) * 128]
            place = row % per_chip
            target[row // per_chip, place : place + 1, :] = source * keep
        places = []
        for pair in range(at.ring):
            for kind in range(3):
                places.append((48 + kind * 8 + 2 * pair + at.core, 6, pair * 3 + kind))
            for part in range(4):
                places.append((72 + (2 * pair + at.core) * 4 + part, 7, pair * 4 + part))
        for place, row, block in places:
            target[lax.div(place, per_chip), pl.ds(lax.rem(place, per_chip), 1), :] = refs.vgrad[
                row : row + 1, block * 128 : (block + 1) * 128
            ]


def squares_of(ref):
    rows, columns = ref.shape

    def body(step, total):
        part = ref[aligned(step * 16, 16), :].astype(F32)
        part = part * part
        part = part[0:8] + part[8:16]
        for column in range(0, columns, 128):
            total = total + part[:, column : column + 128]
        return total

    return lax.fori_loop(0, rows // 16, body, jnp.zeros((8, 128), F32))


def backward_kernel(names, layers, vec_rows, *operands):
    refs = SimpleNamespace(**dict(zip(names, operands)))
    refs.vec_rows = vec_rows
    at = Places()
    ring = at.ring
    sems = (Sems(refs.send_sem), Sems(refs.recv_sem), Sems(refs.store_sem))
    greet((at.other, at.over_x, at.over_y, at.down), 4)
    work = Backward(at, refs, layers)
    work.prefetch(("cot", 0), [(refs.cot_in, refs.grad)])
    work.prefetch_units(layers - 1, ("down", "slope", "up"))
    sums = {}
    for layer in range(layers):
        for name, z_first, x_first in (
            ("qkv", True, True),
            ("proj", True, False),
            ("up", False, True),
            ("down", False, False),
        ):
            sums[name, layer] = Sum(
                at, sems, refs, name, layer, z_first, x_first, work.weight_tile(name, layer)
            )
    vectors = [
        VectorSum(at, sems, None, refs.vec_got.at[layer], refs.vec_hop.at[layer], refs.vec_sum.at[layer])
        for layer in range(layers)
    ]
    refs.square_sum[0] = jnp.zeros((8, 128), F32)
    steps = []

    def free(sem):
        for target in (at.over_x, at.over_y, at.down):
            pl.semaphore_signal(sem, inc=1, device_id=target, device_id_type=pl.DeviceIdType.MESH)

    def wide_steps(layer):
        items = [sums["down", layer], sums["up", layer]]

        def turn(tile):
            for item in items:
                item.middle(tile)
            if tile + 2 < ring:
                for item in items:
                    item.start(tile + 2)
            if tile > 0:
                for item in items:
                    item.finish(tile - 1)

        def begin(tile):
            if tile == 0 and layer + 1 < layers:
                pl.semaphore_wait(refs.free_wide, 3)
            for item in items:
                item.start(tile)

        def end():
            for item in items:
                item.finish(ring - 1)

        def far():
            for item in items:
                item.gather_far()

        def close():
            for item in items:
                item.gather_end()
                refs.square_sum[0] = refs.square_sum[0] + squares_of(item.total())
            if layer > 0:
                for item in items:
                    item.drain()
                free(refs.free_wide)

        turns = [partial(begin, 0), partial(begin, 1)]
        turns += [partial(turn, tile) for tile in range(ring)]
        return turns + [end, far, close]

    def slab_steps(name, layer):
        item = sums[name, layer]

        def begin():
            item.start(0)

        def close():
            item.gather_end()
            refs.square_sum[0] = refs.square_sum[0] + squares_of(item.total())
            if layer > 0:
                item.drain()

        turns = [begin] + [partial(item.ring_step, tile) for tile in range(1, ring)]
        return turns + [item.slab_middle, item.slab_finish, item.gather_far, close]

    def run(steps, count=1):
        for _ in range(count):
            if steps:
                steps.pop(0)()

    late = []
    for layer in reversed(range(layers)):
        last = layer == 0
        wide, proj, qkv = wide_steps(layer), slab_steps("proj", layer), slab_steps("qkv", layer)
        work.units(layer)
        run(late, 3)
        run(wide, 2)
        run(late, 2)
        work.after(layer)
        run(late, 2)
        if layer + 1 == layers:
            run(proj)
        for pair in range(work.pairs):
            work.attend(layer, pair)
            run(wide)
            run(late, 3)
            if layer + 1 == layers and pair > 0:
                run(proj)
        while late:
            run(late)
        if layer + 1 < layers:
            free(refs.free_slab)
            pl.semaphore_wait(refs.free_slab, 3)
            run(proj)
        work.heads(layer)
        run(wide)
        run(proj)
        run(qkv)
        work.entry(layer)
        if last:
            save = pltpu.make_async_copy(refs.grad, refs.input_grad, sems[2].take())
            save.start()
        work.vector_rows(refs.vec_sum.at[layer, 0])
        run(qkv)
        run(wide)
        run(proj)
        vector = [vectors[layer].advance] * 7
        while proj or qkv or vector:
            late += wide[:1] + qkv[:1] + proj[:1] + vector[:1]
            qkv, proj, vector, wide = qkv[1:], proj[1:], vector[1:], wide[1:]
        late = late + wide
        wide = []
    while late:
        run(late)
    save.wait()
    total = refs.square_sum[0]
    for layer in range(layers):
        vec_total = refs.vec_hop[layer, ring - 2]
        refs.vec_out[layer] = vec_total
        part = vec_total * vec_total * 0.125
        for row in range(0, part.shape[0], 8):
            total = total + part[row : row + 8]
    refs.square_sum[0] = total
    copies = []

    def square_copy(src, dst, target):
        copy = remote(src, dst, sems[0].take(), sems[1].take(), target)
        copy.start()
        copies.append(copy)
        copy.wait_recv()

    for idx, target in enumerate((at.other, at.over_x, at.over_y)):
        square_copy(refs.square_sum.at[idx], refs.square_got.at[idx], target)
        refs.square_sum[idx + 1] = refs.square_sum[idx] + refs.square_got[idx]
    total = refs.square_sum[3]
    for hop in range(ring - 1):
        source = refs.square_sum.at[3] if hop == 0 else refs.square_got.at[2 + hop]
        square_copy(source, refs.square_got.at[3 + hop], at.up)
        total = total + refs.square_got[3 + hop]
    refs.square_out[...] = total
    for name in WEIGHTS:
        sums[name, 0].drain()
    for vector in vectors:
        for copy in vector.copies:
            copy.wait_send()
    for copy in copies:
        copy.wait_send()


def backward(kept, layers, vec_rows):
    ring = lax.axis_size(FSDP) // 2
    length, width = kept.cot_out.shape
    qkv_half, up_half = kept.low_out0.shape[1], kept.slope_out0.shape[1]
    half = kept.mixed_out0.shape[1]
    inputs = dict(
        cot_in=kept.cot_out,
        tables=kept.table_out,
        vecs=kept.vecs,
        lse_in=kept.lse_out,
    )
    for layer in range(layers):
        for name in (*WEIGHTS, "normed", "low", "mixed", "after", "normed_two", "active", "slope"):
            inputs[name + "_in" + str(layer)] = getattr(kept, name + "_out" + str(layer))
        entry = kept.clip_out if layer == 0 else getattr(kept, "result_out" + str(layer - 1))
        inputs["entry_in" + str(layer)] = entry
    slabs = dict(
        qkv=(width // ring, qkv_half),
        proj=(half // ring, width),
        up=(width // ring, up_half),
        down=(up_half // ring, width),
    )
    outputs, scratch = {}, {}
    dma, regular = pltpu.SemaphoreType.DMA, pltpu.SemaphoreType.REGULAR
    for name, (rows, columns) in slabs.items():
        for layer in range(layers):
            outputs[name + "_stage" + str(layer)] = ((rows, columns), BF)
            if name in ("qkv", "up"):
                outputs[name + "_arrive" + str(layer)] = ((rows // 2, columns), BF)
        z_first = name in ("qkv", "proj")
        tiles, quarter = 1 if z_first else ring, rows // 4
        scratch[name + "_stream"] = pltpu.VMEM((length, rows), BF)
        scratch[name + "_own"] = pltpu.VMEM((2, rows, columns), BF)
        scratch[name + "_one"] = pltpu.VMEM((tiles, 2 * quarter, columns), BF)
        scratch[name + "_two"] = pltpu.VMEM((tiles, quarter, columns), BF)
        scratch[name + "_three"] = pltpu.VMEM(
            (ring - 1, rows if z_first else quarter, columns), BF
        )
    outputs["input_grad"] = ((length, width), F32)
    outputs["vec_out"] = ((layers, 32, 128), F32)
    outputs["square_out"] = ((8, 128), F32)
    scratch |= dict(
        grad=pltpu.VMEM((length, width), F32),
        aux=pltpu.VMEM((2, ROWS_Q, width), F32),
        aux_sem=dma((2,)),
        part_f=pltpu.VMEM((length, width), F32),
        grad_low=pltpu.VMEM((length, width), BF),
        after_low=pltpu.VMEM((length, width), BF),
        part=pltpu.VMEM((length, width), BF),
        got_one=pltpu.VMEM((length, width), BF),
        got_two=pltpu.VMEM((length, width), BF),
        ups=pltpu.VMEM((length, up_half), BF),
        w_one=pltpu.VMEM((up_half, width), BF),
        w_two=pltpu.VMEM((width, up_half), BF),
        low=pltpu.VMEM((length, qkv_half), BF),
        mixed_grad=pltpu.VMEM((length, half), BF),
        keys_t=pltpu.VMEM((PAIR, length), BF),
        dq=pltpu.VMEM((length, PAIR), F32),
        dk=pltpu.VMEM((length, PAIR), F32),
        dv=pltpu.VMEM((length, PAIR), F32),
        vgrad=pltpu.VMEM((8, up_half), F32),
        vec_got=pltpu.VMEM((layers, 3, ring, 32, 128), F32),
        vec_hop=pltpu.VMEM((layers, ring - 1, 32, 128), F32),
        vec_sum=pltpu.VMEM((layers, 4, ring, 32, 128), F32),
        square_got=pltpu.VMEM((3 + ring - 1, 8, 128), F32),
        square_sum=pltpu.VMEM((4, 8, 128), F32),
        send_sem=dma((120 * layers,)),
        recv_sem=dma((120 * layers,)),
        store_sem=dma((8 * layers,)),
        load_sem=dma((32 * layers,)),
        x_send=dma((2 * layers,)),
        x_recv=dma((2 * layers,)),
        free_wide=regular,
        free_slab=regular,
    )
    in_vmem = ("tables", "vecs", "lse_in", "vec_out", "square_out")
    anywhere = pl.BlockSpec(memory_space=pl.ANY)
    vmem = pl.BlockSpec(memory_space=pltpu.VMEM)
    names = [*inputs, *outputs, *scratch]
    results = pl.pallas_call(
        partial(backward_kernel, names, layers, vec_rows),
        in_specs=[vmem if name in in_vmem else anywhere for name in inputs],
        out_specs=[vmem if name in in_vmem else anywhere for name in outputs],
        out_shape=[jax.ShapeDtypeStruct(*shape) for shape in outputs.values()],
        scratch_shapes=list(scratch.values()),
        compiler_params=pltpu.CompilerParams(
            collective_id=1, has_side_effects=True, vmem_limit_bytes=63 * 1024 * 1024
        ),
        cost_estimate=pl.CostEstimate(
            flops=100_000_000_000, bytes_accessed=600_000_000, transcendentals=0
        ),
        name="backward",
    )(*inputs.values())
    return SimpleNamespace(**dict(zip(outputs, results)))


def fast_device(
    clip_tokens,
    patch_coords,
    out_cotangent,
    vector_params,
    qkv_weight,
    proj_weight,
    up_weight,
    down_weight,
    first_vector,
    first_qkv,
    first_proj,
    first_up,
    first_down,
    second_vector,
    second_qkv,
    second_proj,
    second_up,
    second_down,
):
    masters = (vector_params, qkv_weight, proj_weight, up_weight, down_weight)
    firsts = (first_vector, first_qkv, first_proj, first_up, first_down)
    seconds = (second_vector, second_qkv, second_proj, second_up, second_down)
    layer_count = vector_params.shape[0]
    batch_local, chunk_len = clip_tokens.shape[:2]
    seq_parts = lax.axis_size(SEQ)
    parts = lax.axis_size(FSDP)
    ring = parts // 2
    seq = lax.axis_index(SEQ)
    shard = lax.axis_index(FSDP)
    core = lax.rem(shard, 2)
    even = lax.rem(seq, 2) == 0

    def from_clips(item):
        mine = pick(item.reshape((2, 2, chunk_len) + item.shape[1:]), core)
        pieces = [None, None]
        for turn in range(2):
            piece = jnp.where(even, mine[turn], mine[1 - turn])
            pairs = []
            for src_seq in range(seq_parts):
                for src in range(parts):
                    dst_seq = 2 * (src % 2) + (src_seq + turn) % 2
                    dst = src - src % 2 + src_seq // 2
                    pairs.append((dst_seq * parts + dst, src_seq * parts + src))
            pieces[turn] = lax.ppermute(piece, (SEQ, FSDP), pairs)
        return jnp.where(
            even, jnp.stack([pieces[0], pieces[1]]), jnp.stack([pieces[1], pieces[0]])
        )

    tables = []
    for idx in range(batch_local):
        cosine, sine = rotary_tables(patch_coords[:, idx], HEAD_DIM // 2)
        tables.append(jnp.concatenate([cosine, sine, cosine, sine], axis=1))
    share = vector_params.shape[1]
    vector_rows = vector_params.astype(BF).astype(F32).reshape(-1, 128)
    vector_rows = jnp.pad(vector_rows, ((0, -vector_rows.shape[0] % 8), (0, 0)))
    kept = forward(
        qkv_weight,
        up_weight,
        down_weight,
        proj_weight,
        clip_tokens,
        out_cotangent,
        jnp.stack(tables),
        vector_rows,
        share // 128,
    )
    block_output = from_clips(getattr(kept, "result_out" + str(layer_count - 1)))

    back = backward(kept, layer_count, share // 128)
    input_grad = from_clips(back.input_grad)

    clip_count = batch_local * parts
    norm_value = jnp.sqrt(jnp.sum(back.square_out)) / clip_count
    param_count = sum(master.size for master in masters) * parts
    factor = jnp.minimum(1.0, CLIP_RATIO * math.sqrt(float(param_count)) / (norm_value + 1e-06))

    vector_total = back.vec_out.reshape(layer_count, -1)[:, : 2 * share]
    vector_grad = lax.dynamic_slice_in_dim(vector_total, core * share, share, 1) / clip_count
    vector_new = adam_update(vector_params, vector_grad, first_vector, second_vector, factor)
    updates = [(vector_grad, *vector_new, vector_new[2].astype(BF))]
    for kind, name in enumerate(WEIGHTS):
        parts_of = ("_stage", "_arrive") if name in ("qkv", "up") else ("_stage",)
        updates.append(
            adam_matrix(
                [
                    getattr(back, name + part + str(layer))
                    for layer in range(layer_count)
                    for part in parts_of
                ],
                masters[kind + 1],
                firsts[kind + 1],
                seconds[kind + 1],
                factor,
                core,
                3 if kind == 0 else 1,
                clip_count,
            )
        )
    return (
        block_output,
        input_grad,
        *[item[0] for item in updates],
        norm_value.reshape(1),
        *[item[1] for item in updates],
        *[item[2] for item in updates],
        *[item[3] for item in updates],
        *[item[4] for item in updates],
    )


def solution(mesh):
    in_specs = (
        P(FSDP, SEQ, None),
        P(None, FSDP, SEQ),
        P(FSDP, SEQ, None),
        P(None, FSDP),
        P(None, FSDP, None),
        P(None, FSDP, None),
        P(None, FSDP, None),
        P(None, FSDP, None),
        P(None, FSDP),
        P(None, FSDP, None),
        P(None, FSDP, None),
        P(None, FSDP, None),
        P(None, FSDP, None),
        P(None, FSDP),
        P(None, FSDP, None),
        P(None, FSDP, None),
        P(None, FSDP, None),
        P(None, FSDP, None),
    )
    out_specs = (
        P(FSDP, SEQ, None),
        P(FSDP, SEQ, None),
        P(None, FSDP),
        P(None, FSDP, None),
        P(None, FSDP, None),
        P(None, FSDP, None),
        P(None, FSDP, None),
        P(),
        P(None, FSDP),
        P(None, FSDP, None),
        P(None, FSDP, None),
        P(None, FSDP, None),
        P(None, FSDP, None),
        P(None, FSDP),
        P(None, FSDP, None),
        P(None, FSDP, None),
        P(None, FSDP, None),
        P(None, FSDP, None),
        P(None, FSDP),
        P(None, FSDP, None),
        P(None, FSDP, None),
        P(None, FSDP, None),
        P(None, FSDP, None),
        P(None, FSDP),
        P(None, FSDP, None),
        P(None, FSDP, None),
        P(None, FSDP, None),
        P(None, FSDP, None),
    )
    body = fast_device if fits_fast(mesh) else general_device
    return jax.shard_map(
        body, mesh=mesh, in_specs=in_specs, out_specs=out_specs, check_vma=False
    )
```
